32 devices in a mesh: gx: 2 (over core), gy: 4 (over y, x), gz: 4 (over z).
Axes of the slice: x: 2, y: 2, z: 4, core: 2. Of those that a mesh axis runs over, the one named last changes fastest.
Arguments:
- field: float32 [128, 128, 2048], P('gz', 'gx', 'gy'), may hold values from -6 to 6
Outputs:
- coeffs: float32 [128, 128, 2048], P('gz', 'gx', 'gy')
The draws below stay inside these ranges and needn't reach their ends.
All inputs are finite; a program needn't handle non-finite values.
Results may differ from the reference program's by a relative error of at most 0.000075.
Values sent between devices are 32-bit elements; how exact they have to be, the bound alone decides.
No kernel may reach another device: no remote copies, remote signals or barrier semaphores. Data moves between devices by JAX's collectives and lax.ppermute only.
A program may use at most 128 MiB of HBM per device.

```python
import jax
import jax.numpy as jnp
from jax import lax

NZ = 128
NX = 128
NY = 2048


def block_scale(stream_key, extent, split, smallest, top_value):
    def one(position, parts):
        heights = jax.random.uniform(jax.random.fold_in(jax.random.fold_in(stream_key, 6), position), (parts,), jnp.float32, smallest / len(split), top_value / len(split))
        return jnp.repeat(jnp.exp(heights), extent[position] // parts).reshape((-1,) + (1,) * (len(extent) - position - 1))

    loudness = one(*split[0])
    for cut in split[1:]:
        loudness = loudness * one(*cut)
    return loudness


def scatter_about(own_key, shape, width, limit, pieces=(), kind=jnp.bfloat16):
    level = block_scale(own_key, shape, pieces, -0.22, 0.18) if pieces else 1.0
    result = jax.random.normal(own_key, shape, jnp.float32) * width * level
    return jnp.minimum(jnp.maximum(result, -limit), limit).astype(kind)


def setup_inputs(seed: int = 0) -> dict:
    streams_of = jax.random.split(jax.random.key(seed), 2)
    field = scatter_about(streams_of[0], (NZ, NX, NY), 1.0, 6.0, ((0, 4), (1, 2), (2, 4)), jnp.float32)
    return dict(field=field)


lift_alpha = -1.586134342
lift_beta = -0.05298011854
lift_gamma = 0.8829110762
lift_delta = 0.4435068522
lift_zeta = 1.149604398


def cut_range(values, first_index, last_index, which_dim):
    return lax.slice_in_dim(values, first_index, last_index, axis=which_dim)


def lift_pairs(even_part, odd_part, which_dim):
    pair_count = even_part.shape[which_dim]
    first_odd = cut_range(odd_part, 0, pair_count - 1, which_dim) + lift_alpha * (cut_range(even_part, 0, pair_count - 1, which_dim) + cut_range(even_part, 1, pair_count, which_dim))
    first_even = cut_range(even_part, 1, pair_count - 1, which_dim) + lift_beta * (cut_range(first_odd, 0, pair_count - 2, which_dim) + cut_range(first_odd, 1, pair_count - 1, which_dim))
    second_odd = cut_range(first_odd, 1, pair_count - 2, which_dim) + lift_gamma * (cut_range(first_even, 0, pair_count - 3, which_dim) + cut_range(first_even, 1, pair_count - 2, which_dim))
    second_even = cut_range(first_even, 1, pair_count - 3, which_dim) + lift_delta * (cut_range(second_odd, 0, pair_count - 4, which_dim) + cut_range(second_odd, 1, pair_count - 3, which_dim))
    return second_even * lift_zeta, cut_range(second_odd, 1, pair_count - 3, which_dim) / lift_zeta


def lift_along(volume, which_dim):
    length = volume.shape[which_dim]
    extended = jnp.concatenate([cut_range(volume, length - 4, length, which_dim), volume, cut_range(volume, 0, 4, which_dim)], axis=which_dim)
    even_part = lax.slice_in_dim(extended, 0, length + 8, stride=2, axis=which_dim)
    odd_part = lax.slice_in_dim(extended, 1, length + 8, stride=2, axis=which_dim)
    low_part, high_part = lift_pairs(even_part, odd_part, which_dim)
    return jnp.stack([low_part, high_part], axis=which_dim + 1).reshape(volume.shape)


def one_level(volume):
    volume = lift_along(volume, 1)
    volume = lift_along(volume, 2)
    return lift_along(volume, 0)


def reference(field):
    level_one = one_level(field)
    level_two = one_level(level_one[::2, ::2, ::2])
    level_three = one_level(level_two[::2, ::2, ::2])
    level_two = level_two.at[::2, ::2, ::2].set(level_three)
    return level_one.at[::2, ::2, ::2].set(level_two)
```

```python
import functools

import jax
import jax.numpy as jnp
import ml_dtypes
import numpy as np
from jax import lax
from jax.experimental import pallas as pl
from jax.experimental.pallas import tpu as pltpu
from jax.sharding import PartitionSpec as P

lift_alpha = -1.586134342
lift_beta = -0.05298011854
lift_gamma = 0.8829110762
lift_delta = 0.4435068522
lift_zeta = 1.149604398

BF = jnp.bfloat16
F32 = jnp.float32
MIB = 1024 * 1024


def periodic_lift(u):
    s, d = u[0::2].copy(), u[1::2].copy()
    d = d + lift_alpha * (s + np.roll(s, -1, 0))
    s = s + lift_beta * (np.roll(d, 1, 0) + d)
    d = d + lift_gamma * (s + np.roll(s, -1, 0))
    s = s + lift_delta * (np.roll(d, 1, 0) + d)
    out = np.empty_like(u)
    out[0::2] = s * lift_zeta
    out[1::2] = d / lift_zeta
    return out


@functools.lru_cache(None)
def blocks(n):
    current = np.eye(4 * n)
    found = []
    for level in range(3):
        full = periodic_lift(current)
        m = n >> level
        rows = full[m : 2 * m]
        found.append((rows[:, n : 2 * n], rows[:, :n], rows[:, 2 * n : 3 * n]))
        current = full[0::2]
    return found


def row_space(outer, rank):
    _, sizes, basis = np.linalg.svd(outer, full_matrices=False)
    assert sizes[rank:].max() < 1e-10
    basis = basis[:rank].copy()
    basis[np.abs(basis) < 1e-12] = 0.0
    return basis


LEFT_RANKS = (2, 3, 4)
RIGHT_RANKS = (2, 3, 3)


@functools.lru_cache(None)
def sides(n):
    out = []
    for level, (main, left, right) in enumerate(blocks(n)):
        cl = row_space(left, LEFT_RANKS[level])
        cr = row_space(right, RIGHT_RANKS[level])
        out.append((main, cl, left @ cl.T, cr, right @ cr.T))
    return out


@functools.lru_cache(None)
def joint_sides(n):
    found = blocks(n)
    cl = row_space(np.concatenate([b[1] for b in found]), 6)
    cr = row_space(np.concatenate([b[2] for b in found]), 6)
    maps = [(b[0], b[1] @ cl.T, b[2] @ cr.T) for b in found]
    return cl, cr, maps


def hi_lo(table):
    table = np.asarray(table, np.float32)
    hi = table.astype(ml_dtypes.bfloat16)
    lo = (table - hi.astype(np.float32)).astype(ml_dtypes.bfloat16)
    return hi, lo


def stack_lhs(table):
    hi, lo = hi_lo(table)
    return np.concatenate([hi, lo, hi], axis=1)


def stack_rhs(table):
    hi, lo = hi_lo(table)
    return np.concatenate([hi, hi, lo], axis=0)


def split(values):
    hi = values.astype(BF)
    return hi, (values - hi.astype(F32)).astype(BF)


def dot(a, b):
    return lax.dot_general(a, b, (((1,), (0,)), ((), ())), preferred_element_type=F32)


def dot_t(a, b):
    return lax.dot_general(a, b, (((1,), (1,)), ((), ())), preferred_element_type=F32)


def spread_columns(table, step, width):
    out = np.zeros((table.shape[0], width))
    out[:, ::step] = table
    return out


VM = pl.BlockSpec(memory_space=pltpu.VMEM)


def vmem(shape, dtype=F32):
    return pltpu.VMEM(shape, dtype)


def params(mib):
    return pltpu.CompilerParams(vmem_limit_bytes=mib * MIB)


def x_send(field):
    nz, nx, ny = field.shape
    cl, cr, _ = joint_sides(nx)
    one = stack_lhs(np.concatenate([cl, cr]))
    pair = np.zeros((24, 6 * nx), one.dtype)
    pair[:12, : 3 * nx] = one
    pair[12:, 3 * nx :] = one
    step = 8

    def kernel(u_ref, c_ref, out_ref):
        table = c_ref[...]
        for p in range(step // 2):
            parts = []
            for z in (2 * p, 2 * p + 1):
                hi, lo = split(u_ref[z])
                parts += [hi, hi, lo]
            out_ref[24 * p : 24 * p + 24, :] = dot(table, jnp.concatenate(parts, axis=0))

    return pl.pallas_call(
        kernel,
        grid=(nz // step,),
        in_specs=[pl.BlockSpec((step, nx, ny), lambda i: (i, 0, 0)), VM],
        out_specs=pl.BlockSpec((12 * step, ny), lambda i: (i, 0)),
        out_shape=jax.ShapeDtypeStruct((nz * 12, ny), F32),
        compiler_params=params(16),
        name="x_send",
    )(field, jnp.asarray(pair))


def x_exchange(message):
    count = lax.axis_size("gx")
    right = [(i, (i + 1) % count) for i in range(count)]
    if count == 2:
        return lax.ppermute(message, "gx", right)
    left = [(j, i) for i, j in right]
    rows, ny = message.shape
    grid = message.reshape(rows // 12, 12, ny)
    from_left = lax.ppermute(grid[:, :6], "gx", right)
    from_right = lax.ppermute(grid[:, 6:], "gx", left)
    return jnp.concatenate([from_left, from_right], axis=1).reshape(rows, ny)


def x_apply(field, halo):
    nz, nx, ny = field.shape
    _, _, maps = joint_sides(nx)
    main = np.concatenate([m for m, _, _ in maps])
    outer = np.concatenate([np.concatenate([l, r], axis=1) for _, l, r in maps])
    pad = np.zeros((main.shape[0], 4))
    tables = np.stack(
        [
            stack_lhs(np.concatenate([main, outer, pad], axis=1)),
            stack_lhs(np.concatenate([main, pad, outer], axis=1)),
        ]
    )
    rows = main.shape[0]
    counts = [nx, nx // 2, nx // 4]
    step = 8
    steps = nz // step

    combos = []
    for level, (_, cl, _, cr, _) in enumerate(sides(ny)):
        both = np.zeros((8, 128))
        assert np.abs(cl[:, : ny - 64]).max() == 0 and np.abs(cr[:, 64:]).max() == 0
        both[: cl.shape[0], 64:] = cl[:, ny - 64 :]
        both[4 : 4 + cr.shape[0], :64] = cr[:, :64]
        combos.append(stack_lhs(both))
    combos = np.stack(combos)

    def kernel(u_ref, r_ref, t_ref, c_ref, x1, x2, x3, right_ref, left_ref, e1, e2, e3):
        i = pl.program_id(0)
        lanes = lax.broadcasted_iota(jnp.int32, (rows, 128), 1)
        for z in range(step):
            start = pl.multiple_of(i * (12 * step) + 24 * (z // 2) + 8 * (z % 2), 8)
            hi, lo = split(u_ref[z])
            rhi, rlo = split(r_ref[pl.ds(start, 16), :])
            stacked = jnp.concatenate([hi, rhi, hi, rhi, lo, rlo], axis=0)
            got = dot(t_ref[z % 2], stacked)
            edge = jnp.where(lanes < 64, got[:, :128], got[:, ny - 128 :])
            ehi, elo = split(edge)
            estack = jnp.concatenate([ehi, ehi, elo], axis=1)
            at = 0
            for ref, eref, n in zip((x1, x2, x3), (e1, e2, e3), counts):
                where = pl.ds(pl.multiple_of((i * step + z) * n, 16), n)
                ref[where, :] = got[at : at + n]
                eref[where, :] = estack[at : at + n]
                at += n

        @pl.when(i == steps - 1)
        def _():
            row = 0
            for level, (eref, n) in enumerate(zip((e1, e2, e3), counts)):
                got = dot_t(c_ref[level], eref[...])
                for j in range(nz * n // 512):
                    for c in range(LEFT_RANKS[level]):
                        right_ref[row : row + 1, :] = got[c : c + 1, 512 * j : 512 * j + 512]
                        if c < RIGHT_RANKS[level]:
                            left_ref[row : row + 1, :] = got[4 + c : 5 + c, 512 * j : 512 * j + 512]
                        else:
                            left_ref[row : row + 1, :] = jnp.zeros((1, 512), F32)
                        row += 1
            right_ref[row:, :] = jnp.zeros((24 - row, 512), F32)
            left_ref[row:, :] = jnp.zeros((24 - row, 512), F32)

    return pl.pallas_call(
        kernel,
        grid=(steps,),
        in_specs=[pl.BlockSpec((step, nx, ny), lambda i: (i, 0, 0)), VM, VM, VM],
        out_specs=[VM] * 5,
        out_shape=[vmem((nz * n, ny)) for n in counts] + [jax.ShapeDtypeStruct((24, 512), F32)] * 2,
        scratch_shapes=[pltpu.VMEM((nz * n, 384), BF) for n in counts],
        compiler_params=params(24),
        name="x_apply",
    )(field, halo, jnp.asarray(tables), jnp.asarray(combos))


def z_tables(nz):
    out = []
    for _, cl, pl_, cr, pr in sides(nz):
        out.append((np.concatenate([cl, cr]), np.concatenate([pl_, pr], axis=1)))
    return out


def weighted(parts):
    total = None
    for scalar, get in parts:
        if abs(scalar) < 1e-12:
            continue
        term = get() * np.float32(scalar)
        total = term if total is None else total + term
    return total


def z_combine(xs, nz):
    ny = xs[0].shape[1]
    tables = [t for t, _ in z_tables(nz)]
    counts = [x.shape[0] // nz for x in xs]

    def kernel(x1, x2, x3, o1, o2, o3):
        for ref, out, table, n in zip((x1, x2, x3), (o1, o2, o3), tables, counts):

            def body(k, _, ref=ref, out=out, table=table, n=n):
                row = pl.multiple_of((k // (ny // 128)) * 8, 8)
                lane = pl.multiple_of((k % (ny // 128)) * 128, 128)
                get = {}
                for z in range(nz):
                    if np.abs(table[:, z]).max() > 1e-12:
                        get[z] = ref[pl.ds(pl.multiple_of(z * n + row, 8), 8), pl.ds(lane, 128)]
                for c in range(table.shape[0]):
                    out[pl.ds(pl.multiple_of(c * n + row, 8), 8), pl.ds(lane, 128)] = weighted(
                        [(table[c, z], lambda z=z: get[z]) for z in range(nz)]
                    )
                return 0

            lax.fori_loop(0, (n // 8) * (ny // 128), body, 0)

    return pl.pallas_call(
        kernel,
        in_specs=[VM] * 3,
        out_specs=[VM] * 3,
        out_shape=[vmem((t.shape[0] * n, ny)) for t, n in zip(tables, counts)],
        compiler_params=params(16),
        cost_estimate=pl.CostEstimate(flops=20_000_000, bytes_accessed=6_000_000, transcendentals=0),
        name="z_combine",
    )(*xs)


def y_tables(ny, spread):
    out = []
    for level, (main, _, left, _, right) in enumerate(sides(ny)):
        step = (1 << level) if spread else 1
        width = ny if spread else ny >> level
        fit = lambda t: spread_columns(t.T, step, width)
        out.append((fit(main), fit(left), fit(right)))
    return out


def halo_rows(level, chunk, nz, counts):
    start = 0
    for below in range(level):
        start += (nz * counts[below] // 512) * LEFT_RANKS[below]
    return start + chunk * LEFT_RANKS[level]


def halo_table(left, right, level, chunks, nz, counts):
    base = np.zeros((48, left.shape[1]))
    for chunk in chunks:
        row = halo_rows(level, chunk, nz, counts)
        base[row : row + left.shape[0]] = left
        base[24 + row : 24 + row + right.shape[0]] = right
    hi, lo = hi_lo(base)
    none = np.zeros((32, left.shape[1]), hi.dtype)
    return np.concatenate([hi, hi, none, lo, np.zeros_like(hi), none])


def turned(left_ref, right_ref):
    both = jnp.concatenate([left_ref[...], right_ref[...]], axis=0)
    hi = both.astype(BF).astype(F32)
    wide = jnp.concatenate([hi, both - hi, jnp.zeros((32, 512), F32)], axis=0)
    return wide.T


def y_messages(combined, from_left, from_right, nz):
    ny = combined[0].shape[1]
    tables = z_tables(nz)
    nums = [t.shape[0] for t, _ in tables]
    counts = [c.shape[0] // n for c, n in zip(combined, nums)]
    mains, halos, coefs = [], [], []
    for level, (main, left, right) in enumerate(y_tables(ny, False)):
        mains.append(stack_rhs(main))
        chunks = nz * counts[level] // 512
        halos.append(halo_table(left, right, level, range(chunks), nz, counts))
        per = 512 // counts[level]
        table = tables[level][0]
        coef = np.zeros((nums[level], per, 128), np.float32)
        for c in range(nums[level]):
            for zz in range(per):
                for chunk in range(chunks):
                    row = halo_rows(level, chunk, nz, counts)
                    for lane in range(LEFT_RANKS[level]):
                        for base in (0, 24, 48, 72):
                            coef[c, zz, base + row + lane] = table[c, chunk * per + zz]
        coefs.append(coef.reshape(nums[level] * per, 128))
    heights = [(nums[0] // 2) * counts[0], 3 * counts[1] // 2, 4 * counts[2] // 4]
    height = sum(heights)
    height += -height % 8

    def kernel(c1, c2, c3, fl, fr, m1, m2, m3, h1, h2, h3, k1, k2, k3, right_ref, left_ref):
        halo = turned(fl, fr)
        got = []
        for c_ref, m, h, k, n, num in zip(
            (c1, c2, c3), (m1, m2, m3), (h1, h2, h3), (k1, k2, k3), counts, nums
        ):
            per = 512 // n
            extra = []
            for c in range(num):
                total = None
                for zz in range(per):
                    term = halo[zz * n : zz * n + n] * k[c * per + zz : c * per + zz + 1, :]
                    total = term if total is None else total + term
                extra.append(total)
            ehi, elo = split(jnp.concatenate(extra, axis=0))
            hi, lo = split(c_ref[...])
            got.append(
                dot(jnp.concatenate([hi, lo, hi], axis=1), m[...])
                + dot(jnp.concatenate([ehi, ehi], axis=1), h[...])
                + dot(elo, h[:128])
            )
        for side, ref in enumerate((right_ref, left_ref)):
            at = 0
            for level in range(3):
                n, width = counts[level], ny >> level
                ranks = LEFT_RANKS if side == 0 else RIGHT_RANKS
                first = 0 if side == 0 else LEFT_RANKS[level] * n
                total = ranks[level] * n
                per_row = ny // width
                tall = heights[level]
                for part in range(per_row):
                    use = min(tall, total - part * tall)
                    if use > 0:
                        ref[at : at + use, part * width : (part + 1) * width] = got[level][
                            first + part * tall : first + part * tall + use
                        ]
                    if use < tall:
                        use = max(use, 0)
                        ref[at + use : at + tall, part * width : (part + 1) * width] = jnp.zeros(
                            (tall - use, width), F32
                        )
                at += tall
            if at < height:
                ref[at:, :] = jnp.zeros((height - at, ny), F32)

    return pl.pallas_call(
        kernel,
        in_specs=[VM] * 14,
        out_specs=[VM] * 2,
        out_shape=[jax.ShapeDtypeStruct((height, ny), F32)] * 2,
        compiler_params=params(24),
        name="y_messages",
    )(
        *combined,
        from_left,
        from_right,
        *[jnp.asarray(t) for t in mains],
        *[jnp.asarray(t) for t in halos],
        *[jnp.asarray(t) for t in coefs],
    )


def add(a, b):
    if a is None:
        return b
    return a if b is None else a + b


def scale(a, c):
    return None if a is None else a * np.float32(c)


def open_lift(values, first, last):
    get = values.get
    low, high = first // 2 - 3, last // 2 + 4
    s = {i: get(2 * i) for i in range(low, high + 1)}
    d = {i: get(2 * i + 1) for i in range(low, high + 1)}
    pick = lambda t, i: t.get(i)
    d1 = {i: add(d[i], scale(add(s[i], pick(s, i + 1)), lift_alpha)) for i in range(low, high + 1)}
    s1 = {i: add(s[i], scale(add(pick(d1, i - 1), d1[i]), lift_beta)) for i in range(low, high + 1)}
    d2 = {i: add(d1[i], scale(add(s1[i], pick(s1, i + 1)), lift_gamma)) for i in range(low, high + 1)}
    s2 = {i: add(s1[i], scale(add(pick(d2, i - 1), d2[i]), lift_delta)) for i in range(low, high + 1)}
    out = {}
    for z in range(first, last + 1):
        if z % 2:
            out[z] = scale(d2[z // 2], 1.0 / lift_zeta)
        else:
            out[z] = scale(s2[z // 2], lift_zeta)
    return out


def main_part(xs, from_left, from_right, nz):
    ny = xs[0].shape[1]
    counts = [x.shape[0] // nz for x in xs]
    mains, halos = [], []
    for level, (main, left, right) in enumerate(y_tables(ny, True)):
        mains.append(stack_rhs(main))
        chunks = nz * counts[level] // 512
        halos.append(
            np.stack([halo_table(left, right, level, [c], nz, counts) for c in range(chunks)])
        )

    def kernel(x1, x2, x3, fl, fr, m1, m2, m3, h1, h2, h3, out_ref, y1, y2, y3, w2, halo_ref):
        halo = turned(fl, fr).astype(BF)
        halo_ref[...] = jnp.concatenate([halo, halo], axis=1)
        for x, m, h, y, n in zip((x1, x2, x3), (m1, m2, m3), (h1, h2, h3), (y1, y2, y3), counts):

            def chunk_body(j, _, x=x, m=m, h=h, y=y):
                where = pl.ds(pl.multiple_of(j * 512, 512), 512)
                hi, lo = split(x[where, :])
                y[where, :] = dot(jnp.concatenate([hi, lo, hi], axis=1), m[...]) + dot(
                    halo_ref[...], h[j]
                )
                return 0

            lax.fori_loop(0, nz * n // 512, chunk_body, 0)

        groups = ny // 128

        def place(k):
            return pl.multiple_of((k // groups) * 8, 8), pl.multiple_of((k % groups) * 128, 128)

        def loaded(ref, n, row, lane):
            return {
                z: ref[pl.ds(pl.multiple_of(z * n + row, 8), 8), pl.ds(lane, 128)] for z in range(nz)
            }

        def level_one(k, _):
            row, lane = place(k)
            got = open_lift(loaded(y1, counts[0], row, lane), 0, nz - 1)
            for z in range(nz):
                out_ref[k % groups, z, pl.ds(row, 8), :] = got[z]
            return 0

        lax.fori_loop(0, (counts[0] // 8) * groups, level_one, 0)

        def lows(values, first, last):
            got = open_lift(values, 2 * first, 2 * last)
            return {i: got[2 * i] for i in range(first, last + 1) if got[2 * i] is not None}

        def level_two(k, _):
            row, lane = place(k)
            one = lows(loaded(y2, counts[1], row, lane), -2, nz // 2 + 1)
            got = open_lift(one, 0, nz // 2 - 1)
            for z in range(nz // 2):
                w2[k % groups, pl.ds(pl.multiple_of(z * counts[1] + row, 8), 8), :] = got[z]
            return 0

        lax.fori_loop(0, (counts[1] // 8) * groups, level_two, 0)

        lane_ids = lax.broadcasted_iota(jnp.int32, (8, 128), 1)

        def level_three(k, _):
            row, lane = place(k)
            one = lows(loaded(y3, counts[2], row, lane), -2, nz // 2 + 1)
            two = lows(one, -3, nz // 4 + 2)
            got = open_lift(two, 0, nz // 4 - 1)
            for z in range(nz // 4):
                where = pl.ds(2 * z * counts[1] + 2 * row, 8, stride=2)
                old = w2[k % groups, where, :]
                w2[k % groups, where, :] = jnp.where(lane_ids % 4 == 0, got[z], old)
            return 0

        lax.fori_loop(0, (counts[2] // 8) * groups, level_three, 0)

        def merge(k, _):
            row, _ = place(k)
            for z in range(nz // 2):
                inner = w2[k % groups, pl.ds(pl.multiple_of(z * counts[1] + row, 8), 8), :]
                where = pl.ds(2 * row, 8, stride=2)
                old = out_ref[k % groups, 2 * z, where, :]
                out_ref[k % groups, 2 * z, where, :] = jnp.where(lane_ids % 2 == 0, inner, old)
            return 0

        lax.fori_loop(0, (counts[1] // 8) * groups, merge, 0)

    return pl.pallas_call(
        kernel,
        in_specs=[VM] * 11,
        out_specs=VM,
        out_shape=vmem((ny // 128, nz, counts[0], 128)),
        scratch_shapes=[pltpu.VMEM((nz * n, ny), F32) for n in counts]
        + [pltpu.VMEM((ny // 128, nz // 2 * counts[1], 128), F32), pltpu.VMEM((512, 256), BF)],
        compiler_params=params(32),
        cost_estimate=pl.CostEstimate(
            flops=8_000_000_000, bytes_accessed=20_000_000, transcendentals=0
        ),
        name="main_part",
    )(*xs, from_left, from_right, *[jnp.asarray(t) for t in mains], *[jnp.asarray(t) for t in halos])


def z_apply(inner, from_left, from_right):
    groups, nz, nx, _ = inner.shape
    ny = groups * 128
    maps = [p for _, p in z_tables(nz)]
    counts = [nx, nx // 2, nx // 4]
    tables = []
    for level in (1, 2):
        width = ny >> level
        hi = spread_columns(np.eye(width), 1 << level, ny).astype(ml_dtypes.bfloat16)
        tables.append(np.concatenate([hi, hi]))
    heights = [2 * counts[0], 3 * counts[1] // 2, 4 * counts[2] // 4]
    step = 4

    def kernel(in_ref, fl, fr, t2, t3, out_ref, s1, s2, s3):
        i = pl.program_id(0)

        @pl.when(i == 0)
        def _():
            row_ids = lax.broadcasted_iota(jnp.int32, (nx, ny), 0)
            lane_ids = lax.broadcasted_iota(jnp.int32, (nx, ny), 1)
            inside = ((row_ids % 2) + (lane_ids % 2)) == 0
            s2[...] = jnp.zeros(s2.shape, F32)
            s3[...] = jnp.zeros(s3.shape, F32)
            for side, ref in enumerate((fl, fr)):
                ranks = LEFT_RANKS if side == 0 else RIGHT_RANKS
                for c in range(2):
                    outside = jnp.where(inside, 0.0, ref[c * nx : c * nx + nx, :])
                    for q in range(groups):
                        s1[2 * side + c, q] = outside[:, 128 * q : 128 * q + 128]
                at = heights[0]
                for level, table, to in ((1, t2, s2), (2, t3, s3)):
                    width, tall, n = ny >> level, heights[level], counts[level]
                    flat = jnp.concatenate(
                        [ref[at : at + tall, p * width : p * width + width] for p in range(1 << level)],
                        axis=0,
                    )
                    hi, lo = split(flat)
                    got = dot(jnp.concatenate([hi, lo], axis=1), table[...])
                    first = 0 if side == 0 else LEFT_RANKS[level]
                    for c in range(ranks[level]):
                        for q in range(groups):
                            to[first + c, q, pl.ds(0, n, stride=1 << level), :] = got[
                                c * n : c * n + n, 128 * q : 128 * q + 128
                            ]
                    at += tall

        for z_out in range(nz):

            @pl.when(i == z_out // step)
            def _(z=z_out):
                def body(k, _):
                    q = k % groups
                    row = pl.multiple_of((k // groups) * 8, 8)
                    lane = pl.multiple_of(q * 128, 128)
                    value = in_ref[q, z % step, pl.ds(row, 8), :]
                    extra = None
                    for c in range(4):
                        scalar = maps[0][z, c]
                        if abs(scalar) < 1e-12:
                            continue
                        if z % 2:
                            start = pl.multiple_of((c % 2) * nx + row, 8)
                            term = (fl, fr)[c // 2][pl.ds(start, 8), pl.ds(lane, 128)]
                        else:
                            term = s1[c, q, pl.ds(row, 8), :]
                        extra = add(extra, term * np.float32(scalar))
                    if z % 2 == 0:
                        for c in range(maps[1].shape[1]):
                            scalar = maps[1][z // 2, c]
                            if abs(scalar) > 1e-12:
                                extra = add(extra, s2[c, q, pl.ds(row, 8), :] * np.float32(scalar))
                    if z % 4 == 0:
                        ids = (
                            lax.broadcasted_iota(jnp.int32, (8, 128), 0) % 4
                            + lax.broadcasted_iota(jnp.int32, (8, 128), 1) % 4
                        )
                        third = None
                        for c in range(maps[2].shape[1]):
                            if abs(maps[2][z // 4, c]) > 1e-12:
                                third = add(third, s3[c, q, pl.ds(row, 8), :] * np.float32(maps[2][z // 4, c]))
                        if third is None:
                            third = jnp.zeros((8, 128), F32)
                        if extra is None:
                            extra = jnp.zeros((8, 128), F32)
                        extra = jnp.where(ids == 0, third, extra)
                    if extra is not None:
                        value = value + extra
                    out_ref[z % step, pl.ds(row, 8), pl.ds(lane, 128)] = value
                    return 0

                lax.fori_loop(0, (nx // 8) * groups, body, 0)

    return pl.pallas_call(
        kernel,
        grid=(nz // step,),
        in_specs=[pl.BlockSpec((groups, step, nx, 128), lambda i: (0, i, 0, 0)), VM, VM, VM, VM],
        out_specs=pl.BlockSpec((step, nx, ny), lambda i: (i, 0, 0)),
        out_shape=jax.ShapeDtypeStruct((nz, nx, ny), F32),
        scratch_shapes=[pltpu.VMEM((m.shape[1], groups, nx, 128), F32) for m in maps],
        compiler_params=params(24),
        name="z_apply",
    )(inner, from_left, from_right, *[jnp.asarray(t) for t in tables])


def swap(to_right, to_left, axis):
    count = lax.axis_size(axis)
    right = [(i, (i + 1) % count) for i in range(count)]
    left = [(j, i) for i, j in right]
    return lax.ppermute(to_right, axis, right), lax.ppermute(to_left, axis, left)


def local(field):
    nz = field.shape[0]
    halo = x_exchange(x_send(field))
    x1, x2, x3, to_right, to_left = x_apply(field, halo)
    from_left, from_right = swap(to_right, to_left, "gy")
    combined = z_combine((x1, x2, x3), nz)
    to_right, to_left = y_messages(combined, from_left, from_right, nz)
    below, above = swap(to_right, to_left, "gz")
    inner = main_part((x1, x2, x3), from_left, from_right, nz)
    return z_apply(inner, below, above)


def solution(mesh):
    placed = (P("gz", "gx", "gy"),)
    return jax.shard_map(
        local, mesh=mesh, in_specs=placed, out_specs=P("gz", "gx", "gy"), check_vma=False
    )
```

```python
import functools

import jax
import jax.numpy as jnp
import ml_dtypes
import numpy as np
from jax import lax
from jax.experimental import pallas as pl
from jax.experimental.pallas import tpu as pltpu
from jax.sharding import PartitionSpec as P

lift_alpha = -1.586134342
lift_beta = -0.05298011854
lift_gamma = 0.8829110762
lift_delta = 0.4435068522
lift_zeta = 1.149604398

BF = jnp.bfloat16
F32 = jnp.float32
MIB = 1024 * 1024


def periodic_lift(u):
    s, d = u[0::2].copy(), u[1::2].copy()
    d = d + lift_alpha * (s + np.roll(s, -1, 0))
    s = s + lift_beta * (np.roll(d, 1, 0) + d)
    d = d + lift_gamma * (s + np.roll(s, -1, 0))
    s = s + lift_delta * (np.roll(d, 1, 0) + d)
    out = np.empty_like(u)
    out[0::2] = s * lift_zeta
    out[1::2] = d / lift_zeta
    return out


@functools.lru_cache(None)
def blocks(n):
    current = np.eye(4 * n)
    found = []
    for level in range(3):
        full = periodic_lift(current)
        m = n >> level
        rows = full[m : 2 * m]
        found.append((rows[:, n : 2 * n], rows[:, :n], rows[:, 2 * n : 3 * n]))
        current = full[0::2]
    return found


def row_space(outer, rank):
    _, sizes, basis = np.linalg.svd(outer, full_matrices=False)
    assert sizes[rank:].max() < 1e-10
    basis = basis[:rank].copy()
    basis[np.abs(basis) < 1e-12] = 0.0
    return basis


LEFT_RANKS = (2, 3, 4)
RIGHT_RANKS = (2, 3, 3)


@functools.lru_cache(None)
def sides(n):
    out = []
    for level, (main, left, right) in enumerate(blocks(n)):
        cl = row_space(left, LEFT_RANKS[level])
        cr = row_space(right, RIGHT_RANKS[level])
        out.append((main, cl, left @ cl.T, cr, right @ cr.T))
    return out


@functools.lru_cache(None)
def joint_sides(n):
    found = blocks(n)
    cl = row_space(np.concatenate([b[1] for b in found]), 6)
    cr = row_space(np.concatenate([b[2] for b in found]), 6)
    maps = [(b[0], b[1] @ cl.T, b[2] @ cr.T) for b in found]
    return cl, cr, maps


def hi_lo(table):
    table = np.asarray(table, np.float32)
    hi = table.astype(ml_dtypes.bfloat16)
    lo = (table - hi.astype(np.float32)).astype(ml_dtypes.bfloat16)
    return hi, lo


def stack_lhs(table):
    hi, lo = hi_lo(table)
    return np.concatenate([hi, lo, hi], axis=1)


def stack_rhs(table):
    hi, lo = hi_lo(table)
    return np.concatenate([hi, hi, lo], axis=0)


def split(values):
    hi = values.astype(BF)
    return hi, (values - hi.astype(F32)).astype(BF)


def dot(a, b):
    return lax.dot_general(a, b, (((1,), (0,)), ((), ())), preferred_element_type=F32)


def dot_t(a, b):
    return lax.dot_general(a, b, (((1,), (1,)), ((), ())), preferred_element_type=F32)


def spread_columns(table, step, width):
    out = np.zeros((table.shape[0], width))
    out[:, ::step] = table
    return out


VM = pl.BlockSpec(memory_space=pltpu.VMEM)
HB = pl.BlockSpec(memory_space=pltpu.HBM)


def in_hbm(array):
    return pltpu.with_memory_space_constraint(array, pltpu.HBM)


def vmem(shape, dtype=F32):
    return pltpu.VMEM(shape, dtype)


def params(mib):
    return pltpu.CompilerParams(vmem_limit_bytes=mib * MIB)


def x_send(field):
    nz, nx, ny = field.shape
    cl, cr, _ = joint_sides(nx)
    one = stack_lhs(np.concatenate([cl, cr]))
    pair = np.zeros((24, 6 * nx), one.dtype)
    pair[:12, : 3 * nx] = one
    pair[12:, 3 * nx :] = one
    step = 4
    steps = nz // step

    def kernel(u_hbm, c_hbm, u_ref, out_ref, c_ref, u_sem, c_sem):
        table_copy = pltpu.make_async_copy(c_hbm, c_ref, c_sem)
        copies = [
            pltpu.make_async_copy(
                u_hbm.at[i * step : i * step + step], u_ref.at[i * step : i * step + step], u_sem.at[i]
            )
            for i in range(steps)
        ]
        table_copy.start()
        for copy in copies:
            copy.start()
        table_copy.wait()
        table = c_ref[...]
        for i, copy in enumerate(copies):
            copy.wait()
            for p in range(i * step // 2, (i + 1) * step // 2):
                parts = []
                for z in (2 * p, 2 * p + 1):
                    hi, lo = split(u_ref[z])
                    parts += [hi, hi, lo]
                out_ref[24 * p : 24 * p + 24, :] = dot(table, jnp.concatenate(parts, axis=0))

    return pl.pallas_call(
        kernel,
        in_specs=[HB, HB],
        out_specs=[VM, VM],
        out_shape=[vmem((nz, nx, ny)), vmem((nz * 12, ny))],
        scratch_shapes=[
            pltpu.VMEM(pair.shape, BF),
            pltpu.SemaphoreType.DMA((steps,)),
            pltpu.SemaphoreType.DMA,
        ],
        compiler_params=params(16),
        name="x_send",
    )(in_hbm(field), in_hbm(jnp.asarray(pair)))


def x_exchange(message):
    count = lax.axis_size("gx")
    right = [(i, (i + 1) % count) for i in range(count)]
    if count == 2:
        return lax.ppermute(message, "gx", right)
    left = [(j, i) for i, j in right]
    rows, ny = message.shape
    grid = message.reshape(rows // 12, 12, ny)
    from_left = lax.ppermute(grid[:, :6], "gx", right)
    from_right = lax.ppermute(grid[:, 6:], "gx", left)
    return jnp.concatenate([from_left, from_right], axis=1).reshape(rows, ny)


def x_apply(field, halo):
    nz, nx, ny = field.shape
    _, _, maps = joint_sides(nx)
    main = np.concatenate([m for m, _, _ in maps])
    outer = np.concatenate([np.concatenate([l, r], axis=1) for _, l, r in maps])
    pad = np.zeros((main.shape[0], 4))
    tables = np.stack(
        [
            stack_lhs(np.concatenate([main, outer, pad], axis=1)),
            stack_lhs(np.concatenate([main, pad, outer], axis=1)),
        ]
    )
    rows = main.shape[0]
    counts = [nx, nx // 2, nx // 4]
    step = 8
    steps = nz // step

    combos = []
    for level, (_, cl, _, cr, _) in enumerate(sides(ny)):
        both = np.zeros((8, 128))
        assert np.abs(cl[:, : ny - 64]).max() == 0 and np.abs(cr[:, 64:]).max() == 0
        both[: cl.shape[0], 64:] = cl[:, ny - 64 :]
        both[4 : 4 + cr.shape[0], :64] = cr[:, :64]
        combos.append(stack_lhs(both))
    combos = np.stack(combos)

    def kernel(u_ref, r_ref, t_ref, c_ref, x1, x2, x3, right_ref, left_ref, e1, e2, e3):
        i = pl.program_id(0)
        lanes = lax.broadcasted_iota(jnp.int32, (rows, 128), 1)
        for z in range(step):
            start = pl.multiple_of(i * (12 * step) + 24 * (z // 2) + 8 * (z % 2), 8)
            hi, lo = split(u_ref[i * step + z])
            rhi, rlo = split(r_ref[pl.ds(start, 16), :])
            stacked = jnp.concatenate([hi, rhi, hi, rhi, lo, rlo], axis=0)
            got = dot(t_ref[z % 2], stacked)
            edge = jnp.where(lanes < 64, got[:, :128], got[:, ny - 128 :])
            ehi, elo = split(edge)
            estack = jnp.concatenate([ehi, ehi, elo], axis=1)
            at = 0
            for ref, eref, n in zip((x1, x2, x3), (e1, e2, e3), counts):
                where = pl.ds(pl.multiple_of((i * step + z) * n, 16), n)
                ref[where, :] = got[at : at + n]
                eref[where, :] = estack[at : at + n]
                at += n

        @pl.when(i == steps - 1)
        def _():
            row = 0
            for level, (eref, n) in enumerate(zip((e1, e2, e3), counts)):
                got = dot_t(c_ref[level], eref[...])
                for j in range(nz * n // 512):
                    for c in range(LEFT_RANKS[level]):
                        right_ref[row : row + 1, :] = got[c : c + 1, 512 * j : 512 * j + 512]
                        if c < RIGHT_RANKS[level]:
                            left_ref[row : row + 1, :] = got[4 + c : 5 + c, 512 * j : 512 * j + 512]
                        else:
                            left_ref[row : row + 1, :] = jnp.zeros((1, 512), F32)
                        row += 1
            right_ref[row:, :] = jnp.zeros((24 - row, 512), F32)
            left_ref[row:, :] = jnp.zeros((24 - row, 512), F32)

    return pl.pallas_call(
        kernel,
        grid=(steps,),
        in_specs=[VM] * 4,
        out_specs=[VM] * 5,
        out_shape=[vmem((nz * n, ny)) for n in counts] + [jax.ShapeDtypeStruct((24, 512), F32)] * 2,
        scratch_shapes=[pltpu.VMEM((nz * n, 384), BF) for n in counts],
        compiler_params=params(24),
        name="x_apply",
    )(field, halo, jnp.asarray(tables), jnp.asarray(combos))


def z_tables(nz):
    out = []
    for _, cl, pl_, cr, pr in sides(nz):
        out.append((np.concatenate([cl, cr]), np.concatenate([pl_, pr], axis=1)))
    return out


def weighted(parts):
    total = None
    for scalar, get in parts:
        if abs(scalar) < 1e-12:
            continue
        term = get() * np.float32(scalar)
        total = term if total is None else total + term
    return total


def z_combine(xs, nz):
    ny = xs[0].shape[1]
    tables = [t for t, _ in z_tables(nz)]
    counts = [x.shape[0] // nz for x in xs]

    def kernel(x1, x2, x3, o1, o2, o3):
        for ref, out, table, n in zip((x1, x2, x3), (o1, o2, o3), tables, counts):

            def body(k, _, ref=ref, out=out, table=table, n=n):
                row = pl.multiple_of((k // (ny // 128)) * 8, 8)
                lane = pl.multiple_of((k % (ny // 128)) * 128, 128)
                get = {}
                for z in range(nz):
                    if np.abs(table[:, z]).max() > 1e-12:
                        get[z] = ref[pl.ds(pl.multiple_of(z * n + row, 8), 8), pl.ds(lane, 128)]
                for c in range(table.shape[0]):
                    out[pl.ds(pl.multiple_of(c * n + row, 8), 8), pl.ds(lane, 128)] = weighted(
                        [(table[c, z], lambda z=z: get[z]) for z in range(nz)]
                    )
                return 0

            lax.fori_loop(0, (n // 8) * (ny // 128), body, 0)

    return pl.pallas_call(
        kernel,
        in_specs=[VM] * 3,
        out_specs=[VM] * 3,
        out_shape=[vmem((t.shape[0] * n, ny)) for t, n in zip(tables, counts)],
        compiler_params=params(16),
        cost_estimate=pl.CostEstimate(flops=20_000_000, bytes_accessed=6_000_000, transcendentals=0),
        name="z_combine",
    )(*xs)


def y_tables(ny, spread):
    out = []
    for level, (main, _, left, _, right) in enumerate(sides(ny)):
        step = (1 << level) if spread else 1
        width = ny if spread else ny >> level
        fit = lambda t: spread_columns(t.T, step, width)
        out.append((fit(main), fit(left), fit(right)))
    return out


def halo_rows(level, chunk, nz, counts):
    start = 0
    for below in range(level):
        start += (nz * counts[below] // 512) * LEFT_RANKS[below]
    return start + chunk * LEFT_RANKS[level]


def halo_table(left, right, level, chunks, nz, counts):
    base = np.zeros((48, left.shape[1]))
    for chunk in chunks:
        row = halo_rows(level, chunk, nz, counts)
        base[row : row + left.shape[0]] = left
        base[24 + row : 24 + row + right.shape[0]] = right
    hi, lo = hi_lo(base)
    none = np.zeros((32, left.shape[1]), hi.dtype)
    return np.concatenate([hi, hi, none, lo, np.zeros_like(hi), none])


def turned(left_ref, right_ref):
    both = jnp.concatenate([left_ref[...], right_ref[...]], axis=0)
    hi = both.astype(BF).astype(F32)
    wide = jnp.concatenate([hi, both - hi, jnp.zeros((32, 512), F32)], axis=0)
    return wide.T


def y_messages(combined, from_left, from_right, nz):
    ny = combined[0].shape[1]
    tables = z_tables(nz)
    nums = [t.shape[0] for t, _ in tables]
    counts = [c.shape[0] // n for c, n in zip(combined, nums)]
    mains, halos, coefs = [], [], []
    for level, (main, left, right) in enumerate(y_tables(ny, False)):
        mains.append(stack_rhs(main))
        chunks = nz * counts[level] // 512
        halos.append(halo_table(left, right, level, range(chunks), nz, counts))
        per = 512 // counts[level]
        table = tables[level][0]
        coef = np.zeros((nums[level], per, 128), np.float32)
        for c in range(nums[level]):
            for zz in range(per):
                for chunk in range(chunks):
                    row = halo_rows(level, chunk, nz, counts)
                    for lane in range(LEFT_RANKS[level]):
                        for base in (0, 24, 48, 72):
                            coef[c, zz, base + row + lane] = table[c, chunk * per + zz]
        coefs.append(coef.reshape(nums[level] * per, 128))
    heights = [(nums[0] // 2) * counts[0], 3 * counts[1] // 2, 4 * counts[2] // 4]
    height = sum(heights)
    height += -height % 8

    def kernel(c1, c2, c3, fl, fr, m1, m2, m3, h1, h2, h3, k1, k2, k3, right_ref, left_ref):
        halo = turned(fl, fr)
        got = []
        for c_ref, m, h, k, n, num in zip(
            (c1, c2, c3), (m1, m2, m3), (h1, h2, h3), (k1, k2, k3), counts, nums
        ):
            per = 512 // n
            extra = []
            for c in range(num):
                total = None
                for zz in range(per):
                    term = halo[zz * n : zz * n + n] * k[c * per + zz : c * per + zz + 1, :]
                    total = term if total is None else total + term
                extra.append(total)
            ehi, elo = split(jnp.concatenate(extra, axis=0))
            hi, lo = split(c_ref[...])
            got.append(
                dot(jnp.concatenate([hi, lo, hi], axis=1), m[...])
                + dot(jnp.concatenate([ehi, ehi], axis=1), h[...])
                + dot(elo, h[:128])
            )
        for side, ref in enumerate((right_ref, left_ref)):
            at = 0
            for level in range(3):
                n, width = counts[level], ny >> level
                ranks = LEFT_RANKS if side == 0 else RIGHT_RANKS
                first = 0 if side == 0 else LEFT_RANKS[level] * n
                total = ranks[level] * n
                per_row = ny // width
                tall = heights[level]
                for part in range(per_row):
                    use = min(tall, total - part * tall)
                    if use > 0:
                        ref[at : at + use, part * width : (part + 1) * width] = got[level][
                            first + part * tall : first + part * tall + use
                        ]
                    if use < tall:
                        use = max(use, 0)
                        ref[at + use : at + tall, part * width : (part + 1) * width] = jnp.zeros(
                            (tall - use, width), F32
                        )
                at += tall
            if at < height:
                ref[at:, :] = jnp.zeros((height - at, ny), F32)

    return pl.pallas_call(
        kernel,
        in_specs=[VM] * 14,
        out_specs=[VM] * 2,
        out_shape=[jax.ShapeDtypeStruct((height, ny), F32)] * 2,
        compiler_params=params(24),
        name="y_messages",
    )(
        *combined,
        from_left,
        from_right,
        *[jnp.asarray(t) for t in mains],
        *[jnp.asarray(t) for t in halos],
        *[jnp.asarray(t) for t in coefs],
    )


def add(a, b):
    if a is None:
        return b
    return a if b is None else a + b


def scale(a, c):
    return None if a is None else a * np.float32(c)


def open_lift(values, first, last):
    get = values.get
    low, high = first // 2 - 3, last // 2 + 4
    s = {i: get(2 * i) for i in range(low, high + 1)}
    d = {i: get(2 * i + 1) for i in range(low, high + 1)}
    pick = lambda t, i: t.get(i)
    d1 = {i: add(d[i], scale(add(s[i], pick(s, i + 1)), lift_alpha)) for i in range(low, high + 1)}
    s1 = {i: add(s[i], scale(add(pick(d1, i - 1), d1[i]), lift_beta)) for i in range(low, high + 1)}
    d2 = {i: add(d1[i], scale(add(s1[i], pick(s1, i + 1)), lift_gamma)) for i in range(low, high + 1)}
    s2 = {i: add(s1[i], scale(add(pick(d2, i - 1), d2[i]), lift_delta)) for i in range(low, high + 1)}
    out = {}
    for z in range(first, last + 1):
        if z % 2:
            out[z] = scale(d2[z // 2], 1.0 / lift_zeta)
        else:
            out[z] = scale(s2[z // 2], lift_zeta)
    return out


def touched_layers(nz):
    one, two, three = [np.abs(p).max(axis=1) > 1e-12 for _, p in z_tables(nz)]
    hit = lambda z: one[z] or (z % 2 == 0 and two[z // 2]) or (z % 4 == 0 and three[z // 4])
    return [z for z in range(nz) if hit(z)]


def main_part(xs, from_left, from_right, nz):
    ny = xs[0].shape[1]
    untouched = [z for z in range(nz) if z not in touched_layers(nz)]
    counts = [x.shape[0] // nz for x in xs]
    mains, halos = [], []
    for level, (main, left, right) in enumerate(y_tables(ny, True)):
        mains.append(stack_rhs(main))
        chunks = nz * counts[level] // 512
        halos.append(
            np.stack([halo_table(left, right, level, [c], nz, counts) for c in range(chunks)])
        )

    def kernel(x1, x2, x3, fl, fr, m1, m2, m3, h1, h2, h3, out_ref, hbm, y1, y2, y3, w2, halo_ref, sem):
        halo = turned(fl, fr).astype(BF)
        halo_ref[...] = jnp.concatenate([halo, halo], axis=1)
        for x, m, h, y, n in zip((x1, x2, x3), (m1, m2, m3), (h1, h2, h3), (y1, y2, y3), counts):

            def chunk_body(j, _, x=x, m=m, h=h, y=y):
                where = pl.ds(pl.multiple_of(j * 512, 512), 512)
                hi, lo = split(x[where, :])
                y[where, :] = dot(jnp.concatenate([hi, lo, hi], axis=1), m[...]) + dot(
                    halo_ref[...], h[j]
                )
                return 0

            lax.fori_loop(0, nz * n // 512, chunk_body, 0)

        groups = ny // 128

        def place(k):
            return pl.multiple_of((k // groups) * 8, 8), pl.multiple_of((k % groups) * 128, 128)

        def loaded(ref, n, row, lane):
            return {
                z: ref[pl.ds(pl.multiple_of(z * n + row, 8), 8), pl.ds(lane, 128)] for z in range(nz)
            }

        def level_one(k, _):
            row, lane = place(k)
            got = open_lift(loaded(y1, counts[0], row, lane), 0, nz - 1)
            for z in range(nz):
                out_ref[k % groups, z, pl.ds(row, 8), :] = got[z]
            return 0

        lax.fori_loop(0, (counts[0] // 8) * groups, level_one, 0)

        def lows(values, first, last):
            got = open_lift(values, 2 * first, 2 * last)
            return {i: got[2 * i] for i in range(first, last + 1) if got[2 * i] is not None}

        def level_two(k, _):
            row, lane = place(k)
            one = lows(loaded(y2, counts[1], row, lane), -2, nz // 2 + 1)
            got = open_lift(one, 0, nz // 2 - 1)
            for z in range(nz // 2):
                w2[k % groups, pl.ds(pl.multiple_of(z * counts[1] + row, 8), 8), :] = got[z]
            return 0

        lax.fori_loop(0, (counts[1] // 8) * groups, level_two, 0)

        lane_ids = lax.broadcasted_iota(jnp.int32, (8, 128), 1)

        def level_three(k, _):
            row, lane = place(k)
            one = lows(loaded(y3, counts[2], row, lane), -2, nz // 2 + 1)
            two = lows(one, -3, nz // 4 + 2)
            got = open_lift(two, 0, nz // 4 - 1)
            for z in range(nz // 4):
                where = pl.ds(2 * z * counts[1] + 2 * row, 8, stride=2)
                old = w2[k % groups, where, :]
                w2[k % groups, where, :] = jnp.where(lane_ids % 4 == 0, got[z], old)
            return 0

        lax.fori_loop(0, (counts[2] // 8) * groups, level_three, 0)

        def merge(k, _):
            row, _ = place(k)
            for z in range(nz // 2):
                inner = w2[k % groups, pl.ds(pl.multiple_of(z * counts[1] + row, 8), 8), :]
                where = pl.ds(2 * row, 8, stride=2)
                old = out_ref[k % groups, 2 * z, where, :]
                out_ref[k % groups, 2 * z, where, :] = jnp.where(lane_ids % 2 == 0, inner, old)
            return 0

        lax.fori_loop(0, (counts[1] // 8) * groups, merge, 0)

        copies = [
            pltpu.make_async_copy(
                out_ref.at[q, z], hbm.at[z, :, 128 * q : 128 * q + 128], sem.at[z]
            )
            for z in untouched
            for q in range(groups)
        ]
        for copy in copies:
            copy.start()
        for copy in copies:
            copy.wait()

    return pl.pallas_call(
        kernel,
        in_specs=[VM] * 11,
        out_specs=[VM, HB],
        out_shape=[vmem((ny // 128, nz, counts[0], 128)), pltpu.HBM((nz, counts[0], ny), F32)],
        scratch_shapes=[pltpu.VMEM((nz * n, ny), F32) for n in counts]
        + [pltpu.VMEM((ny // 128, nz // 2 * counts[1], 128), F32), pltpu.VMEM((512, 256), BF), pltpu.SemaphoreType.DMA((nz,))],
        compiler_params=params(32),
        cost_estimate=pl.CostEstimate(
            flops=8_000_000_000, bytes_accessed=20_000_000, transcendentals=0
        ),
        name="main_part",
    )(*xs, from_left, from_right, *[jnp.asarray(t) for t in mains], *[jnp.asarray(t) for t in halos])


def z_apply(inner, partial, from_left, from_right):
    groups, nz, nx, _ = inner.shape
    ny = groups * 128
    maps = [p for _, p in z_tables(nz)]
    counts = [nx, nx // 2, nx // 4]
    tables = []
    for level in (1, 2):
        width = ny >> level
        hi = spread_columns(np.eye(width), 1 << level, ny).astype(ml_dtypes.bfloat16)
        tables.append(np.concatenate([hi, hi]))
    heights = [2 * counts[0], 3 * counts[1] // 2, 4 * counts[2] // 4]
    touched = touched_layers(nz)

    def kernel(in_ref, base_hbm, fl, fr, t2, t3, out_hbm, s1, s2, s3, buf, sem):
        del base_hbm
        s3[...] = jnp.zeros(s3.shape, F32)
        for side, ref in enumerate((fl, fr)):
            for c in range(2):
                for q in range(groups):
                    s1[2 * side + c, q] = ref[c * nx : c * nx + nx, 128 * q : 128 * q + 128]
            ranks = LEFT_RANKS if side == 0 else RIGHT_RANKS
            at = heights[0]
            for level, table, to in ((1, t2, s2), (2, t3, s3)):
                width, tall, n = ny >> level, heights[level], counts[level]
                flat = jnp.concatenate(
                    [ref[at : at + tall, p * width : p * width + width] for p in range(1 << level)],
                    axis=0,
                )
                hi, lo = split(flat)
                got = dot(jnp.concatenate([hi, lo], axis=1), table[...])
                first = 0 if side == 0 else LEFT_RANKS[level]
                for c in range(ranks[level]):
                    for q in range(groups):
                        piece = got[c * n : c * n + n, 128 * q : 128 * q + 128]
                        if level == 1:
                            to[first + c, q] = piece
                        else:
                            to[first + c, q, pl.ds(0, n, stride=2), :] = piece
                at += tall

        lanes = lax.broadcasted_iota(jnp.int32, (8, 128), 1)
        even_lane = lanes % 2 == 0
        third_cell = (lax.broadcasted_iota(jnp.int32, (8, 128), 0) % 2 + lanes % 4) == 0

        def summed(table_row, get):
            total = None
            for c, scalar in enumerate(table_row):
                if abs(scalar) > 1e-12:
                    total = add(total, get(c) * np.float32(scalar))
            return total

        copies = []
        for slot, z in enumerate(touched):

            def body(t, _, z=z, slot=slot):
                full = pl.multiple_of(16 * t, 8)
                half = pl.multiple_of(8 * t, 8)
                for q in range(groups):
                    if z % 2:
                        for more in (0, 8):
                            rows = pl.ds(full + more, 8)
                            extra = summed(maps[0][z], lambda c: s1[c, q, rows, :])
                            buf[slot, q, rows, :] = add(in_ref[q, z, rows, :], extra)
                        continue
                    evens = pl.ds(16 * t, 8, stride=2)
                    odds = pl.ds(16 * t + 1, 8, stride=2)
                    extra = summed(maps[0][z], lambda c: s1[c, q, odds, :])
                    buf[slot, q, odds, :] = add(in_ref[q, z, odds, :], extra)
                    rows = pl.ds(half, 8)
                    extra = summed(maps[1][z // 2], lambda c: s2[c, q, rows, :])
                    if z % 4 == 0:
                        third = summed(maps[2][z // 4], lambda c: s3[c, q, rows, :])
                        third = 0.0 if third is None else third
                        extra = jnp.where(third_cell, third, 0.0 if extra is None else extra)
                    one = summed(maps[0][z], lambda c: s1[c, q, evens, :])
                    if one is not None:
                        extra = jnp.where(even_lane, 0.0 if extra is None else extra, one)
                    buf[slot, q, evens, :] = add(in_ref[q, z, evens, :], extra)
                return 0

            lax.fori_loop(0, nx // 16, body, 0)
            for q in range(groups):
                copy = pltpu.make_async_copy(
                    buf.at[slot, q], out_hbm.at[z, :, 128 * q : 128 * q + 128], sem.at[slot]
                )
                copy.start()
                copies.append(copy)
        for copy in copies:
            copy.wait()

    return pl.pallas_call(
        kernel,
        in_specs=[VM, HB, VM, VM, VM, VM],
        out_specs=HB,
        out_shape=jax.ShapeDtypeStruct((nz, nx, ny), F32),
        input_output_aliases={1: 0},
        scratch_shapes=[
            pltpu.VMEM((4, groups, nx, 128), F32),
            pltpu.VMEM((maps[1].shape[1], groups, nx // 2, 128), F32),
            pltpu.VMEM((maps[2].shape[1], groups, nx // 2, 128), F32),
            pltpu.VMEM((len(touched), groups, nx, 128), F32),
            pltpu.SemaphoreType.DMA((len(touched),)),
        ],
        compiler_params=params(24),
        name="z_apply",
    )(inner, partial, from_left, from_right, *[jnp.asarray(t) for t in tables])


def swap(to_right, to_left, axis):
    count = lax.axis_size(axis)
    right = [(i, (i + 1) % count) for i in range(count)]
    left = [(j, i) for i, j in right]
    return lax.ppermute(to_right, axis, right), lax.ppermute(to_left, axis, left)


def local(field):
    nz = field.shape[0]
    field, message = x_send(field)
    halo = x_exchange(message)
    x1, x2, x3, to_right, to_left = x_apply(field, halo)
    from_left, from_right = swap(to_right, to_left, "gy")
    combined = z_combine((x1, x2, x3), nz)
    to_right, to_left = y_messages(combined, from_left, from_right, nz)
    below, above = swap(to_right, to_left, "gz")
    inner, partial = main_part((x1, x2, x3), from_left, from_right, nz)
    return z_apply(inner, partial, below, above)


def solution(mesh):
    placed = (P("gz", "gx", "gy"),)
    return jax.shard_map(
        local, mesh=mesh, in_specs=placed, out_specs=P("gz", "gx", "gy"), check_vma=False
    )
```

```python
import functools

import jax
import jax.numpy as jnp
import ml_dtypes
import numpy as np
from jax import lax
from jax.experimental import pallas as pl
from jax.experimental.pallas import tpu as pltpu
from jax.sharding import PartitionSpec as P

lift_alpha = -1.586134342
lift_beta = -0.05298011854
lift_gamma = 0.8829110762
lift_delta = 0.4435068522
lift_zeta = 1.149604398

BF = jnp.bfloat16
F32 = jnp.float32
MIB = 1024 * 1024


def periodic_lift(u):
    s, d = u[0::2].copy(), u[1::2].copy()
    d = d + lift_alpha * (s + np.roll(s, -1, 0))
    s = s + lift_beta * (np.roll(d, 1, 0) + d)
    d = d + lift_gamma * (s + np.roll(s, -1, 0))
    s = s + lift_delta * (np.roll(d, 1, 0) + d)
    out = np.empty_like(u)
    out[0::2] = s * lift_zeta
    out[1::2] = d / lift_zeta
    return out


@functools.lru_cache(None)
def blocks(n):
    current = np.eye(4 * n)
    found = []
    for level in range(3):
        full = periodic_lift(current)
        m = n >> level
        rows = full[m : 2 * m]
        found.append((rows[:, n : 2 * n], rows[:, :n], rows[:, 2 * n : 3 * n]))
        current = full[0::2]
    return found


def row_space(outer, rank):
    _, sizes, basis = np.linalg.svd(outer, full_matrices=False)
    assert sizes[rank:].max() < 1e-10
    basis = basis[:rank].copy()
    basis[np.abs(basis) < 1e-12] = 0.0
    return basis


LEFT_RANKS = (2, 3, 4)
RIGHT_RANKS = (2, 3, 3)


@functools.lru_cache(None)
def sides(n):
    out = []
    for level, (main, left, right) in enumerate(blocks(n)):
        cl = row_space(left, LEFT_RANKS[level])
        cr = row_space(right, RIGHT_RANKS[level])
        out.append((main, cl, left @ cl.T, cr, right @ cr.T))
    return out


def nested_space(outer):
    first = row_space(outer[0], 2)
    every = np.concatenate(outer)
    rest = every - every @ first.T @ first
    return np.concatenate([first, row_space(rest, 4)])


@functools.lru_cache(None)
def joint_sides(n):
    found = blocks(n)
    cl = nested_space([b[1] for b in found])
    cr = nested_space([b[2] for b in found])
    maps = [(b[0], b[1] @ cl.T, b[2] @ cr.T) for b in found]
    return cl, cr, maps


def hi_lo(table):
    table = np.asarray(table, np.float32)
    hi = table.astype(ml_dtypes.bfloat16)
    lo = (table - hi.astype(np.float32)).astype(ml_dtypes.bfloat16)
    return hi, lo


def stack_lhs(table):
    hi, lo = hi_lo(table)
    return np.concatenate([hi, lo, hi], axis=1)


def stack_rhs(table):
    hi, lo = hi_lo(table)
    return np.concatenate([hi, hi, lo], axis=0)


def split(values):
    hi = values.astype(BF)
    return hi, (values - hi.astype(F32)).astype(BF)


def dot(a, b):
    return lax.dot_general(a, b, (((1,), (0,)), ((), ())), preferred_element_type=F32)


def dot_t(a, b):
    return lax.dot_general(a, b, (((1,), (1,)), ((), ())), preferred_element_type=F32)


def spread_columns(table, step, width):
    out = np.zeros((table.shape[0], width))
    out[:, ::step] = table
    return out


VM = pl.BlockSpec(memory_space=pltpu.VMEM)
HB = pl.BlockSpec(memory_space=pltpu.HBM)


def in_hbm(array):
    return pltpu.with_memory_space_constraint(array, pltpu.HBM)


def vmem(shape, dtype=F32):
    return pltpu.VMEM(shape, dtype)


def params(mib):
    return pltpu.CompilerParams(vmem_limit_bytes=mib * MIB)


def x_send(field):
    nz, nx, ny = field.shape
    cl, cr, _ = joint_sides(nx)
    one = stack_lhs(np.concatenate([cl, cr]))
    pair = np.zeros((24, 6 * nx), one.dtype)
    pair[:12, : 3 * nx] = one
    pair[12:, 3 * nx :] = one
    step = 4
    steps = nz // step
    order = [0, steps - 1] + list(range(1, steps - 1))
    flight = 3
    _, low, _, high, _ = sides(nz)[0]
    assert np.abs(low[:, :-step]).max() == 0 and np.abs(high[:, step:]).max() == 0

    def kernel(u_hbm, c_hbm, u_ref, out_ref, up_ref, down_ref, c_ref, u_sem, c_sem):
        table_copy = pltpu.make_async_copy(c_hbm, c_ref, c_sem)
        copies = [
            pltpu.make_async_copy(
                u_hbm.at[i * step : i * step + step], u_ref.at[i * step : i * step + step], u_sem.at[i]
            )
            for i in range(steps)
        ]
        for i in order[:flight]:
            copies[i].start()
        table_copy.start()
        table_copy.wait()
        table = c_ref[...]
        for turn, i in enumerate(order):
            copies[i].wait()
            if turn + flight < steps:
                copies[order[turn + flight]].start()
            for p in range(i * step // 2, (i + 1) * step // 2):
                parts = []
                for z in (2 * p, 2 * p + 1):
                    hi, lo = split(u_ref[z])
                    parts += [hi, hi, lo]
                out_ref[24 * p : 24 * p + 24, :] = dot(table, jnp.concatenate(parts, axis=0))
            if i in order[:2]:
                combos, ref = (high, down_ref) if i == 0 else (low, up_ref)
                for c in range(2):
                    ref[c * nx : c * nx + nx, :] = weighted(
                        [(combos[c, z], lambda z=z: u_ref[z]) for z in range(i * step, (i + 1) * step)]
                    )

    return pl.pallas_call(
        kernel,
        in_specs=[HB, HB],
        out_specs=[VM] * 4,
        out_shape=[vmem((nz, nx, ny)), vmem((nz * 12, ny)), vmem((2 * nx, ny)), vmem((2 * nx, ny))],
        scratch_shapes=[
            pltpu.VMEM(pair.shape, BF),
            pltpu.SemaphoreType.DMA((steps,)),
            pltpu.SemaphoreType.DMA,
        ],
        compiler_params=params(16),
        name="x_send",
    )(in_hbm(field), in_hbm(jnp.asarray(pair)))


def x_exchange(message):
    count = lax.axis_size("gx")
    right = [(i, (i + 1) % count) for i in range(count)]
    if count == 2:
        return lax.ppermute(message, "gx", right)
    left = [(j, i) for i, j in right]
    rows, ny = message.shape
    grid = message.reshape(rows // 12, 12, ny)
    from_left = lax.ppermute(grid[:, :6], "gx", right)
    from_right = lax.ppermute(grid[:, 6:], "gx", left)
    return jnp.concatenate([from_left, from_right], axis=1).reshape(rows, ny)


def x_apply(field, halo):
    nz, nx, ny = field.shape
    _, _, maps = joint_sides(nx)
    main = np.concatenate([m for m, _, _ in maps])
    outer = np.concatenate([np.concatenate([l, r], axis=1) for _, l, r in maps])
    pad = np.zeros((main.shape[0], 4))
    tables = np.stack(
        [
            stack_lhs(np.concatenate([main, outer, pad], axis=1)),
            stack_lhs(np.concatenate([main, pad, outer], axis=1)),
        ]
    )
    rows = main.shape[0]
    counts = [nx, nx // 2, nx // 4]
    step = 8
    steps = nz // step

    combos = []
    for level, (_, cl, _, cr, _) in enumerate(sides(ny)):
        both = np.zeros((8, 128))
        assert np.abs(cl[:, : ny - 64]).max() == 0 and np.abs(cr[:, 64:]).max() == 0
        both[: cl.shape[0], 64:] = cl[:, ny - 64 :]
        both[4 : 4 + cr.shape[0], :64] = cr[:, :64]
        combos.append(stack_lhs(both))
    combos = np.stack(combos)

    def kernel(u_ref, r_ref, t_ref, c_ref, x1, x2, x3, right_ref, left_ref, e1, e2, e3):
        i = pl.program_id(0)
        lanes = lax.broadcasted_iota(jnp.int32, (rows, 128), 1)
        for z in range(step):
            start = pl.multiple_of(i * (12 * step) + 24 * (z // 2) + 8 * (z % 2), 8)
            hi, lo = split(u_ref[i * step + z])
            rhi, rlo = split(r_ref[pl.ds(start, 16), :])
            stacked = jnp.concatenate([hi, rhi, hi, rhi, lo, rlo], axis=0)
            got = dot(t_ref[z % 2], stacked)
            edge = jnp.where(lanes < 64, got[:, :128], got[:, ny - 128 :])
            ehi, elo = split(edge)
            estack = jnp.concatenate([ehi, ehi, elo], axis=1)
            at = 0
            for ref, eref, n in zip((x1, x2, x3), (e1, e2, e3), counts):
                where = pl.ds(pl.multiple_of((i * step + z) * n, 16), n)
                ref[i * step + z] = got[at : at + n]
                eref[where, :] = estack[at : at + n]
                at += n

        @pl.when(i == steps - 1)
        def _():
            row = 0
            for level, (eref, n) in enumerate(zip((e1, e2, e3), counts)):
                got = dot_t(c_ref[level], eref[...])
                for j in range(nz * n // 512):
                    for c in range(LEFT_RANKS[level]):
                        right_ref[row : row + 1, :] = got[c : c + 1, 512 * j : 512 * j + 512]
                        if c < RIGHT_RANKS[level]:
                            left_ref[row : row + 1, :] = got[4 + c : 5 + c, 512 * j : 512 * j + 512]
                        else:
                            left_ref[row : row + 1, :] = jnp.zeros((1, 512), F32)
                        row += 1
            right_ref[row:, :] = jnp.zeros((24 - row, 512), F32)
            left_ref[row:, :] = jnp.zeros((24 - row, 512), F32)

    return pl.pallas_call(
        kernel,
        grid=(steps,),
        in_specs=[VM] * 4,
        out_specs=[VM] * 5,
        out_shape=[vmem((nz, n, ny)) for n in counts] + [jax.ShapeDtypeStruct((24, 512), F32)] * 2,
        scratch_shapes=[pltpu.VMEM((nz * n, 384), BF) for n in counts],
        compiler_params=params(24),
        name="x_apply",
    )(field, halo, jnp.asarray(tables), jnp.asarray(combos))


def z_tables(nz):
    out = []
    for _, cl, pl_, cr, pr in sides(nz):
        out.append((np.concatenate([cl, cr]), np.concatenate([pl_, pr], axis=1)))
    return out


def weighted(parts):
    total = None
    for scalar, get in parts:
        if abs(scalar) < 1e-12:
            continue
        term = get() * np.float32(scalar)
        total = term if total is None else total + term
    return total


def z_combine(x2, x3, halo):
    nz, _, ny = x2.shape
    tables = [t for t, _ in z_tables(nz)]
    counts = [x2.shape[1], x3.shape[1]]
    groups = ny // 128

    def kernel(x2, x3, r_ref, o2, o3, of):
        for ref, out, table, n in zip((x2, x3), (o2, o3), tables[1:], counts):

            def body(k, _, ref=ref, out=out, table=table, n=n):
                row = pl.multiple_of((k // groups) * 8, 8)
                lane = pl.multiple_of((k % groups) * 128, 128)
                get = {}
                for z in range(nz):
                    if np.abs(table[:, z]).max() > 1e-12:
                        get[z] = ref[z, pl.ds(row, 8), pl.ds(lane, 128)]
                for c in range(table.shape[0]):
                    out[pl.ds(pl.multiple_of(c * n + row, 8), 8), pl.ds(lane, 128)] = weighted(
                        [(table[c, z], lambda z=z: get[z]) for z in range(nz)]
                    )
                return 0

            lax.fori_loop(0, (n // 8) * groups, body, 0)
        for c in range(4):
            got = weighted(
                [(tables[0][c, z], lambda z=z: r_ref[12 * z : 12 * z + 12, :]) for z in range(nz)]
            )
            of[4 * c : 4 * c + 2, :] = got[0:2]
            of[4 * c + 2 : 4 * c + 4, :] = got[6:8]

    return pl.pallas_call(
        kernel,
        in_specs=[VM] * 3,
        out_specs=[VM] * 3,
        out_shape=[vmem((t.shape[0] * n, ny)) for t, n in zip(tables[1:], counts)] + [vmem((16, ny))],
        compiler_params=params(16),
        cost_estimate=pl.CostEstimate(flops=20_000_000, bytes_accessed=6_000_000, transcendentals=0),
        name="z_combine",
    )(x2, x3, halo)


def y_tables(ny, spread):
    out = []
    for level, (main, _, left, _, right) in enumerate(sides(ny)):
        step = (1 << level) if spread else 1
        width = ny if spread else ny >> level
        fit = lambda t: spread_columns(t.T, step, width)
        out.append((fit(main), fit(left), fit(right)))
    return out


def halo_rows(level, chunk, nz, counts):
    start = 0
    for below in range(level):
        start += (nz * counts[below] // 512) * LEFT_RANKS[below]
    return start + chunk * LEFT_RANKS[level]


LEFT_AT, RIGHT_AT = 32, 56


def halo_base(left, right, level, nz, counts):
    base = np.zeros((128, left.shape[1]))
    for chunk in range(nz * counts[level] // 512):
        row = halo_rows(level, chunk, nz, counts)
        base[LEFT_AT + row : LEFT_AT + row + left.shape[0]] = left
        base[RIGHT_AT + row : RIGHT_AT + row + right.shape[0]] = right
    return base


def turned(left_ref, right_ref):
    wide = jnp.concatenate(
        [jnp.zeros((LEFT_AT, 512), F32), left_ref[...], right_ref[...], jnp.zeros((48, 512), F32)], axis=0
    )
    return wide.T


def band_tables(level, nz, counts, ny):
    assert ny == 512
    main, left, right = y_tables(ny, True)[level]
    base = halo_base(left, right, level, nz, counts)
    own, edge = [], []
    for j in range(2):
        cols = slice(256 * j, 256 * j + 256)
        own.append(stack_rhs(main[cols, cols]))
        tile = base[:, cols].copy()
        if j == 0:
            tile[:32] = main[256:288, cols]
            assert np.abs(main[288:, cols]).max() == 0
        else:
            tile[96:] = main[224:256, cols]
            assert np.abs(main[:224, cols]).max() == 0
        edge.append(stack_rhs(tile))
    return np.stack(own), np.stack(edge)


def three(values):
    hi, lo = split(values)
    return jnp.concatenate([hi, lo, hi], axis=1)


def banded(rows, edge, own_ref, edge_ref):
    edges = three(edge)
    out = []
    for j in range(2):
        own = three(rows[:, 256 * j : 256 * j + 256])
        out.append(dot(own, own_ref[j]) + dot(edges, edge_ref[j]))
    return jnp.concatenate(out, axis=1)


def plain_edge(rows):
    lanes = lax.broadcasted_iota(jnp.int32, (rows.shape[0], 128), 1)
    before = jnp.where(lanes >= 96, rows[:, 128:256], 0.0)
    return jnp.where(lanes < 32, rows[:, 256:384], before)


def late_rows(counts, ny):
    return [3 * counts[1] * (ny // 2) // ny, 4 * counts[2] * (ny // 4) // ny, 8, 8]


def y_messages(combined, from_left, from_right, nz, band_one):
    c2, c3, cf = combined
    ny = c2.shape[1]
    tables = z_tables(nz)
    nums = [t.shape[0] for t, _ in tables]
    counts = [2 * c2.shape[0] // nums[1], c2.shape[0] // nums[1], c3.shape[0] // nums[2]]
    mains, halos, coefs = [], [], []
    for level, (main, left, right) in enumerate(y_tables(ny, False)):
        mains.append(stack_rhs(main))
        halos.append(stack_rhs(halo_base(left, right, level, nz, counts)))
        chunks = nz * counts[level] // 512
        per = 512 // counts[level]
        table = tables[level][0]
        coef = np.zeros((nums[level], per, 128), np.float32)
        for c in range(nums[level]):
            for zz in range(per):
                for chunk in range(chunks):
                    row = halo_rows(level, chunk, nz, counts)
                    for lane in range(LEFT_RANKS[level]):
                        for base in (LEFT_AT, RIGHT_AT):
                            coef[c, zz, base + row + lane] = table[c, chunk * per + zz]
        coefs.append(coef.reshape(nums[level] * per, 128))
    heights = late_rows(counts, ny)
    height = sum(heights)

    def kernel(c2, c3, cf, fl, fr, own1, edge1, m2, m3, h2, h3, k1, k2, k3, up_ref, down_ref):
        halo = turned(fl, fr)

        def reduced(k, n, num):
            per = 512 // n
            extra = []
            for c in range(num):
                total = None
                for zz in range(per):
                    if np.abs(coefs_of[n][c * per + zz]).max() > 1e-12:
                        term = halo[zz * n : zz * n + n] * k[c * per + zz : c * per + zz + 1, :]
                        total = term if total is None else total + term
                extra.append(total)
            return extra

        coefs_of = dict(zip(counts, coefs))
        got = []
        for c_ref, m, h, k, n, num in zip((c2, c3), (m2, m3), (h2, h3), (k2, k3), counts[1:], nums[1:]):
            extra = jnp.concatenate(reduced(k, n, num), axis=0)
            got.append(dot(three(c_ref[...]), m[...]) + dot(three(extra), h[...]))
        frame = cf[...]
        frame = banded(frame, plain_edge(frame), own1, edge1)
        ones = reduced(k1, counts[0], 4)
        rows8 = lax.broadcasted_iota(jnp.int32, (8, 128), 0)
        for side, ref in enumerate((up_ref, down_ref)):
            at = 0
            for level in (1, 2):
                n, width = counts[level], ny >> level
                ranks = LEFT_RANKS if side == 0 else RIGHT_RANKS
                first = 0 if side == 0 else LEFT_RANKS[level] * n
                total = ranks[level] * n
                tall = heights[level - 1]
                for part in range(1 << level):
                    use = max(min(tall, total - part * tall), 0)
                    lanes = slice(part * width, (part + 1) * width)
                    if use > 0:
                        ref[at : at + use, lanes] = got[level - 1][
                            first + part * tall : first + part * tall + use
                        ]
                    if use < tall:
                        ref[at + use : at + tall, lanes] = jnp.zeros((tall - use, width), F32)
                at += tall
            ref[at : at + 8, :] = frame[8 * side : 8 * side + 8]
            at += 8
            turn = jnp.concatenate(ones[2 * side : 2 * side + 2], axis=0).T
            both = []
            for start in (LEFT_AT, RIGHT_AT):
                v = turn[start : start + 8]
                v = v + pltpu.roll(v, 4, 0)
                both.append(v + pltpu.roll(v, 2, 0))
            ref[at:, :128] = jnp.where(rows8 < 2, both[0], both[1])
            ref[at:, 128:] = jnp.zeros((8, ny - 128), F32)

    return pl.pallas_call(
        kernel,
        in_specs=[VM] * 14,
        out_specs=[VM] * 2,
        out_shape=[vmem((height, ny))] * 2,
        compiler_params=params(24),
        name="y_messages",
    )(
        c2,
        c3,
        cf,
        from_left,
        from_right,
        *band_one,
        *[jnp.asarray(t) for t in mains[1:]],
        *[jnp.asarray(t) for t in halos[1:]],
        *[jnp.asarray(t) for t in coefs],
    )


def add(a, b):
    if a is None:
        return b
    return a if b is None else a + b


def scale(a, c):
    return None if a is None else a * np.float32(c)


def open_lift(values, first, last):
    get = values.get
    low, high = first // 2 - 3, last // 2 + 4
    s = {i: get(2 * i) for i in range(low, high + 1)}
    d = {i: get(2 * i + 1) for i in range(low, high + 1)}
    pick = lambda t, i: t.get(i)
    d1 = {i: add(d[i], scale(add(s[i], pick(s, i + 1)), lift_alpha)) for i in range(low, high + 1)}
    s1 = {i: add(s[i], scale(add(pick(d1, i - 1), d1[i]), lift_beta)) for i in range(low, high + 1)}
    d2 = {i: add(d1[i], scale(add(s1[i], pick(s1, i + 1)), lift_gamma)) for i in range(low, high + 1)}
    s2 = {i: add(s1[i], scale(add(pick(d2, i - 1), d2[i]), lift_delta)) for i in range(low, high + 1)}
    out = {}
    for z in range(first, last + 1):
        if z % 2:
            out[z] = scale(d2[z // 2], 1.0 / lift_zeta)
        else:
            out[z] = scale(s2[z // 2], lift_zeta)
    return out


def touched_layers(nz):
    one, two, three = [np.abs(p).max(axis=1) > 1e-12 for _, p in z_tables(nz)]
    hit = lambda z: one[z] or (z % 2 == 0 and two[z // 2]) or (z % 4 == 0 and three[z // 4])
    return [z for z in range(nz) if hit(z)]


def main_part(xs, from_left, from_right, below, above, bands):
    nz, nx, ny = xs[0].shape
    counts = [nx, nx // 2, nx // 4]
    changed = touched_layers(nz)
    untouched = [z for z in range(nz) if z not in changed]
    groups = ny // 128
    _, _, maps = joint_sides(nx)
    x_table = stack_lhs(maps[0][0])
    masks = []
    for level in range(3):
        chunks = nz * counts[level] // 512
        mask = np.zeros((chunks, 128), np.float32)
        for chunk in range(chunks):
            row = halo_rows(level, chunk, nz, counts)
            for base in (LEFT_AT, RIGHT_AT):
                mask[chunk, base + row : base + row + LEFT_RANKS[level]] = 1.0
        masks.append(mask)
    mask_rows = np.concatenate(masks + [np.zeros((8 - sum(m.shape[0] for m in masks) % 8, 128), np.float32)])
    mask_at = [0, masks[0].shape[0], masks[0].shape[0] + masks[1].shape[0]]

    def kernel(x1, x2, x3, fl, fr, b1, a1, o1, e1, o2, e2, o3, e3, xt, mk, out_ref, w_ref, hbm, w2, halo_ref, sem):
        halo_ref[...] = turned(fl, fr)
        lanes = lax.broadcasted_iota(jnp.int32, (8, 128), 1)
        after, before = lanes < 32, lanes >= 96

        def in_y(x, level, row, own, edge):
            n = counts[level]
            per = 512 // n
            values = x[:, pl.ds(row, 8), :]
            edges = []
            for z in range(nz):
                at = mask_at[level] + z // per
                turn = halo_ref[pl.ds(pl.multiple_of((z % per) * n + row, 8), 8), :] * mk[at : at + 1, :]
                edges.append(
                    jnp.where(after, values[z, :, 256:384], jnp.where(before, values[z, :, 128:256], turn))
                )
            got = banded(
                values.reshape(nz * 8, ny), jnp.concatenate(edges, axis=0), own, edge
            )
            return {z: got[8 * z : 8 * z + 8] for z in range(nz)}

        def store(to, values, row, indices, height=None):
            for z in indices:
                for q in range(groups):
                    piece = values[z][:, 128 * q : 128 * q + 128]
                    if height is None:
                        to[q, z, pl.ds(row, 8), :] = piece
                    else:
                        to[q, pl.ds(pl.multiple_of(z * height + row, 8), 8), :] = piece

        def level_one(k, _):
            row = pl.multiple_of(k * 8, 8)
            got = open_lift(in_y(x1, 0, row, o1, e1), 0, nz - 1)
            store(out_ref, got, row, range(nz))
            return 0

        lax.fori_loop(0, counts[0] // 8, level_one, 0)

        def leaving(layers):
            return [
                pltpu.make_async_copy(
                    out_ref.at[q, z], hbm.at[z, :, 128 * q : 128 * q + 128], sem.at[z]
                )
                for z in layers
                for q in range(groups)
            ]

        copies = leaving([z for z in untouched if z % 2])
        for copy in copies:
            copy.start()

        def lows(values, first, last):
            got = open_lift(values, 2 * first, 2 * last)
            return {i: got[2 * i] for i in range(first, last + 1) if got[2 * i] is not None}

        def level_two(k, _):
            row = pl.multiple_of(k * 8, 8)
            one = lows(in_y(x2, 1, row, o2, e2), -2, nz // 2 + 1)
            store(w2, open_lift(one, 0, nz // 2 - 1), row, range(nz // 2), counts[1])
            return 0

        lax.fori_loop(0, counts[1] // 8, level_two, 0)

        def level_three(k, _):
            row = pl.multiple_of(k * 8, 8)
            one = lows(in_y(x3, 2, row, o3, e3), -2, nz // 2 + 1)
            two = lows(one, -3, nz // 4 + 2)
            got = open_lift(two, 0, nz // 4 - 1)
            for z in range(nz // 4):
                where = pl.ds(2 * z * counts[1] + 2 * row, 8, stride=2)
                for q in range(groups):
                    piece = got[z][:, 128 * q : 128 * q + 128]
                    w2[q, where, :] = jnp.where(lanes % 4 == 0, piece, w2[q, where, :])
            return 0

        lax.fori_loop(0, counts[2] // 8, level_three, 0)

        def merge(k, _):
            row = pl.multiple_of((k // groups) * 8, 8)
            q = k % groups
            where = pl.ds(2 * row, 8, stride=2)
            for z in range(nz // 2):
                inner = w2[q, pl.ds(pl.multiple_of(z * counts[1] + row, 8), 8), :]
                out_ref[q, 2 * z, where, :] = jnp.where(lanes % 2 == 0, inner, out_ref[q, 2 * z, where, :])
            return 0

        lax.fori_loop(0, (counts[1] // 8) * groups, merge, 0)
        more = leaving([z for z in untouched if z % 2 == 0])
        for copy in more:
            copy.start()

        early = []
        for ref in (b1, a1):
            for c in range(2):
                hi, lo = split(ref[c * nx : c * nx + nx, :])
                early.append(dot(xt[...], jnp.concatenate([hi, hi, lo], axis=0)))
        early = jnp.concatenate(early, axis=0)
        w_ref[...] = banded(early, plain_edge(early), o1, e1)

        for copy in copies + more:
            copy.wait()

    flat = [t for band in bands for t in band]
    return pl.pallas_call(
        kernel,
        in_specs=[VM] * 15,
        out_specs=[VM, VM, HB],
        out_shape=[
            vmem((groups, nz, nx, 128)),
            vmem((4 * nx, ny)),
            pltpu.HBM((nz, nx, ny), F32),
        ],
        scratch_shapes=[
            pltpu.VMEM((groups, nz // 2 * counts[1], 128), F32),
            pltpu.VMEM((512, 128), F32),
            pltpu.SemaphoreType.DMA((nz,)),
        ],
        compiler_params=params(32),
        cost_estimate=pl.CostEstimate(
            flops=8_000_000_000, bytes_accessed=20_000_000, transcendentals=0
        ),
        name="main_part",
    )(*xs, from_left, from_right, below, above, *flat, jnp.asarray(x_table), jnp.asarray(mask_rows))


def z_apply(inner, partial, early, from_left, from_right):
    groups, nz, nx, _ = inner.shape
    ny = groups * 128
    maps = [p for _, p in z_tables(nz)]
    counts = [nx, nx // 2, nx // 4]
    tables = []
    for level in (1, 2):
        width = ny >> level
        hi = spread_columns(np.eye(width), 1 << level, ny).astype(ml_dtypes.bfloat16)
        tables.append(np.concatenate([hi, hi]))
    heights = late_rows(counts, ny)
    _, _, x_maps = joint_sides(nx)
    frame = np.zeros((4 * nx, 16))
    for c in range(4):
        frame[c * nx : c * nx + nx, 4 * c : 4 * c + 2] = x_maps[0][1][:, :2]
        frame[c * nx : c * nx + nx, 4 * c + 2 : 4 * c + 4] = x_maps[0][2][:, :2]
        assert np.abs(x_maps[0][1][:, 2:]).max() < 1e-12 and np.abs(x_maps[0][2][:, 2:]).max() < 1e-12
    _, left, right = y_tables(ny, True)[0]
    side_rows = np.zeros((128, ny))
    side_rows[:2], side_rows[2:4] = left, right
    touched = touched_layers(nz)

    def kernel(in_ref, base_hbm, w_ref, fl, fr, t2, t3, xf, yf, out_hbm, s1, s2, s3, buf, sem):
        del base_hbm
        s3[...] = jnp.zeros(s3.shape, F32)
        at = heights[0] + heights[1]
        hi, lo = split(jnp.concatenate([fl[at : at + 8, :], fr[at : at + 8, :]], axis=0))
        at += 8
        none = jnp.zeros((120, 128), F32)
        turn = [jnp.concatenate([ref[at : at + 8, :128], none], axis=0).T for ref in (fl, fr)]
        first = (
            w_ref[...]
            + dot(xf[...], jnp.concatenate([hi, hi, lo], axis=0))
            + dot(three(jnp.concatenate(turn, axis=0)), yf[...])
        )
        for c in range(4):
            for q in range(groups):
                s1[c, q] = first[c * nx : c * nx + nx, 128 * q : 128 * q + 128]
        for side, ref in enumerate((fl, fr)):
            ranks = LEFT_RANKS if side == 0 else RIGHT_RANKS
            at = 0
            for level, table, to in ((1, t2, s2), (2, t3, s3)):
                width, tall, n = ny >> level, heights[level - 1], counts[level]
                flat = jnp.concatenate(
                    [ref[at : at + tall, p * width : p * width + width] for p in range(1 << level)],
                    axis=0,
                )
                hi, lo = split(flat)
                got = dot(jnp.concatenate([hi, lo], axis=1), table[...])
                first = 0 if side == 0 else LEFT_RANKS[level]
                for c in range(ranks[level]):
                    for q in range(groups):
                        piece = got[c * n : c * n + n, 128 * q : 128 * q + 128]
                        if level == 1:
                            to[first + c, q] = piece
                        else:
                            to[first + c, q, pl.ds(0, n, stride=2), :] = piece
                at += tall

        lanes = lax.broadcasted_iota(jnp.int32, (8, 128), 1)
        even_lane = lanes % 2 == 0
        third_cell = (lax.broadcasted_iota(jnp.int32, (8, 128), 0) % 2 + lanes % 4) == 0

        def summed(table_row, get):
            total = None
            for c, scalar in enumerate(table_row):
                if abs(scalar) > 1e-12:
                    total = add(total, get(c) * np.float32(scalar))
            return total

        copies = []
        for slot, z in enumerate(touched):

            def body(t, _, z=z, slot=slot):
                full = pl.multiple_of(16 * t, 8)
                half = pl.multiple_of(8 * t, 8)
                for q in range(groups):
                    if z % 2:
                        for more in (0, 8):
                            rows = pl.ds(full + more, 8)
                            extra = summed(maps[0][z], lambda c: s1[c, q, rows, :])
                            buf[slot, q, rows, :] = add(in_ref[q, z, rows, :], extra)
                        continue
                    evens = pl.ds(16 * t, 8, stride=2)
                    odds = pl.ds(16 * t + 1, 8, stride=2)
                    extra = summed(maps[0][z], lambda c: s1[c, q, odds, :])
                    buf[slot, q, odds, :] = add(in_ref[q, z, odds, :], extra)
                    rows = pl.ds(half, 8)
                    extra = summed(maps[1][z // 2], lambda c: s2[c, q, rows, :])
                    if z % 4 == 0:
                        third = summed(maps[2][z // 4], lambda c: s3[c, q, rows, :])
                        third = 0.0 if third is None else third
                        extra = jnp.where(third_cell, third, 0.0 if extra is None else extra)
                    one = summed(maps[0][z], lambda c: s1[c, q, evens, :])
                    if one is not None:
                        extra = jnp.where(even_lane, 0.0 if extra is None else extra, one)
                    buf[slot, q, evens, :] = add(in_ref[q, z, evens, :], extra)
                return 0

            lax.fori_loop(0, nx // 16, body, 0)
            for q in range(groups):
                copy = pltpu.make_async_copy(
                    buf.at[slot, q], out_hbm.at[z, :, 128 * q : 128 * q + 128], sem.at[slot]
                )
                copy.start()
                copies.append(copy)
        for copy in copies:
            copy.wait()

    return pl.pallas_call(
        kernel,
        in_specs=[VM, HB] + [VM] * 7,
        out_specs=HB,
        out_shape=jax.ShapeDtypeStruct((nz, nx, ny), F32),
        input_output_aliases={1: 0},
        scratch_shapes=[
            pltpu.VMEM((4, groups, nx, 128), F32),
            pltpu.VMEM((maps[1].shape[1], groups, nx // 2, 128), F32),
            pltpu.VMEM((maps[2].shape[1], groups, nx // 2, 128), F32),
            pltpu.VMEM((len(touched), groups, nx, 128), F32),
            pltpu.SemaphoreType.DMA((len(touched),)),
        ],
        compiler_params=params(24),
        name="z_apply",
    )(
        inner,
        partial,
        early,
        from_left,
        from_right,
        *[jnp.asarray(t) for t in tables],
        jnp.asarray(stack_lhs(frame)),
        jnp.asarray(stack_rhs(side_rows)),
    )


def swap(to_right, to_left, axis):
    count = lax.axis_size(axis)
    right = [(i, (i + 1) % count) for i in range(count)]
    left = [(j, i) for i, j in right]
    return lax.ppermute(to_right, axis, right), lax.ppermute(to_left, axis, left)


def local(field):
    nz, nx, ny = field.shape
    counts = [nx, nx // 2, nx // 4]
    bands = [[jnp.asarray(t) for t in band_tables(level, nz, counts, ny)] for level in range(3)]
    field, message, up, down = x_send(field)
    halo = x_exchange(message)
    below, above = swap(up, down, "gz")
    x1, x2, x3, to_right, to_left = x_apply(field, halo)
    from_left, from_right = swap(to_right, to_left, "gy")
    combined = z_combine(x2, x3, halo)
    up, down = y_messages(combined, from_left, from_right, nz, bands[0])
    late_below, late_above = swap(up, down, "gz")
    inner, early, partial = main_part((x1, x2, x3), from_left, from_right, below, above, bands)
    return z_apply(inner, partial, early, late_below, late_above)


def solution(mesh):
    placed = (P("gz", "gx", "gy"),)
    return jax.shard_map(
        local, mesh=mesh, in_specs=placed, out_specs=P("gz", "gx", "gy"), check_vma=False
    )
```

```python
import functools

import jax
import jax.numpy as jnp
import ml_dtypes
import numpy as np
from jax import lax
from jax.experimental import pallas as pl
from jax.experimental.pallas import tpu as pltpu
from jax.sharding import PartitionSpec as P

lift_alpha = -1.586134342
lift_beta = -0.05298011854
lift_gamma = 0.8829110762
lift_delta = 0.4435068522
lift_zeta = 1.149604398

BF = jnp.bfloat16
F32 = jnp.float32
MIB = 1024 * 1024


def periodic_lift(u):
    s, d = u[0::2].copy(), u[1::2].copy()
    d = d + lift_alpha * (s + np.roll(s, -1, 0))
    s = s + lift_beta * (np.roll(d, 1, 0) + d)
    d = d + lift_gamma * (s + np.roll(s, -1, 0))
    s = s + lift_delta * (np.roll(d, 1, 0) + d)
    out = np.empty_like(u)
    out[0::2] = s * lift_zeta
    out[1::2] = d / lift_zeta
    return out


@functools.lru_cache(None)
def blocks(n):
    current = np.eye(4 * n)
    found = []
    for level in range(3):
        full = periodic_lift(current)
        m = n >> level
        rows = full[m : 2 * m]
        found.append((rows[:, n : 2 * n], rows[:, :n], rows[:, 2 * n : 3 * n]))
        current = full[0::2]
    return found


def row_space(outer, rank):
    _, sizes, basis = np.linalg.svd(outer, full_matrices=False)
    assert sizes[rank:].max() < 1e-10
    basis = basis[:rank].copy()
    basis[np.abs(basis) < 1e-12] = 0.0
    return basis


LEFT_RANKS = (2, 3, 4)
RIGHT_RANKS = (2, 3, 3)


@functools.lru_cache(None)
def sides(n):
    out = []
    for level, (main, left, right) in enumerate(blocks(n)):
        cl = row_space(left, LEFT_RANKS[level])
        cr = row_space(right, RIGHT_RANKS[level])
        out.append((main, cl, left @ cl.T, cr, right @ cr.T))
    return out


def nested_space(outer):
    first = row_space(outer[0], 2)
    every = np.concatenate(outer)
    rest = every - every @ first.T @ first
    return np.concatenate([first, row_space(rest, 4)])


@functools.lru_cache(None)
def joint_sides(n):
    found = blocks(n)
    cl = nested_space([b[1] for b in found])
    cr = nested_space([b[2] for b in found])
    maps = [(b[0], b[1] @ cl.T, b[2] @ cr.T) for b in found]
    return cl, cr, maps


def hi_lo(table):
    table = np.asarray(table, np.float32)
    hi = table.astype(ml_dtypes.bfloat16)
    lo = (table - hi.astype(np.float32)).astype(ml_dtypes.bfloat16)
    return hi, lo


def stack_lhs(table):
    hi, lo = hi_lo(table)
    return np.concatenate([hi, lo, hi], axis=1)


def stack_rhs(table):
    hi, lo = hi_lo(table)
    return np.concatenate([hi, hi, lo], axis=0)


def split(values):
    hi = values.astype(BF)
    return hi, (values - hi.astype(F32)).astype(BF)


def dot(a, b):
    return lax.dot_general(a, b, (((1,), (0,)), ((), ())), preferred_element_type=F32)


def dot_t(a, b):
    return lax.dot_general(a, b, (((1,), (1,)), ((), ())), preferred_element_type=F32)


def spread_columns(table, step, width):
    out = np.zeros((table.shape[0], width))
    out[:, ::step] = table
    return out


VM = pl.BlockSpec(memory_space=pltpu.VMEM)
HB = pl.BlockSpec(memory_space=pltpu.HBM)


def in_hbm(array):
    return pltpu.with_memory_space_constraint(array, pltpu.HBM)


def vmem(shape, dtype=F32):
    return pltpu.VMEM(shape, dtype)


def params(mib):
    return pltpu.CompilerParams(vmem_limit_bytes=mib * MIB)


def x_send(field):
    nz, nx, ny = field.shape
    cl, cr, _ = joint_sides(nx)
    one = np.concatenate([cl, cr])
    group = 4
    wide = np.kron(np.eye(group), one)
    hi_rows, lo_rows = hi_lo(wide)
    pair = np.concatenate([hi_rows, lo_rows])
    height = 12 * group
    step = 8
    steps = nz // step
    order = [0, steps - 1] + list(range(1, steps - 1))
    flight = 2
    _, low, _, high, _ = sides(nz)[0]
    assert np.abs(low[:, :-step]).max() == 0 and np.abs(high[:, step:]).max() == 0

    def kernel(u_hbm, c_hbm, u_ref, out_ref, up_ref, down_ref, c_ref, u_sem, c_sem):
        table_copy = pltpu.make_async_copy(c_hbm, c_ref, c_sem)
        copies = [
            pltpu.make_async_copy(
                u_hbm.at[i * step : i * step + step], u_ref.at[i * step : i * step + step], u_sem.at[i]
            )
            for i in range(steps)
        ]
        for i in order[:flight]:
            copies[i].start()
        table_copy.start()
        table_copy.wait()
        table = c_ref[...]
        for turn, i in enumerate(order):
            copies[i].wait()
            if turn + flight < steps:
                copies[order[turn + flight]].start()
            for g in range(i * step // group, (i + 1) * step // group):
                hi, lo = split(u_ref[group * g : group * g + group].reshape(group * nx, ny))
                both = dot(table, hi)
                out_ref[height * g : height * g + height, :] = (
                    both[:height] + both[height:] + dot(table[:height], lo)
                )
            if i in order[:2]:
                combos, ref = (high, down_ref) if i == 0 else (low, up_ref)
                for c in range(2):
                    ref[c * nx : c * nx + nx, :] = weighted(
                        [(combos[c, z], lambda z=z: u_ref[z]) for z in range(i * step, (i + 1) * step)]
                    )

    return pl.pallas_call(
        kernel,
        in_specs=[HB, HB],
        out_specs=[VM] * 4,
        out_shape=[vmem((nz, nx, ny)), vmem((nz * 12, ny)), vmem((2 * nx, ny)), vmem((2 * nx, ny))],
        scratch_shapes=[
            pltpu.VMEM(pair.shape, BF),
            pltpu.SemaphoreType.DMA((steps,)),
            pltpu.SemaphoreType.DMA,
        ],
        compiler_params=params(16),
        name="x_send",
    )(in_hbm(field), in_hbm(jnp.asarray(pair)))


def x_exchange(message):
    count = lax.axis_size("gx")
    right = [(i, (i + 1) % count) for i in range(count)]
    if count == 2:
        return lax.ppermute(message, "gx", right)
    left = [(j, i) for i, j in right]
    rows, ny = message.shape
    grid = message.reshape(rows // 12, 12, ny)
    from_left = lax.ppermute(grid[:, :6], "gx", right)
    from_right = lax.ppermute(grid[:, 6:], "gx", left)
    return jnp.concatenate([from_left, from_right], axis=1).reshape(rows, ny)


def x_apply(field, halo):
    nz, nx, ny = field.shape
    _, _, maps = joint_sides(nx)
    main = np.concatenate([m for m, _, _ in maps])
    outer = np.concatenate([np.concatenate([l, r], axis=1) for _, l, r in maps])
    pad = np.zeros((main.shape[0], 4))
    tables = np.stack(
        [
            stack_lhs(np.concatenate([main, outer, pad], axis=1)),
            stack_lhs(np.concatenate([main, pad, outer], axis=1)),
        ]
    )
    rows = main.shape[0]
    counts = [nx, nx // 2, nx // 4]
    step = 8
    steps = nz // step

    combos = []
    for level, (_, cl, _, cr, _) in enumerate(sides(ny)):
        both = np.zeros((8, 128))
        assert np.abs(cl[:, : ny - 64]).max() == 0 and np.abs(cr[:, 64:]).max() == 0
        both[: cl.shape[0], 64:] = cl[:, ny - 64 :]
        both[4 : 4 + cr.shape[0], :64] = cr[:, :64]
        combos.append(stack_lhs(both))
    combos = np.stack(combos)

    def kernel(u_ref, r_ref, t_ref, c_ref, x1, x2, x3, right_ref, left_ref, e1, e2, e3):
        i = pl.program_id(0)
        lanes = lax.broadcasted_iota(jnp.int32, (rows, 128), 1)
        for z in range(step):
            start = pl.multiple_of(i * (12 * step) + 24 * (z // 2) + 8 * (z % 2), 8)
            hi, lo = split(u_ref[i * step + z])
            rhi, rlo = split(r_ref[pl.ds(start, 16), :])
            stacked = jnp.concatenate([hi, rhi, hi, rhi, lo, rlo], axis=0)
            got = dot(t_ref[z % 2], stacked)
            edge = jnp.where(lanes < 64, got[:, :128], got[:, ny - 128 :])
            ehi, elo = split(edge)
            estack = jnp.concatenate([ehi, ehi, elo], axis=1)
            at = 0
            for ref, eref, n in zip((x1, x2, x3), (e1, e2, e3), counts):
                where = pl.ds(pl.multiple_of((i * step + z) * n, 16), n)
                ref[i * step + z] = got[at : at + n]
                eref[where, :] = estack[at : at + n]
                at += n

        @pl.when(i == steps - 1)
        def _():
            row = 0
            for level, (eref, n) in enumerate(zip((e1, e2, e3), counts)):
                got = dot_t(c_ref[level], eref[...])
                for j in range(nz * n // 512):
                    for c in range(LEFT_RANKS[level]):
                        right_ref[row : row + 1, :] = got[c : c + 1, 512 * j : 512 * j + 512]
                        if c < RIGHT_RANKS[level]:
                            left_ref[row : row + 1, :] = got[4 + c : 5 + c, 512 * j : 512 * j + 512]
                        else:
                            left_ref[row : row + 1, :] = jnp.zeros((1, 512), F32)
                        row += 1
            right_ref[row:, :] = jnp.zeros((24 - row, 512), F32)
            left_ref[row:, :] = jnp.zeros((24 - row, 512), F32)

    return pl.pallas_call(
        kernel,
        grid=(steps,),
        in_specs=[VM] * 4,
        out_specs=[VM] * 5,
        out_shape=[vmem((nz, n, ny)) for n in counts] + [jax.ShapeDtypeStruct((24, 512), F32)] * 2,
        scratch_shapes=[pltpu.VMEM((nz * n, 384), BF) for n in counts],
        compiler_params=params(24),
        name="x_apply",
    )(field, halo, jnp.asarray(tables), jnp.asarray(combos))


def add(a, b):
    if a is None:
        return b
    return a if b is None else a + b


def scale(a, c):
    return None if a is None else a * np.float32(c)


def open_lift(values, first, last):
    get = values.get
    low, high = first // 2 - 3, last // 2 + 4
    s = {i: get(2 * i) for i in range(low, high + 1)}
    d = {i: get(2 * i + 1) for i in range(low, high + 1)}
    pick = lambda t, i: t.get(i)
    d1 = {i: add(d[i], scale(add(s[i], pick(s, i + 1)), lift_alpha)) for i in range(low, high + 1)}
    s1 = {i: add(s[i], scale(add(pick(d1, i - 1), d1[i]), lift_beta)) for i in range(low, high + 1)}
    d2 = {i: add(d1[i], scale(add(s1[i], pick(s1, i + 1)), lift_gamma)) for i in range(low, high + 1)}
    s2 = {i: add(s1[i], scale(add(pick(d2, i - 1), d2[i]), lift_delta)) for i in range(low, high + 1)}
    out = {}
    for z in range(first, last + 1):
        if z % 2:
            out[z] = scale(d2[z // 2], 1.0 / lift_zeta)
        else:
            out[z] = scale(s2[z // 2], lift_zeta)
    return out


def lows(values, first, last):
    got = open_lift(values, 2 * first, 2 * last)
    return {i: got[2 * i] for i in range(first, last + 1) if got[2 * i] is not None}


def own_levels(values, nz, level):
    if level >= 1:
        values = lows(values, -2, nz // 2 + 1)
    if level >= 2:
        values = lows(values, -3, nz // 4 + 2)
    return open_lift(values, 0, (nz >> level) - 1)


def z_tables(nz):
    out = []
    for _, cl, pl_, cr, pr in sides(nz):
        out.append((np.concatenate([cl, cr]), np.concatenate([pl_, pr], axis=1)))
    return out


def weighted(parts):
    total = None
    for scalar, get in parts:
        if abs(scalar) < 1e-12:
            continue
        term = get() * np.float32(scalar)
        total = term if total is None else total + term
    return total


def z_first(x2, x3, halo):
    nz, _, ny = x2.shape
    tables = [t for t, _ in z_tables(nz)]
    counts = [x2.shape[1], x3.shape[1]]
    groups = ny // 128

    def kernel(x2, x3, r_ref, o2, o3, of, y2, y3):
        for level, ref, out, own, table, n in zip((1, 2), (x2, x3), (o2, o3), (y2, y3), tables[1:], counts):

            def body(k, _, level=level, ref=ref, out=out, own=own, table=table, n=n):
                row = pl.multiple_of((k // groups) * 8, 8)
                lane = pl.multiple_of((k % groups) * 128, 128)
                get = {}
                for z in range(nz):
                    get[z] = ref[z, pl.ds(row, 8), pl.ds(lane, 128)]
                for z, value in own_levels(get, nz, level).items():
                    own[z, pl.ds(row, 8), pl.ds(lane, 128)] = value
                for c in range(table.shape[0]):
                    out[pl.ds(pl.multiple_of(c * n + row, 8), 8), pl.ds(lane, 128)] = weighted(
                        [(table[c, z], lambda z=z: get[z]) for z in range(nz)]
                    )
                return 0

            lax.fori_loop(0, (n // 8) * groups, body, 0)
        for c in range(4):
            got = weighted(
                [(tables[0][c, z], lambda z=z: r_ref[12 * z : 12 * z + 12, :]) for z in range(nz)]
            )
            of[4 * c : 4 * c + 2, :] = got[0:2]
            of[4 * c + 2 : 4 * c + 4, :] = got[6:8]

    return pl.pallas_call(
        kernel,
        in_specs=[VM] * 3,
        out_specs=[VM] * 5,
        out_shape=[vmem((t.shape[0] * n, ny)) for t, n in zip(tables[1:], counts)]
        + [vmem((16, ny)), vmem((nz // 2, counts[0], ny)), vmem((nz // 4, counts[1], ny))],
        compiler_params=params(16),
        cost_estimate=pl.CostEstimate(flops=20_000_000, bytes_accessed=6_000_000, transcendentals=0),
        name="z_first",
    )(x2, x3, halo)


def y_tables(ny, spread):
    out = []
    for level, (main, _, left, _, right) in enumerate(sides(ny)):
        step = (1 << level) if spread else 1
        width = ny if spread else ny >> level
        fit = lambda t: spread_columns(t.T, step, width)
        out.append((fit(main), fit(left), fit(right)))
    return out


def halo_rows(level, chunk, nz, counts):
    start = 0
    for below in range(level):
        start += (nz * counts[below] // 512) * LEFT_RANKS[below]
    return start + chunk * LEFT_RANKS[level]


LEFT_AT, RIGHT_AT = 32, 56


def halo_base(left, right, level, nz, counts):
    base = np.zeros((128, left.shape[1]))
    for chunk in range(nz * counts[level] // 512):
        row = halo_rows(level, chunk, nz, counts)
        base[LEFT_AT + row : LEFT_AT + row + left.shape[0]] = left
        base[RIGHT_AT + row : RIGHT_AT + row + right.shape[0]] = right
    return base


def turned(left_ref, right_ref):
    wide = jnp.concatenate(
        [jnp.zeros((LEFT_AT, 512), F32), left_ref[...], right_ref[...], jnp.zeros((48, 512), F32)], axis=0
    )
    return wide.T


def band_tables(level, nz, counts, ny):
    assert ny == 512
    main, left, right = y_tables(ny, True)[level]
    base = halo_base(left, right, level, nz, counts)
    own, edge = [], []
    for j in range(2):
        cols = slice(256 * j, 256 * j + 256)
        own.append(stack_rhs(main[cols, cols]))
        tile = base[:, cols].copy()
        if j == 0:
            tile[:32] = main[256:288, cols]
            assert np.abs(main[288:, cols]).max() == 0
        else:
            tile[96:] = main[224:256, cols]
            assert np.abs(main[:224, cols]).max() == 0
        edge.append(stack_rhs(tile))
    return np.stack(own), np.stack(edge)


def three(values):
    hi, lo = split(values)
    return jnp.concatenate([hi, lo, hi], axis=1)


def banded(rows, edge, own_ref, edge_ref):
    edges = three(edge)
    out = []
    for j in range(2):
        own = three(rows[:, 256 * j : 256 * j + 256])
        out.append(dot(own, own_ref[j]) + dot(edges, edge_ref[j]))
    return jnp.concatenate(out, axis=1)


def plain_edge(rows):
    lanes = lax.broadcasted_iota(jnp.int32, (rows.shape[0], 128), 1)
    before = jnp.where(lanes >= 96, rows[:, 128:256], 0.0)
    return jnp.where(lanes < 32, rows[:, 256:384], before)


def late_rows(counts, ny):
    return [3 * counts[1] * (ny // 2) // ny, 4 * counts[2] * (ny // 4) // ny, 8, 8]


def y_messages(combined, from_left, from_right, nz, band_one):
    c2, c3, cf = combined
    ny = c2.shape[1]
    tables = z_tables(nz)
    nums = [t.shape[0] for t, _ in tables]
    counts = [2 * c2.shape[0] // nums[1], c2.shape[0] // nums[1], c3.shape[0] // nums[2]]
    mains, halos, coefs = [], [], []
    for level, (main, left, right) in enumerate(y_tables(ny, False)):
        mains.append(stack_rhs(main))
        halos.append(stack_rhs(halo_base(left, right, level, nz, counts)))
        chunks = nz * counts[level] // 512
        per = 512 // counts[level]
        table = tables[level][0]
        coef = np.zeros((nums[level], per, 128), np.float32)
        for c in range(nums[level]):
            for zz in range(per):
                for chunk in range(chunks):
                    row = halo_rows(level, chunk, nz, counts)
                    for lane in range(LEFT_RANKS[level]):
                        for base in (LEFT_AT, RIGHT_AT):
                            coef[c, zz, base + row + lane] = table[c, chunk * per + zz]
        coefs.append(coef.reshape(nums[level] * per, 128))
    heights = late_rows(counts, ny)
    height = sum(heights)

    def kernel(c2, c3, cf, fl, fr, own1, edge1, m2, m3, h2, h3, k1, k2, k3, up_ref, down_ref):
        halo = turned(fl, fr)

        def reduced(k, n, num):
            per = 512 // n
            extra = []
            for c in range(num):
                total = None
                for zz in range(per):
                    if np.abs(coefs_of[n][c * per + zz]).max() > 1e-12:
                        term = halo[zz * n : zz * n + n] * k[c * per + zz : c * per + zz + 1, :]
                        total = term if total is None else total + term
                extra.append(total)
            return extra

        coefs_of = dict(zip(counts, coefs))
        got = []
        for c_ref, m, h, k, n, num in zip((c2, c3), (m2, m3), (h2, h3), (k2, k3), counts[1:], nums[1:]):
            extra = jnp.concatenate(reduced(k, n, num), axis=0)
            got.append(dot(three(c_ref[...]), m[...]) + dot(three(extra), h[...]))
        frame = cf[...]
        frame = banded(frame, plain_edge(frame), own1, edge1)
        ones = reduced(k1, counts[0], 4)
        rows8 = lax.broadcasted_iota(jnp.int32, (8, 128), 0)
        for side, ref in enumerate((up_ref, down_ref)):
            at = 0
            for level in (1, 2):
                n, width = counts[level], ny >> level
                ranks = LEFT_RANKS if side == 0 else RIGHT_RANKS
                first = 0 if side == 0 else LEFT_RANKS[level] * n
                total = ranks[level] * n
                tall = heights[level - 1]
                for part in range(1 << level):
                    use = max(min(tall, total - part * tall), 0)
                    lanes = slice(part * width, (part + 1) * width)
                    if use > 0:
                        ref[at : at + use, lanes] = got[level - 1][
                            first + part * tall : first + part * tall + use
                        ]
                    if use < tall:
                        ref[at + use : at + tall, lanes] = jnp.zeros((tall - use, width), F32)
                at += tall
            ref[at : at + 8, :] = frame[8 * side : 8 * side + 8]
            at += 8
            turn = jnp.concatenate(ones[2 * side : 2 * side + 2], axis=0).T
            both = []
            for start in (LEFT_AT, RIGHT_AT):
                v = turn[start : start + 8]
                v = v + pltpu.roll(v, 4, 0)
                both.append(v + pltpu.roll(v, 2, 0))
            ref[at:, :128] = jnp.where(rows8 < 2, both[0], both[1])
            ref[at:, 128:] = jnp.zeros((8, ny - 128), F32)

    return pl.pallas_call(
        kernel,
        in_specs=[VM] * 14,
        out_specs=[VM] * 2,
        out_shape=[vmem((height, ny))] * 2,
        compiler_params=params(24),
        name="y_messages",
    )(
        c2,
        c3,
        cf,
        from_left,
        from_right,
        *band_one,
        *[jnp.asarray(t) for t in mains[1:]],
        *[jnp.asarray(t) for t in halos[1:]],
        *[jnp.asarray(t) for t in coefs],
    )


def touched_layers(nz):
    one, two, three = [np.abs(p).max(axis=1) > 1e-12 for _, p in z_tables(nz)]
    hit = lambda z: one[z] or (z % 2 == 0 and two[z // 2]) or (z % 4 == 0 and three[z // 4])
    return [z for z in range(nz) if hit(z)]


def main_part(xs, from_left, from_right, below, above, bands):
    nz, nx, ny = xs[0].shape
    counts = [nx, nx // 2, nx // 4]
    changed = touched_layers(nz)
    untouched = [z for z in range(nz) if z not in changed]
    groups = ny // 128
    _, _, maps = joint_sides(nx)
    x_table = stack_lhs(maps[0][0])
    masks = []
    for level in range(3):
        chunks = nz * counts[level] // 512
        per = 512 // counts[level]
        lanes_of = np.zeros((chunks, 128))
        for chunk in range(chunks):
            row = halo_rows(level, chunk, nz, counts)
            for base in (LEFT_AT, RIGHT_AT):
                lanes_of[chunk, base + row : base + row + LEFT_RANKS[level]] = 1.0
        if level == 0:
            masks.append(lanes_of)
        else:
            own = sides(nz)[level][0]
            lanes = np.einsum("ocz,cl->ozl", own.reshape(own.shape[0], chunks, per), lanes_of)
            masks.append(lanes.reshape(-1, 128))
    masks = [np.concatenate([m, np.zeros((-m.shape[0] % 8, 128))]).astype(np.float32) for m in masks]

    def kernel(x1, x2, x3, fl, fr, b1, a1, o1, e1, o2, e2, o3, e3, xt, k1, k2, k3, out_ref, w_ref, hbm, w2, halo_ref, sem):
        halo_ref[...] = turned(fl, fr)
        lanes = lax.broadcasted_iota(jnp.int32, (8, 128), 1)
        after, before = lanes < 32, lanes >= 96

        def in_y(x, level, row, own, edge, mk):
            n = counts[level]
            per = 512 // n
            layers = nz >> level
            values = x[:, pl.ds(row, 8), :]
            turns = [halo_ref[pl.ds(pl.multiple_of(zz * n + row, 8), 8), :] for zz in range(per)]
            edges = []
            for z in range(layers):
                if level == 0:
                    turn = turns[z % per] * mk[z // per : z // per + 1, :]
                else:
                    turn = None
                    for zz in range(per):
                        if np.abs(masks[level][z * per + zz]).max() > 1e-12:
                            turn = add(turn, turns[zz] * mk[z * per + zz : z * per + zz + 1, :])
                edges.append(
                    jnp.where(after, values[z, :, 256:384], jnp.where(before, values[z, :, 128:256], turn))
                )
            got = banded(
                values.reshape(layers * 8, ny), jnp.concatenate(edges, axis=0), own, edge
            )
            return {z: got[8 * z : 8 * z + 8] for z in range(layers)}

        def store(to, values, row, indices, height=None):
            for z in indices:
                for q in range(groups):
                    piece = values[z][:, 128 * q : 128 * q + 128]
                    if height is None:
                        to[q, z, pl.ds(row, 8), :] = piece
                    else:
                        to[q, pl.ds(pl.multiple_of(z * height + row, 8), 8), :] = piece

        def level_one(k, _):
            row = pl.multiple_of(k * 8, 8)
            got = own_levels(in_y(x1, 0, row, o1, e1, k1), nz, 0)
            store(out_ref, got, row, range(nz))
            return 0

        lax.fori_loop(0, counts[0] // 8, level_one, 0, unroll=2)

        def leaving(layers):
            return [
                pltpu.make_async_copy(
                    out_ref.at[q, z], hbm.at[z, :, 128 * q : 128 * q + 128], sem.at[z]
                )
                for z in layers
                for q in range(groups)
            ]

        copies = leaving([z for z in untouched if z % 2])
        for copy in copies:
            copy.start()

        def level_two(k, _):
            row = pl.multiple_of(k * 8, 8)
            store(w2, in_y(x2, 1, row, o2, e2, k2), row, range(nz // 2), counts[1])
            return 0

        lax.fori_loop(0, counts[1] // 8, level_two, 0)

        def level_three(k, _):
            row = pl.multiple_of(k * 8, 8)
            got = in_y(x3, 2, row, o3, e3, k3)
            for z in range(nz // 4):
                where = pl.ds(2 * z * counts[1] + 2 * row, 8, stride=2)
                for q in range(groups):
                    piece = got[z][:, 128 * q : 128 * q + 128]
                    w2[q, where, :] = jnp.where(lanes % 4 == 0, piece, w2[q, where, :])
            return 0

        lax.fori_loop(0, counts[2] // 8, level_three, 0)

        def merge(k, _):
            row = pl.multiple_of((k // groups) * 8, 8)
            q = k % groups
            where = pl.ds(2 * row, 8, stride=2)
            for z in range(nz // 2):
                inner = w2[q, pl.ds(pl.multiple_of(z * counts[1] + row, 8), 8), :]
                out_ref[q, 2 * z, where, :] = jnp.where(lanes % 2 == 0, inner, out_ref[q, 2 * z, where, :])
            return 0

        lax.fori_loop(0, (counts[1] // 8) * groups, merge, 0)
        more = leaving([z for z in untouched if z % 2 == 0])
        for copy in more:
            copy.start()

        early = []
        for ref in (b1, a1):
            for c in range(2):
                hi, lo = split(ref[c * nx : c * nx + nx, :])
                early.append(dot(xt[...], jnp.concatenate([hi, hi, lo], axis=0)))
        early = jnp.concatenate(early, axis=0)
        w_ref[...] = banded(early, plain_edge(early), o1, e1)

        for copy in copies + more:
            copy.wait()

    flat = [t for band in bands for t in band]
    return pl.pallas_call(
        kernel,
        in_specs=[VM] * 17,
        out_specs=[VM, VM, HB],
        out_shape=[
            vmem((groups, nz, nx, 128)),
            vmem((4 * nx, ny)),
            pltpu.HBM((nz, nx, ny), F32),
        ],
        scratch_shapes=[
            pltpu.VMEM((groups, nz // 2 * counts[1], 128), F32),
            pltpu.VMEM((512, 128), F32),
            pltpu.SemaphoreType.DMA((nz,)),
        ],
        compiler_params=params(32),
        cost_estimate=pl.CostEstimate(
            flops=8_000_000_000, bytes_accessed=20_000_000, transcendentals=0
        ),
        name="main_part",
    )(*xs, from_left, from_right, below, above, *flat, jnp.asarray(x_table), *[jnp.asarray(m) for m in masks])


def z_apply(inner, partial, early, from_left, from_right):
    groups, nz, nx, _ = inner.shape
    ny = groups * 128
    maps = [p for _, p in z_tables(nz)]
    counts = [nx, nx // 2, nx // 4]
    tables = []
    for level in (1, 2):
        width = ny >> level
        hi = spread_columns(np.eye(width), 1 << level, ny).astype(ml_dtypes.bfloat16)
        tables.append(np.concatenate([hi, hi]))
    heights = late_rows(counts, ny)
    _, _, x_maps = joint_sides(nx)
    frame = np.zeros((4 * nx, 16))
    for c in range(4):
        frame[c * nx : c * nx + nx, 4 * c : 4 * c + 2] = x_maps[0][1][:, :2]
        frame[c * nx : c * nx + nx, 4 * c + 2 : 4 * c + 4] = x_maps[0][2][:, :2]
        assert np.abs(x_maps[0][1][:, 2:]).max() < 1e-12 and np.abs(x_maps[0][2][:, 2:]).max() < 1e-12
    _, left, right = y_tables(ny, True)[0]
    side_hi, side_lo = hi_lo(np.concatenate([left, right, np.zeros((4, ny))]))
    side_rows = np.concatenate([side_hi, side_hi, side_lo, np.zeros((104, ny), side_hi.dtype)])
    touched = touched_layers(nz)

    def kernel(in_ref, base_hbm, w_ref, fl, fr, t2, t3, xf, yf, out_hbm, s1, s2, s3, buf, sem):
        del base_hbm
        s3[...] = jnp.zeros(s3.shape, F32)
        at = heights[0] + heights[1]
        hi, lo = split(jnp.concatenate([fl[at : at + 8, :], fr[at : at + 8, :]], axis=0))
        at += 8
        none = jnp.zeros((104, 128), F32)
        turn = []
        for ref in (fl, fr):
            values = ref[at : at + 8, :128]
            high = values.astype(BF).astype(F32)
            turn.append(jnp.concatenate([high, values - high, high, none], axis=0).T.astype(BF))
        left_hand = jnp.concatenate([jnp.concatenate(turn, axis=0), xf[...]], axis=1)
        first = w_ref[...] + dot(left_hand, jnp.concatenate([yf[...], hi, hi, lo], axis=0))
        for c in range(4):
            for q in range(groups):
                s1[c, q] = first[c * nx : c * nx + nx, 128 * q : 128 * q + 128]
        at = 0
        for level, table, to in ((1, t2, s2), (2, t3, s3)):
            width, tall, n = ny >> level, heights[level - 1], counts[level]
            flat = jnp.concatenate(
                [
                    ref[at : at + tall, p * width : p * width + width]
                    for ref in (fl, fr)
                    for p in range(1 << level)
                ],
                axis=0,
            )
            hi, lo = split(flat)
            got = dot(jnp.concatenate([hi, lo], axis=1), table[...])
            for c in range(LEFT_RANKS[level] + RIGHT_RANKS[level]):
                start = c * n
                if c >= LEFT_RANKS[level]:
                    start += (tall << level) - LEFT_RANKS[level] * n
                for q in range(groups):
                    piece = got[start : start + n, 128 * q : 128 * q + 128]
                    if level == 1:
                        to[c, q] = piece
                    else:
                        to[c, q, pl.ds(0, n, stride=2), :] = piece
            at += tall

        lanes = lax.broadcasted_iota(jnp.int32, (8, 128), 1)
        even_lane = lanes % 2 == 0
        third_cell = (lax.broadcasted_iota(jnp.int32, (8, 128), 0) % 2 + lanes % 4) == 0

        def summed(table_row, get):
            total = None
            for c, scalar in enumerate(table_row):
                if abs(scalar) > 1e-12:
                    total = add(total, get(c) * np.float32(scalar))
            return total

        copies = []
        for slot, z in enumerate(touched):

            def body(t, _, z=z, slot=slot):
                full = pl.multiple_of(16 * t, 8)
                half = pl.multiple_of(8 * t, 8)
                for q in range(groups):
                    if z % 2:
                        for more in (0, 8):
                            rows = pl.ds(full + more, 8)
                            extra = summed(maps[0][z], lambda c: s1[c, q, rows, :])
                            buf[slot, q, rows, :] = add(in_ref[q, z, rows, :], extra)
                        continue
                    evens = pl.ds(16 * t, 8, stride=2)
                    odds = pl.ds(16 * t + 1, 8, stride=2)
                    extra = summed(maps[0][z], lambda c: s1[c, q, odds, :])
                    buf[slot, q, odds, :] = add(in_ref[q, z, odds, :], extra)
                    rows = pl.ds(half, 8)
                    extra = summed(maps[1][z // 2], lambda c: s2[c, q, rows, :])
                    if z % 4 == 0:
                        third = summed(maps[2][z // 4], lambda c: s3[c, q, rows, :])
                        third = 0.0 if third is None else third
                        extra = jnp.where(third_cell, third, 0.0 if extra is None else extra)
                    one = summed(maps[0][z], lambda c: s1[c, q, evens, :])
                    if one is not None:
                        extra = jnp.where(even_lane, 0.0 if extra is None else extra, one)
                    buf[slot, q, evens, :] = add(in_ref[q, z, evens, :], extra)
                return 0

            lax.fori_loop(0, nx // 16, body, 0)
            for q in range(groups):
                copy = pltpu.make_async_copy(
                    buf.at[slot, q], out_hbm.at[z, :, 128 * q : 128 * q + 128], sem.at[slot]
                )
                copy.start()
                copies.append(copy)
        for copy in copies:
            copy.wait()

    return pl.pallas_call(
        kernel,
        in_specs=[VM, HB] + [VM] * 7,
        out_specs=HB,
        out_shape=jax.ShapeDtypeStruct((nz, nx, ny), F32),
        input_output_aliases={1: 0},
        scratch_shapes=[
            pltpu.VMEM((4, groups, nx, 128), F32),
            pltpu.VMEM((maps[1].shape[1], groups, nx // 2, 128), F32),
            pltpu.VMEM((maps[2].shape[1], groups, nx // 2, 128), F32),
            pltpu.VMEM((len(touched), groups, nx, 128), F32),
            pltpu.SemaphoreType.DMA((len(touched),)),
        ],
        compiler_params=params(24),
        name="z_apply",
    )(
        inner,
        partial,
        early,
        from_left,
        from_right,
        *[jnp.asarray(t) for t in tables],
        jnp.asarray(stack_lhs(frame)),
        jnp.asarray(side_rows),
    )


def swap(to_right, to_left, axis):
    count = lax.axis_size(axis)
    right = [(i, (i + 1) % count) for i in range(count)]
    left = [(j, i) for i, j in right]
    return lax.ppermute(to_right, axis, right), lax.ppermute(to_left, axis, left)


def local(field):
    nz, nx, ny = field.shape
    counts = [nx, nx // 2, nx // 4]
    bands = [[jnp.asarray(t) for t in band_tables(level, nz, counts, ny)] for level in range(3)]
    field, message, up, down = x_send(field)
    halo = x_exchange(message)
    below, above = swap(up, down, "gz")
    x1, x2, x3, to_right, to_left = x_apply(field, halo)
    from_left, from_right = swap(to_right, to_left, "gy")
    *combined, own2, own3 = z_first(x2, x3, halo)
    up, down = y_messages(combined, from_left, from_right, nz, bands[0])
    late_below, late_above = swap(up, down, "gz")
    inner, early, partial = main_part((x1, own2, own3), from_left, from_right, below, above, bands)
    return z_apply(inner, partial, early, late_below, late_above)


def solution(mesh):
    placed = (P("gz", "gx", "gy"),)
    return jax.shard_map(
        local, mesh=mesh, in_specs=placed, out_specs=P("gz", "gx", "gy"), check_vma=False
    )
```

```python
import functools

import jax
import jax.numpy as jnp
import ml_dtypes
import numpy as np
from jax import lax
from jax.experimental import pallas as pl
from jax.experimental.pallas import tpu as pltpu
from jax.sharding import PartitionSpec as P

lift_alpha = -1.586134342
lift_beta = -0.05298011854
lift_gamma = 0.8829110762
lift_delta = 0.4435068522
lift_zeta = 1.149604398

BF = jnp.bfloat16
F32 = jnp.float32
MIB = 1024 * 1024


def periodic_lift(u):
    s, d = u[0::2].copy(), u[1::2].copy()
    d = d + lift_alpha * (s + np.roll(s, -1, 0))
    s = s + lift_beta * (np.roll(d, 1, 0) + d)
    d = d + lift_gamma * (s + np.roll(s, -1, 0))
    s = s + lift_delta * (np.roll(d, 1, 0) + d)
    out = np.empty_like(u)
    out[0::2] = s * lift_zeta
    out[1::2] = d / lift_zeta
    return out


@functools.lru_cache(None)
def blocks(n):
    current = np.eye(4 * n)
    found = []
    for level in range(3):
        full = periodic_lift(current)
        m = n >> level
        rows = full[m : 2 * m]
        found.append((rows[:, n : 2 * n], rows[:, :n], rows[:, 2 * n : 3 * n]))
        current = full[0::2]
    return found


def row_space(outer, rank):
    _, sizes, basis = np.linalg.svd(outer, full_matrices=False)
    assert sizes[rank:].max() < 1e-10
    basis = basis[:rank].copy()
    basis[np.abs(basis) < 1e-12] = 0.0
    return basis


LEFT_RANKS = (2, 3, 4)
RIGHT_RANKS = (2, 3, 3)


@functools.lru_cache(None)
def sides(n):
    out = []
    for level, (main, left, right) in enumerate(blocks(n)):
        cl = row_space(left, LEFT_RANKS[level])
        cr = row_space(right, RIGHT_RANKS[level])
        out.append((main, cl, left @ cl.T, cr, right @ cr.T))
    return out


def nested_space(outer):
    first = row_space(outer[0], 2)
    every = np.concatenate(outer)
    rest = every - every @ first.T @ first
    return np.concatenate([first, row_space(rest, 4)])


@functools.lru_cache(None)
def joint_sides(n):
    found = blocks(n)
    cl = nested_space([b[1] for b in found])
    cr = nested_space([b[2] for b in found])
    maps = [(b[0], b[1] @ cl.T, b[2] @ cr.T) for b in found]
    return cl, cr, maps


def hi_lo(table):
    table = np.asarray(table, np.float32)
    hi = table.astype(ml_dtypes.bfloat16)
    lo = (table - hi.astype(np.float32)).astype(ml_dtypes.bfloat16)
    return hi, lo


def stack_lhs(table):
    hi, lo = hi_lo(table)
    return np.concatenate([hi, lo, hi], axis=1)


def stack_rhs(table):
    hi, lo = hi_lo(table)
    return np.concatenate([hi, hi, lo], axis=0)


def split(values):
    hi = values.astype(BF)
    return hi, (values - hi.astype(F32)).astype(BF)


def dot(a, b):
    return lax.dot_general(a, b, (((1,), (0,)), ((), ())), preferred_element_type=F32)


def dot_t(a, b):
    return lax.dot_general(a, b, (((1,), (1,)), ((), ())), preferred_element_type=F32)


def spread_columns(table, step, width):
    out = np.zeros((table.shape[0], width))
    out[:, ::step] = table
    return out


VM = pl.BlockSpec(memory_space=pltpu.VMEM)
HB = pl.BlockSpec(memory_space=pltpu.HBM)


def in_hbm(array):
    return pltpu.with_memory_space_constraint(array, pltpu.HBM)


def vmem(shape, dtype=F32):
    return pltpu.VMEM(shape, dtype)


def params(mib):
    return pltpu.CompilerParams(vmem_limit_bytes=mib * MIB)


def x_send(field):
    nz, nx, ny = field.shape
    cl, cr, _ = joint_sides(nx)
    one = np.concatenate([cl, cr])
    group = 4
    wide = np.kron(np.eye(group), one)
    hi_rows, lo_rows = hi_lo(wide)
    pair = np.concatenate([hi_rows, lo_rows])
    height = 12 * group
    step = 8
    steps = nz // step
    order = [0, steps - 1] + list(range(1, steps - 1))
    flight = 2
    _, low, _, high, _ = sides(nz)[0]
    assert np.abs(low[:, :-step]).max() == 0 and np.abs(high[:, step:]).max() == 0

    def kernel(u_hbm, c_hbm, u_ref, out_ref, up_ref, down_ref, c_ref, u_sem, c_sem):
        table_copy = pltpu.make_async_copy(c_hbm, c_ref, c_sem)
        copies = [
            pltpu.make_async_copy(
                u_hbm.at[i * step : i * step + step], u_ref.at[i * step : i * step + step], u_sem.at[i]
            )
            for i in range(steps)
        ]
        for i in order[:flight]:
            copies[i].start()
        table_copy.start()
        table_copy.wait()
        table = c_ref[...]
        for turn, i in enumerate(order):
            copies[i].wait()
            if turn + flight < steps:
                copies[order[turn + flight]].start()
            for g in range(i * step // group, (i + 1) * step // group):
                hi, lo = split(u_ref[group * g : group * g + group].reshape(group * nx, ny))
                both = dot(table, hi)
                out_ref[height * g : height * g + height, :] = (
                    both[:height] + both[height:] + dot(table[:height], lo)
                )
            if i in order[:2]:
                combos, ref = (high, down_ref) if i == 0 else (low, up_ref)
                for c in range(2):
                    ref[c * nx : c * nx + nx, :] = weighted(
                        [(combos[c, z], lambda z=z: u_ref[z]) for z in range(i * step, (i + 1) * step)]
                    )

    return pl.pallas_call(
        kernel,
        in_specs=[HB, HB],
        out_specs=[VM] * 4,
        out_shape=[vmem((nz, nx, ny)), vmem((nz * 12, ny)), vmem((2 * nx, ny)), vmem((2 * nx, ny))],
        scratch_shapes=[
            pltpu.VMEM(pair.shape, BF),
            pltpu.SemaphoreType.DMA((steps,)),
            pltpu.SemaphoreType.DMA,
        ],
        compiler_params=params(16),
        name="x_send",
    )(in_hbm(field), in_hbm(jnp.asarray(pair)))


def x_exchange(message):
    count = lax.axis_size("gx")
    right = [(i, (i + 1) % count) for i in range(count)]
    if count == 2:
        return lax.ppermute(message, "gx", right)
    left = [(j, i) for i, j in right]
    rows, ny = message.shape
    grid = message.reshape(rows // 12, 12, ny)
    from_left = lax.ppermute(grid[:, :6], "gx", right)
    from_right = lax.ppermute(grid[:, 6:], "gx", left)
    return jnp.concatenate([from_left, from_right], axis=1).reshape(rows, ny)


def x_apply(field, halo):
    nz, nx, ny = field.shape
    _, _, maps = joint_sides(nx)
    main = np.concatenate([m for m, _, _ in maps])
    outer = np.concatenate([np.concatenate([l, r], axis=1) for _, l, r in maps])
    pad = np.zeros((main.shape[0], 4))
    tables = np.stack(
        [
            stack_lhs(np.concatenate([main, outer, pad], axis=1)),
            stack_lhs(np.concatenate([main, pad, outer], axis=1)),
        ]
    )
    rows = main.shape[0]
    counts = [nx, nx // 2, nx // 4]
    step = 8
    steps = nz // step

    combos = []
    for level, (_, cl, _, cr, _) in enumerate(sides(ny)):
        both = np.zeros((8, 128))
        assert np.abs(cl[:, : ny - 64]).max() == 0 and np.abs(cr[:, 64:]).max() == 0
        both[: cl.shape[0], 64:] = cl[:, ny - 64 :]
        both[4 : 4 + cr.shape[0], :64] = cr[:, :64]
        combos.append(stack_lhs(both))
    combos = np.stack(combos)

    def kernel(u_ref, r_ref, t_ref, c_ref, x1, x2, x3, right_ref, left_ref, e1, e2, e3):
        i = pl.program_id(0)
        lanes = lax.broadcasted_iota(jnp.int32, (rows, 128), 1)
        for z in range(step):
            start = pl.multiple_of(i * (12 * step) + 24 * (z // 2) + 8 * (z % 2), 8)
            hi, lo = split(u_ref[i * step + z])
            rhi, rlo = split(r_ref[pl.ds(start, 16), :])
            stacked = jnp.concatenate([hi, rhi, hi, rhi, lo, rlo], axis=0)
            got = dot(t_ref[z % 2], stacked)
            edge = jnp.where(lanes < 64, got[:, :128], got[:, ny - 128 :])
            ehi, elo = split(edge)
            estack = jnp.concatenate([ehi, ehi, elo], axis=1)
            at = 0
            for ref, eref, n in zip((x1, x2, x3), (e1, e2, e3), counts):
                where = pl.ds(pl.multiple_of((i * step + z) * n, 16), n)
                ref[i * step + z] = got[at : at + n]
                eref[where, :] = estack[at : at + n]
                at += n

        @pl.when(i == steps - 1)
        def _():
            row = 0
            for level, (eref, n) in enumerate(zip((e1, e2, e3), counts)):
                got = dot_t(c_ref[level], eref[...])
                for j in range(nz * n // 512):
                    for c in range(LEFT_RANKS[level]):
                        right_ref[row : row + 1, :] = got[c : c + 1, 512 * j : 512 * j + 512]
                        if c < RIGHT_RANKS[level]:
                            left_ref[row : row + 1, :] = got[4 + c : 5 + c, 512 * j : 512 * j + 512]
                        else:
                            left_ref[row : row + 1, :] = jnp.zeros((1, 512), F32)
                        row += 1
            right_ref[row:, :] = jnp.zeros((24 - row, 512), F32)
            left_ref[row:, :] = jnp.zeros((24 - row, 512), F32)

    return pl.pallas_call(
        kernel,
        grid=(steps,),
        in_specs=[VM] * 4,
        out_specs=[VM] * 5,
        out_shape=[vmem((nz, n, ny)) for n in counts] + [jax.ShapeDtypeStruct((24, 512), F32)] * 2,
        scratch_shapes=[pltpu.VMEM((nz * n, 384), BF) for n in counts],
        compiler_params=params(24),
        name="x_apply",
    )(field, halo, jnp.asarray(tables), jnp.asarray(combos))


def add(a, b):
    if a is None:
        return b
    return a if b is None else a + b


def scale(a, c):
    return None if a is None else a * np.float32(c)


def open_lift(values, first, last):
    get = values.get
    low, high = first // 2 - 3, last // 2 + 4
    s = {i: get(2 * i) for i in range(low, high + 1)}
    d = {i: get(2 * i + 1) for i in range(low, high + 1)}
    pick = lambda t, i: t.get(i)
    d1 = {i: add(d[i], scale(add(s[i], pick(s, i + 1)), lift_alpha)) for i in range(low, high + 1)}
    s1 = {i: add(s[i], scale(add(pick(d1, i - 1), d1[i]), lift_beta)) for i in range(low, high + 1)}
    d2 = {i: add(d1[i], scale(add(s1[i], pick(s1, i + 1)), lift_gamma)) for i in range(low, high + 1)}
    s2 = {i: add(s1[i], scale(add(pick(d2, i - 1), d2[i]), lift_delta)) for i in range(low, high + 1)}
    out = {}
    for z in range(first, last + 1):
        if z % 2:
            out[z] = scale(d2[z // 2], 1.0 / lift_zeta)
        else:
            out[z] = scale(s2[z // 2], lift_zeta)
    return out


def lows(values, first, last):
    got = open_lift(values, 2 * first, 2 * last)
    return {i: got[2 * i] for i in range(first, last + 1) if got[2 * i] is not None}


def own_levels(values, nz, level):
    if level >= 1:
        values = lows(values, -2, nz // 2 + 1)
    if level >= 2:
        values = lows(values, -3, nz // 4 + 2)
    return open_lift(values, 0, (nz >> level) - 1)


def z_tables(nz):
    out = []
    for _, cl, pl_, cr, pr in sides(nz):
        out.append((np.concatenate([cl, cr]), np.concatenate([pl_, pr], axis=1)))
    return out


def weighted(parts):
    total = None
    for scalar, get in parts:
        if abs(scalar) < 1e-12:
            continue
        term = get() * np.float32(scalar)
        total = term if total is None else total + term
    return total


def z_first(x2, x3, halo):
    nz, _, ny = x2.shape
    tables = [t for t, _ in z_tables(nz)]
    counts = [x2.shape[1], x3.shape[1]]
    groups = ny // 128

    def kernel(x2, x3, r_ref, o2, o3, of, y2, y3):
        for level, ref, out, own, table, n in zip((1, 2), (x2, x3), (o2, o3), (y2, y3), tables[1:], counts):

            def body(k, _, level=level, ref=ref, out=out, own=own, table=table, n=n):
                row = pl.multiple_of((k // groups) * 8, 8)
                lane = pl.multiple_of((k % groups) * 128, 128)
                get = {}
                for z in range(nz):
                    get[z] = ref[z, pl.ds(row, 8), pl.ds(lane, 128)]
                for z, value in own_levels(get, nz, level).items():
                    own[z, pl.ds(row, 8), pl.ds(lane, 128)] = value
                for c in range(table.shape[0]):
                    out[pl.ds(pl.multiple_of(c * n + row, 8), 8), pl.ds(lane, 128)] = weighted(
                        [(table[c, z], lambda z=z: get[z]) for z in range(nz)]
                    )
                return 0

            lax.fori_loop(0, (n // 8) * groups, body, 0)
        for c in range(4):
            got = weighted(
                [(tables[0][c, z], lambda z=z: r_ref[12 * z : 12 * z + 12, :]) for z in range(nz)]
            )
            of[4 * c : 4 * c + 2, :] = got[0:2]
            of[4 * c + 2 : 4 * c + 4, :] = got[6:8]

    return pl.pallas_call(
        kernel,
        in_specs=[VM] * 3,
        out_specs=[VM] * 5,
        out_shape=[vmem((t.shape[0] * n, ny)) for t, n in zip(tables[1:], counts)]
        + [vmem((16, ny)), vmem((nz // 2, counts[0], ny)), vmem((nz // 4, counts[1], ny))],
        compiler_params=params(16),
        cost_estimate=pl.CostEstimate(flops=20_000_000, bytes_accessed=6_000_000, transcendentals=0),
        name="z_first",
    )(x2, x3, halo)


def y_tables(ny, spread):
    out = []
    for level, (main, _, left, _, right) in enumerate(sides(ny)):
        step = (1 << level) if spread else 1
        width = ny if spread else ny >> level
        fit = lambda t: spread_columns(t.T, step, width)
        out.append((fit(main), fit(left), fit(right)))
    return out


def halo_rows(level, chunk, nz, counts):
    start = 0
    for below in range(level):
        start += (nz * counts[below] // 512) * LEFT_RANKS[below]
    return start + chunk * LEFT_RANKS[level]


LEFT_AT, RIGHT_AT = 32, 56


def halo_base(left, right, level, nz, counts):
    base = np.zeros((128, left.shape[1]))
    for chunk in range(nz * counts[level] // 512):
        row = halo_rows(level, chunk, nz, counts)
        base[LEFT_AT + row : LEFT_AT + row + left.shape[0]] = left
        base[RIGHT_AT + row : RIGHT_AT + row + right.shape[0]] = right
    return base


def turned(left_ref, right_ref):
    wide = jnp.concatenate(
        [jnp.zeros((LEFT_AT, 512), F32), left_ref[...], right_ref[...], jnp.zeros((48, 512), F32)], axis=0
    )
    return wide.T


def band_tables(level, nz, counts, ny):
    assert ny == 512
    main, left, right = y_tables(ny, True)[level]
    base = halo_base(left, right, level, nz, counts)
    own, edge = [], []
    for j in range(2):
        cols = slice(256 * j, 256 * j + 256)
        own.append(stack_rhs(main[cols, cols]))
        tile = base[:, cols].copy()
        if j == 0:
            tile[:32] = main[256:288, cols]
            assert np.abs(main[288:, cols]).max() == 0
        else:
            tile[96:] = main[224:256, cols]
            assert np.abs(main[:224, cols]).max() == 0
        edge.append(stack_rhs(tile))
    return np.stack(own), np.stack(edge)


def three(values):
    hi, lo = split(values)
    return jnp.concatenate([hi, lo, hi], axis=1)


def banded(rows, edge, own_ref, edge_ref):
    edges = three(edge)
    out = []
    for j in range(2):
        own = three(rows[:, 256 * j : 256 * j + 256])
        out.append(dot(own, own_ref[j]) + dot(edges, edge_ref[j]))
    return jnp.concatenate(out, axis=1)


def plain_edge(rows):
    lanes = lax.broadcasted_iota(jnp.int32, (rows.shape[0], 128), 1)
    before = jnp.where(lanes >= 96, rows[:, 128:256], 0.0)
    return jnp.where(lanes < 32, rows[:, 256:384], before)


def late_rows(counts, ny):
    return [3 * counts[1] * (ny // 2) // ny, 4 * counts[2] * (ny // 4) // ny, 8, 8]


def y_messages(combined, from_left, from_right, nz, band_one):
    c2, c3, cf = combined
    ny = c2.shape[1]
    tables = z_tables(nz)
    nums = [t.shape[0] for t, _ in tables]
    counts = [2 * c2.shape[0] // nums[1], c2.shape[0] // nums[1], c3.shape[0] // nums[2]]
    mains, halos, coefs = [], [], []
    for level, (main, left, right) in enumerate(y_tables(ny, False)):
        mains.append(stack_rhs(main))
        halos.append(stack_rhs(halo_base(left, right, level, nz, counts)))
        chunks = nz * counts[level] // 512
        per = 512 // counts[level]
        table = tables[level][0]
        coef = np.zeros((nums[level], per, 128), np.float32)
        for c in range(nums[level]):
            for zz in range(per):
                for chunk in range(chunks):
                    row = halo_rows(level, chunk, nz, counts)
                    for lane in range(LEFT_RANKS[level]):
                        for base in (LEFT_AT, RIGHT_AT):
                            coef[c, zz, base + row + lane] = table[c, chunk * per + zz]
        coefs.append(coef.reshape(nums[level] * per, 128))
    heights = late_rows(counts, ny)
    height = sum(heights)

    def kernel(c2, c3, cf, fl, fr, own1, edge1, m2, m3, h2, h3, k1, k2, k3, up_ref, down_ref):
        halo = turned(fl, fr)

        def reduced(k, n, num):
            per = 512 // n
            extra = []
            for c in range(num):
                total = None
                for zz in range(per):
                    if np.abs(coefs_of[n][c * per + zz]).max() > 1e-12:
                        term = halo[zz * n : zz * n + n] * k[c * per + zz : c * per + zz + 1, :]
                        total = term if total is None else total + term
                extra.append(total)
            return extra

        coefs_of = dict(zip(counts, coefs))
        got = []
        for c_ref, m, h, k, n, num in zip((c2, c3), (m2, m3), (h2, h3), (k2, k3), counts[1:], nums[1:]):
            extra = jnp.concatenate(reduced(k, n, num), axis=0)
            got.append(dot(three(c_ref[...]), m[...]) + dot(three(extra), h[...]))
        frame = cf[...]
        frame = banded(frame, plain_edge(frame), own1, edge1)
        ones = reduced(k1, counts[0], 4)
        rows8 = lax.broadcasted_iota(jnp.int32, (8, 128), 0)
        for side, ref in enumerate((up_ref, down_ref)):
            at = 0
            for level in (1, 2):
                n, width = counts[level], ny >> level
                ranks = LEFT_RANKS if side == 0 else RIGHT_RANKS
                first = 0 if side == 0 else LEFT_RANKS[level] * n
                total = ranks[level] * n
                tall = heights[level - 1]
                for part in range(1 << level):
                    use = max(min(tall, total - part * tall), 0)
                    lanes = slice(part * width, (part + 1) * width)
                    if use > 0:
                        ref[at : at + use, lanes] = got[level - 1][
                            first + part * tall : first + part * tall + use
                        ]
                    if use < tall:
                        ref[at + use : at + tall, lanes] = jnp.zeros((tall - use, width), F32)
                at += tall
            ref[at : at + 8, :] = frame[8 * side : 8 * side + 8]
            at += 8
            turn = jnp.concatenate(ones[2 * side : 2 * side + 2], axis=0).T
            both = []
            for start in (LEFT_AT, RIGHT_AT):
                v = turn[start : start + 8]
                v = v + pltpu.roll(v, 4, 0)
                both.append(v + pltpu.roll(v, 2, 0))
            ref[at:, :128] = jnp.where(rows8 < 2, both[0], both[1])
            ref[at:, 128:] = jnp.zeros((8, ny - 128), F32)

    return pl.pallas_call(
        kernel,
        in_specs=[VM] * 14,
        out_specs=[VM] * 2,
        out_shape=[vmem((height, ny))] * 2,
        compiler_params=params(24),
        name="y_messages",
    )(
        c2,
        c3,
        cf,
        from_left,
        from_right,
        *band_one,
        *[jnp.asarray(t) for t in mains[1:]],
        *[jnp.asarray(t) for t in halos[1:]],
        *[jnp.asarray(t) for t in coefs],
    )


def touched_layers(nz):
    one, two, three = [np.abs(p).max(axis=1) > 1e-12 for _, p in z_tables(nz)]
    hit = lambda z: one[z] or (z % 2 == 0 and two[z // 2]) or (z % 4 == 0 and three[z // 4])
    return [z for z in range(nz) if hit(z)]


def main_part(xs, from_left, from_right, below, above, bands):
    nz, nx, ny = xs[0].shape
    counts = [nx, nx // 2, nx // 4]
    changed = touched_layers(nz)
    untouched = [z for z in range(nz) if z not in changed]
    groups = ny // 128
    _, _, maps = joint_sides(nx)
    x_table = stack_lhs(maps[0][0])
    masks = []
    for level in range(3):
        chunks = nz * counts[level] // 512
        per = 512 // counts[level]
        lanes_of = np.zeros((chunks, 128))
        for chunk in range(chunks):
            row = halo_rows(level, chunk, nz, counts)
            for base in (LEFT_AT, RIGHT_AT):
                lanes_of[chunk, base + row : base + row + LEFT_RANKS[level]] = 1.0
        if level == 0:
            masks.append(lanes_of)
        else:
            own = sides(nz)[level][0]
            lanes = np.einsum("ocz,cl->ozl", own.reshape(own.shape[0], chunks, per), lanes_of)
            masks.append(lanes.reshape(-1, 128))
    masks = [np.concatenate([m, np.zeros((-m.shape[0] % 8, 128))]).astype(np.float32) for m in masks]

    def kernel(x1, x2, x3, fl, fr, b1, a1, o1, e1, o2, e2, o3, e3, xt, k1, k2, k3, out_ref, w_ref, hbm, w2, halo_ref, sem):
        halo_ref[...] = turned(fl, fr)
        lanes = lax.broadcasted_iota(jnp.int32, (8, 128), 1)
        wide = lax.broadcasted_iota(jnp.int32, (32, 128), 1)
        after, before = wide < 32, wide >= 96

        def in_y(x, level, row, tall, own, edge, mk):
            n = counts[level]
            per = 512 // n
            layers = nz >> level
            values = x[:, row : row + tall, :]
            turns = [halo_ref[zz * n + row : zz * n + row + tall, :] for zz in range(per)]
            edges = []
            for z in range(layers):
                if level == 0:
                    turn = turns[z % per] * mk[z // per : z // per + 1, :]
                else:
                    turn = None
                    for zz in range(per):
                        if np.abs(masks[level][z * per + zz]).max() > 1e-12:
                            turn = add(turn, turns[zz] * mk[z * per + zz : z * per + zz + 1, :])
                edges.append(
                    jnp.where(
                        after[:tall],
                        values[z, :, 256:384],
                        jnp.where(before[:tall], values[z, :, 128:256], turn),
                    )
                )
            got = banded(
                values.reshape(layers * tall, ny), jnp.concatenate(edges, axis=0), own, edge
            )
            return {z: got[tall * z : tall * z + tall] for z in range(layers)}

        def store(to, values, row, indices, height=None):
            for z in indices:
                for q in range(groups):
                    piece = values[z][:, 128 * q : 128 * q + 128]
                    tall = piece.shape[0]
                    if height is None:
                        to[q, z, row : row + tall, :] = piece
                    else:
                        to[q, z * height + row : z * height + row + tall, :] = piece

        for row in range(0, counts[0], 16):
            got = own_levels(in_y(x1, 0, row, 16, o1, e1, k1), nz, 0)
            store(out_ref, got, row, range(nz))

        def leaving(layers):
            return [
                pltpu.make_async_copy(
                    out_ref.at[q, z], hbm.at[z, :, 128 * q : 128 * q + 128], sem.at[z]
                )
                for z in layers
                for q in range(groups)
            ]

        copies = leaving([z for z in untouched if z % 2])
        for copy in copies:
            copy.start()

        store(w2, in_y(x2, 1, 0, counts[1], o2, e2, k2), 0, range(nz // 2), counts[1])
        got = in_y(x3, 2, 0, counts[2], o3, e3, k3)
        for z in range(nz // 4):
            for row in range(0, counts[2], 8):
                where = pl.ds(2 * z * counts[1] + 2 * row, 8, stride=2)
                for q in range(groups):
                    piece = got[z][row : row + 8, 128 * q : 128 * q + 128]
                    w2[q, where, :] = jnp.where(lanes % 4 == 0, piece, w2[q, where, :])

        def merge(k, _):
            row = pl.multiple_of((k // groups) * 8, 8)
            q = k % groups
            where = pl.ds(2 * row, 8, stride=2)
            for z in range(nz // 2):
                inner = w2[q, pl.ds(pl.multiple_of(z * counts[1] + row, 8), 8), :]
                out_ref[q, 2 * z, where, :] = jnp.where(lanes % 2 == 0, inner, out_ref[q, 2 * z, where, :])
            return 0

        lax.fori_loop(0, (counts[1] // 8) * groups, merge, 0)
        more = leaving([z for z in untouched if z % 2 == 0])
        for copy in more:
            copy.start()

        early = []
        for ref in (b1, a1):
            for c in range(2):
                hi, lo = split(ref[c * nx : c * nx + nx, :])
                early.append(dot(xt[...], jnp.concatenate([hi, hi, lo], axis=0)))
        early = jnp.concatenate(early, axis=0)
        w_ref[...] = banded(early, plain_edge(early), o1, e1)

        for copy in copies + more:
            copy.wait()

    flat = [t for band in bands for t in band]
    return pl.pallas_call(
        kernel,
        in_specs=[VM] * 17,
        out_specs=[VM, VM, HB],
        out_shape=[
            vmem((groups, nz, nx, 128)),
            vmem((4 * nx, ny)),
            pltpu.HBM((nz, nx, ny), F32),
        ],
        scratch_shapes=[
            pltpu.VMEM((groups, nz // 2 * counts[1], 128), F32),
            pltpu.VMEM((512, 128), F32),
            pltpu.SemaphoreType.DMA((nz,)),
        ],
        compiler_params=params(32),
        cost_estimate=pl.CostEstimate(
            flops=8_000_000_000, bytes_accessed=20_000_000, transcendentals=0
        ),
        name="main_part",
    )(*xs, from_left, from_right, below, above, *flat, jnp.asarray(x_table), *[jnp.asarray(m) for m in masks])


def z_apply(inner, partial, early, from_left, from_right):
    groups, nz, nx, _ = inner.shape
    ny = groups * 128
    maps = [p for _, p in z_tables(nz)]
    counts = [nx, nx // 2, nx // 4]
    tables = []
    for level in (1, 2):
        width = ny >> level
        hi = spread_columns(np.eye(width), 1 << level, ny).astype(ml_dtypes.bfloat16)
        tables.append(np.concatenate([hi, hi]))
    heights = late_rows(counts, ny)
    _, _, x_maps = joint_sides(nx)
    frame = np.zeros((4 * nx, 16))
    for c in range(4):
        frame[c * nx : c * nx + nx, 4 * c : 4 * c + 2] = x_maps[0][1][:, :2]
        frame[c * nx : c * nx + nx, 4 * c + 2 : 4 * c + 4] = x_maps[0][2][:, :2]
        assert np.abs(x_maps[0][1][:, 2:]).max() < 1e-12 and np.abs(x_maps[0][2][:, 2:]).max() < 1e-12
    _, left, right = y_tables(ny, True)[0]
    side_hi, side_lo = hi_lo(np.concatenate([left, right, np.zeros((4, ny))]))
    side_rows = np.concatenate([side_hi, side_hi, side_lo, np.zeros((104, ny), side_hi.dtype)])
    touched = touched_layers(nz)

    def kernel(in_ref, base_hbm, w_ref, fl, fr, t2, t3, xf, yf, out_hbm, s1, s2, s3, buf, sem):
        del base_hbm
        s3[...] = jnp.zeros(s3.shape, F32)
        at = heights[0] + heights[1]
        hi, lo = split(jnp.concatenate([fl[at : at + 8, :], fr[at : at + 8, :]], axis=0))
        at += 8
        none = jnp.zeros((104, 128), F32)
        turn = []
        for ref in (fl, fr):
            values = ref[at : at + 8, :128]
            high = values.astype(BF).astype(F32)
            turn.append(jnp.concatenate([high, values - high, high, none], axis=0).T.astype(BF))
        left_hand = jnp.concatenate([jnp.concatenate(turn, axis=0), xf[...]], axis=1)
        first = w_ref[...] + dot(left_hand, jnp.concatenate([yf[...], hi, hi, lo], axis=0))
        for c in range(4):
            for q in range(groups):
                s1[c, q] = first[c * nx : c * nx + nx, 128 * q : 128 * q + 128]
        at = 0
        for level, table, to in ((1, t2, s2), (2, t3, s3)):
            width, tall, n = ny >> level, heights[level - 1], counts[level]
            flat = jnp.concatenate(
                [
                    ref[at : at + tall, p * width : p * width + width]
                    for ref in (fl, fr)
                    for p in range(1 << level)
                ],
                axis=0,
            )
            hi, lo = split(flat)
            got = dot(jnp.concatenate([hi, lo], axis=1), table[...])
            for c in range(LEFT_RANKS[level] + RIGHT_RANKS[level]):
                start = c * n
                if c >= LEFT_RANKS[level]:
                    start += (tall << level) - LEFT_RANKS[level] * n
                for q in range(groups):
                    piece = got[start : start + n, 128 * q : 128 * q + 128]
                    if level == 1:
                        to[c, q] = piece
                    else:
                        to[c, q, pl.ds(0, n, stride=2), :] = piece
            at += tall

        lanes = lax.broadcasted_iota(jnp.int32, (8, 128), 1)
        even_lane = lanes % 2 == 0
        third_cell = (lax.broadcasted_iota(jnp.int32, (8, 128), 0) % 2 + lanes % 4) == 0

        def summed(table_row, get):
            total = None
            for c, scalar in enumerate(table_row):
                if abs(scalar) > 1e-12:
                    total = add(total, get(c) * np.float32(scalar))
            return total

        copies = []
        for slot, z in enumerate(touched):

            for t in range(nx // 16):
                full, half = 16 * t, 8 * t
                for q in range(groups):
                    if z % 2:
                        for more in (0, 8):
                            rows = pl.ds(full + more, 8)
                            extra = summed(maps[0][z], lambda c: s1[c, q, rows, :])
                            buf[slot, q, rows, :] = add(in_ref[q, z, rows, :], extra)
                        continue
                    evens = pl.ds(16 * t, 8, stride=2)
                    odds = pl.ds(16 * t + 1, 8, stride=2)
                    extra = summed(maps[0][z], lambda c: s1[c, q, odds, :])
                    buf[slot, q, odds, :] = add(in_ref[q, z, odds, :], extra)
                    rows = pl.ds(half, 8)
                    extra = summed(maps[1][z // 2], lambda c: s2[c, q, rows, :])
                    if z % 4 == 0:
                        third = summed(maps[2][z // 4], lambda c: s3[c, q, rows, :])
                        third = 0.0 if third is None else third
                        extra = jnp.where(third_cell, third, 0.0 if extra is None else extra)
                    one = summed(maps[0][z], lambda c: s1[c, q, evens, :])
                    if one is not None:
                        extra = jnp.where(even_lane, 0.0 if extra is None else extra, one)
                    buf[slot, q, evens, :] = add(in_ref[q, z, evens, :], extra)
            for q in range(groups):
                copy = pltpu.make_async_copy(
                    buf.at[slot, q], out_hbm.at[z, :, 128 * q : 128 * q + 128], sem.at[slot]
                )
                copy.start()
                copies.append(copy)
        for copy in copies:
            copy.wait()

    return pl.pallas_call(
        kernel,
        in_specs=[VM, HB] + [VM] * 7,
        out_specs=HB,
        out_shape=jax.ShapeDtypeStruct((nz, nx, ny), F32),
        input_output_aliases={1: 0},
        scratch_shapes=[
            pltpu.VMEM((4, groups, nx, 128), F32),
            pltpu.VMEM((maps[1].shape[1], groups, nx // 2, 128), F32),
            pltpu.VMEM((maps[2].shape[1], groups, nx // 2, 128), F32),
            pltpu.VMEM((len(touched), groups, nx, 128), F32),
            pltpu.SemaphoreType.DMA((len(touched),)),
        ],
        compiler_params=params(24),
        name="z_apply",
    )(
        inner,
        partial,
        early,
        from_left,
        from_right,
        *[jnp.asarray(t) for t in tables],
        jnp.asarray(stack_lhs(frame)),
        jnp.asarray(side_rows),
    )


def swap(to_right, to_left, axis):
    count = lax.axis_size(axis)
    right = [(i, (i + 1) % count) for i in range(count)]
    left = [(j, i) for i, j in right]
    return lax.ppermute(to_right, axis, right), lax.ppermute(to_left, axis, left)


def local(field):
    nz, nx, ny = field.shape
    counts = [nx, nx // 2, nx // 4]
    bands = [[jnp.asarray(t) for t in band_tables(level, nz, counts, ny)] for level in range(3)]
    field, message, up, down = x_send(field)
    halo = x_exchange(message)
    below, above = swap(up, down, "gz")
    x1, x2, x3, to_right, to_left = x_apply(field, halo)
    from_left, from_right = swap(to_right, to_left, "gy")
    *combined, own2, own3 = z_first(x2, x3, halo)
    up, down = y_messages(combined, from_left, from_right, nz, bands[0])
    late_below, late_above = swap(up, down, "gz")
    inner, early, partial = main_part((x1, own2, own3), from_left, from_right, below, above, bands)
    return z_apply(inner, partial, early, late_below, late_above)


def solution(mesh):
    placed = (P("gz", "gx", "gy"),)
    return jax.shard_map(
        local, mesh=mesh, in_specs=placed, out_specs=P("gz", "gx", "gy"), check_vma=False
    )
```

```python
import functools

import jax
import jax.numpy as jnp
import ml_dtypes
import numpy as np
from jax import lax
from jax.experimental import pallas as pl
from jax.experimental.pallas import tpu as pltpu
from jax.sharding import PartitionSpec as P

lift_alpha = -1.586134342
lift_beta = -0.05298011854
lift_gamma = 0.8829110762
lift_delta = 0.4435068522
lift_zeta = 1.149604398

BF = jnp.bfloat16
F32 = jnp.float32
MIB = 1024 * 1024


def periodic_lift(u):
    s, d = u[0::2].copy(), u[1::2].copy()
    d = d + lift_alpha * (s + np.roll(s, -1, 0))
    s = s + lift_beta * (np.roll(d, 1, 0) + d)
    d = d + lift_gamma * (s + np.roll(s, -1, 0))
    s = s + lift_delta * (np.roll(d, 1, 0) + d)
    out = np.empty_like(u)
    out[0::2] = s * lift_zeta
    out[1::2] = d / lift_zeta
    return out


@functools.lru_cache(None)
def blocks(n):
    current = np.eye(4 * n)
    found = []
    for level in range(3):
        full = periodic_lift(current)
        m = n >> level
        rows = full[m : 2 * m]
        found.append((rows[:, n : 2 * n], rows[:, :n], rows[:, 2 * n : 3 * n]))
        current = full[0::2]
    return found


def row_space(outer, rank):
    _, sizes, basis = np.linalg.svd(outer, full_matrices=False)
    assert sizes[rank:].max() < 1e-10
    basis = basis[:rank].copy()
    basis[np.abs(basis) < 1e-12] = 0.0
    return basis


LEFT_RANKS = (2, 3, 4)
RIGHT_RANKS = (2, 3, 3)


@functools.lru_cache(None)
def sides(n):
    out = []
    for level, (main, left, right) in enumerate(blocks(n)):
        cl = row_space(left, LEFT_RANKS[level])
        cr = row_space(right, RIGHT_RANKS[level])
        out.append((main, cl, left @ cl.T, cr, right @ cr.T))
    return out


def nested_space(outer):
    first = row_space(outer[0], 2)
    every = np.concatenate(outer)
    rest = every - every @ first.T @ first
    return np.concatenate([first, row_space(rest, 4)])


@functools.lru_cache(None)
def joint_sides(n):
    found = blocks(n)
    cl = nested_space([b[1] for b in found])
    cr = nested_space([b[2] for b in found])
    maps = [(b[0], b[1] @ cl.T, b[2] @ cr.T) for b in found]
    return cl, cr, maps


def hi_lo(table):
    table = np.asarray(table, np.float32)
    hi = table.astype(ml_dtypes.bfloat16)
    lo = (table - hi.astype(np.float32)).astype(ml_dtypes.bfloat16)
    return hi, lo


def stack_lhs(table):
    hi, lo = hi_lo(table)
    return np.concatenate([hi, lo, hi], axis=1)


def stack_rhs(table):
    hi, lo = hi_lo(table)
    return np.concatenate([hi, hi, lo], axis=0)


def split(values):
    hi = values.astype(BF)
    return hi, (values - hi.astype(F32)).astype(BF)


def dot(a, b):
    return lax.dot_general(a, b, (((1,), (0,)), ((), ())), preferred_element_type=F32)


def dot_t(a, b):
    return lax.dot_general(a, b, (((1,), (1,)), ((), ())), preferred_element_type=F32)


def spread_columns(table, step, width):
    out = np.zeros((table.shape[0], width))
    out[:, ::step] = table
    return out


VM = pl.BlockSpec(memory_space=pltpu.VMEM)
HB = pl.BlockSpec(memory_space=pltpu.HBM)


def in_hbm(array):
    return pltpu.with_memory_space_constraint(array, pltpu.HBM)


def vmem(shape, dtype=F32):
    return pltpu.VMEM(shape, dtype)


def params(mib):
    return pltpu.CompilerParams(vmem_limit_bytes=mib * MIB)


def x_send(field):
    nz, nx, ny = field.shape
    cl, cr, _ = joint_sides(nx)
    one = np.concatenate([cl, cr])
    group = 4
    wide = np.kron(np.eye(group), one)
    hi_rows, lo_rows = hi_lo(wide)
    pair = np.concatenate([hi_rows, lo_rows])
    height = 12 * group
    step = 4
    steps = nz // step
    order = [0, steps - 1] + list(range(1, steps - 1))
    flight = 4
    _, low, _, high, _ = sides(nz)[0]
    assert np.abs(low[:, :-step]).max() == 0 and np.abs(high[:, step:]).max() == 0

    def kernel(u_hbm, c_hbm, u_ref, out_ref, up_ref, down_ref, c_ref, u_sem, c_sem):
        table_copy = pltpu.make_async_copy(c_hbm, c_ref, c_sem)
        copies = [
            pltpu.make_async_copy(
                u_hbm.at[i * step : i * step + step], u_ref.at[i * step : i * step + step], u_sem.at[i]
            )
            for i in range(steps)
        ]
        for i in order[:flight]:
            copies[i].start()
        table_copy.start()
        table_copy.wait()
        table = c_ref[...]
        for turn, i in enumerate(order):
            copies[i].wait()
            if turn + flight < steps:
                copies[order[turn + flight]].start()
            for g in range(i * step // group, (i + 1) * step // group):
                hi, lo = split(u_ref[group * g : group * g + group].reshape(group * nx, ny))
                both = dot(table, hi)
                out_ref[height * g : height * g + height, :] = (
                    both[:height] + both[height:] + dot(table[:height], lo)
                )
            if i in order[:2]:
                combos, ref = (high, down_ref) if i == 0 else (low, up_ref)
                for c in range(2):
                    ref[c * nx : c * nx + nx, :] = weighted(
                        [(combos[c, z], lambda z=z: u_ref[z]) for z in range(i * step, (i + 1) * step)]
                    )

    return pl.pallas_call(
        kernel,
        in_specs=[HB, HB],
        out_specs=[VM] * 4,
        out_shape=[vmem((nz, nx, ny)), vmem((nz * 12, ny)), vmem((2 * nx, ny)), vmem((2 * nx, ny))],
        scratch_shapes=[
            pltpu.VMEM(pair.shape, BF),
            pltpu.SemaphoreType.DMA((steps,)),
            pltpu.SemaphoreType.DMA,
        ],
        compiler_params=params(16),
        name="x_send",
    )(in_hbm(field), in_hbm(jnp.asarray(pair)))


def x_exchange(message):
    count = lax.axis_size("gx")
    right = [(i, (i + 1) % count) for i in range(count)]
    if count == 2:
        return lax.ppermute(message, "gx", right)
    left = [(j, i) for i, j in right]
    rows, ny = message.shape
    grid = message.reshape(rows // 12, 12, ny)
    from_left = lax.ppermute(grid[:, :6], "gx", right)
    from_right = lax.ppermute(grid[:, 6:], "gx", left)
    return jnp.concatenate([from_left, from_right], axis=1).reshape(rows, ny)


def x_apply(field, halo):
    nz, nx, ny = field.shape
    _, _, maps = joint_sides(nx)
    main = np.concatenate([m for m, _, _ in maps])
    outer = np.concatenate([np.concatenate([l, r], axis=1) for _, l, r in maps])
    pad = np.zeros((main.shape[0], 4))
    tables = np.stack(
        [
            stack_lhs(np.concatenate([main, outer, pad], axis=1)),
            stack_lhs(np.concatenate([main, pad, outer], axis=1)),
        ]
    )
    rows = main.shape[0]
    counts = [nx, nx // 2, nx // 4]
    step = 8
    steps = nz // step

    combos = []
    for level, (_, cl, _, cr, _) in enumerate(sides(ny)):
        both = np.zeros((8, 128))
        assert np.abs(cl[:, : ny - 64]).max() == 0 and np.abs(cr[:, 64:]).max() == 0
        both[: cl.shape[0], 64:] = cl[:, ny - 64 :]
        both[4 : 4 + cr.shape[0], :64] = cr[:, :64]
        combos.append(stack_lhs(both))
    combos = np.stack(combos)

    def kernel(u_ref, r_ref, t_ref, c_ref, x1, x2, x3, right_ref, left_ref, e1, e2, e3):
        i = pl.program_id(0)
        lanes = lax.broadcasted_iota(jnp.int32, (rows, 128), 1)
        for z in range(step):
            start = pl.multiple_of(i * (12 * step) + 24 * (z // 2) + 8 * (z % 2), 8)
            hi, lo = split(u_ref[i * step + z])
            rhi, rlo = split(r_ref[pl.ds(start, 16), :])
            stacked = jnp.concatenate([hi, rhi, hi, rhi, lo, rlo], axis=0)
            got = dot(t_ref[z % 2], stacked)
            edge = jnp.where(lanes < 64, got[:, :128], got[:, ny - 128 :])
            ehi, elo = split(edge)
            estack = jnp.concatenate([ehi, ehi, elo], axis=1)
            at = 0
            for ref, eref, n in zip((x1, x2, x3), (e1, e2, e3), counts):
                where = pl.ds(pl.multiple_of((i * step + z) * n, 16), n)
                ref[i * step + z] = got[at : at + n]
                eref[where, :] = estack[at : at + n]
                at += n

        @pl.when(i == steps - 1)
        def _():
            row = 0
            for level, (eref, n) in enumerate(zip((e1, e2, e3), counts)):
                got = dot_t(c_ref[level], eref[...])
                for j in range(nz * n // 512):
                    for c in range(LEFT_RANKS[level]):
                        right_ref[row : row + 1, :] = got[c : c + 1, 512 * j : 512 * j + 512]
                        if c < RIGHT_RANKS[level]:
                            left_ref[row : row + 1, :] = got[4 + c : 5 + c, 512 * j : 512 * j + 512]
                        else:
                            left_ref[row : row + 1, :] = jnp.zeros((1, 512), F32)
                        row += 1
            right_ref[row:, :] = jnp.zeros((24 - row, 512), F32)
            left_ref[row:, :] = jnp.zeros((24 - row, 512), F32)

    return pl.pallas_call(
        kernel,
        grid=(steps,),
        in_specs=[VM] * 4,
        out_specs=[VM] * 5,
        out_shape=[vmem((nz, n, ny)) for n in counts] + [jax.ShapeDtypeStruct((24, 512), F32)] * 2,
        scratch_shapes=[pltpu.VMEM((nz * n, 384), BF) for n in counts],
        compiler_params=params(24),
        name="x_apply",
    )(field, halo, jnp.asarray(tables), jnp.asarray(combos))


def add(a, b):
    if a is None:
        return b
    return a if b is None else a + b


def scale(a, c):
    return None if a is None else a * np.float32(c)


def open_lift(values, first, last):
    get = values.get
    low, high = first // 2 - 3, last // 2 + 4
    s = {i: get(2 * i) for i in range(low, high + 1)}
    d = {i: get(2 * i + 1) for i in range(low, high + 1)}
    pick = lambda t, i: t.get(i)
    d1 = {i: add(d[i], scale(add(s[i], pick(s, i + 1)), lift_alpha)) for i in range(low, high + 1)}
    s1 = {i: add(s[i], scale(add(pick(d1, i - 1), d1[i]), lift_beta)) for i in range(low, high + 1)}
    d2 = {i: add(d1[i], scale(add(s1[i], pick(s1, i + 1)), lift_gamma)) for i in range(low, high + 1)}
    s2 = {i: add(s1[i], scale(add(pick(d2, i - 1), d2[i]), lift_delta)) for i in range(low, high + 1)}
    out = {}
    for z in range(first, last + 1):
        if z % 2:
            out[z] = scale(d2[z // 2], 1.0 / lift_zeta)
        else:
            out[z] = scale(s2[z // 2], lift_zeta)
    return out


def lows(values, first, last):
    got = open_lift(values, 2 * first, 2 * last)
    return {i: got[2 * i] for i in range(first, last + 1) if got[2 * i] is not None}


def own_levels(values, nz, level):
    if level >= 1:
        values = lows(values, -2, nz // 2 + 1)
    if level >= 2:
        values = lows(values, -3, nz // 4 + 2)
    return open_lift(values, 0, (nz >> level) - 1)


def z_tables(nz):
    out = []
    for _, cl, pl_, cr, pr in sides(nz):
        out.append((np.concatenate([cl, cr]), np.concatenate([pl_, pr], axis=1)))
    return out


def weighted(parts):
    total = None
    for scalar, get in parts:
        if abs(scalar) < 1e-12:
            continue
        term = get() * np.float32(scalar)
        total = term if total is None else total + term
    return total


def z_first(x2, x3, halo):
    nz, _, ny = x2.shape
    tables = [t for t, _ in z_tables(nz)]
    counts = [x2.shape[1], x3.shape[1]]
    groups = ny // 128

    def kernel(x2, x3, r_ref, o2, o3, of, y2, y3):
        for level, ref, out, own, table, n in zip((1, 2), (x2, x3), (o2, o3), (y2, y3), tables[1:], counts):

            def body(k, _, level=level, ref=ref, out=out, own=own, table=table, n=n):
                row = pl.multiple_of((k // groups) * 8, 8)
                lane = pl.multiple_of((k % groups) * 128, 128)
                get = {}
                for z in range(nz):
                    get[z] = ref[z, pl.ds(row, 8), pl.ds(lane, 128)]
                for z, value in own_levels(get, nz, level).items():
                    own[z, pl.ds(row, 8), pl.ds(lane, 128)] = value
                for c in range(table.shape[0]):
                    out[pl.ds(pl.multiple_of(c * n + row, 8), 8), pl.ds(lane, 128)] = weighted(
                        [(table[c, z], lambda z=z: get[z]) for z in range(nz)]
                    )
                return 0

            lax.fori_loop(0, (n // 8) * groups, body, 0)
        for c in range(4):
            got = weighted(
                [(tables[0][c, z], lambda z=z: r_ref[12 * z : 12 * z + 12, :]) for z in range(nz)]
            )
            of[4 * c : 4 * c + 2, :] = got[0:2]
            of[4 * c + 2 : 4 * c + 4, :] = got[6:8]

    return pl.pallas_call(
        kernel,
        in_specs=[VM] * 3,
        out_specs=[VM] * 5,
        out_shape=[vmem((t.shape[0] * n, ny)) for t, n in zip(tables[1:], counts)]
        + [vmem((16, ny)), vmem((nz // 2, counts[0], ny)), vmem((nz // 4, counts[1], ny))],
        compiler_params=params(16),
        cost_estimate=pl.CostEstimate(flops=20_000_000, bytes_accessed=6_000_000, transcendentals=0),
        name="z_first",
    )(x2, x3, halo)


def y_tables(ny, spread):
    out = []
    for level, (main, _, left, _, right) in enumerate(sides(ny)):
        step = (1 << level) if spread else 1
        width = ny if spread else ny >> level
        fit = lambda t: spread_columns(t.T, step, width)
        out.append((fit(main), fit(left), fit(right)))
    return out


def halo_rows(level, chunk, nz, counts):
    start = 0
    for below in range(level):
        start += (nz * counts[below] // 512) * LEFT_RANKS[below]
    return start + chunk * LEFT_RANKS[level]


LEFT_AT, RIGHT_AT = 32, 56


def halo_base(left, right, level, nz, counts):
    base = np.zeros((128, left.shape[1]))
    for chunk in range(nz * counts[level] // 512):
        row = halo_rows(level, chunk, nz, counts)
        base[LEFT_AT + row : LEFT_AT + row + left.shape[0]] = left
        base[RIGHT_AT + row : RIGHT_AT + row + right.shape[0]] = right
    return base


def turned(left_ref, right_ref):
    wide = jnp.concatenate(
        [jnp.zeros((LEFT_AT, 512), F32), left_ref[...], right_ref[...], jnp.zeros((48, 512), F32)], axis=0
    )
    return wide.T


def band_tables(level, nz, counts, ny):
    assert ny == 512
    main, left, right = y_tables(ny, True)[level]
    base = halo_base(left, right, level, nz, counts)
    own, edge = [], []
    for j in range(2):
        cols = slice(256 * j, 256 * j + 256)
        own.append(stack_rhs(main[cols, cols]))
        tile = base[:, cols].copy()
        if j == 0:
            tile[:32] = main[256:288, cols]
            assert np.abs(main[288:, cols]).max() == 0
        else:
            tile[96:] = main[224:256, cols]
            assert np.abs(main[:224, cols]).max() == 0
        edge.append(stack_rhs(tile))
    return np.stack(own), np.stack(edge)


def three(values):
    hi, lo = split(values)
    return jnp.concatenate([hi, lo, hi], axis=1)


def banded(rows, edge, own_ref, edge_ref):
    edges = three(edge)
    out = []
    for j in range(2):
        own = three(rows[:, 256 * j : 256 * j + 256])
        out.append(dot(own, own_ref[j]) + dot(edges, edge_ref[j]))
    return jnp.concatenate(out, axis=1)


def plain_edge(rows):
    lanes = lax.broadcasted_iota(jnp.int32, (rows.shape[0], 128), 1)
    before = jnp.where(lanes >= 96, rows[:, 128:256], 0.0)
    return jnp.where(lanes < 32, rows[:, 256:384], before)


def late_rows(side, counts, ny):
    ranks = LEFT_RANKS if side == 0 else RIGHT_RANKS
    parts = [ranks[1] * counts[1] * ny // 256, ranks[2] * counts[2] * ny // 512, ny // 16, 8]
    return [0] + [int(n) for n in np.cumsum(parts)]


def y_messages(combined, from_left, from_right, nz, band_one):
    c2, c3, cf = combined
    ny = c2.shape[1]
    tables = z_tables(nz)
    nums = [t.shape[0] for t, _ in tables]
    counts = [2 * c2.shape[0] // nums[1], c2.shape[0] // nums[1], c3.shape[0] // nums[2]]
    mains, halos, coefs = [], [], []
    for level, (main, left, right) in enumerate(y_tables(ny, False)):
        mains.append(stack_rhs(main))
        halos.append(stack_rhs(halo_base(left, right, level, nz, counts)))
        chunks = nz * counts[level] // 512
        per = 512 // counts[level]
        table = tables[level][0]
        coef = np.zeros((nums[level], per, 128), np.float32)
        for c in range(nums[level]):
            for zz in range(per):
                for chunk in range(chunks):
                    row = halo_rows(level, chunk, nz, counts)
                    for lane in range(LEFT_RANKS[level]):
                        for base in (LEFT_AT, RIGHT_AT):
                            coef[c, zz, base + row + lane] = table[c, chunk * per + zz]
        coefs.append(coef.reshape(nums[level] * per, 128))
    places = [late_rows(side, counts, ny) for side in (0, 1)]

    def kernel(c2, c3, cf, fl, fr, own1, edge1, m2, m3, h2, h3, k1, k2, k3, up_ref, down_ref):
        halo = turned(fl, fr)

        def reduced(k, n, num):
            per = 512 // n
            extra = []
            for c in range(num):
                total = None
                for zz in range(per):
                    if np.abs(coefs_of[n][c * per + zz]).max() > 1e-12:
                        term = halo[zz * n : zz * n + n] * k[c * per + zz : c * per + zz + 1, :]
                        total = term if total is None else total + term
                extra.append(total)
            return extra

        coefs_of = dict(zip(counts, coefs))
        got = []
        for c_ref, m, h, k, n, num in zip((c2, c3), (m2, m3), (h2, h3), (k2, k3), counts[1:], nums[1:]):
            extra = jnp.concatenate(reduced(k, n, num), axis=0)
            got.append(dot(three(c_ref[...]), m[...]) + dot(three(extra), h[...]))
        frame = cf[...]
        frame = banded(frame, plain_edge(frame), own1, edge1)
        ones = reduced(k1, counts[0], 4)
        rows8 = lax.broadcasted_iota(jnp.int32, (8, 128), 0)
        for side, ref in enumerate((up_ref, down_ref)):
            at = places[side]
            for level in (1, 2):
                n, lane_groups = counts[level], (ny >> level) // 128
                ranks = LEFT_RANKS if side == 0 else RIGHT_RANKS
                first = 0 if side == 0 else LEFT_RANKS[level] * n
                row = at[level - 1]
                for c in range(ranks[level]):
                    for p in range(lane_groups):
                        ref[row : row + n, :] = got[level - 1][
                            first + c * n : first + c * n + n, 128 * p : 128 * p + 128
                        ]
                        row += n
            for p in range(ny // 128):
                ref[at[2] + 8 * p : at[2] + 8 * p + 8, :] = frame[
                    8 * side : 8 * side + 8, 128 * p : 128 * p + 128
                ]
            turn = jnp.concatenate(ones[2 * side : 2 * side + 2], axis=0).T
            both = []
            for start in (LEFT_AT, RIGHT_AT):
                v = turn[start : start + 8]
                v = v + pltpu.roll(v, 4, 0)
                both.append(v + pltpu.roll(v, 2, 0))
            ref[at[3] : at[4], :] = jnp.where(rows8 < 2, both[0], both[1])

    return pl.pallas_call(
        kernel,
        in_specs=[VM] * 14,
        out_specs=[VM] * 2,
        out_shape=[vmem((at[-1], 128)) for at in places],
        compiler_params=params(24),
        name="y_messages",
    )(
        c2,
        c3,
        cf,
        from_left,
        from_right,
        *band_one,
        *[jnp.asarray(t) for t in mains[1:]],
        *[jnp.asarray(t) for t in halos[1:]],
        *[jnp.asarray(t) for t in coefs],
    )


def touched_layers(nz):
    one, two, three = [np.abs(p).max(axis=1) > 1e-12 for _, p in z_tables(nz)]
    hit = lambda z: one[z] or (z % 2 == 0 and two[z // 2]) or (z % 4 == 0 and three[z // 4])
    return [z for z in range(nz) if hit(z)]


def main_part(xs, from_left, from_right, below, above, bands):
    nz, nx, ny = xs[0].shape
    counts = [nx, nx // 2, nx // 4]
    changed = touched_layers(nz)
    untouched = [z for z in range(nz) if z not in changed]
    groups = ny // 128
    _, _, maps = joint_sides(nx)
    x_table = stack_lhs(maps[0][0])
    masks = []
    for level in range(3):
        chunks = nz * counts[level] // 512
        per = 512 // counts[level]
        lanes_of = np.zeros((chunks, 128))
        for chunk in range(chunks):
            row = halo_rows(level, chunk, nz, counts)
            for base in (LEFT_AT, RIGHT_AT):
                lanes_of[chunk, base + row : base + row + LEFT_RANKS[level]] = 1.0
        if level == 0:
            masks.append(lanes_of)
        else:
            own = sides(nz)[level][0]
            lanes = np.einsum("ocz,cl->ozl", own.reshape(own.shape[0], chunks, per), lanes_of)
            masks.append(lanes.reshape(-1, 128))
    masks = [np.concatenate([m, np.zeros((-m.shape[0] % 8, 128))]).astype(np.float32) for m in masks]

    def kernel(x1, x2, x3, fl, fr, b1, a1, o1, e1, o2, e2, o3, e3, xt, k1, k2, k3, out_ref, w_ref, hbm, w2, halo_ref, sem):
        halo_ref[...] = turned(fl, fr)
        lanes = lax.broadcasted_iota(jnp.int32, (8, 128), 1)
        wide = lax.broadcasted_iota(jnp.int32, (32, 128), 1)
        after, before = wide < 32, wide >= 96

        def in_y(x, level, row, tall, own, edge, mk):
            n = counts[level]
            per = 512 // n
            layers = nz >> level
            values = x[:, row : row + tall, :]
            turns = [halo_ref[zz * n + row : zz * n + row + tall, :] for zz in range(per)]
            edges = []
            for z in range(layers):
                if level == 0:
                    turn = turns[z % per] * mk[z // per : z // per + 1, :]
                else:
                    turn = None
                    for zz in range(per):
                        if np.abs(masks[level][z * per + zz]).max() > 1e-12:
                            turn = add(turn, turns[zz] * mk[z * per + zz : z * per + zz + 1, :])
                edges.append(
                    jnp.where(
                        after[:tall],
                        values[z, :, 256:384],
                        jnp.where(before[:tall], values[z, :, 128:256], turn),
                    )
                )
            got = banded(
                values.reshape(layers * tall, ny), jnp.concatenate(edges, axis=0), own, edge
            )
            return {z: got[tall * z : tall * z + tall] for z in range(layers)}

        def store(to, values, row, indices, height=None):
            for z in indices:
                for q in range(groups):
                    piece = values[z][:, 128 * q : 128 * q + 128]
                    tall = piece.shape[0]
                    if height is None:
                        to[q, z, row : row + tall, :] = piece
                    else:
                        to[q, z * height + row : z * height + row + tall, :] = piece

        for row in range(0, counts[0], 16):
            got = own_levels(in_y(x1, 0, row, 16, o1, e1, k1), nz, 0)
            store(out_ref, got, row, range(nz))

        def leaving(layers):
            return [
                pltpu.make_async_copy(
                    out_ref.at[q, z], hbm.at[z, :, 128 * q : 128 * q + 128], sem.at[z]
                )
                for z in layers
                for q in range(groups)
            ]

        copies = leaving([z for z in untouched if z % 2])
        for copy in copies:
            copy.start()

        store(w2, in_y(x2, 1, 0, counts[1], o2, e2, k2), 0, range(nz // 2), counts[1])
        got = in_y(x3, 2, 0, counts[2], o3, e3, k3)
        for z in range(nz // 4):
            for row in range(0, counts[2], 8):
                where = pl.ds(2 * z * counts[1] + 2 * row, 8, stride=2)
                for q in range(groups):
                    piece = got[z][row : row + 8, 128 * q : 128 * q + 128]
                    w2[q, where, :] = jnp.where(lanes % 4 == 0, piece, w2[q, where, :])

        def merge(k, _):
            row = pl.multiple_of((k // groups) * 8, 8)
            q = k % groups
            where = pl.ds(2 * row, 8, stride=2)
            for z in range(nz // 2):
                inner = w2[q, pl.ds(pl.multiple_of(z * counts[1] + row, 8), 8), :]
                out_ref[q, 2 * z, where, :] = jnp.where(lanes % 2 == 0, inner, out_ref[q, 2 * z, where, :])
            return 0

        lax.fori_loop(0, (counts[1] // 8) * groups, merge, 0)
        more = leaving([z for z in untouched if z % 2 == 0])
        for copy in more:
            copy.start()

        early = []
        for ref in (b1, a1):
            for c in range(2):
                hi, lo = split(ref[c * nx : c * nx + nx, :])
                early.append(dot(xt[...], jnp.concatenate([hi, hi, lo], axis=0)))
        early = jnp.concatenate(early, axis=0)
        w_ref[...] = banded(early, plain_edge(early), o1, e1)

        for copy in copies + more:
            copy.wait()

    flat = [t for band in bands for t in band]
    return pl.pallas_call(
        kernel,
        in_specs=[VM] * 17,
        out_specs=[VM, VM, HB],
        out_shape=[
            vmem((groups, nz, nx, 128)),
            vmem((4 * nx, ny)),
            pltpu.HBM((nz, nx, ny), F32),
        ],
        scratch_shapes=[
            pltpu.VMEM((groups, nz // 2 * counts[1], 128), F32),
            pltpu.VMEM((512, 128), F32),
            pltpu.SemaphoreType.DMA((nz,)),
        ],
        compiler_params=params(32),
        cost_estimate=pl.CostEstimate(
            flops=8_000_000_000, bytes_accessed=20_000_000, transcendentals=0
        ),
        name="main_part",
    )(*xs, from_left, from_right, below, above, *flat, jnp.asarray(x_table), *[jnp.asarray(m) for m in masks])


def z_apply(inner, partial, early, from_left, from_right):
    groups, nz, nx, _ = inner.shape
    ny = groups * 128
    maps = [p for _, p in z_tables(nz)]
    counts = [nx, nx // 2, nx // 4]
    tables = []
    for level in (1, 2):
        width = ny >> level
        hi = spread_columns(np.eye(width), 1 << level, ny).astype(ml_dtypes.bfloat16)
        tables.append(np.concatenate([hi, hi]))
    places = [late_rows(side, counts, ny) for side in (0, 1)]
    _, _, x_maps = joint_sides(nx)
    frame = np.zeros((4 * nx, 16))
    for c in range(4):
        frame[c * nx : c * nx + nx, 4 * c : 4 * c + 2] = x_maps[0][1][:, :2]
        frame[c * nx : c * nx + nx, 4 * c + 2 : 4 * c + 4] = x_maps[0][2][:, :2]
        assert np.abs(x_maps[0][1][:, 2:]).max() < 1e-12 and np.abs(x_maps[0][2][:, 2:]).max() < 1e-12
    _, left, right = y_tables(ny, True)[0]
    side_hi, side_lo = hi_lo(np.concatenate([left, right, np.zeros((4, ny))]))
    side_rows = np.concatenate([side_hi, side_hi, side_lo, np.zeros((104, ny), side_hi.dtype)])
    touched = touched_layers(nz)

    def kernel(in_ref, base_hbm, w_ref, fl, fr, t2, t3, xf, yf, out_hbm, s1, s2, s3, buf, sem):
        del base_hbm
        s3[...] = jnp.zeros(s3.shape, F32)
        halos = [
            jnp.concatenate([ref[at[2] + 8 * p : at[2] + 8 * p + 8, :] for p in range(groups)], axis=1)
            for ref, at in zip((fl, fr), places)
        ]
        hi, lo = split(jnp.concatenate(halos, axis=0))
        none = jnp.zeros((104, 128), F32)
        turn = []
        for ref, at in zip((fl, fr), places):
            values = ref[at[3] : at[4], :]
            high = values.astype(BF).astype(F32)
            turn.append(jnp.concatenate([high, values - high, high, none], axis=0).T.astype(BF))
        left_hand = jnp.concatenate([jnp.concatenate(turn, axis=0), xf[...]], axis=1)
        first = w_ref[...] + dot(left_hand, jnp.concatenate([yf[...], hi, hi, lo], axis=0))
        for c in range(4):
            for q in range(groups):
                s1[c, q] = first[c * nx : c * nx + nx, 128 * q : 128 * q + 128]
        for level, table, to in ((1, t2, s2), (2, t3, s3)):
            n, lane_groups = counts[level], (ny >> level) // 128
            pieces = []
            for side, ref in enumerate((fl, fr)):
                row = places[side][level - 1]
                for c in range((LEFT_RANKS, RIGHT_RANKS)[side][level]):
                    pieces.append(
                        jnp.concatenate(
                            [ref[row + p * n : row + p * n + n, :] for p in range(lane_groups)], axis=1
                        )
                    )
                    row += lane_groups * n
            flat = jnp.concatenate(pieces, axis=0)
            hi, lo = split(flat)
            got = dot(jnp.concatenate([hi, lo], axis=1), table[...])
            for c in range(LEFT_RANKS[level] + RIGHT_RANKS[level]):
                start = c * n
                for q in range(groups):
                    piece = got[start : start + n, 128 * q : 128 * q + 128]
                    if level == 1:
                        to[c, q] = piece
                    else:
                        to[c, q, pl.ds(0, n, stride=2), :] = piece

        lanes = lax.broadcasted_iota(jnp.int32, (8, 128), 1)
        even_lane = lanes % 2 == 0
        third_cell = (lax.broadcasted_iota(jnp.int32, (8, 128), 0) % 2 + lanes % 4) == 0

        def summed(table_row, get):
            total = None
            for c, scalar in enumerate(table_row):
                if abs(scalar) > 1e-12:
                    total = add(total, get(c) * np.float32(scalar))
            return total

        copies = []
        for slot, z in enumerate(touched):

            for t in range(nx // 16):
                full, half = 16 * t, 8 * t
                for q in range(groups):
                    if z % 2:
                        for more in (0, 8):
                            rows = pl.ds(full + more, 8)
                            extra = summed(maps[0][z], lambda c: s1[c, q, rows, :])
                            buf[slot, q, rows, :] = add(in_ref[q, z, rows, :], extra)
                        continue
                    evens = pl.ds(16 * t, 8, stride=2)
                    odds = pl.ds(16 * t + 1, 8, stride=2)
                    extra = summed(maps[0][z], lambda c: s1[c, q, odds, :])
                    buf[slot, q, odds, :] = add(in_ref[q, z, odds, :], extra)
                    rows = pl.ds(half, 8)
                    extra = summed(maps[1][z // 2], lambda c: s2[c, q, rows, :])
                    if z % 4 == 0:
                        third = summed(maps[2][z // 4], lambda c: s3[c, q, rows, :])
                        third = 0.0 if third is None else third
                        extra = jnp.where(third_cell, third, 0.0 if extra is None else extra)
                    one = summed(maps[0][z], lambda c: s1[c, q, evens, :])
                    if one is not None:
                        extra = jnp.where(even_lane, 0.0 if extra is None else extra, one)
                    buf[slot, q, evens, :] = add(in_ref[q, z, evens, :], extra)
            for q in range(groups):
                copy = pltpu.make_async_copy(
                    buf.at[slot, q], out_hbm.at[z, :, 128 * q : 128 * q + 128], sem.at[slot]
                )
                copy.start()
                copies.append(copy)
        for copy in copies:
            copy.wait()

    return pl.pallas_call(
        kernel,
        in_specs=[VM, HB] + [VM] * 7,
        out_specs=HB,
        out_shape=jax.ShapeDtypeStruct((nz, nx, ny), F32),
        input_output_aliases={1: 0},
        scratch_shapes=[
            pltpu.VMEM((4, groups, nx, 128), F32),
            pltpu.VMEM((maps[1].shape[1], groups, nx // 2, 128), F32),
            pltpu.VMEM((maps[2].shape[1], groups, nx // 2, 128), F32),
            pltpu.VMEM((len(touched), groups, nx, 128), F32),
            pltpu.SemaphoreType.DMA((len(touched),)),
        ],
        compiler_params=params(24),
        name="z_apply",
    )(
        inner,
        partial,
        early,
        from_left,
        from_right,
        *[jnp.asarray(t) for t in tables],
        jnp.asarray(stack_lhs(frame)),
        jnp.asarray(side_rows),
    )


def swap(to_right, to_left, axis):
    count = lax.axis_size(axis)
    right = [(i, (i + 1) % count) for i in range(count)]
    left = [(j, i) for i, j in right]
    return lax.ppermute(to_right, axis, right), lax.ppermute(to_left, axis, left)


def local(field):
    nz, nx, ny = field.shape
    counts = [nx, nx // 2, nx // 4]
    bands = [[jnp.asarray(t) for t in band_tables(level, nz, counts, ny)] for level in range(3)]
    field, message, up, down = x_send(field)
    halo = x_exchange(message)
    below, above = swap(up, down, "gz")
    x1, x2, x3, to_right, to_left = x_apply(field, halo)
    from_left, from_right = swap(to_right, to_left, "gy")
    *combined, own2, own3 = z_first(x2, x3, halo)
    up, down = y_messages(combined, from_left, from_right, nz, bands[0])
    late_below, late_above = swap(up, down, "gz")
    inner, early, partial = main_part((x1, own2, own3), from_left, from_right, below, above, bands)
    return z_apply(inner, partial, early, late_below, late_above)


def solution(mesh):
    placed = (P("gz", "gx", "gy"),)
    return jax.shard_map(
        local, mesh=mesh, in_specs=placed, out_specs=P("gz", "gx", "gy"), check_vma=False
    )
```

```python
import functools

import jax
import jax.numpy as jnp
import ml_dtypes
import numpy as np
from jax import lax
from jax.experimental import pallas as pl
from jax.experimental.pallas import tpu as pltpu
from jax.sharding import PartitionSpec as P

lift_alpha = -1.586134342
lift_beta = -0.05298011854
lift_gamma = 0.8829110762
lift_delta = 0.4435068522
lift_zeta = 1.149604398

BF = jnp.bfloat16
F32 = jnp.float32
MIB = 1024 * 1024


def periodic_lift(u):
    s, d = u[0::2].copy(), u[1::2].copy()
    d = d + lift_alpha * (s + np.roll(s, -1, 0))
    s = s + lift_beta * (np.roll(d, 1, 0) + d)
    d = d + lift_gamma * (s + np.roll(s, -1, 0))
    s = s + lift_delta * (np.roll(d, 1, 0) + d)
    out = np.empty_like(u)
    out[0::2] = s * lift_zeta
    out[1::2] = d / lift_zeta
    return out


@functools.lru_cache(None)
def blocks(n):
    current = np.eye(4 * n)
    found = []
    for level in range(3):
        full = periodic_lift(current)
        m = n >> level
        rows = full[m : 2 * m]
        found.append((rows[:, n : 2 * n], rows[:, :n], rows[:, 2 * n : 3 * n]))
        current = full[0::2]
    return found


def row_space(outer, rank):
    _, sizes, basis = np.linalg.svd(outer, full_matrices=False)
    assert sizes[rank:].max() < 1e-10
    basis = basis[:rank].copy()
    basis[np.abs(basis) < 1e-12] = 0.0
    return basis


LEFT_RANKS = (2, 3, 4)
RIGHT_RANKS = (2, 3, 3)


@functools.lru_cache(None)
def sides(n):
    out = []
    for level, (main, left, right) in enumerate(blocks(n)):
        cl = row_space(left, LEFT_RANKS[level])
        cr = row_space(right, RIGHT_RANKS[level])
        out.append((main, cl, left @ cl.T, cr, right @ cr.T))
    return out


def nested_space(outer):
    first = row_space(outer[0], 2)
    every = np.concatenate(outer)
    rest = every - every @ first.T @ first
    return np.concatenate([first, row_space(rest, 4)])


@functools.lru_cache(None)
def joint_sides(n):
    found = blocks(n)
    cl = nested_space([b[1] for b in found])
    cr = nested_space([b[2] for b in found])
    maps = [(b[0], b[1] @ cl.T, b[2] @ cr.T) for b in found]
    return cl, cr, maps


def hi_lo(table):
    table = np.asarray(table, np.float32)
    hi = table.astype(ml_dtypes.bfloat16)
    lo = (table - hi.astype(np.float32)).astype(ml_dtypes.bfloat16)
    return hi, lo


def stack_lhs(table):
    hi, lo = hi_lo(table)
    return np.concatenate([hi, lo, hi], axis=1)


def stack_rhs(table):
    hi, lo = hi_lo(table)
    return np.concatenate([hi, hi, lo], axis=0)


def split(values):
    hi = values.astype(BF)
    return hi, (values - hi.astype(F32)).astype(BF)


def dot(a, b):
    return lax.dot_general(a, b, (((1,), (0,)), ((), ())), preferred_element_type=F32)


def dot_t(a, b):
    return lax.dot_general(a, b, (((1,), (1,)), ((), ())), preferred_element_type=F32)


def spread_columns(table, step, width):
    out = np.zeros((table.shape[0], width))
    out[:, ::step] = table
    return out


VM = pl.BlockSpec(memory_space=pltpu.VMEM)
HB = pl.BlockSpec(memory_space=pltpu.HBM)
SHORT = pl.CostEstimate(flops=1000, bytes_accessed=1000, transcendentals=0)


def in_hbm(array):
    return pltpu.with_memory_space_constraint(array, pltpu.HBM)


def vmem(shape, dtype=F32):
    return pltpu.VMEM(shape, dtype)


def params(mib):
    return pltpu.CompilerParams(vmem_limit_bytes=mib * MIB)


def x_send(field):
    nz, nx, ny = field.shape
    cl, cr, _ = joint_sides(nx)
    one = np.concatenate([cl, cr])
    group = 4
    wide = np.kron(np.eye(group), one)
    hi_rows, lo_rows = hi_lo(wide)
    pair = np.concatenate([hi_rows, lo_rows])
    height = 12 * group
    step = 8
    steps = nz // step
    order = [0, steps - 1] + list(range(1, steps - 1))
    _, low, _, high, _ = sides(nz)[0]
    assert np.abs(low[:, :-step]).max() == 0 and np.abs(high[:, step:]).max() == 0

    def kernel(u_hbm, c_hbm, u_ref, out_ref, up_ref, down_ref, c_ref, u_sem, c_sem):
        table_copy = pltpu.make_async_copy(c_hbm, c_ref, c_sem)
        copies = [
            pltpu.make_async_copy(
                u_hbm.at[i * step : i * step + step], u_ref.at[i * step : i * step + step], u_sem.at[i]
            )
            for i in range(steps)
        ]
        table_copy.start()
        for i in order:
            copies[i].start()
        table_copy.wait()
        table = c_ref[...]
        for i in order:
            copies[i].wait()
            for g in range(i * step // group, (i + 1) * step // group):
                hi, lo = split(u_ref[group * g : group * g + group].reshape(group * nx, ny))
                both = dot(table, hi)
                out_ref[height * g : height * g + height, :] = (
                    both[:height] + both[height:] + dot(table[:height], lo)
                )
            if i in order[:2]:
                combos, ref = (high, down_ref) if i == 0 else (low, up_ref)
                for c in range(2):
                    ref[c * nx : c * nx + nx, :] = weighted(
                        [(combos[c, z], lambda z=z: u_ref[z]) for z in range(i * step, (i + 1) * step)]
                    )

    return pl.pallas_call(
        kernel,
        in_specs=[HB, HB],
        out_specs=[VM] * 4,
        out_shape=[vmem((nz, nx, ny)), vmem((nz * 12, ny)), vmem((2 * nx, ny)), vmem((2 * nx, ny))],
        scratch_shapes=[
            pltpu.VMEM(pair.shape, BF),
            pltpu.SemaphoreType.DMA((steps,)),
            pltpu.SemaphoreType.DMA,
        ],
        compiler_params=params(16),
        cost_estimate=SHORT,
        name="x_send",
    )(in_hbm(field), in_hbm(jnp.asarray(pair)))


def x_exchange(message):
    count = lax.axis_size("gx")
    right = [(i, (i + 1) % count) for i in range(count)]
    if count == 2:
        return lax.ppermute(message, "gx", right)
    left = [(j, i) for i, j in right]
    rows, ny = message.shape
    grid = message.reshape(rows // 12, 12, ny)
    from_left = lax.ppermute(grid[:, :6], "gx", right)
    from_right = lax.ppermute(grid[:, 6:], "gx", left)
    return jnp.concatenate([from_left, from_right], axis=1).reshape(rows, ny)


def x_apply(field, halo):
    nz, nx, ny = field.shape
    _, _, maps = joint_sides(nx)
    main = np.concatenate([m for m, _, _ in maps])
    outer = np.concatenate([np.concatenate([l, r], axis=1) for _, l, r in maps])
    pad = np.zeros((main.shape[0], 4))
    tables = np.stack(
        [
            stack_lhs(np.concatenate([main, outer, pad], axis=1)),
            stack_lhs(np.concatenate([main, pad, outer], axis=1)),
        ]
    )
    rows = main.shape[0]
    counts = [nx, nx // 2, nx // 4]
    step = 8
    steps = nz // step

    combos = []
    for level, (_, cl, _, cr, _) in enumerate(sides(ny)):
        both = np.zeros((8, 128))
        assert np.abs(cl[:, : ny - 64]).max() == 0 and np.abs(cr[:, 64:]).max() == 0
        both[: cl.shape[0], 64:] = cl[:, ny - 64 :]
        both[4 : 4 + cr.shape[0], :64] = cr[:, :64]
        combos.append(stack_lhs(both))
    combos = np.stack(combos)

    def kernel(u_ref, r_ref, t_ref, c_ref, x1, x2, x3, right_ref, left_ref, e1, e2, e3):
        i = pl.program_id(0)
        lanes = lax.broadcasted_iota(jnp.int32, (rows, 128), 1)
        for z in range(step):
            start = pl.multiple_of(i * (12 * step) + 24 * (z // 2) + 8 * (z % 2), 8)
            hi, lo = split(u_ref[i * step + z])
            rhi, rlo = split(r_ref[pl.ds(start, 16), :])
            stacked = jnp.concatenate([hi, rhi, hi, rhi, lo, rlo], axis=0)
            got = dot(t_ref[z % 2], stacked)
            edge = jnp.where(lanes < 64, got[:, :128], got[:, ny - 128 :])
            ehi, elo = split(edge)
            estack = jnp.concatenate([ehi, ehi, elo], axis=1)
            at = 0
            for ref, eref, n in zip((x1, x2, x3), (e1, e2, e3), counts):
                where = pl.ds(pl.multiple_of((i * step + z) * n, 16), n)
                ref[i * step + z] = got[at : at + n]
                eref[where, :] = estack[at : at + n]
                at += n

        @pl.when(i == steps - 1)
        def _():
            row = 0
            for level, (eref, n) in enumerate(zip((e1, e2, e3), counts)):
                got = dot_t(c_ref[level], eref[...])
                for j in range(nz * n // 512):
                    for c in range(LEFT_RANKS[level]):
                        right_ref[row : row + 1, :] = got[c : c + 1, 512 * j : 512 * j + 512]
                        if c < RIGHT_RANKS[level]:
                            left_ref[row : row + 1, :] = got[4 + c : 5 + c, 512 * j : 512 * j + 512]
                        else:
                            left_ref[row : row + 1, :] = jnp.zeros((1, 512), F32)
                        row += 1
            right_ref[row:, :] = jnp.zeros((24 - row, 512), F32)
            left_ref[row:, :] = jnp.zeros((24 - row, 512), F32)

    return pl.pallas_call(
        kernel,
        grid=(steps,),
        in_specs=[VM] * 4,
        out_specs=[VM] * 5,
        out_shape=[vmem((nz, n, ny)) for n in counts] + [jax.ShapeDtypeStruct((24, 512), F32)] * 2,
        scratch_shapes=[pltpu.VMEM((nz * n, 384), BF) for n in counts],
        compiler_params=params(24),
        cost_estimate=SHORT,
        name="x_apply",
    )(field, halo, jnp.asarray(tables), jnp.asarray(combos))


def add(a, b):
    if a is None:
        return b
    return a if b is None else a + b


def scale(a, c):
    return None if a is None else a * np.float32(c)


def open_lift(values, first, last):
    get = values.get
    low, high = first // 2 - 3, last // 2 + 4
    s = {i: get(2 * i) for i in range(low, high + 1)}
    d = {i: get(2 * i + 1) for i in range(low, high + 1)}
    pick = lambda t, i: t.get(i)
    d1 = {i: add(d[i], scale(add(s[i], pick(s, i + 1)), lift_alpha)) for i in range(low, high + 1)}
    s1 = {i: add(s[i], scale(add(pick(d1, i - 1), d1[i]), lift_beta)) for i in range(low, high + 1)}
    d2 = {i: add(d1[i], scale(add(s1[i], pick(s1, i + 1)), lift_gamma)) for i in range(low, high + 1)}
    s2 = {i: add(s1[i], scale(add(pick(d2, i - 1), d2[i]), lift_delta)) for i in range(low, high + 1)}
    out = {}
    for z in range(first, last + 1):
        if z % 2:
            out[z] = scale(d2[z // 2], 1.0 / lift_zeta)
        else:
            out[z] = scale(s2[z // 2], lift_zeta)
    return out


def lows(values, first, last):
    got = open_lift(values, 2 * first, 2 * last)
    return {i: got[2 * i] for i in range(first, last + 1) if got[2 * i] is not None}


def own_levels(values, nz, level):
    if level >= 1:
        values = lows(values, -2, nz // 2 + 1)
    if level >= 2:
        values = lows(values, -3, nz // 4 + 2)
    return open_lift(values, 0, (nz >> level) - 1)


def z_tables(nz):
    out = []
    for _, cl, pl_, cr, pr in sides(nz):
        out.append((np.concatenate([cl, cr]), np.concatenate([pl_, pr], axis=1)))
    return out


def weighted(parts):
    total = None
    for scalar, get in parts:
        if abs(scalar) < 1e-12:
            continue
        term = get() * np.float32(scalar)
        total = term if total is None else total + term
    return total


def z_first(x2, x3, halo):
    nz, _, ny = x2.shape
    tables = [t for t, _ in z_tables(nz)]
    counts = [x2.shape[1], x3.shape[1]]
    groups = ny // 128

    def kernel(x2, x3, r_ref, o2, o3, of, y2, y3):
        for level, ref, out, own, table, n in zip((1, 2), (x2, x3), (o2, o3), (y2, y3), tables[1:], counts):

            def body(k, _, level=level, ref=ref, out=out, own=own, table=table, n=n):
                row = pl.multiple_of((k // groups) * 8, 8)
                lane = pl.multiple_of((k % groups) * 128, 128)
                get = {}
                for z in range(nz):
                    get[z] = ref[z, pl.ds(row, 8), pl.ds(lane, 128)]
                for z, value in own_levels(get, nz, level).items():
                    own[z, pl.ds(row, 8), pl.ds(lane, 128)] = value
                for c in range(table.shape[0]):
                    out[pl.ds(pl.multiple_of(c * n + row, 8), 8), pl.ds(lane, 128)] = weighted(
                        [(table[c, z], lambda z=z: get[z]) for z in range(nz)]
                    )
                return 0

            lax.fori_loop(0, (n // 8) * groups, body, 0)
        for c in range(4):
            got = weighted(
                [(tables[0][c, z], lambda z=z: r_ref[12 * z : 12 * z + 12, :]) for z in range(nz)]
            )
            of[4 * c : 4 * c + 2, :] = got[0:2]
            of[4 * c + 2 : 4 * c + 4, :] = got[6:8]

    return pl.pallas_call(
        kernel,
        in_specs=[VM] * 3,
        out_specs=[VM] * 5,
        out_shape=[vmem((t.shape[0] * n, ny)) for t, n in zip(tables[1:], counts)]
        + [vmem((16, ny)), vmem((nz // 2, counts[0], ny)), vmem((nz // 4, counts[1], ny))],
        compiler_params=params(16),
        cost_estimate=SHORT,
        name="z_first",
    )(x2, x3, halo)


def y_tables(ny, spread):
    out = []
    for level, (main, _, left, _, right) in enumerate(sides(ny)):
        step = (1 << level) if spread else 1
        width = ny if spread else ny >> level
        fit = lambda t: spread_columns(t.T, step, width)
        out.append((fit(main), fit(left), fit(right)))
    return out


def halo_rows(level, chunk, nz, counts):
    start = 0
    for below in range(level):
        start += (nz * counts[below] // 512) * LEFT_RANKS[below]
    return start + chunk * LEFT_RANKS[level]


LEFT_AT, RIGHT_AT = 32, 56


def halo_base(left, right, level, nz, counts):
    base = np.zeros((128, left.shape[1]))
    for chunk in range(nz * counts[level] // 512):
        row = halo_rows(level, chunk, nz, counts)
        base[LEFT_AT + row : LEFT_AT + row + left.shape[0]] = left
        base[RIGHT_AT + row : RIGHT_AT + row + right.shape[0]] = right
    return base


def turned(left_ref, right_ref):
    wide = jnp.concatenate(
        [jnp.zeros((LEFT_AT, 512), F32), left_ref[...], right_ref[...], jnp.zeros((48, 512), F32)], axis=0
    )
    return wide.T


def band_tables(level, nz, counts, ny):
    assert ny == 512
    main, left, right = y_tables(ny, True)[level]
    base = halo_base(left, right, level, nz, counts)
    own, edge = [], []
    for j in range(2):
        cols = slice(256 * j, 256 * j + 256)
        own.append(stack_rhs(main[cols, cols]))
        tile = base[:, cols].copy()
        if j == 0:
            tile[:32] = main[256:288, cols]
            assert np.abs(main[288:, cols]).max() == 0
        else:
            tile[96:] = main[224:256, cols]
            assert np.abs(main[:224, cols]).max() == 0
        edge.append(stack_rhs(tile))
    return np.stack(own), np.stack(edge)


def three(values):
    hi, lo = split(values)
    return jnp.concatenate([hi, lo, hi], axis=1)


def banded(rows, edge, own_ref, edge_ref):
    edges = three(edge)
    out = []
    for j in range(2):
        own = three(rows[:, 256 * j : 256 * j + 256])
        out.append(dot(own, own_ref[j]) + dot(edges, edge_ref[j]))
    return jnp.concatenate(out, axis=1)


def plain_edge(rows):
    lanes = lax.broadcasted_iota(jnp.int32, (rows.shape[0], 128), 1)
    before = jnp.where(lanes >= 96, rows[:, 128:256], 0.0)
    return jnp.where(lanes < 32, rows[:, 256:384], before)


def late_rows(side, counts, ny):
    ranks = LEFT_RANKS if side == 0 else RIGHT_RANKS
    parts = [ranks[1] * counts[1] * ny // 256, ranks[2] * counts[2] * ny // 512, ny // 16, 8]
    return [0] + [int(n) for n in np.cumsum(parts)]


def y_messages(combined, from_left, from_right, nz, band_one):
    c2, c3, cf = combined
    ny = c2.shape[1]
    tables = z_tables(nz)
    nums = [t.shape[0] for t, _ in tables]
    counts = [2 * c2.shape[0] // nums[1], c2.shape[0] // nums[1], c3.shape[0] // nums[2]]
    mains, halos, coefs = [], [], []
    for level, (main, left, right) in enumerate(y_tables(ny, False)):
        mains.append(stack_rhs(main))
        halos.append(stack_rhs(halo_base(left, right, level, nz, counts)))
        chunks = nz * counts[level] // 512
        per = 512 // counts[level]
        table = tables[level][0]
        coef = np.zeros((nums[level], per, 128), np.float32)
        for c in range(nums[level]):
            for zz in range(per):
                for chunk in range(chunks):
                    row = halo_rows(level, chunk, nz, counts)
                    for lane in range(LEFT_RANKS[level]):
                        for base in (LEFT_AT, RIGHT_AT):
                            coef[c, zz, base + row + lane] = table[c, chunk * per + zz]
        coefs.append(coef.reshape(nums[level] * per, 128))
    places = [late_rows(side, counts, ny) for side in (0, 1)]

    def kernel(c2, c3, cf, fl, fr, own1, edge1, m2, m3, h2, h3, k1, k2, k3, up_ref, down_ref):
        halo = turned(fl, fr)

        def reduced(k, n, num):
            per = 512 // n
            extra = []
            for c in range(num):
                total = None
                for zz in range(per):
                    if np.abs(coefs_of[n][c * per + zz]).max() > 1e-12:
                        term = halo[zz * n : zz * n + n] * k[c * per + zz : c * per + zz + 1, :]
                        total = term if total is None else total + term
                extra.append(total)
            return extra

        coefs_of = dict(zip(counts, coefs))
        got = []
        for c_ref, m, h, k, n, num in zip((c2, c3), (m2, m3), (h2, h3), (k2, k3), counts[1:], nums[1:]):
            extra = jnp.concatenate(reduced(k, n, num), axis=0)
            got.append(dot(three(c_ref[...]), m[...]) + dot(three(extra), h[...]))
        frame = cf[...]
        frame = banded(frame, plain_edge(frame), own1, edge1)
        ones = reduced(k1, counts[0], 4)
        rows8 = lax.broadcasted_iota(jnp.int32, (8, 128), 0)
        for side, ref in enumerate((up_ref, down_ref)):
            at = places[side]
            for level in (1, 2):
                n, lane_groups = counts[level], (ny >> level) // 128
                ranks = LEFT_RANKS if side == 0 else RIGHT_RANKS
                first = 0 if side == 0 else LEFT_RANKS[level] * n
                row = at[level - 1]
                for c in range(ranks[level]):
                    for p in range(lane_groups):
                        ref[row : row + n, :] = got[level - 1][
                            first + c * n : first + c * n + n, 128 * p : 128 * p + 128
                        ]
                        row += n
            for p in range(ny // 128):
                ref[at[2] + 8 * p : at[2] + 8 * p + 8, :] = frame[
                    8 * side : 8 * side + 8, 128 * p : 128 * p + 128
                ]
            turn = jnp.concatenate(ones[2 * side : 2 * side + 2], axis=0).T
            both = []
            for start in (LEFT_AT, RIGHT_AT):
                v = turn[start : start + 8]
                v = v + pltpu.roll(v, 4, 0)
                both.append(v + pltpu.roll(v, 2, 0))
            ref[at[3] : at[4], :] = jnp.where(rows8 < 2, both[0], both[1])

    return pl.pallas_call(
        kernel,
        in_specs=[VM] * 14,
        out_specs=[VM] * 2,
        out_shape=[vmem((at[-1], 128)) for at in places],
        compiler_params=params(24),
        cost_estimate=SHORT,
        name="y_messages",
    )(
        c2,
        c3,
        cf,
        from_left,
        from_right,
        *band_one,
        *[jnp.asarray(t) for t in mains[1:]],
        *[jnp.asarray(t) for t in halos[1:]],
        *[jnp.asarray(t) for t in coefs],
    )


def touched_layers(nz):
    one, two, three = [np.abs(p).max(axis=1) > 1e-12 for _, p in z_tables(nz)]
    hit = lambda z: one[z] or (z % 2 == 0 and two[z // 2]) or (z % 4 == 0 and three[z // 4])
    return [z for z in range(nz) if hit(z)]


def main_part(xs, from_left, from_right, bands):
    nz, nx, ny = xs[0].shape
    counts = [nx, nx // 2, nx // 4]
    changed = touched_layers(nz)
    untouched = [z for z in range(nz) if z not in changed]
    groups = ny // 128
    masks = []
    for level in range(3):
        chunks = nz * counts[level] // 512
        per = 512 // counts[level]
        lanes_of = np.zeros((chunks, 128))
        for chunk in range(chunks):
            row = halo_rows(level, chunk, nz, counts)
            for base in (LEFT_AT, RIGHT_AT):
                lanes_of[chunk, base + row : base + row + LEFT_RANKS[level]] = 1.0
        if level == 0:
            masks.append(lanes_of)
        else:
            own = sides(nz)[level][0]
            lanes = np.einsum("ocz,cl->ozl", own.reshape(own.shape[0], chunks, per), lanes_of)
            masks.append(lanes.reshape(-1, 128))
    masks = [np.concatenate([m, np.zeros((-m.shape[0] % 8, 128))]).astype(np.float32) for m in masks]

    def kernel(x1, x2, x3, fl, fr, o1, e1, o2, e2, o3, e3, k1, k2, k3, out_ref, done_ref, hbm, w2, halo_ref, sem):
        halo_ref[...] = turned(fl, fr)
        lanes = lax.broadcasted_iota(jnp.int32, (8, 128), 1)
        wide = lax.broadcasted_iota(jnp.int32, (32, 128), 1)
        after, before = wide < 32, wide >= 96

        def in_y(x, level, row, tall, own, edge, mk):
            n = counts[level]
            per = 512 // n
            layers = nz >> level
            values = x[:, row : row + tall, :]
            turns = [halo_ref[zz * n + row : zz * n + row + tall, :] for zz in range(per)]
            edges = []
            for z in range(layers):
                if level == 0:
                    turn = turns[z % per] * mk[z // per : z // per + 1, :]
                else:
                    turn = None
                    for zz in range(per):
                        if np.abs(masks[level][z * per + zz]).max() > 1e-12:
                            turn = add(turn, turns[zz] * mk[z * per + zz : z * per + zz + 1, :])
                edges.append(
                    jnp.where(
                        after[:tall],
                        values[z, :, 256:384],
                        jnp.where(before[:tall], values[z, :, 128:256], turn),
                    )
                )
            got = banded(
                values.reshape(layers * tall, ny), jnp.concatenate(edges, axis=0), own, edge
            )
            return {z: got[tall * z : tall * z + tall] for z in range(layers)}

        def store(to, values, row, indices, height=None):
            for z in indices:
                for q in range(groups):
                    piece = values[z][:, 128 * q : 128 * q + 128]
                    tall = piece.shape[0]
                    if height is None:
                        to[q, z, row : row + tall, :] = piece
                    else:
                        to[q, z * height + row : z * height + row + tall, :] = piece

        for row in range(0, counts[0], 16):
            got = own_levels(in_y(x1, 0, row, 16, o1, e1, k1), nz, 0)
            store(out_ref, got, row, range(nz))

        def leaving(layers):
            return [
                pltpu.make_async_copy(
                    out_ref.at[q, z], hbm.at[z, :, 128 * q : 128 * q + 128], sem.at[z]
                )
                for z in layers
                for q in range(groups)
            ]

        copies = leaving([z for z in untouched if z % 2])
        for copy in copies:
            copy.start()

        store(w2, in_y(x2, 1, 0, counts[1], o2, e2, k2), 0, range(nz // 2), counts[1])
        got = in_y(x3, 2, 0, counts[2], o3, e3, k3)
        for z in range(nz // 4):
            for row in range(0, counts[2], 8):
                where = pl.ds(2 * z * counts[1] + 2 * row, 8, stride=2)
                for q in range(groups):
                    piece = got[z][row : row + 8, 128 * q : 128 * q + 128]
                    w2[q, where, :] = jnp.where(lanes % 4 == 0, piece, w2[q, where, :])

        def merge(k, _):
            row = pl.multiple_of((k // groups) * 8, 8)
            q = k % groups
            where = pl.ds(2 * row, 8, stride=2)
            for z in range(nz // 2):
                inner = w2[q, pl.ds(pl.multiple_of(z * counts[1] + row, 8), 8), :]
                out_ref[q, 2 * z, where, :] = jnp.where(lanes % 2 == 0, inner, out_ref[q, 2 * z, where, :])
            return 0

        lax.fori_loop(0, (counts[1] // 8) * groups, merge, 0)
        more = leaving([z for z in untouched if z % 2 == 0])
        for copy in more:
            copy.start()

        done_ref[...] = jnp.zeros((8, 128), F32)
        for copy in copies + more:
            copy.wait()

    flat = [t for band in bands for t in band]
    return pl.pallas_call(
        kernel,
        in_specs=[VM] * 14,
        out_specs=[VM, VM, HB],
        out_shape=[
            vmem((groups, nz, nx, 128)),
            vmem((8, 128)),
            pltpu.HBM((nz, nx, ny), F32),
        ],
        scratch_shapes=[
            pltpu.VMEM((groups, nz // 2 * counts[1], 128), F32),
            pltpu.VMEM((512, 128), F32),
            pltpu.SemaphoreType.DMA((nz,)),
        ],
        compiler_params=params(32),
        cost_estimate=SHORT,
        name="main_part",
    )(*xs, from_left, from_right, *flat, *[jnp.asarray(m) for m in masks])


def early_part(below, above, band, after):
    nx, ny = below.shape[0] // 2, below.shape[1]
    _, _, maps = joint_sides(nx)

    def kernel(b1, a1, o1, e1, xt, after_ref, w_ref):
        del after_ref
        early = []
        for ref in (b1, a1):
            for c in range(2):
                hi, lo = split(ref[c * nx : c * nx + nx, :])
                early.append(dot(xt[...], jnp.concatenate([hi, hi, lo], axis=0)))
        early = jnp.concatenate(early, axis=0)
        w_ref[...] = banded(early, plain_edge(early), o1, e1)

    return pl.pallas_call(
        kernel,
        in_specs=[VM] * 6,
        out_specs=VM,
        out_shape=vmem((4 * nx, ny)),
        compiler_params=params(16),
        cost_estimate=SHORT,
        name="early_part",
    )(below, above, *band, jnp.asarray(stack_lhs(maps[0][0])), after)


def z_apply(inner, partial, early, from_left, from_right):
    groups, nz, nx, _ = inner.shape
    ny = groups * 128
    maps = [p for _, p in z_tables(nz)]
    counts = [nx, nx // 2, nx // 4]
    tables = []
    for level in (1, 2):
        width = ny >> level
        hi = spread_columns(np.eye(width), 1 << level, ny).astype(ml_dtypes.bfloat16)
        tables.append(np.concatenate([hi, hi]))
    places = [late_rows(side, counts, ny) for side in (0, 1)]
    _, _, x_maps = joint_sides(nx)
    frame = np.zeros((4 * nx, 16))
    for c in range(4):
        frame[c * nx : c * nx + nx, 4 * c : 4 * c + 2] = x_maps[0][1][:, :2]
        frame[c * nx : c * nx + nx, 4 * c + 2 : 4 * c + 4] = x_maps[0][2][:, :2]
        assert np.abs(x_maps[0][1][:, 2:]).max() < 1e-12 and np.abs(x_maps[0][2][:, 2:]).max() < 1e-12
    _, left, right = y_tables(ny, True)[0]
    side_hi, side_lo = hi_lo(np.concatenate([left, right, np.zeros((4, ny))]))
    side_rows = np.concatenate([side_hi, side_hi, side_lo, np.zeros((104, ny), side_hi.dtype)])
    touched = sorted(touched_layers(nz), key=lambda z: np.abs(maps[0][z]).max() > 1e-12)

    def kernel(in_ref, base_hbm, w_ref, fl, fr, t2, t3, xf, yf, out_hbm, s1, s2, s3, buf, sem):
        del base_hbm
        s3[...] = jnp.zeros(s3.shape, F32)
        halos = [
            jnp.concatenate([ref[at[2] + 8 * p : at[2] + 8 * p + 8, :] for p in range(groups)], axis=1)
            for ref, at in zip((fl, fr), places)
        ]
        hi, lo = split(jnp.concatenate(halos, axis=0))
        none = jnp.zeros((104, 128), F32)
        turn = []
        for ref, at in zip((fl, fr), places):
            values = ref[at[3] : at[4], :]
            high = values.astype(BF).astype(F32)
            turn.append(jnp.concatenate([high, values - high, high, none], axis=0).T.astype(BF))
        left_hand = jnp.concatenate([jnp.concatenate(turn, axis=0), xf[...]], axis=1)
        first = w_ref[...] + dot(left_hand, jnp.concatenate([yf[...], hi, hi, lo], axis=0))
        for c in range(4):
            for q in range(groups):
                s1[c, q] = first[c * nx : c * nx + nx, 128 * q : 128 * q + 128]
        for level, table, to in ((1, t2, s2), (2, t3, s3)):
            n, lane_groups = counts[level], (ny >> level) // 128
            pieces = []
            for side, ref in enumerate((fl, fr)):
                row = places[side][level - 1]
                for c in range((LEFT_RANKS, RIGHT_RANKS)[side][level]):
                    pieces.append(
                        jnp.concatenate(
                            [ref[row + p * n : row + p * n + n, :] for p in range(lane_groups)], axis=1
                        )
                    )
                    row += lane_groups * n
            flat = jnp.concatenate(pieces, axis=0)
            hi, lo = split(flat)
            got = dot(jnp.concatenate([hi, lo], axis=1), table[...])
            for c in range(LEFT_RANKS[level] + RIGHT_RANKS[level]):
                start = c * n
                for q in range(groups):
                    piece = got[start : start + n, 128 * q : 128 * q + 128]
                    if level == 1:
                        to[c, q] = piece
                    else:
                        to[c, q, pl.ds(0, n, stride=2), :] = piece

        lanes = lax.broadcasted_iota(jnp.int32, (8, 128), 1)
        even_lane = lanes % 2 == 0
        third_cell = (lax.broadcasted_iota(jnp.int32, (8, 128), 0) % 2 + lanes % 4) == 0

        def summed(table_row, get):
            total = None
            for c, scalar in enumerate(table_row):
                if abs(scalar) > 1e-12:
                    total = add(total, get(c) * np.float32(scalar))
            return total

        copies = []
        for slot, z in enumerate(touched):

            for t in range(nx // 16):
                full, half = 16 * t, 8 * t
                for q in range(groups):
                    if z % 2:
                        for more in (0, 8):
                            rows = pl.ds(full + more, 8)
                            extra = summed(maps[0][z], lambda c: s1[c, q, rows, :])
                            buf[slot, q, rows, :] = add(in_ref[q, z, rows, :], extra)
                        continue
                    evens = pl.ds(16 * t, 8, stride=2)
                    odds = pl.ds(16 * t + 1, 8, stride=2)
                    extra = summed(maps[0][z], lambda c: s1[c, q, odds, :])
                    buf[slot, q, odds, :] = add(in_ref[q, z, odds, :], extra)
                    rows = pl.ds(half, 8)
                    extra = summed(maps[1][z // 2], lambda c: s2[c, q, rows, :])
                    if z % 4 == 0:
                        third = summed(maps[2][z // 4], lambda c: s3[c, q, rows, :])
                        third = 0.0 if third is None else third
                        extra = jnp.where(third_cell, third, 0.0 if extra is None else extra)
                    one = summed(maps[0][z], lambda c: s1[c, q, evens, :])
                    if one is not None:
                        extra = jnp.where(even_lane, 0.0 if extra is None else extra, one)
                    buf[slot, q, evens, :] = add(in_ref[q, z, evens, :], extra)
            for q in range(groups):
                copy = pltpu.make_async_copy(
                    buf.at[slot, q], out_hbm.at[z, :, 128 * q : 128 * q + 128], sem.at[slot]
                )
                copy.start()
                copies.append(copy)
        for copy in copies:
            copy.wait()

    return pl.pallas_call(
        kernel,
        in_specs=[VM, HB] + [VM] * 7,
        out_specs=HB,
        out_shape=jax.ShapeDtypeStruct((nz, nx, ny), F32),
        input_output_aliases={1: 0},
        scratch_shapes=[
            pltpu.VMEM((4, groups, nx, 128), F32),
            pltpu.VMEM((maps[1].shape[1], groups, nx // 2, 128), F32),
            pltpu.VMEM((maps[2].shape[1], groups, nx // 2, 128), F32),
            pltpu.VMEM((len(touched), groups, nx, 128), F32),
            pltpu.SemaphoreType.DMA((len(touched),)),
        ],
        compiler_params=params(24),
        name="z_apply",
    )(
        inner,
        partial,
        early,
        from_left,
        from_right,
        *[jnp.asarray(t) for t in tables],
        jnp.asarray(stack_lhs(frame)),
        jnp.asarray(side_rows),
    )


def swap(to_right, to_left, axis):
    count = lax.axis_size(axis)
    right = [(i, (i + 1) % count) for i in range(count)]
    left = [(j, i) for i, j in right]
    return lax.ppermute(to_right, axis, right), lax.ppermute(to_left, axis, left)


def local(field):
    nz, nx, ny = field.shape
    counts = [nx, nx // 2, nx // 4]
    bands = [[jnp.asarray(t) for t in band_tables(level, nz, counts, ny)] for level in range(3)]
    field, message, up, down = x_send(field)
    halo = x_exchange(message)
    below, above = swap(up, down, "gz")
    x1, x2, x3, to_right, to_left = x_apply(field, halo)
    from_left, from_right = swap(to_right, to_left, "gy")
    *combined, own2, own3 = z_first(x2, x3, halo)
    up, down = y_messages(combined, from_left, from_right, nz, bands[0])
    late_below, late_above = swap(up, down, "gz")
    inner, done, partial = main_part((x1, own2, own3), from_left, from_right, bands)
    early = early_part(below, above, bands[0], done)
    return z_apply(inner, partial, early, late_below, late_above)


def solution(mesh):
    placed = (P("gz", "gx", "gy"),)
    return jax.shard_map(
        local, mesh=mesh, in_specs=placed, out_specs=P("gz", "gx", "gy"), check_vma=False
    )
```

```python
import functools

import jax
import jax.numpy as jnp
import ml_dtypes
import numpy as np
from jax import lax
from jax.experimental import pallas as pl
from jax.experimental.pallas import tpu as pltpu
from jax.sharding import PartitionSpec as P

lift_alpha = -1.586134342
lift_beta = -0.05298011854
lift_gamma = 0.8829110762
lift_delta = 0.4435068522
lift_zeta = 1.149604398

BF = jnp.bfloat16
F32 = jnp.float32
MIB = 1024 * 1024


def periodic_lift(u):
    s, d = u[0::2].copy(), u[1::2].copy()
    d = d + lift_alpha * (s + np.roll(s, -1, 0))
    s = s + lift_beta * (np.roll(d, 1, 0) + d)
    d = d + lift_gamma * (s + np.roll(s, -1, 0))
    s = s + lift_delta * (np.roll(d, 1, 0) + d)
    out = np.empty_like(u)
    out[0::2] = s * lift_zeta
    out[1::2] = d / lift_zeta
    return out


@functools.lru_cache(None)
def blocks(n):
    current = np.eye(4 * n)
    found = []
    for level in range(3):
        full = periodic_lift(current)
        m = n >> level
        rows = full[m : 2 * m]
        found.append((rows[:, n : 2 * n], rows[:, :n], rows[:, 2 * n : 3 * n]))
        current = full[0::2]
    return found


def row_space(outer, rank):
    _, sizes, basis = np.linalg.svd(outer, full_matrices=False)
    assert sizes[rank:].max() < 1e-10
    basis = basis[:rank].copy()
    basis[np.abs(basis) < 1e-12] = 0.0
    return basis


LEFT_RANKS = (2, 3, 4)
RIGHT_RANKS = (2, 3, 3)


@functools.lru_cache(None)
def sides(n):
    out = []
    for level, (main, left, right) in enumerate(blocks(n)):
        cl = row_space(left, LEFT_RANKS[level])
        cr = row_space(right, RIGHT_RANKS[level])
        out.append((main, cl, left @ cl.T, cr, right @ cr.T))
    return out


def nested_space(outer):
    first = row_space(outer[0], 2)
    every = np.concatenate(outer)
    rest = every - every @ first.T @ first
    return np.concatenate([first, row_space(rest, 4)])


@functools.lru_cache(None)
def joint_sides(n):
    found = blocks(n)
    cl = nested_space([b[1] for b in found])
    cr = nested_space([b[2] for b in found])
    maps = [(b[0], b[1] @ cl.T, b[2] @ cr.T) for b in found]
    return cl, cr, maps


def hi_lo(table):
    table = np.asarray(table, np.float32)
    hi = table.astype(ml_dtypes.bfloat16)
    lo = (table - hi.astype(np.float32)).astype(ml_dtypes.bfloat16)
    return hi, lo


def stack_lhs(table):
    hi, lo = hi_lo(table)
    return np.concatenate([hi, lo, hi], axis=1)


def stack_rhs(table):
    hi, lo = hi_lo(table)
    return np.concatenate([hi, hi, lo], axis=0)


def split(values):
    hi = values.astype(BF)
    return hi, (values - hi.astype(F32)).astype(BF)


def dot(a, b):
    return lax.dot_general(a, b, (((1,), (0,)), ((), ())), preferred_element_type=F32)


def dot_t(a, b):
    return lax.dot_general(a, b, (((1,), (1,)), ((), ())), preferred_element_type=F32)


def spread_columns(table, step, width):
    out = np.zeros((table.shape[0], width))
    out[:, ::step] = table
    return out


VM = pl.BlockSpec(memory_space=pltpu.VMEM)
HB = pl.BlockSpec(memory_space=pltpu.HBM)
SHORT = pl.CostEstimate(flops=1000, bytes_accessed=1000, transcendentals=0)


def in_hbm(array):
    return pltpu.with_memory_space_constraint(array, pltpu.HBM)


def vmem(shape, dtype=F32):
    return pltpu.VMEM(shape, dtype)


def params(mib):
    return pltpu.CompilerParams(vmem_limit_bytes=mib * MIB)


def x_send(field):
    nz, nx, ny = field.shape
    cl, cr, _ = joint_sides(nx)
    one = np.concatenate([cl, cr])
    group = 4
    wide = np.kron(np.eye(group), one)
    hi_rows, lo_rows = hi_lo(wide)
    pair = np.concatenate([hi_rows, lo_rows])
    height = 12 * group
    step = 8
    steps = nz // step
    order = [0, steps - 1] + list(range(1, steps - 1))
    _, low, _, high, _ = sides(nz)[0]
    assert np.abs(low[:, :-step]).max() == 0 and np.abs(high[:, step:]).max() == 0

    def kernel(u_hbm, c_hbm, u_ref, out_ref, up_ref, down_ref, c_ref, u_sem, c_sem):
        table_copy = pltpu.make_async_copy(c_hbm, c_ref, c_sem)
        copies = [
            pltpu.make_async_copy(
                u_hbm.at[i * step : i * step + step], u_ref.at[i * step : i * step + step], u_sem.at[i]
            )
            for i in range(steps)
        ]
        table_copy.start()
        for i in order:
            copies[i].start()
        table_copy.wait()
        table = c_ref[...]
        for i in order:
            copies[i].wait()
            for g in range(i * step // group, (i + 1) * step // group):
                hi, lo = split(u_ref[group * g : group * g + group].reshape(group * nx, ny))
                both = dot(table, hi)
                out_ref[height * g : height * g + height, :] = (
                    both[:height] + both[height:] + dot(table[:height], lo)
                )
            if i in order[:2]:
                combos, ref = (high, down_ref) if i == 0 else (low, up_ref)
                for c in range(2):
                    ref[c * nx : c * nx + nx, :] = weighted(
                        [(combos[c, z], lambda z=z: u_ref[z]) for z in range(i * step, (i + 1) * step)]
                    )

    return pl.pallas_call(
        kernel,
        in_specs=[HB, HB],
        out_specs=[VM] * 4,
        out_shape=[vmem((nz, nx, ny)), vmem((nz * 12, ny)), vmem((2 * nx, ny)), vmem((2 * nx, ny))],
        scratch_shapes=[
            pltpu.VMEM(pair.shape, BF),
            pltpu.SemaphoreType.DMA((steps,)),
            pltpu.SemaphoreType.DMA,
        ],
        compiler_params=params(16),
        cost_estimate=SHORT,
        name="x_send",
    )(in_hbm(field), in_hbm(jnp.asarray(pair)))


def x_exchange(message):
    count = lax.axis_size("gx")
    right = [(i, (i + 1) % count) for i in range(count)]
    if count == 2:
        return lax.ppermute(message, "gx", right)
    left = [(j, i) for i, j in right]
    rows, ny = message.shape
    grid = message.reshape(rows // 12, 12, ny)
    from_left = lax.ppermute(grid[:, :6], "gx", right)
    from_right = lax.ppermute(grid[:, 6:], "gx", left)
    return jnp.concatenate([from_left, from_right], axis=1).reshape(rows, ny)


def x_apply(field, halo):
    nz, nx, ny = field.shape
    _, _, maps = joint_sides(nx)
    main = np.concatenate([m for m, _, _ in maps])
    outer = np.concatenate([np.concatenate([l, r], axis=1) for _, l, r in maps])
    pad = np.zeros((main.shape[0], 4))
    tables = np.stack(
        [
            stack_lhs(np.concatenate([main, outer, pad], axis=1)),
            stack_lhs(np.concatenate([main, pad, outer], axis=1)),
        ]
    )
    rows = main.shape[0]
    counts = [nx, nx // 2, nx // 4]
    step = 8
    steps = nz // step

    combos = []
    for level, (_, cl, _, cr, _) in enumerate(sides(ny)):
        both = np.zeros((8, 128))
        assert np.abs(cl[:, : ny - 64]).max() == 0 and np.abs(cr[:, 64:]).max() == 0
        both[: cl.shape[0], 64:] = cl[:, ny - 64 :]
        both[4 : 4 + cr.shape[0], :64] = cr[:, :64]
        combos.append(stack_lhs(both))
    combos = np.stack(combos)

    def kernel(u_ref, r_ref, t_ref, c_ref, x1, x2, x3, right_ref, left_ref, e1, e2, e3):
        i = pl.program_id(0)
        lanes = lax.broadcasted_iota(jnp.int32, (rows, 128), 1)
        for z in range(step):
            start = pl.multiple_of(i * (12 * step) + 24 * (z // 2) + 8 * (z % 2), 8)
            hi, lo = split(u_ref[i * step + z])
            rhi, rlo = split(r_ref[pl.ds(start, 16), :])
            stacked = jnp.concatenate([hi, rhi, hi, rhi, lo, rlo], axis=0)
            got = dot(t_ref[z % 2], stacked)
            edge = jnp.where(lanes < 64, got[:, :128], got[:, ny - 128 :])
            ehi, elo = split(edge)
            estack = jnp.concatenate([ehi, ehi, elo], axis=1)
            at = 0
            for ref, eref, n in zip((x1, x2, x3), (e1, e2, e3), counts):
                where = pl.ds(pl.multiple_of((i * step + z) * n, 16), n)
                ref[i * step + z] = got[at : at + n]
                eref[where, :] = estack[at : at + n]
                at += n

        @pl.when(i == steps - 1)
        def _():
            row = 0
            for level, (eref, n) in enumerate(zip((e1, e2, e3), counts)):
                got = dot_t(c_ref[level], eref[...])
                for j in range(nz * n // 512):
                    for c in range(LEFT_RANKS[level]):
                        right_ref[row : row + 1, :] = got[c : c + 1, 512 * j : 512 * j + 512]
                        if c < RIGHT_RANKS[level]:
                            left_ref[row : row + 1, :] = got[4 + c : 5 + c, 512 * j : 512 * j + 512]
                        else:
                            left_ref[row : row + 1, :] = jnp.zeros((1, 512), F32)
                        row += 1
            right_ref[row:, :] = jnp.zeros((24 - row, 512), F32)
            left_ref[row:, :] = jnp.zeros((24 - row, 512), F32)

    return pl.pallas_call(
        kernel,
        grid=(steps,),
        in_specs=[VM] * 4,
        out_specs=[VM] * 5,
        out_shape=[vmem((nz, n, ny)) for n in counts] + [jax.ShapeDtypeStruct((24, 512), F32)] * 2,
        scratch_shapes=[pltpu.VMEM((nz * n, 384), BF) for n in counts],
        compiler_params=params(24),
        cost_estimate=SHORT,
        name="x_apply",
    )(field, halo, jnp.asarray(tables), jnp.asarray(combos))


def add(a, b):
    if a is None:
        return b
    return a if b is None else a + b


def scale(a, c):
    return None if a is None else a * np.float32(c)


def open_lift(values, first, last):
    get = values.get
    low, high = first // 2 - 3, last // 2 + 4
    s = {i: get(2 * i) for i in range(low, high + 1)}
    d = {i: get(2 * i + 1) for i in range(low, high + 1)}
    pick = lambda t, i: t.get(i)
    d1 = {i: add(d[i], scale(add(s[i], pick(s, i + 1)), lift_alpha)) for i in range(low, high + 1)}
    s1 = {i: add(s[i], scale(add(pick(d1, i - 1), d1[i]), lift_beta)) for i in range(low, high + 1)}
    d2 = {i: add(d1[i], scale(add(s1[i], pick(s1, i + 1)), lift_gamma)) for i in range(low, high + 1)}
    s2 = {i: add(s1[i], scale(add(pick(d2, i - 1), d2[i]), lift_delta)) for i in range(low, high + 1)}
    out = {}
    for z in range(first, last + 1):
        if z % 2:
            out[z] = scale(d2[z // 2], 1.0 / lift_zeta)
        else:
            out[z] = scale(s2[z // 2], lift_zeta)
    return out


def lows(values, first, last):
    got = open_lift(values, 2 * first, 2 * last)
    return {i: got[2 * i] for i in range(first, last + 1) if got[2 * i] is not None}


def own_levels(values, nz, level):
    if level >= 1:
        values = lows(values, -2, nz // 2 + 1)
    if level >= 2:
        values = lows(values, -3, nz // 4 + 2)
    return open_lift(values, 0, (nz >> level) - 1)


def z_tables(nz):
    out = []
    for _, cl, pl_, cr, pr in sides(nz):
        out.append((np.concatenate([cl, cr]), np.concatenate([pl_, pr], axis=1)))
    return out


def weighted(parts):
    total = None
    for scalar, get in parts:
        if abs(scalar) < 1e-12:
            continue
        term = get() * np.float32(scalar)
        total = term if total is None else total + term
    return total


def z_first(x2, x3, halo):
    nz, _, ny = x2.shape
    tables = [t for t, _ in z_tables(nz)]
    counts = [x2.shape[1], x3.shape[1]]
    groups = ny // 128

    def kernel(x2, x3, r_ref, o2, o3, of, y2, y3):
        for level, ref, out, own, table, n in zip((1, 2), (x2, x3), (o2, o3), (y2, y3), tables[1:], counts):

            def body(k, _, level=level, ref=ref, out=out, own=own, table=table, n=n):
                row = pl.multiple_of((k // groups) * 8, 8)
                lane = pl.multiple_of((k % groups) * 128, 128)
                get = {}
                for z in range(nz):
                    get[z] = ref[z, pl.ds(row, 8), pl.ds(lane, 128)]
                for z, value in own_levels(get, nz, level).items():
                    own[z, pl.ds(row, 8), pl.ds(lane, 128)] = value
                for c in range(table.shape[0]):
                    out[pl.ds(pl.multiple_of(c * n + row, 8), 8), pl.ds(lane, 128)] = weighted(
                        [(table[c, z], lambda z=z: get[z]) for z in range(nz)]
                    )
                return 0

            lax.fori_loop(0, (n // 8) * groups, body, 0)
        for c in range(4):
            got = weighted(
                [(tables[0][c, z], lambda z=z: r_ref[12 * z : 12 * z + 12, :]) for z in range(nz)]
            )
            of[4 * c : 4 * c + 2, :] = got[0:2]
            of[4 * c + 2 : 4 * c + 4, :] = got[6:8]

    return pl.pallas_call(
        kernel,
        in_specs=[VM] * 3,
        out_specs=[VM] * 5,
        out_shape=[vmem((t.shape[0] * n, ny)) for t, n in zip(tables[1:], counts)]
        + [vmem((16, ny)), vmem((nz // 2, counts[0], ny)), vmem((nz // 4, counts[1], ny))],
        compiler_params=params(16),
        cost_estimate=SHORT,
        name="z_first",
    )(x2, x3, halo)


def y_tables(ny, spread):
    out = []
    for level, (main, _, left, _, right) in enumerate(sides(ny)):
        step = (1 << level) if spread else 1
        width = ny if spread else ny >> level
        fit = lambda t: spread_columns(t.T, step, width)
        out.append((fit(main), fit(left), fit(right)))
    return out


def halo_rows(level, chunk, nz, counts):
    start = 0
    for below in range(level):
        start += (nz * counts[below] // 512) * LEFT_RANKS[below]
    return start + chunk * LEFT_RANKS[level]


LEFT_AT, RIGHT_AT = 32, 56


def halo_base(left, right, level, nz, counts):
    base = np.zeros((128, left.shape[1]))
    for chunk in range(nz * counts[level] // 512):
        row = halo_rows(level, chunk, nz, counts)
        base[LEFT_AT + row : LEFT_AT + row + left.shape[0]] = left
        base[RIGHT_AT + row : RIGHT_AT + row + right.shape[0]] = right
    return base


def turned(left_ref, right_ref):
    wide = jnp.concatenate(
        [jnp.zeros((LEFT_AT, 512), F32), left_ref[...], right_ref[...], jnp.zeros((48, 512), F32)], axis=0
    )
    return wide.T


def band_tables(level, nz, counts, ny):
    assert ny == 512
    main, left, right = y_tables(ny, True)[level]
    base = halo_base(left, right, level, nz, counts)
    own, edge = [], []
    for j in range(2):
        cols = slice(256 * j, 256 * j + 256)
        own.append(stack_rhs(main[cols, cols]))
        tile = base[:, cols].copy()
        if j == 0:
            tile[:32] = main[256:288, cols]
            assert np.abs(main[288:, cols]).max() == 0
        else:
            tile[96:] = main[224:256, cols]
            assert np.abs(main[:224, cols]).max() == 0
        edge.append(stack_rhs(tile))
    return np.stack(own), np.stack(edge)


def three(values):
    hi, lo = split(values)
    return jnp.concatenate([hi, lo, hi], axis=1)


def banded(rows, edge, own_ref, edge_ref):
    edges = three(edge)
    out = []
    for j in range(2):
        own = three(rows[:, 256 * j : 256 * j + 256])
        out.append(dot(own, own_ref[j]) + dot(edges, edge_ref[j]))
    return jnp.concatenate(out, axis=1)


def plain_edge(rows):
    lanes = lax.broadcasted_iota(jnp.int32, (rows.shape[0], 128), 1)
    before = jnp.where(lanes >= 96, rows[:, 128:256], 0.0)
    return jnp.where(lanes < 32, rows[:, 256:384], before)


def late_rows(side, counts, ny):
    ranks = LEFT_RANKS if side == 0 else RIGHT_RANKS
    parts = [ranks[1] * counts[1] * ny // 256, ranks[2] * counts[2] * ny // 512, ny // 16, 8]
    return [0] + [int(n) for n in np.cumsum(parts)]


def late_heights(counts, ny):
    up, down = [late_rows(side, counts, ny)[-1] for side in (0, 1)]
    return up, max(down, up + 8)


def y_messages(combined, from_left, from_right, nz, band_one):
    c2, c3, cf = combined
    ny = c2.shape[1]
    tables = z_tables(nz)
    nums = [t.shape[0] for t, _ in tables]
    counts = [2 * c2.shape[0] // nums[1], c2.shape[0] // nums[1], c3.shape[0] // nums[2]]
    mains, halos, coefs = [], [], []
    for level, (main, left, right) in enumerate(y_tables(ny, False)):
        mains.append(stack_rhs(main))
        halos.append(stack_rhs(halo_base(left, right, level, nz, counts)))
        chunks = nz * counts[level] // 512
        per = 512 // counts[level]
        table = tables[level][0]
        coef = np.zeros((nums[level], per, 128), np.float32)
        for c in range(nums[level]):
            for zz in range(per):
                for chunk in range(chunks):
                    row = halo_rows(level, chunk, nz, counts)
                    for lane in range(LEFT_RANKS[level]):
                        for base in (LEFT_AT, RIGHT_AT):
                            coef[c, zz, base + row + lane] = table[c, chunk * per + zz]
        coefs.append(coef.reshape(nums[level] * per, 128))
    places = [late_rows(side, counts, ny) for side in (0, 1)]
    heights = late_heights(counts, ny)

    def kernel(c2, c3, cf, fl, fr, own1, edge1, m2, m3, h2, h3, k1, k2, k3, down_ref, up_ref):
        halo = turned(fl, fr)

        def reduced(k, n, num):
            per = 512 // n
            extra = []
            for c in range(num):
                total = None
                for zz in range(per):
                    if np.abs(coefs_of[n][c * per + zz]).max() > 1e-12:
                        term = halo[zz * n : zz * n + n] * k[c * per + zz : c * per + zz + 1, :]
                        total = term if total is None else total + term
                extra.append(total)
            return extra

        coefs_of = dict(zip(counts, coefs))
        got = []
        for c_ref, m, h, k, n, num in zip((c2, c3), (m2, m3), (h2, h3), (k2, k3), counts[1:], nums[1:]):
            extra = jnp.concatenate(reduced(k, n, num), axis=0)
            got.append(dot(three(c_ref[...]), m[...]) + dot(three(extra), h[...]))
        frame = cf[...]
        frame = banded(frame, plain_edge(frame), own1, edge1)
        ones = reduced(k1, counts[0], 4)
        rows8 = lax.broadcasted_iota(jnp.int32, (8, 128), 0)
        for side, ref in enumerate((up_ref, down_ref)):
            at = places[side]
            for level in (1, 2):
                n, lane_groups = counts[level], (ny >> level) // 128
                ranks = LEFT_RANKS if side == 0 else RIGHT_RANKS
                first = 0 if side == 0 else LEFT_RANKS[level] * n
                row = at[level - 1]
                for c in range(ranks[level]):
                    for p in range(lane_groups):
                        ref[row : row + n, :] = got[level - 1][
                            first + c * n : first + c * n + n, 128 * p : 128 * p + 128
                        ]
                        row += n
            for p in range(ny // 128):
                ref[at[2] + 8 * p : at[2] + 8 * p + 8, :] = frame[
                    8 * side : 8 * side + 8, 128 * p : 128 * p + 128
                ]
            turn = jnp.concatenate(ones[2 * side : 2 * side + 2], axis=0).T
            both = []
            for start in (LEFT_AT, RIGHT_AT):
                v = turn[start : start + 8]
                v = v + pltpu.roll(v, 4, 0)
                both.append(v + pltpu.roll(v, 2, 0))
            ref[at[3] : at[4], :] = jnp.where(rows8 < 2, both[0], both[1])
            if heights[side] > at[4]:
                ref[at[4] :, :] = jnp.zeros((heights[side] - at[4], 128), F32)

    return pl.pallas_call(
        kernel,
        in_specs=[VM] * 14,
        out_specs=[VM] * 2,
        out_shape=[vmem((height, 128)) for height in reversed(heights)],
        compiler_params=params(24),
        cost_estimate=SHORT,
        name="y_messages",
    )(
        c2,
        c3,
        cf,
        from_left,
        from_right,
        *band_one,
        *[jnp.asarray(t) for t in mains[1:]],
        *[jnp.asarray(t) for t in halos[1:]],
        *[jnp.asarray(t) for t in coefs],
    )


def touched_layers(nz):
    one, two, three = [np.abs(p).max(axis=1) > 1e-12 for _, p in z_tables(nz)]
    hit = lambda z: one[z] or (z % 2 == 0 and two[z // 2]) or (z % 4 == 0 and three[z // 4])
    return [z for z in range(nz) if hit(z)]


def main_part(xs, from_left, from_right, bands):
    nz, nx, ny = xs[0].shape
    counts = [nx, nx // 2, nx // 4]
    changed = touched_layers(nz)
    untouched = [z for z in range(nz) if z not in changed]
    groups = ny // 128
    masks = []
    for level in range(3):
        chunks = nz * counts[level] // 512
        per = 512 // counts[level]
        lanes_of = np.zeros((chunks, 128))
        for chunk in range(chunks):
            row = halo_rows(level, chunk, nz, counts)
            for base in (LEFT_AT, RIGHT_AT):
                lanes_of[chunk, base + row : base + row + LEFT_RANKS[level]] = 1.0
        if level == 0:
            masks.append(lanes_of)
        else:
            own = sides(nz)[level][0]
            lanes = np.einsum("ocz,cl->ozl", own.reshape(own.shape[0], chunks, per), lanes_of)
            masks.append(lanes.reshape(-1, 128))
    masks = [np.concatenate([m, np.zeros((-m.shape[0] % 8, 128))]).astype(np.float32) for m in masks]

    def kernel(x1, x2, x3, fl, fr, o1, e1, o2, e2, o3, e3, k1, k2, k3, out_ref, done_ref, hbm, w2, halo_ref, sem):
        halo_ref[...] = turned(fl, fr)
        lanes = lax.broadcasted_iota(jnp.int32, (8, 128), 1)
        wide = lax.broadcasted_iota(jnp.int32, (32, 128), 1)
        after, before = wide < 32, wide >= 96

        def in_y(x, level, row, tall, own, edge, mk):
            n = counts[level]
            per = 512 // n
            layers = nz >> level
            values = x[:, row : row + tall, :]
            turns = [halo_ref[zz * n + row : zz * n + row + tall, :] for zz in range(per)]
            edges = []
            for z in range(layers):
                if level == 0:
                    turn = turns[z % per] * mk[z // per : z // per + 1, :]
                else:
                    turn = None
                    for zz in range(per):
                        if np.abs(masks[level][z * per + zz]).max() > 1e-12:
                            turn = add(turn, turns[zz] * mk[z * per + zz : z * per + zz + 1, :])
                edges.append(
                    jnp.where(
                        after[:tall],
                        values[z, :, 256:384],
                        jnp.where(before[:tall], values[z, :, 128:256], turn),
                    )
                )
            got = banded(
                values.reshape(layers * tall, ny), jnp.concatenate(edges, axis=0), own, edge
            )
            return {z: got[tall * z : tall * z + tall] for z in range(layers)}

        def store(to, values, row, indices, height=None):
            for z in indices:
                for q in range(groups):
                    piece = values[z][:, 128 * q : 128 * q + 128]
                    tall = piece.shape[0]
                    if height is None:
                        to[q, z, row : row + tall, :] = piece
                    else:
                        to[q, z * height + row : z * height + row + tall, :] = piece

        for row in range(0, counts[0], 16):
            got = own_levels(in_y(x1, 0, row, 16, o1, e1, k1), nz, 0)
            store(out_ref, got, row, range(nz))

        def leaving(layers):
            return [
                pltpu.make_async_copy(
                    out_ref.at[q, z], hbm.at[z, :, 128 * q : 128 * q + 128], sem.at[z]
                )
                for z in layers
                for q in range(groups)
            ]

        copies = leaving([z for z in untouched if z % 2])
        for copy in copies:
            copy.start()

        store(w2, in_y(x2, 1, 0, counts[1], o2, e2, k2), 0, range(nz // 2), counts[1])
        got = in_y(x3, 2, 0, counts[2], o3, e3, k3)
        for z in range(nz // 4):
            for row in range(0, counts[2], 8):
                where = pl.ds(2 * z * counts[1] + 2 * row, 8, stride=2)
                for q in range(groups):
                    piece = got[z][row : row + 8, 128 * q : 128 * q + 128]
                    w2[q, where, :] = jnp.where(lanes % 4 == 0, piece, w2[q, where, :])

        def merge(k, _):
            row = pl.multiple_of((k // groups) * 8, 8)
            q = k % groups
            where = pl.ds(2 * row, 8, stride=2)
            for z in range(nz // 2):
                inner = w2[q, pl.ds(pl.multiple_of(z * counts[1] + row, 8), 8), :]
                out_ref[q, 2 * z, where, :] = jnp.where(lanes % 2 == 0, inner, out_ref[q, 2 * z, where, :])
            return 0

        lax.fori_loop(0, (counts[1] // 8) * groups, merge, 0)
        more = leaving([z for z in untouched if z % 2 == 0])
        for copy in more:
            copy.start()

        done_ref[...] = jnp.zeros((8, 128), F32)
        for copy in copies + more:
            copy.wait()

    flat = [t for band in bands for t in band]
    return pl.pallas_call(
        kernel,
        in_specs=[VM] * 14,
        out_specs=[VM, VM, HB],
        out_shape=[
            vmem((groups, nz, nx, 128)),
            vmem((8, 128)),
            pltpu.HBM((nz, nx, ny), F32),
        ],
        scratch_shapes=[
            pltpu.VMEM((groups, nz // 2 * counts[1], 128), F32),
            pltpu.VMEM((512, 128), F32),
            pltpu.SemaphoreType.DMA((nz,)),
        ],
        compiler_params=params(32),
        cost_estimate=SHORT,
        name="main_part",
    )(*xs, from_left, from_right, *flat, *[jnp.asarray(m) for m in masks])


def early_part(below, above, band, after):
    nx, ny = below.shape[0] // 2, below.shape[1]
    _, _, maps = joint_sides(nx)

    def kernel(b1, a1, o1, e1, xt, after_ref, w_ref):
        del after_ref
        early = []
        for ref in (b1, a1):
            for c in range(2):
                hi, lo = split(ref[c * nx : c * nx + nx, :])
                early.append(dot(xt[...], jnp.concatenate([hi, hi, lo], axis=0)))
        early = jnp.concatenate(early, axis=0)
        w_ref[...] = banded(early, plain_edge(early), o1, e1)

    return pl.pallas_call(
        kernel,
        in_specs=[VM] * 6,
        out_specs=VM,
        out_shape=vmem((4 * nx, ny)),
        compiler_params=params(16),
        cost_estimate=SHORT,
        name="early_part",
    )(below, above, *band, jnp.asarray(stack_lhs(maps[0][0])), after)


def z_apply(inner, partial, early, from_left, from_right):
    groups, nz, nx, _ = inner.shape
    ny = groups * 128
    maps = [p for _, p in z_tables(nz)]
    counts = [nx, nx // 2, nx // 4]
    tables = []
    for level in (1, 2):
        width = ny >> level
        hi = spread_columns(np.eye(width), 1 << level, ny).astype(ml_dtypes.bfloat16)
        tables.append(np.concatenate([hi, hi]))
    places = [late_rows(side, counts, ny) for side in (0, 1)]
    _, _, x_maps = joint_sides(nx)
    frame = np.zeros((4 * nx, 16))
    for c in range(4):
        frame[c * nx : c * nx + nx, 4 * c : 4 * c + 2] = x_maps[0][1][:, :2]
        frame[c * nx : c * nx + nx, 4 * c + 2 : 4 * c + 4] = x_maps[0][2][:, :2]
        assert np.abs(x_maps[0][1][:, 2:]).max() < 1e-12 and np.abs(x_maps[0][2][:, 2:]).max() < 1e-12
    _, left, right = y_tables(ny, True)[0]
    side_hi, side_lo = hi_lo(np.concatenate([left, right, np.zeros((4, ny))]))
    side_rows = np.concatenate([side_hi, side_hi, side_lo, np.zeros((104, ny), side_hi.dtype)])
    touched = sorted(touched_layers(nz), key=lambda z: np.abs(maps[0][z]).max() > 1e-12)

    def kernel(in_ref, base_hbm, w_ref, fl, fr, t2, t3, xf, yf, out_hbm, s1, s2, s3, buf, sem):
        del base_hbm
        s3[...] = jnp.zeros(s3.shape, F32)
        halos = [
            jnp.concatenate([ref[at[2] + 8 * p : at[2] + 8 * p + 8, :] for p in range(groups)], axis=1)
            for ref, at in zip((fl, fr), places)
        ]
        hi, lo = split(jnp.concatenate(halos, axis=0))
        none = jnp.zeros((104, 128), F32)
        turn = []
        for ref, at in zip((fl, fr), places):
            values = ref[at[3] : at[4], :]
            high = values.astype(BF).astype(F32)
            turn.append(jnp.concatenate([high, values - high, high, none], axis=0).T.astype(BF))
        left_hand = jnp.concatenate([jnp.concatenate(turn, axis=0), xf[...]], axis=1)
        first = w_ref[...] + dot(left_hand, jnp.concatenate([yf[...], hi, hi, lo], axis=0))
        for c in range(4):
            for q in range(groups):
                s1[c, q] = first[c * nx : c * nx + nx, 128 * q : 128 * q + 128]
        for level, table, to in ((1, t2, s2), (2, t3, s3)):
            n, lane_groups = counts[level], (ny >> level) // 128
            pieces = []
            for side, ref in enumerate((fl, fr)):
                row = places[side][level - 1]
                for c in range((LEFT_RANKS, RIGHT_RANKS)[side][level]):
                    pieces.append(
                        jnp.concatenate(
                            [ref[row + p * n : row + p * n + n, :] for p in range(lane_groups)], axis=1
                        )
                    )
                    row += lane_groups * n
            flat = jnp.concatenate(pieces, axis=0)
            hi, lo = split(flat)
            got = dot(jnp.concatenate([hi, lo], axis=1), table[...])
            for c in range(LEFT_RANKS[level] + RIGHT_RANKS[level]):
                start = c * n
                for q in range(groups):
                    piece = got[start : start + n, 128 * q : 128 * q + 128]
                    if level == 1:
                        to[c, q] = piece
                    else:
                        to[c, q, pl.ds(0, n, stride=2), :] = piece

        lanes = lax.broadcasted_iota(jnp.int32, (8, 128), 1)
        even_lane = lanes % 2 == 0
        third_cell = (lax.broadcasted_iota(jnp.int32, (8, 128), 0) % 2 + lanes % 4) == 0

        def summed(table_row, get):
            total = None
            for c, scalar in enumerate(table_row):
                if abs(scalar) > 1e-12:
                    total = add(total, get(c) * np.float32(scalar))
            return total

        copies = []
        for slot, z in enumerate(touched):

            for t in range(nx // 16):
                full, half = 16 * t, 8 * t
                for q in range(groups):
                    if z % 2:
                        for more in (0, 8):
                            rows = pl.ds(full + more, 8)
                            extra = summed(maps[0][z], lambda c: s1[c, q, rows, :])
                            buf[slot, q, rows, :] = add(in_ref[q, z, rows, :], extra)
                        continue
                    evens = pl.ds(16 * t, 8, stride=2)
                    odds = pl.ds(16 * t + 1, 8, stride=2)
                    extra = summed(maps[0][z], lambda c: s1[c, q, odds, :])
                    buf[slot, q, odds, :] = add(in_ref[q, z, odds, :], extra)
                    rows = pl.ds(half, 8)
                    extra = summed(maps[1][z // 2], lambda c: s2[c, q, rows, :])
                    if z % 4 == 0:
                        third = summed(maps[2][z // 4], lambda c: s3[c, q, rows, :])
                        third = 0.0 if third is None else third
                        extra = jnp.where(third_cell, third, 0.0 if extra is None else extra)
                    one = summed(maps[0][z], lambda c: s1[c, q, evens, :])
                    if one is not None:
                        extra = jnp.where(even_lane, 0.0 if extra is None else extra, one)
                    buf[slot, q, evens, :] = add(in_ref[q, z, evens, :], extra)
            for q in range(groups):
                copy = pltpu.make_async_copy(
                    buf.at[slot, q], out_hbm.at[z, :, 128 * q : 128 * q + 128], sem.at[slot]
                )
                copy.start()
                copies.append(copy)
        for copy in copies:
            copy.wait()

    return pl.pallas_call(
        kernel,
        in_specs=[VM, HB] + [VM] * 7,
        out_specs=HB,
        out_shape=jax.ShapeDtypeStruct((nz, nx, ny), F32),
        input_output_aliases={1: 0},
        scratch_shapes=[
            pltpu.VMEM((4, groups, nx, 128), F32),
            pltpu.VMEM((maps[1].shape[1], groups, nx // 2, 128), F32),
            pltpu.VMEM((maps[2].shape[1], groups, nx // 2, 128), F32),
            pltpu.VMEM((len(touched), groups, nx, 128), F32),
            pltpu.SemaphoreType.DMA((len(touched),)),
        ],
        compiler_params=params(24),
        name="z_apply",
    )(
        inner,
        partial,
        early,
        from_left,
        from_right,
        *[jnp.asarray(t) for t in tables],
        jnp.asarray(stack_lhs(frame)),
        jnp.asarray(side_rows),
    )


def swap(to_right, to_left, axis):
    count = lax.axis_size(axis)
    right = [(i, (i + 1) % count) for i in range(count)]
    left = [(j, i) for i, j in right]
    return lax.ppermute(to_right, axis, right), lax.ppermute(to_left, axis, left)


def local(field):
    nz, nx, ny = field.shape
    counts = [nx, nx // 2, nx // 4]
    bands = [[jnp.asarray(t) for t in band_tables(level, nz, counts, ny)] for level in range(3)]
    field, message, up, down = x_send(field)
    halo = x_exchange(message)
    below, above = swap(up, down, "gz")
    x1, x2, x3, to_right, to_left = x_apply(field, halo)
    from_left, from_right = swap(to_right, to_left, "gy")
    *combined, own2, own3 = z_first(x2, x3, halo)
    down, up = y_messages(combined, from_left, from_right, nz, bands[0])
    late_below, late_above = swap(up, down, "gz")
    inner, done, partial = main_part((x1, own2, own3), from_left, from_right, bands)
    early = early_part(below, above, bands[0], done)
    return z_apply(inner, partial, early, late_below, late_above)


def solution(mesh):
    placed = (P("gz", "gx", "gy"),)
    return jax.shard_map(
        local, mesh=mesh, in_specs=placed, out_specs=P("gz", "gx", "gy"), check_vma=False
    )
```

```python
import functools

import jax
import jax.numpy as jnp
import ml_dtypes
import numpy as np
from jax import lax
from jax.experimental import pallas as pl
from jax.experimental.pallas import tpu as pltpu
from jax.sharding import PartitionSpec as P

lift_alpha = -1.586134342
lift_beta = -0.05298011854
lift_gamma = 0.8829110762
lift_delta = 0.4435068522
lift_zeta = 1.149604398

BF = jnp.bfloat16
F32 = jnp.float32
MIB = 1024 * 1024


def periodic_lift(u):
    s, d = u[0::2].copy(), u[1::2].copy()
    d = d + lift_alpha * (s + np.roll(s, -1, 0))
    s = s + lift_beta * (np.roll(d, 1, 0) + d)
    d = d + lift_gamma * (s + np.roll(s, -1, 0))
    s = s + lift_delta * (np.roll(d, 1, 0) + d)
    out = np.empty_like(u)
    out[0::2] = s * lift_zeta
    out[1::2] = d / lift_zeta
    return out


@functools.lru_cache(None)
def blocks(n):
    current = np.eye(4 * n)
    found = []
    for level in range(3):
        full = periodic_lift(current)
        m = n >> level
        rows = full[m : 2 * m]
        found.append((rows[:, n : 2 * n], rows[:, :n], rows[:, 2 * n : 3 * n]))
        current = full[0::2]
    return found


def row_space(outer, rank):
    _, sizes, basis = np.linalg.svd(outer, full_matrices=False)
    assert sizes[rank:].max() < 1e-10
    basis = basis[:rank].copy()
    basis[np.abs(basis) < 1e-12] = 0.0
    return basis


LEFT_RANKS = (2, 3, 4)
RIGHT_RANKS = (2, 3, 3)


@functools.lru_cache(None)
def sides(n):
    out = []
    for level, (main, left, right) in enumerate(blocks(n)):
        cl = row_space(left, LEFT_RANKS[level])
        cr = row_space(right, RIGHT_RANKS[level])
        out.append((main, cl, left @ cl.T, cr, right @ cr.T))
    return out


def nested_space(outer):
    first = row_space(outer[0], 2)
    every = np.concatenate(outer)
    rest = every - every @ first.T @ first
    return np.concatenate([first, row_space(rest, 4)])


@functools.lru_cache(None)
def joint_sides(n):
    found = blocks(n)
    cl = nested_space([b[1] for b in found])
    cr = nested_space([b[2] for b in found])
    maps = [(b[0], b[1] @ cl.T, b[2] @ cr.T) for b in found]
    return cl, cr, maps


def hi_lo(table):
    table = np.asarray(table, np.float32)
    hi = table.astype(ml_dtypes.bfloat16)
    lo = (table - hi.astype(np.float32)).astype(ml_dtypes.bfloat16)
    return hi, lo


def stack_lhs(table):
    hi, lo = hi_lo(table)
    return np.concatenate([hi, lo, hi], axis=1)


def stack_rhs(table):
    hi, lo = hi_lo(table)
    return np.concatenate([hi, hi, lo], axis=0)


def split(values):
    hi = values.astype(BF)
    return hi, (values - hi.astype(F32)).astype(BF)


def dot(a, b):
    return lax.dot_general(a, b, (((1,), (0,)), ((), ())), preferred_element_type=F32)


def dot_t(a, b):
    return lax.dot_general(a, b, (((1,), (1,)), ((), ())), preferred_element_type=F32)


def spread_columns(table, step, width):
    out = np.zeros((table.shape[0], width))
    out[:, ::step] = table
    return out


VM = pl.BlockSpec(memory_space=pltpu.VMEM)
HB = pl.BlockSpec(memory_space=pltpu.HBM)
SHORT = pl.CostEstimate(flops=1000, bytes_accessed=1000, transcendentals=0)


def in_hbm(array):
    return pltpu.with_memory_space_constraint(array, pltpu.HBM)


def vmem(shape, dtype=F32):
    return pltpu.VMEM(shape, dtype)


def params(mib):
    return pltpu.CompilerParams(vmem_limit_bytes=mib * MIB)


def x_send(field):
    nz, nx, ny = field.shape
    cl, cr, _ = joint_sides(nx)
    one = np.concatenate([cl, cr])
    group = 4
    wide = np.kron(np.eye(group), one)
    hi_rows, lo_rows = hi_lo(wide)
    pair = np.concatenate([hi_rows, lo_rows])
    height = 12 * group
    step = 8
    steps = nz // step
    order = [0, steps - 1] + list(range(1, steps - 1))
    _, low, _, high, _ = sides(nz)[0]
    assert np.abs(low[:, :-step]).max() == 0 and np.abs(high[:, step:]).max() == 0

    def kernel(u_hbm, c_hbm, u_ref, out_ref, up_ref, down_ref, c_ref, u_sem, c_sem):
        table_copy = pltpu.make_async_copy(c_hbm, c_ref, c_sem)
        copies = [
            pltpu.make_async_copy(
                u_hbm.at[i * step : i * step + step], u_ref.at[i * step : i * step + step], u_sem.at[i]
            )
            for i in range(steps)
        ]
        table_copy.start()
        for i in order:
            copies[i].start()
        table_copy.wait()
        table = c_ref[...]
        for i in order:
            copies[i].wait()
            for g in range(i * step // group, (i + 1) * step // group):
                hi, lo = split(u_ref[group * g : group * g + group].reshape(group * nx, ny))
                both = dot(table, hi)
                out_ref[height * g : height * g + height, :] = (
                    both[:height] + both[height:] + dot(table[:height], lo)
                )
            if i in order[:2]:
                combos, ref = (high, down_ref) if i == 0 else (low, up_ref)
                for c in range(2):
                    ref[c * nx : c * nx + nx, :] = weighted(
                        [(combos[c, z], lambda z=z: u_ref[z]) for z in range(i * step, (i + 1) * step)]
                    )

    return pl.pallas_call(
        kernel,
        in_specs=[HB, HB],
        out_specs=[VM] * 4,
        out_shape=[vmem((nz, nx, ny)), vmem((nz * 12, ny)), vmem((2 * nx, ny)), vmem((2 * nx, ny))],
        scratch_shapes=[
            pltpu.VMEM(pair.shape, BF),
            pltpu.SemaphoreType.DMA((steps,)),
            pltpu.SemaphoreType.DMA,
        ],
        compiler_params=params(16),
        cost_estimate=SHORT,
        name="x_send",
    )(in_hbm(field), in_hbm(jnp.asarray(pair)))


def x_exchange(message):
    count = lax.axis_size("gx")
    right = [(i, (i + 1) % count) for i in range(count)]
    if count == 2:
        return lax.ppermute(message, "gx", right)
    left = [(j, i) for i, j in right]
    rows, ny = message.shape
    grid = message.reshape(rows // 12, 12, ny)
    from_left = lax.ppermute(grid[:, :6], "gx", right)
    from_right = lax.ppermute(grid[:, 6:], "gx", left)
    return jnp.concatenate([from_left, from_right], axis=1).reshape(rows, ny)


def x_apply(field, halo):
    nz, nx, ny = field.shape
    _, _, maps = joint_sides(nx)
    main = np.concatenate([m for m, _, _ in maps])
    outer = np.concatenate([np.concatenate([l, r], axis=1) for _, l, r in maps])
    pad = np.zeros((main.shape[0], 4))
    tables = np.stack(
        [
            stack_lhs(np.concatenate([main, outer, pad], axis=1)),
            stack_lhs(np.concatenate([main, pad, outer], axis=1)),
        ]
    )
    rows = main.shape[0]
    counts = [nx, nx // 2, nx // 4]
    step = 8
    steps = nz // step

    combos = []
    for level, (_, cl, _, cr, _) in enumerate(sides(ny)):
        both = np.zeros((8, 128))
        assert np.abs(cl[:, : ny - 64]).max() == 0 and np.abs(cr[:, 64:]).max() == 0
        both[: cl.shape[0], 64:] = cl[:, ny - 64 :]
        both[4 : 4 + cr.shape[0], :64] = cr[:, :64]
        combos.append(stack_lhs(both))
    combos = np.stack(combos)

    def kernel(u_ref, r_ref, t_ref, c_ref, x1, x2, x3, right_ref, left_ref, e1, e2, e3):
        i = pl.program_id(0)
        lanes = lax.broadcasted_iota(jnp.int32, (rows, 128), 1)
        for z in range(step):
            start = pl.multiple_of(i * (12 * step) + 24 * (z // 2) + 8 * (z % 2), 8)
            hi, lo = split(u_ref[i * step + z])
            rhi, rlo = split(r_ref[pl.ds(start, 16), :])
            stacked = jnp.concatenate([hi, rhi, hi, rhi, lo, rlo], axis=0)
            got = dot(t_ref[z % 2], stacked)
            edge = jnp.where(lanes < 64, got[:, :128], got[:, ny - 128 :])
            ehi, elo = split(edge)
            estack = jnp.concatenate([ehi, ehi, elo], axis=1)
            at = 0
            for ref, eref, n in zip((x1, x2, x3), (e1, e2, e3), counts):
                where = pl.ds(pl.multiple_of((i * step + z) * n, 16), n)
                ref[i * step + z] = got[at : at + n]
                eref[where, :] = estack[at : at + n]
                at += n

        @pl.when(i == steps - 1)
        def _():
            row = 0
            for level, (eref, n) in enumerate(zip((e1, e2, e3), counts)):
                got = dot_t(c_ref[level], eref[...])
                for j in range(nz * n // 512):
                    for c in range(LEFT_RANKS[level]):
                        right_ref[row : row + 1, :] = got[c : c + 1, 512 * j : 512 * j + 512]
                        if c < RIGHT_RANKS[level]:
                            left_ref[row : row + 1, :] = got[4 + c : 5 + c, 512 * j : 512 * j + 512]
                        else:
                            left_ref[row : row + 1, :] = jnp.zeros((1, 512), F32)
                        row += 1
            right_ref[row:, :] = jnp.zeros((24 - row, 512), F32)
            left_ref[row:, :] = jnp.zeros((24 - row, 512), F32)

    return pl.pallas_call(
        kernel,
        grid=(steps,),
        in_specs=[VM] * 4,
        out_specs=[VM] * 5,
        out_shape=[vmem((nz, n, ny)) for n in counts] + [jax.ShapeDtypeStruct((24, 512), F32)] * 2,
        scratch_shapes=[pltpu.VMEM((nz * n, 384), BF) for n in counts],
        compiler_params=params(24),
        cost_estimate=SHORT,
        name="x_apply",
    )(field, halo, jnp.asarray(tables), jnp.asarray(combos))


def add(a, b):
    if a is None:
        return b
    return a if b is None else a + b


def scale(a, c):
    return None if a is None else a * np.float32(c)


def open_lift(values, first, last):
    get = values.get
    low, high = first // 2 - 3, last // 2 + 4
    s = {i: get(2 * i) for i in range(low, high + 1)}
    d = {i: get(2 * i + 1) for i in range(low, high + 1)}
    pick = lambda t, i: t.get(i)
    d1 = {i: add(d[i], scale(add(s[i], pick(s, i + 1)), lift_alpha)) for i in range(low, high + 1)}
    s1 = {i: add(s[i], scale(add(pick(d1, i - 1), d1[i]), lift_beta)) for i in range(low, high + 1)}
    d2 = {i: add(d1[i], scale(add(s1[i], pick(s1, i + 1)), lift_gamma)) for i in range(low, high + 1)}
    s2 = {i: add(s1[i], scale(add(pick(d2, i - 1), d2[i]), lift_delta)) for i in range(low, high + 1)}
    out = {}
    for z in range(first, last + 1):
        if z % 2:
            out[z] = scale(d2[z // 2], 1.0 / lift_zeta)
        else:
            out[z] = scale(s2[z // 2], lift_zeta)
    return out


def lows(values, first, last):
    got = open_lift(values, 2 * first, 2 * last)
    return {i: got[2 * i] for i in range(first, last + 1) if got[2 * i] is not None}


def own_levels(values, nz, level):
    if level >= 1:
        values = lows(values, -2, nz // 2 + 1)
    if level >= 2:
        values = lows(values, -3, nz // 4 + 2)
    return open_lift(values, 0, (nz >> level) - 1)


def z_tables(nz):
    out = []
    for _, cl, pl_, cr, pr in sides(nz):
        out.append((np.concatenate([cl, cr]), np.concatenate([pl_, pr], axis=1)))
    return out


def weighted(parts):
    total = None
    for scalar, get in parts:
        if abs(scalar) < 1e-12:
            continue
        term = get() * np.float32(scalar)
        total = term if total is None else total + term
    return total


def z_first(x2, x3, halo):
    nz, _, ny = x2.shape
    tables = [t for t, _ in z_tables(nz)]
    counts = [x2.shape[1], x3.shape[1]]
    groups = ny // 128

    def kernel(x2, x3, r_ref, o2, o3, of, y2, y3):
        for level, ref, out, own, table, n in zip((1, 2), (x2, x3), (o2, o3), (y2, y3), tables[1:], counts):

            def body(k, _, level=level, ref=ref, out=out, own=own, table=table, n=n):
                row = pl.multiple_of((k // groups) * 8, 8)
                lane = pl.multiple_of((k % groups) * 128, 128)
                get = {}
                for z in range(nz):
                    get[z] = ref[z, pl.ds(row, 8), pl.ds(lane, 128)]
                for z, value in own_levels(get, nz, level).items():
                    own[z, pl.ds(row, 8), pl.ds(lane, 128)] = value
                for c in range(table.shape[0]):
                    out[pl.ds(pl.multiple_of(c * n + row, 8), 8), pl.ds(lane, 128)] = weighted(
                        [(table[c, z], lambda z=z: get[z]) for z in range(nz)]
                    )
                return 0

            lax.fori_loop(0, (n // 8) * groups, body, 0)
        for c in range(4):
            got = weighted(
                [(tables[0][c, z], lambda z=z: r_ref[12 * z : 12 * z + 12, :]) for z in range(nz)]
            )
            of[4 * c : 4 * c + 2, :] = got[0:2]
            of[4 * c + 2 : 4 * c + 4, :] = got[6:8]

    return pl.pallas_call(
        kernel,
        in_specs=[VM] * 3,
        out_specs=[VM] * 5,
        out_shape=[vmem((t.shape[0] * n, ny)) for t, n in zip(tables[1:], counts)]
        + [vmem((16, ny)), vmem((nz // 2, counts[0], ny)), vmem((nz // 4, counts[1], ny))],
        compiler_params=params(16),
        cost_estimate=SHORT,
        name="z_first",
    )(x2, x3, halo)


def y_tables(ny, spread):
    out = []
    for level, (main, _, left, _, right) in enumerate(sides(ny)):
        step = (1 << level) if spread else 1
        width = ny if spread else ny >> level
        fit = lambda t: spread_columns(t.T, step, width)
        out.append((fit(main), fit(left), fit(right)))
    return out


def halo_rows(level, chunk, nz, counts):
    start = 0
    for below in range(level):
        start += (nz * counts[below] // 512) * LEFT_RANKS[below]
    return start + chunk * LEFT_RANKS[level]


LEFT_AT, RIGHT_AT = 32, 56


def halo_base(left, right, level, nz, counts):
    base = np.zeros((128, left.shape[1]))
    for chunk in range(nz * counts[level] // 512):
        row = halo_rows(level, chunk, nz, counts)
        base[LEFT_AT + row : LEFT_AT + row + left.shape[0]] = left
        base[RIGHT_AT + row : RIGHT_AT + row + right.shape[0]] = right
    return base


def turned(left_ref, right_ref):
    wide = jnp.concatenate(
        [jnp.zeros((LEFT_AT, 512), F32), left_ref[...], right_ref[...], jnp.zeros((48, 512), F32)], axis=0
    )
    return wide.T


def band_tables(level, nz, counts, ny):
    assert ny == 512
    main, left, right = y_tables(ny, True)[level]
    base = halo_base(left, right, level, nz, counts)
    own, edge = [], []
    for j in range(2):
        cols = slice(256 * j, 256 * j + 256)
        own.append(stack_rhs(main[cols, cols]))
        tile = base[:, cols].copy()
        if j == 0:
            tile[:32] = main[256:288, cols]
            assert np.abs(main[288:, cols]).max() == 0
        else:
            tile[96:] = main[224:256, cols]
            assert np.abs(main[:224, cols]).max() == 0
        edge.append(stack_rhs(tile))
    return np.stack(own), np.stack(edge)


def three(values):
    hi, lo = split(values)
    return jnp.concatenate([hi, lo, hi], axis=1)


def banded(rows, edge, own_ref, edge_ref):
    edges = three(edge)
    out = []
    for j in range(2):
        own = three(rows[:, 256 * j : 256 * j + 256])
        out.append(dot(own, own_ref[j]) + dot(edges, edge_ref[j]))
    return jnp.concatenate(out, axis=1)


def plain_edge(rows):
    lanes = lax.broadcasted_iota(jnp.int32, (rows.shape[0], 128), 1)
    before = jnp.where(lanes >= 96, rows[:, 128:256], 0.0)
    return jnp.where(lanes < 32, rows[:, 256:384], before)


def late_rows(side, counts, ny):
    ranks = LEFT_RANKS if side == 0 else RIGHT_RANKS
    parts = [ranks[1] * counts[1] * ny // 256, ranks[2] * counts[2] * ny // 512, ny // 16, 8]
    return [0] + [int(n) for n in np.cumsum(parts)]


def late_heights(counts, ny):
    return (max(late_rows(side, counts, ny)[-1] for side in (0, 1)),) * 2


def y_messages(combined, from_left, from_right, nz, band_one):
    c2, c3, cf = combined
    ny = c2.shape[1]
    tables = z_tables(nz)
    nums = [t.shape[0] for t, _ in tables]
    counts = [2 * c2.shape[0] // nums[1], c2.shape[0] // nums[1], c3.shape[0] // nums[2]]
    mains, halos, coefs = [], [], []
    for level, (main, left, right) in enumerate(y_tables(ny, False)):
        mains.append(stack_rhs(main))
        halos.append(stack_rhs(halo_base(left, right, level, nz, counts)))
        chunks = nz * counts[level] // 512
        per = 512 // counts[level]
        table = tables[level][0]
        coef = np.zeros((nums[level], per, 128), np.float32)
        for c in range(nums[level]):
            for zz in range(per):
                for chunk in range(chunks):
                    row = halo_rows(level, chunk, nz, counts)
                    for lane in range(LEFT_RANKS[level]):
                        for base in (LEFT_AT, RIGHT_AT):
                            coef[c, zz, base + row + lane] = table[c, chunk * per + zz]
        coefs.append(coef.reshape(nums[level] * per, 128))
    places = [late_rows(side, counts, ny) for side in (0, 1)]
    heights = late_heights(counts, ny)

    def kernel(c2, c3, cf, fl, fr, own1, edge1, m2, m3, h2, h3, k1, k2, k3, down_ref, up_ref):
        halo = turned(fl, fr)

        def reduced(k, n, num):
            per = 512 // n
            extra = []
            for c in range(num):
                total = None
                for zz in range(per):
                    if np.abs(coefs_of[n][c * per + zz]).max() > 1e-12:
                        term = halo[zz * n : zz * n + n] * k[c * per + zz : c * per + zz + 1, :]
                        total = term if total is None else total + term
                extra.append(total)
            return extra

        coefs_of = dict(zip(counts, coefs))
        got = []
        for c_ref, m, h, k, n, num in zip((c2, c3), (m2, m3), (h2, h3), (k2, k3), counts[1:], nums[1:]):
            extra = jnp.concatenate(reduced(k, n, num), axis=0)
            got.append(dot(three(c_ref[...]), m[...]) + dot(three(extra), h[...]))
        frame = cf[...]
        frame = banded(frame, plain_edge(frame), own1, edge1)
        ones = reduced(k1, counts[0], 4)
        rows8 = lax.broadcasted_iota(jnp.int32, (8, 128), 0)
        for side, ref in enumerate((up_ref, down_ref)):
            at = places[side]
            for level in (1, 2):
                n, lane_groups = counts[level], (ny >> level) // 128
                ranks = LEFT_RANKS if side == 0 else RIGHT_RANKS
                first = 0 if side == 0 else LEFT_RANKS[level] * n
                row = at[level - 1]
                for c in range(ranks[level]):
                    for p in range(lane_groups):
                        ref[row : row + n, :] = got[level - 1][
                            first + c * n : first + c * n + n, 128 * p : 128 * p + 128
                        ]
                        row += n
            for p in range(ny // 128):
                ref[at[2] + 8 * p : at[2] + 8 * p + 8, :] = frame[
                    8 * side : 8 * side + 8, 128 * p : 128 * p + 128
                ]
            turn = jnp.concatenate(ones[2 * side : 2 * side + 2], axis=0).T
            both = []
            for start in (LEFT_AT, RIGHT_AT):
                v = turn[start : start + 8]
                v = v + pltpu.roll(v, 4, 0)
                both.append(v + pltpu.roll(v, 2, 0))
            ref[at[3] : at[4], :] = jnp.where(rows8 < 2, both[0], both[1])
            if heights[side] > at[4]:
                ref[at[4] :, :] = jnp.zeros((heights[side] - at[4], 128), F32)

    return pl.pallas_call(
        kernel,
        in_specs=[VM] * 14,
        out_specs=[VM] * 2,
        out_shape=[vmem((height, 128)) for height in reversed(heights)],
        compiler_params=params(24),
        cost_estimate=SHORT,
        name="y_messages",
    )(
        c2,
        c3,
        cf,
        from_left,
        from_right,
        *band_one,
        *[jnp.asarray(t) for t in mains[1:]],
        *[jnp.asarray(t) for t in halos[1:]],
        *[jnp.asarray(t) for t in coefs],
    )


def touched_layers(nz):
    one, two, three = [np.abs(p).max(axis=1) > 1e-12 for _, p in z_tables(nz)]
    hit = lambda z: one[z] or (z % 2 == 0 and two[z // 2]) or (z % 4 == 0 and three[z // 4])
    return [z for z in range(nz) if hit(z)]


def main_part(xs, from_left, from_right, bands):
    nz, nx, ny = xs[0].shape
    counts = [nx, nx // 2, nx // 4]
    changed = touched_layers(nz)
    untouched = [z for z in range(nz) if z not in changed]
    groups = ny // 128
    masks = []
    for level in range(3):
        chunks = nz * counts[level] // 512
        per = 512 // counts[level]
        lanes_of = np.zeros((chunks, 128))
        for chunk in range(chunks):
            row = halo_rows(level, chunk, nz, counts)
            for base in (LEFT_AT, RIGHT_AT):
                lanes_of[chunk, base + row : base + row + LEFT_RANKS[level]] = 1.0
        if level == 0:
            masks.append(lanes_of)
        else:
            own = sides(nz)[level][0]
            lanes = np.einsum("ocz,cl->ozl", own.reshape(own.shape[0], chunks, per), lanes_of)
            masks.append(lanes.reshape(-1, 128))
    masks = [np.concatenate([m, np.zeros((-m.shape[0] % 8, 128))]).astype(np.float32) for m in masks]

    def kernel(x1, x2, x3, fl, fr, o1, e1, o2, e2, o3, e3, k1, k2, k3, out_ref, done_ref, hbm, w2, halo_ref, sem):
        halo_ref[...] = turned(fl, fr)
        lanes = lax.broadcasted_iota(jnp.int32, (8, 128), 1)
        wide = lax.broadcasted_iota(jnp.int32, (32, 128), 1)
        after, before = wide < 32, wide >= 96

        def in_y(x, level, row, tall, own, edge, mk):
            n = counts[level]
            per = 512 // n
            layers = nz >> level
            values = x[:, row : row + tall, :]
            turns = [halo_ref[zz * n + row : zz * n + row + tall, :] for zz in range(per)]
            edges = []
            for z in range(layers):
                if level == 0:
                    turn = turns[z % per] * mk[z // per : z // per + 1, :]
                else:
                    turn = None
                    for zz in range(per):
                        if np.abs(masks[level][z * per + zz]).max() > 1e-12:
                            turn = add(turn, turns[zz] * mk[z * per + zz : z * per + zz + 1, :])
                edges.append(
                    jnp.where(
                        after[:tall],
                        values[z, :, 256:384],
                        jnp.where(before[:tall], values[z, :, 128:256], turn),
                    )
                )
            got = banded(
                values.reshape(layers * tall, ny), jnp.concatenate(edges, axis=0), own, edge
            )
            return {z: got[tall * z : tall * z + tall] for z in range(layers)}

        def store(to, values, row, indices, height=None):
            for z in indices:
                for q in range(groups):
                    piece = values[z][:, 128 * q : 128 * q + 128]
                    tall = piece.shape[0]
                    if height is None:
                        to[q, z, row : row + tall, :] = piece
                    else:
                        to[q, z * height + row : z * height + row + tall, :] = piece

        for row in range(0, counts[0], 16):
            got = own_levels(in_y(x1, 0, row, 16, o1, e1, k1), nz, 0)
            store(out_ref, got, row, range(nz))

        def leaving(layers):
            return [
                pltpu.make_async_copy(
                    out_ref.at[q, z], hbm.at[z, :, 128 * q : 128 * q + 128], sem.at[z]
                )
                for z in layers
                for q in range(groups)
            ]

        copies = leaving([z for z in untouched if z % 2])
        for copy in copies:
            copy.start()

        store(w2, in_y(x2, 1, 0, counts[1], o2, e2, k2), 0, range(nz // 2), counts[1])
        got = in_y(x3, 2, 0, counts[2], o3, e3, k3)
        for z in range(nz // 4):
            for row in range(0, counts[2], 8):
                where = pl.ds(2 * z * counts[1] + 2 * row, 8, stride=2)
                for q in range(groups):
                    piece = got[z][row : row + 8, 128 * q : 128 * q + 128]
                    w2[q, where, :] = jnp.where(lanes % 4 == 0, piece, w2[q, where, :])

        def merge(k, _):
            row = pl.multiple_of((k // groups) * 8, 8)
            q = k % groups
            where = pl.ds(2 * row, 8, stride=2)
            for z in range(nz // 2):
                inner = w2[q, pl.ds(pl.multiple_of(z * counts[1] + row, 8), 8), :]
                out_ref[q, 2 * z, where, :] = jnp.where(lanes % 2 == 0, inner, out_ref[q, 2 * z, where, :])
            return 0

        lax.fori_loop(0, (counts[1] // 8) * groups, merge, 0)
        more = leaving([z for z in untouched if z % 2 == 0])
        for copy in more:
            copy.start()

        done_ref[...] = jnp.zeros((8, 128), F32)
        for copy in copies + more:
            copy.wait()

    flat = [t for band in bands for t in band]
    return pl.pallas_call(
        kernel,
        in_specs=[VM] * 14,
        out_specs=[VM, VM, HB],
        out_shape=[
            vmem((groups, nz, nx, 128)),
            vmem((8, 128)),
            pltpu.HBM((nz, nx, ny), F32),
        ],
        scratch_shapes=[
            pltpu.VMEM((groups, nz // 2 * counts[1], 128), F32),
            pltpu.VMEM((512, 128), F32),
            pltpu.SemaphoreType.DMA((nz,)),
        ],
        compiler_params=params(32),
        cost_estimate=SHORT,
        name="main_part",
    )(*xs, from_left, from_right, *flat, *[jnp.asarray(m) for m in masks])


def early_part(below, above, band, after):
    nx, ny = below.shape[0] // 2, below.shape[1]
    _, _, maps = joint_sides(nx)

    def kernel(a1, b1, o1, e1, xt, after_ref, w_ref):
        del after_ref
        early = []
        for ref in (b1, a1):
            for c in range(2):
                hi, lo = split(ref[c * nx : c * nx + nx, :])
                early.append(dot(xt[...], jnp.concatenate([hi, hi, lo], axis=0)))
        early = jnp.concatenate(early, axis=0)
        w_ref[...] = banded(early, plain_edge(early), o1, e1)

    return pl.pallas_call(
        kernel,
        in_specs=[VM] * 6,
        out_specs=VM,
        out_shape=vmem((4 * nx, ny)),
        compiler_params=params(16),
        cost_estimate=SHORT,
        name="early_part",
    )(above, below, *band, jnp.asarray(stack_lhs(maps[0][0])), after)


def z_apply(inner, partial, early, from_left, from_right):
    groups, nz, nx, _ = inner.shape
    ny = groups * 128
    maps = [p for _, p in z_tables(nz)]
    counts = [nx, nx // 2, nx // 4]
    tables = []
    for level in (1, 2):
        width = ny >> level
        hi = spread_columns(np.eye(width), 1 << level, ny).astype(ml_dtypes.bfloat16)
        tables.append(np.concatenate([hi, hi]))
    places = [late_rows(side, counts, ny) for side in (0, 1)]
    _, _, x_maps = joint_sides(nx)
    frame = np.zeros((4 * nx, 16))
    for c in range(4):
        frame[c * nx : c * nx + nx, 4 * c : 4 * c + 2] = x_maps[0][1][:, :2]
        frame[c * nx : c * nx + nx, 4 * c + 2 : 4 * c + 4] = x_maps[0][2][:, :2]
        assert np.abs(x_maps[0][1][:, 2:]).max() < 1e-12 and np.abs(x_maps[0][2][:, 2:]).max() < 1e-12
    _, left, right = y_tables(ny, True)[0]
    side_hi, side_lo = hi_lo(np.concatenate([left, right, np.zeros((4, ny))]))
    side_rows = np.concatenate([side_hi, side_hi, side_lo, np.zeros((104, ny), side_hi.dtype)])
    touched = sorted(touched_layers(nz), key=lambda z: np.abs(maps[0][z]).max() > 1e-12)

    def kernel(in_ref, base_hbm, w_ref, fr, fl, t2, t3, xf, yf, out_hbm, s1, s2, s3, buf, sem):
        del base_hbm
        s3[...] = jnp.zeros(s3.shape, F32)
        halos = [
            jnp.concatenate([ref[at[2] + 8 * p : at[2] + 8 * p + 8, :] for p in range(groups)], axis=1)
            for ref, at in zip((fl, fr), places)
        ]
        hi, lo = split(jnp.concatenate(halos, axis=0))
        none = jnp.zeros((104, 128), F32)
        turn = []
        for ref, at in zip((fl, fr), places):
            values = ref[at[3] : at[4], :]
            high = values.astype(BF).astype(F32)
            turn.append(jnp.concatenate([high, values - high, high, none], axis=0).T.astype(BF))
        left_hand = jnp.concatenate([jnp.concatenate(turn, axis=0), xf[...]], axis=1)
        first = w_ref[...] + dot(left_hand, jnp.concatenate([yf[...], hi, hi, lo], axis=0))
        for c in range(4):
            for q in range(groups):
                s1[c, q] = first[c * nx : c * nx + nx, 128 * q : 128 * q + 128]
        for level, table, to in ((1, t2, s2), (2, t3, s3)):
            n, lane_groups = counts[level], (ny >> level) // 128
            pieces = []
            for side, ref in enumerate((fl, fr)):
                row = places[side][level - 1]
                for c in range((LEFT_RANKS, RIGHT_RANKS)[side][level]):
                    pieces.append(
                        jnp.concatenate(
                            [ref[row + p * n : row + p * n + n, :] for p in range(lane_groups)], axis=1
                        )
                    )
                    row += lane_groups * n
            flat = jnp.concatenate(pieces, axis=0)
            hi, lo = split(flat)
            got = dot(jnp.concatenate([hi, lo], axis=1), table[...])
            for c in range(LEFT_RANKS[level] + RIGHT_RANKS[level]):
                start = c * n
                for q in range(groups):
                    piece = got[start : start + n, 128 * q : 128 * q + 128]
                    if level == 1:
                        to[c, q] = piece
                    else:
                        to[c, q, pl.ds(0, n, stride=2), :] = piece

        lanes = lax.broadcasted_iota(jnp.int32, (8, 128), 1)
        even_lane = lanes % 2 == 0
        third_cell = (lax.broadcasted_iota(jnp.int32, (8, 128), 0) % 2 + lanes % 4) == 0

        def summed(table_row, get):
            total = None
            for c, scalar in enumerate(table_row):
                if abs(scalar) > 1e-12:
                    total = add(total, get(c) * np.float32(scalar))
            return total

        copies = []
        for slot, z in enumerate(touched):

            for t in range(nx // 16):
                full, half = 16 * t, 8 * t
                for q in range(groups):
                    if z % 2:
                        for more in (0, 8):
                            rows = pl.ds(full + more, 8)
                            extra = summed(maps[0][z], lambda c: s1[c, q, rows, :])
                            buf[slot, q, rows, :] = add(in_ref[q, z, rows, :], extra)
                        continue
                    evens = pl.ds(16 * t, 8, stride=2)
                    odds = pl.ds(16 * t + 1, 8, stride=2)
                    extra = summed(maps[0][z], lambda c: s1[c, q, odds, :])
                    buf[slot, q, odds, :] = add(in_ref[q, z, odds, :], extra)
                    rows = pl.ds(half, 8)
                    extra = summed(maps[1][z // 2], lambda c: s2[c, q, rows, :])
                    if z % 4 == 0:
                        third = summed(maps[2][z // 4], lambda c: s3[c, q, rows, :])
                        third = 0.0 if third is None else third
                        extra = jnp.where(third_cell, third, 0.0 if extra is None else extra)
                    one = summed(maps[0][z], lambda c: s1[c, q, evens, :])
                    if one is not None:
                        extra = jnp.where(even_lane, 0.0 if extra is None else extra, one)
                    buf[slot, q, evens, :] = add(in_ref[q, z, evens, :], extra)
            for q in range(groups):
                copy = pltpu.make_async_copy(
                    buf.at[slot, q], out_hbm.at[z, :, 128 * q : 128 * q + 128], sem.at[slot]
                )
                copy.start()
                copies.append(copy)
        for copy in copies:
            copy.wait()

    return pl.pallas_call(
        kernel,
        in_specs=[VM, HB] + [VM] * 7,
        out_specs=HB,
        out_shape=jax.ShapeDtypeStruct((nz, nx, ny), F32),
        input_output_aliases={1: 0},
        scratch_shapes=[
            pltpu.VMEM((4, groups, nx, 128), F32),
            pltpu.VMEM((maps[1].shape[1], groups, nx // 2, 128), F32),
            pltpu.VMEM((maps[2].shape[1], groups, nx // 2, 128), F32),
            pltpu.VMEM((len(touched), groups, nx, 128), F32),
            pltpu.SemaphoreType.DMA((len(touched),)),
        ],
        compiler_params=params(24),
        name="z_apply",
    )(
        inner,
        partial,
        early,
        from_right,
        from_left,
        *[jnp.asarray(t) for t in tables],
        jnp.asarray(stack_lhs(frame)),
        jnp.asarray(side_rows),
    )


def swap(to_right, to_left, axis):
    count = lax.axis_size(axis)
    right = [(i, (i + 1) % count) for i in range(count)]
    left = [(j, i) for i, j in right]
    return lax.ppermute(to_right, axis, right), lax.ppermute(to_left, axis, left)


def local(field):
    nz, nx, ny = field.shape
    counts = [nx, nx // 2, nx // 4]
    bands = [[jnp.asarray(t) for t in band_tables(level, nz, counts, ny)] for level in range(3)]
    field, message, up, down = x_send(field)
    halo = x_exchange(message)
    below, above = swap(up, down, "gz")
    x1, x2, x3, to_right, to_left = x_apply(field, halo)
    from_left, from_right = swap(to_right, to_left, "gy")
    *combined, own2, own3 = z_first(x2, x3, halo)
    down, up = y_messages(combined, from_left, from_right, nz, bands[0])
    late_below, late_above = swap(up, down, "gz")
    inner, done, partial = main_part((x1, own2, own3), from_left, from_right, bands)
    early = early_part(below, above, bands[0], done)
    return z_apply(inner, partial, early, late_below, late_above)


def solution(mesh):
    placed = (P("gz", "gx", "gy"),)
    return jax.shard_map(
        local, mesh=mesh, in_specs=placed, out_specs=P("gz", "gx", "gy"), check_vma=False
    )
```

```python
import functools

import jax
import jax.numpy as jnp
import ml_dtypes
import numpy as np
from jax import lax
from jax.experimental import pallas as pl
from jax.experimental.pallas import tpu as pltpu
from jax.sharding import PartitionSpec as P

lift_alpha = -1.586134342
lift_beta = -0.05298011854
lift_gamma = 0.8829110762
lift_delta = 0.4435068522
lift_zeta = 1.149604398

BF = jnp.bfloat16
F32 = jnp.float32
MIB = 1024 * 1024


def periodic_lift(u):
    s, d = u[0::2].copy(), u[1::2].copy()
    d = d + lift_alpha * (s + np.roll(s, -1, 0))
    s = s + lift_beta * (np.roll(d, 1, 0) + d)
    d = d + lift_gamma * (s + np.roll(s, -1, 0))
    s = s + lift_delta * (np.roll(d, 1, 0) + d)
    out = np.empty_like(u)
    out[0::2] = s * lift_zeta
    out[1::2] = d / lift_zeta
    return out


@functools.lru_cache(None)
def blocks(n):
    current = np.eye(4 * n)
    found = []
    for level in range(3):
        full = periodic_lift(current)
        m = n >> level
        rows = full[m : 2 * m]
        found.append((rows[:, n : 2 * n], rows[:, :n], rows[:, 2 * n : 3 * n]))
        current = full[0::2]
    return found


def row_space(outer, rank):
    _, sizes, basis = np.linalg.svd(outer, full_matrices=False)
    assert sizes[rank:].max() < 1e-10
    basis = basis[:rank].copy()
    basis[np.abs(basis) < 1e-12] = 0.0
    return basis


LEFT_RANKS = (2, 3, 4)
RIGHT_RANKS = (2, 3, 3)


@functools.lru_cache(None)
def sides(n):
    out = []
    for level, (main, left, right) in enumerate(blocks(n)):
        cl = row_space(left, LEFT_RANKS[level])
        cr = row_space(right, RIGHT_RANKS[level])
        out.append((main, cl, left @ cl.T, cr, right @ cr.T))
    return out


def nested_space(outer):
    first = row_space(outer[0], 2)
    every = np.concatenate(outer)
    rest = every - every @ first.T @ first
    return np.concatenate([first, row_space(rest, 4)])


@functools.lru_cache(None)
def joint_sides(n):
    found = blocks(n)
    cl = nested_space([b[1] for b in found])
    cr = nested_space([b[2] for b in found])
    maps = [(b[0], b[1] @ cl.T, b[2] @ cr.T) for b in found]
    return cl, cr, maps


def hi_lo(table):
    table = np.asarray(table, np.float32)
    hi = table.astype(ml_dtypes.bfloat16)
    lo = (table - hi.astype(np.float32)).astype(ml_dtypes.bfloat16)
    return hi, lo


def stack_lhs(table):
    hi, lo = hi_lo(table)
    return np.concatenate([hi, lo, hi], axis=1)


def stack_rhs(table):
    hi, lo = hi_lo(table)
    return np.concatenate([hi, hi, lo], axis=0)


def split(values):
    hi = values.astype(BF)
    return hi, (values - hi.astype(F32)).astype(BF)


def dot(a, b):
    return lax.dot_general(a, b, (((1,), (0,)), ((), ())), preferred_element_type=F32)


def dot_t(a, b):
    return lax.dot_general(a, b, (((1,), (1,)), ((), ())), preferred_element_type=F32)


def spread_columns(table, step, width):
    out = np.zeros((table.shape[0], width))
    out[:, ::step] = table
    return out


VM = pl.BlockSpec(memory_space=pltpu.VMEM)
HB = pl.BlockSpec(memory_space=pltpu.HBM)
SHORT = pl.CostEstimate(flops=1000, bytes_accessed=1000, transcendentals=0)


def in_hbm(array):
    return pltpu.with_memory_space_constraint(array, pltpu.HBM)


def vmem(shape, dtype=F32):
    return pltpu.VMEM(shape, dtype)


def params(mib):
    return pltpu.CompilerParams(vmem_limit_bytes=mib * MIB)


def x_send(field):
    nz, nx, ny = field.shape
    cl, cr, _ = joint_sides(nx)
    one = np.concatenate([cl, cr])
    group = 4
    wide = np.kron(np.eye(group), one)
    hi_rows, lo_rows = hi_lo(wide)
    pair = np.concatenate([hi_rows, lo_rows])
    height = 12 * group
    step = 8
    steps = nz // step
    order = [0, steps - 1] + list(range(1, steps - 1))
    _, low, _, high, _ = sides(nz)[0]
    assert np.abs(low[:, :-step]).max() == 0 and np.abs(high[:, step:]).max() == 0

    def kernel(u_hbm, c_hbm, u_ref, out_ref, up_ref, down_ref, c_ref, u_sem, c_sem):
        table_copy = pltpu.make_async_copy(c_hbm, c_ref, c_sem)
        copies = [
            pltpu.make_async_copy(
                u_hbm.at[i * step : i * step + step], u_ref.at[i * step : i * step + step], u_sem.at[i]
            )
            for i in range(steps)
        ]
        table_copy.start()
        for i in order:
            copies[i].start()
        table_copy.wait()
        table = c_ref[...]
        for i in order:
            copies[i].wait()
            for g in range(i * step // group, (i + 1) * step // group):
                hi, lo = split(u_ref[group * g : group * g + group].reshape(group * nx, ny))
                both = dot(table, hi)
                out_ref[height * g : height * g + height, :] = (
                    both[:height] + both[height:] + dot(table[:height], lo)
                )
            if i in order[:2]:
                combos, ref = (high, down_ref) if i == 0 else (low, up_ref)
                for c in range(2):
                    ref[c * nx : c * nx + nx, :] = weighted(
                        [(combos[c, z], lambda z=z: u_ref[z]) for z in range(i * step, (i + 1) * step)]
                    )

    return pl.pallas_call(
        kernel,
        in_specs=[HB, HB],
        out_specs=[VM] * 4,
        out_shape=[vmem((nz, nx, ny)), vmem((nz * 12, ny)), vmem((2 * nx, ny)), vmem((2 * nx, ny))],
        scratch_shapes=[
            pltpu.VMEM(pair.shape, BF),
            pltpu.SemaphoreType.DMA((steps,)),
            pltpu.SemaphoreType.DMA,
        ],
        compiler_params=params(16),
        cost_estimate=SHORT,
        name="x_send",
    )(in_hbm(field), in_hbm(jnp.asarray(pair)))


def x_exchange(message):
    count = lax.axis_size("gx")
    right = [(i, (i + 1) % count) for i in range(count)]
    if count == 2:
        return lax.ppermute(message, "gx", right)
    left = [(j, i) for i, j in right]
    rows, ny = message.shape
    grid = message.reshape(rows // 12, 12, ny)
    from_left = lax.ppermute(grid[:, :6], "gx", right)
    from_right = lax.ppermute(grid[:, 6:], "gx", left)
    return jnp.concatenate([from_left, from_right], axis=1).reshape(rows, ny)


def x_apply(field, halo):
    nz, nx, ny = field.shape
    _, _, maps = joint_sides(nx)
    main = np.concatenate([m for m, _, _ in maps])
    outer = np.concatenate([np.concatenate([l, r], axis=1) for _, l, r in maps])
    pad = np.zeros((main.shape[0], 4))
    tables = np.stack(
        [
            stack_lhs(np.concatenate([main, outer, pad], axis=1)),
            stack_lhs(np.concatenate([main, pad, outer], axis=1)),
        ]
    )
    rows = main.shape[0]
    counts = [nx, nx // 2, nx // 4]
    step = 8
    steps = nz // step

    combos = []
    for level, (_, cl, _, cr, _) in enumerate(sides(ny)):
        both = np.zeros((8, 128))
        assert np.abs(cl[:, : ny - 64]).max() == 0 and np.abs(cr[:, 64:]).max() == 0
        both[: cl.shape[0], 64:] = cl[:, ny - 64 :]
        both[4 : 4 + cr.shape[0], :64] = cr[:, :64]
        combos.append(stack_lhs(both))
    combos = np.stack(combos)

    def kernel(u_ref, r_ref, t_ref, c_ref, x1, x2, x3, right_ref, left_ref, e1, e2, e3):
        i = pl.program_id(0)
        lanes = lax.broadcasted_iota(jnp.int32, (rows, 128), 1)
        for z in range(step):
            start = pl.multiple_of(i * (12 * step) + 24 * (z // 2) + 8 * (z % 2), 8)
            hi, lo = split(u_ref[i * step + z])
            rhi, rlo = split(r_ref[pl.ds(start, 16), :])
            stacked = jnp.concatenate([hi, rhi, hi, rhi, lo, rlo], axis=0)
            got = dot(t_ref[z % 2], stacked)
            edge = jnp.where(lanes < 64, got[:, :128], got[:, ny - 128 :])
            ehi, elo = split(edge)
            estack = jnp.concatenate([ehi, ehi, elo], axis=1)
            at = 0
            for ref, eref, n in zip((x1, x2, x3), (e1, e2, e3), counts):
                where = pl.ds(pl.multiple_of((i * step + z) * n, 16), n)
                ref[i * step + z] = got[at : at + n]
                eref[where, :] = estack[at : at + n]
                at += n

        @pl.when(i == steps - 1)
        def _():
            row = 0
            for level, (eref, n) in enumerate(zip((e1, e2, e3), counts)):
                got = dot_t(c_ref[level], eref[...])
                for j in range(nz * n // 512):
                    for c in range(LEFT_RANKS[level]):
                        right_ref[row : row + 1, :] = got[c : c + 1, 512 * j : 512 * j + 512]
                        if c < RIGHT_RANKS[level]:
                            left_ref[row : row + 1, :] = got[4 + c : 5 + c, 512 * j : 512 * j + 512]
                        else:
                            left_ref[row : row + 1, :] = jnp.zeros((1, 512), F32)
                        row += 1
            right_ref[row:, :] = jnp.zeros((24 - row, 512), F32)
            left_ref[row:, :] = jnp.zeros((24 - row, 512), F32)

    return pl.pallas_call(
        kernel,
        grid=(steps,),
        in_specs=[VM] * 4,
        out_specs=[VM] * 5,
        out_shape=[vmem((nz, n, ny)) for n in counts] + [jax.ShapeDtypeStruct((24, 512), F32)] * 2,
        scratch_shapes=[pltpu.VMEM((nz * n, 384), BF) for n in counts],
        compiler_params=params(24),
        cost_estimate=SHORT,
        name="x_apply",
    )(field, halo, jnp.asarray(tables), jnp.asarray(combos))


def add(a, b):
    if a is None:
        return b
    return a if b is None else a + b


def scale(a, c):
    return None if a is None else a * np.float32(c)


def open_lift(values, first, last):
    get = values.get
    low, high = first // 2 - 3, last // 2 + 4
    s = {i: get(2 * i) for i in range(low, high + 1)}
    d = {i: get(2 * i + 1) for i in range(low, high + 1)}
    pick = lambda t, i: t.get(i)
    d1 = {i: add(d[i], scale(add(s[i], pick(s, i + 1)), lift_alpha)) for i in range(low, high + 1)}
    s1 = {i: add(s[i], scale(add(pick(d1, i - 1), d1[i]), lift_beta)) for i in range(low, high + 1)}
    d2 = {i: add(d1[i], scale(add(s1[i], pick(s1, i + 1)), lift_gamma)) for i in range(low, high + 1)}
    s2 = {i: add(s1[i], scale(add(pick(d2, i - 1), d2[i]), lift_delta)) for i in range(low, high + 1)}
    out = {}
    for z in range(first, last + 1):
        if z % 2:
            out[z] = scale(d2[z // 2], 1.0 / lift_zeta)
        else:
            out[z] = scale(s2[z // 2], lift_zeta)
    return out


def lows(values, first, last):
    got = open_lift(values, 2 * first, 2 * last)
    return {i: got[2 * i] for i in range(first, last + 1) if got[2 * i] is not None}


def own_levels(values, nz, level):
    if level >= 1:
        values = lows(values, -2, nz // 2 + 1)
    if level >= 2:
        values = lows(values, -3, nz // 4 + 2)
    return open_lift(values, 0, (nz >> level) - 1)


def z_tables(nz):
    out = []
    for _, cl, pl_, cr, pr in sides(nz):
        out.append((np.concatenate([cl, cr]), np.concatenate([pl_, pr], axis=1)))
    return out


def weighted(parts):
    total = None
    for scalar, get in parts:
        if abs(scalar) < 1e-12:
            continue
        term = get() * np.float32(scalar)
        total = term if total is None else total + term
    return total


def z_first(x2, x3, halo):
    nz, _, ny = x2.shape
    tables = [t for t, _ in z_tables(nz)]
    counts = [x2.shape[1], x3.shape[1]]
    groups = ny // 128

    def kernel(x2, x3, r_ref, o2, o3, of, y2, y3):
        for level, ref, out, own, table, n in zip((1, 2), (x2, x3), (o2, o3), (y2, y3), tables[1:], counts):

            def body(k, _, level=level, ref=ref, out=out, own=own, table=table, n=n):
                row = pl.multiple_of((k // groups) * 8, 8)
                lane = pl.multiple_of((k % groups) * 128, 128)
                get = {}
                for z in range(nz):
                    get[z] = ref[z, pl.ds(row, 8), pl.ds(lane, 128)]
                for z, value in own_levels(get, nz, level).items():
                    own[z, pl.ds(row, 8), pl.ds(lane, 128)] = value
                for c in range(table.shape[0]):
                    out[pl.ds(pl.multiple_of(c * n + row, 8), 8), pl.ds(lane, 128)] = weighted(
                        [(table[c, z], lambda z=z: get[z]) for z in range(nz)]
                    )
                return 0

            lax.fori_loop(0, (n // 8) * groups, body, 0)
        for c in range(4):
            got = weighted(
                [(tables[0][c, z], lambda z=z: r_ref[12 * z : 12 * z + 12, :]) for z in range(nz)]
            )
            of[4 * c : 4 * c + 2, :] = got[0:2]
            of[4 * c + 2 : 4 * c + 4, :] = got[6:8]

    return pl.pallas_call(
        kernel,
        in_specs=[VM] * 3,
        out_specs=[VM] * 5,
        out_shape=[vmem((t.shape[0] * n, ny)) for t, n in zip(tables[1:], counts)]
        + [vmem((16, ny)), vmem((nz // 2, counts[0], ny)), vmem((nz // 4, counts[1], ny))],
        compiler_params=params(16),
        cost_estimate=SHORT,
        name="z_first",
    )(x2, x3, halo)


def y_tables(ny, spread):
    out = []
    for level, (main, _, left, _, right) in enumerate(sides(ny)):
        step = (1 << level) if spread else 1
        width = ny if spread else ny >> level
        fit = lambda t: spread_columns(t.T, step, width)
        out.append((fit(main), fit(left), fit(right)))
    return out


def halo_rows(level, chunk, nz, counts):
    start = 0
    for below in range(level):
        start += (nz * counts[below] // 512) * LEFT_RANKS[below]
    return start + chunk * LEFT_RANKS[level]


LEFT_AT, RIGHT_AT = 32, 56


def halo_base(left, right, level, nz, counts):
    base = np.zeros((128, left.shape[1]))
    for chunk in range(nz * counts[level] // 512):
        row = halo_rows(level, chunk, nz, counts)
        base[LEFT_AT + row : LEFT_AT + row + left.shape[0]] = left
        base[RIGHT_AT + row : RIGHT_AT + row + right.shape[0]] = right
    return base


def turned(left_ref, right_ref):
    wide = jnp.concatenate(
        [jnp.zeros((LEFT_AT, 512), F32), left_ref[...], right_ref[...], jnp.zeros((48, 512), F32)], axis=0
    )
    return wide.T


def band_tables(level, nz, counts, ny):
    assert ny == 512
    main, left, right = y_tables(ny, True)[level]
    base = halo_base(left, right, level, nz, counts)
    own, edge = [], []
    for j in range(2):
        cols = slice(256 * j, 256 * j + 256)
        own.append(stack_rhs(main[cols, cols]))
        tile = base[:, cols].copy()
        if j == 0:
            tile[:32] = main[256:288, cols]
            assert np.abs(main[288:, cols]).max() == 0
        else:
            tile[96:] = main[224:256, cols]
            assert np.abs(main[:224, cols]).max() == 0
        edge.append(stack_rhs(tile))
    return np.stack(own), np.stack(edge)


def three(values):
    hi, lo = split(values)
    return jnp.concatenate([hi, lo, hi], axis=1)


def banded(rows, edge, own_ref, edge_ref):
    edges = three(edge)
    out = []
    for j in range(2):
        own = three(rows[:, 256 * j : 256 * j + 256])
        out.append(dot(own, own_ref[j]) + dot(edges, edge_ref[j]))
    return jnp.concatenate(out, axis=1)


def plain_edge(rows):
    lanes = lax.broadcasted_iota(jnp.int32, (rows.shape[0], 128), 1)
    before = jnp.where(lanes >= 96, rows[:, 128:256], 0.0)
    return jnp.where(lanes < 32, rows[:, 256:384], before)


def late_rows(side, counts, ny):
    ranks = LEFT_RANKS if side == 0 else RIGHT_RANKS
    parts = [ranks[1] * counts[1] * ny // 256, ranks[2] * counts[2] * ny // 512, ny // 16, 8]
    return [0] + [int(n) for n in np.cumsum(parts)]


def late_heights(counts, ny):
    return (max(late_rows(side, counts, ny)[-1] for side in (0, 1)),) * 2


def y_messages(combined, from_left, from_right, nz, band_one):
    c2, c3, cf = combined
    ny = c2.shape[1]
    tables = z_tables(nz)
    nums = [t.shape[0] for t, _ in tables]
    counts = [2 * c2.shape[0] // nums[1], c2.shape[0] // nums[1], c3.shape[0] // nums[2]]
    mains, halos, coefs = [], [], []
    for level, (main, left, right) in enumerate(y_tables(ny, False)):
        mains.append(stack_rhs(main))
        halos.append(stack_rhs(halo_base(left, right, level, nz, counts)))
        chunks = nz * counts[level] // 512
        per = 512 // counts[level]
        table = tables[level][0]
        coef = np.zeros((nums[level], per, 128), np.float32)
        for c in range(nums[level]):
            for zz in range(per):
                for chunk in range(chunks):
                    row = halo_rows(level, chunk, nz, counts)
                    for lane in range(LEFT_RANKS[level]):
                        for base in (LEFT_AT, RIGHT_AT):
                            coef[c, zz, base + row + lane] = table[c, chunk * per + zz]
        coefs.append(coef.reshape(nums[level] * per, 128))
    places = [late_rows(side, counts, ny) for side in (0, 1)]
    heights = late_heights(counts, ny)

    def kernel(c2, c3, cf, fl, fr, own1, edge1, m2, m3, h2, h3, k1, k2, k3, down_ref, up_ref):
        halo = turned(fl, fr)

        def reduced(k, n, num):
            per = 512 // n
            extra = []
            for c in range(num):
                total = None
                for zz in range(per):
                    if np.abs(coefs_of[n][c * per + zz]).max() > 1e-12:
                        term = halo[zz * n : zz * n + n] * k[c * per + zz : c * per + zz + 1, :]
                        total = term if total is None else total + term
                extra.append(total)
            return extra

        coefs_of = dict(zip(counts, coefs))
        got = []
        for c_ref, m, h, k, n, num in zip((c2, c3), (m2, m3), (h2, h3), (k2, k3), counts[1:], nums[1:]):
            extra = jnp.concatenate(reduced(k, n, num), axis=0)
            got.append(dot(three(c_ref[...]), m[...]) + dot(three(extra), h[...]))
        frame = cf[...]
        frame = banded(frame, plain_edge(frame), own1, edge1)
        ones = reduced(k1, counts[0], 4)
        rows8 = lax.broadcasted_iota(jnp.int32, (8, 128), 0)
        for side, ref in enumerate((up_ref, down_ref)):
            at = places[side]
            for level in (1, 2):
                n, lane_groups = counts[level], (ny >> level) // 128
                ranks = LEFT_RANKS if side == 0 else RIGHT_RANKS
                first = 0 if side == 0 else LEFT_RANKS[level] * n
                row = at[level - 1]
                for c in range(ranks[level]):
                    for p in range(lane_groups):
                        ref[row : row + n, :] = got[level - 1][
                            first + c * n : first + c * n + n, 128 * p : 128 * p + 128
                        ]
                        row += n
            for p in range(ny // 128):
                ref[at[2] + 8 * p : at[2] + 8 * p + 8, :] = frame[
                    8 * side : 8 * side + 8, 128 * p : 128 * p + 128
                ]
            turn = jnp.concatenate(ones[2 * side : 2 * side + 2], axis=0).T
            both = []
            for start in (LEFT_AT, RIGHT_AT):
                v = turn[start : start + 8]
                v = v + pltpu.roll(v, 4, 0)
                both.append(v + pltpu.roll(v, 2, 0))
            ref[at[3] : at[4], :] = jnp.where(rows8 < 2, both[0], both[1])
            if heights[side] > at[4]:
                ref[at[4] :, :] = jnp.zeros((heights[side] - at[4], 128), F32)

    return pl.pallas_call(
        kernel,
        in_specs=[VM] * 14,
        out_specs=[VM] * 2,
        out_shape=[vmem((height, 128)) for height in reversed(heights)],
        compiler_params=params(24),
        cost_estimate=SHORT,
        name="y_messages",
    )(
        c2,
        c3,
        cf,
        from_left,
        from_right,
        *band_one,
        *[jnp.asarray(t) for t in mains[1:]],
        *[jnp.asarray(t) for t in halos[1:]],
        *[jnp.asarray(t) for t in coefs],
    )


def touched_layers(nz):
    one, two, three = [np.abs(p).max(axis=1) > 1e-12 for _, p in z_tables(nz)]
    hit = lambda z: one[z] or (z % 2 == 0 and two[z // 2]) or (z % 4 == 0 and three[z // 4])
    return [z for z in range(nz) if hit(z)]


def main_part(xs, from_left, from_right, bands):
    nz, nx, ny = xs[0].shape
    counts = [nx, nx // 2, nx // 4]
    changed = touched_layers(nz)
    untouched = [z for z in range(nz) if z not in changed]
    groups = ny // 128
    masks = []
    for level in range(3):
        chunks = nz * counts[level] // 512
        per = 512 // counts[level]
        lanes_of = np.zeros((chunks, 128))
        for chunk in range(chunks):
            row = halo_rows(level, chunk, nz, counts)
            for base in (LEFT_AT, RIGHT_AT):
                lanes_of[chunk, base + row : base + row + LEFT_RANKS[level]] = 1.0
        if level == 0:
            masks.append(lanes_of)
        else:
            own = sides(nz)[level][0]
            lanes = np.einsum("ocz,cl->ozl", own.reshape(own.shape[0], chunks, per), lanes_of)
            masks.append(lanes.reshape(-1, 128))
    masks = [np.concatenate([m, np.zeros((-m.shape[0] % 8, 128))]).astype(np.float32) for m in masks]

    def kernel(x1, x2, x3, fl, fr, o1, e1, o2, e2, o3, e3, k1, k2, k3, out_ref, done_ref, hbm, w2, halo_ref, sem):
        halo_ref[...] = turned(fl, fr)
        lanes = lax.broadcasted_iota(jnp.int32, (8, 128), 1)
        wide = lax.broadcasted_iota(jnp.int32, (32, 128), 1)
        after, before = wide < 32, wide >= 96

        def in_y(x, level, row, tall, own, edge, mk):
            n = counts[level]
            per = 512 // n
            layers = nz >> level
            values = x[:, row : row + tall, :]
            turns = [halo_ref[zz * n + row : zz * n + row + tall, :] for zz in range(per)]
            edges = []
            for z in range(layers):
                if level == 0:
                    turn = turns[z % per] * mk[z // per : z // per + 1, :]
                else:
                    turn = None
                    for zz in range(per):
                        if np.abs(masks[level][z * per + zz]).max() > 1e-12:
                            turn = add(turn, turns[zz] * mk[z * per + zz : z * per + zz + 1, :])
                edges.append(
                    jnp.where(
                        after[:tall],
                        values[z, :, 256:384],
                        jnp.where(before[:tall], values[z, :, 128:256], turn),
                    )
                )
            got = banded(
                values.reshape(layers * tall, ny), jnp.concatenate(edges, axis=0), own, edge
            )
            return {z: got[tall * z : tall * z + tall] for z in range(layers)}

        def store(to, values, row, indices, height=None):
            for z in indices:
                for q in range(groups):
                    piece = values[z][:, 128 * q : 128 * q + 128]
                    tall = piece.shape[0]
                    if height is None:
                        to[q, z, row : row + tall, :] = piece
                    else:
                        to[q, z * height + row : z * height + row + tall, :] = piece

        for row in range(0, counts[0], 16):
            got = own_levels(in_y(x1, 0, row, 16, o1, e1, k1), nz, 0)
            store(out_ref, got, row, range(nz))

        def leaving(layers):
            return [
                pltpu.make_async_copy(
                    out_ref.at[q, z], hbm.at[z, :, 128 * q : 128 * q + 128], sem.at[z]
                )
                for z in layers
                for q in range(groups)
            ]

        copies = leaving([z for z in untouched if z % 2])
        for copy in copies:
            copy.start()

        store(w2, in_y(x2, 1, 0, counts[1], o2, e2, k2), 0, range(nz // 2), counts[1])
        got = in_y(x3, 2, 0, counts[2], o3, e3, k3)
        for z in range(nz // 4):
            for row in range(0, counts[2], 8):
                where = pl.ds(2 * z * counts[1] + 2 * row, 8, stride=2)
                for q in range(groups):
                    piece = got[z][row : row + 8, 128 * q : 128 * q + 128]
                    w2[q, where, :] = jnp.where(lanes % 4 == 0, piece, w2[q, where, :])

        def merge(k, _):
            row = pl.multiple_of((k // groups) * 8, 8)
            q = k % groups
            where = pl.ds(2 * row, 8, stride=2)
            for z in range(nz // 2):
                inner = w2[q, pl.ds(pl.multiple_of(z * counts[1] + row, 8), 8), :]
                out_ref[q, 2 * z, where, :] = jnp.where(lanes % 2 == 0, inner, out_ref[q, 2 * z, where, :])
            return 0

        lax.fori_loop(0, (counts[1] // 8) * groups, merge, 0)
        more = leaving([z for z in untouched if z % 2 == 0])
        for copy in more:
            copy.start()

        done_ref[...] = jnp.zeros((8, 128), F32)
        for copy in copies + more:
            copy.wait()

    flat = [t for band in bands for t in band]
    return pl.pallas_call(
        kernel,
        in_specs=[VM] * 14,
        out_specs=[VM, VM, HB],
        out_shape=[
            vmem((groups, nz, nx, 128)),
            vmem((8, 128)),
            pltpu.HBM((nz, nx, ny), F32),
        ],
        scratch_shapes=[
            pltpu.VMEM((groups, nz // 2 * counts[1], 128), F32),
            pltpu.VMEM((512, 128), F32),
            pltpu.SemaphoreType.DMA((nz,)),
        ],
        compiler_params=params(32),
        cost_estimate=SHORT,
        name="main_part",
    )(*xs, from_left, from_right, *flat, *[jnp.asarray(m) for m in masks])


def early_part(below, above, band, after):
    nx, ny = below.shape[0] // 2, below.shape[1]
    _, _, maps = joint_sides(nx)

    def kernel(b1, a1, o1, e1, xt, after_ref, w_ref):
        del after_ref
        early = []
        for ref in (b1, a1):
            for c in range(2):
                hi, lo = split(ref[c * nx : c * nx + nx, :])
                early.append(dot(xt[...], jnp.concatenate([hi, hi, lo], axis=0)))
        early = jnp.concatenate(early, axis=0)
        w_ref[...] = banded(early, plain_edge(early), o1, e1)

    return pl.pallas_call(
        kernel,
        in_specs=[VM] * 6,
        out_specs=VM,
        out_shape=vmem((4 * nx, ny)),
        compiler_params=params(16),
        cost_estimate=SHORT,
        name="early_part",
    )(below, above, *band, jnp.asarray(stack_lhs(maps[0][0])), after)


def z_apply(inner, partial, early, from_left, from_right):
    groups, nz, nx, _ = inner.shape
    ny = groups * 128
    maps = [p for _, p in z_tables(nz)]
    counts = [nx, nx // 2, nx // 4]
    tables = []
    for level in (1, 2):
        width = ny >> level
        hi = spread_columns(np.eye(width), 1 << level, ny).astype(ml_dtypes.bfloat16)
        tables.append(np.concatenate([hi, hi]))
    places = [late_rows(side, counts, ny) for side in (0, 1)]
    _, _, x_maps = joint_sides(nx)
    frame = np.zeros((4 * nx, 16))
    for c in range(4):
        frame[c * nx : c * nx + nx, 4 * c : 4 * c + 2] = x_maps[0][1][:, :2]
        frame[c * nx : c * nx + nx, 4 * c + 2 : 4 * c + 4] = x_maps[0][2][:, :2]
        assert np.abs(x_maps[0][1][:, 2:]).max() < 1e-12 and np.abs(x_maps[0][2][:, 2:]).max() < 1e-12
    _, left, right = y_tables(ny, True)[0]
    side_hi, side_lo = hi_lo(np.concatenate([left, right, np.zeros((4, ny))]))
    side_rows = np.concatenate([side_hi, side_hi, side_lo, np.zeros((104, ny), side_hi.dtype)])
    touched = sorted(touched_layers(nz), key=lambda z: np.abs(maps[0][z]).max() > 1e-12)

    def kernel(in_ref, base_hbm, w_ref, fr, fl, t2, t3, xf, yf, out_hbm, s1, s2, s3, buf, sem):
        del base_hbm
        s2[...] = jnp.zeros(s2.shape, F32)
        s3[...] = jnp.zeros(s3.shape, F32)
        halos = [
            jnp.concatenate([ref[at[2] + 8 * p : at[2] + 8 * p + 8, :] for p in range(groups)], axis=1)
            for ref, at in zip((fl, fr), places)
        ]
        hi, lo = split(jnp.concatenate(halos, axis=0))
        none = jnp.zeros((104, 128), F32)
        turn = []
        for ref, at in zip((fl, fr), places):
            values = ref[at[3] : at[4], :]
            high = values.astype(BF).astype(F32)
            turn.append(jnp.concatenate([high, values - high, high, none], axis=0).T.astype(BF))
        left_hand = jnp.concatenate([jnp.concatenate(turn, axis=0), xf[...]], axis=1)
        first = w_ref[...] + dot(left_hand, jnp.concatenate([yf[...], hi, hi, lo], axis=0))
        for c in range(4):
            for q in range(groups):
                s1[c, q] = first[c * nx : c * nx + nx, 128 * q : 128 * q + 128]
        for level, table, to in ((1, t2, s2), (2, t3, s3)):
            n, lane_groups = counts[level], (ny >> level) // 128
            pieces = []
            for side, ref in enumerate((fl, fr)):
                row = places[side][level - 1]
                for c in range((LEFT_RANKS, RIGHT_RANKS)[side][level]):
                    pieces.append(
                        jnp.concatenate(
                            [ref[row + p * n : row + p * n + n, :] for p in range(lane_groups)], axis=1
                        )
                    )
                    row += lane_groups * n
            flat = jnp.concatenate(pieces, axis=0)
            hi, lo = split(flat)
            got = dot(jnp.concatenate([hi, lo], axis=1), table[...])
            for c in range(LEFT_RANKS[level] + RIGHT_RANKS[level]):
                start = c * n
                for q in range(groups):
                    piece = got[start : start + n, 128 * q : 128 * q + 128]
                    to[c, q, pl.ds(0, n, stride=1 << level), :] = piece

        row_ids = lax.broadcasted_iota(jnp.int32, (8, 128), 0)
        lane_ids = lax.broadcasted_iota(jnp.int32, (8, 128), 1)
        second_cell = row_ids % 2 + lane_ids % 2 == 0
        third_cell = row_ids % 4 + lane_ids % 4 == 0

        def summed(table_row, get):
            total = None
            for c, scalar in enumerate(table_row):
                if abs(scalar) > 1e-12:
                    total = add(total, get(c) * np.float32(scalar))
            return total

        copies = []
        for slot, z in enumerate(touched):

            for row in range(0, nx, 8):
                rows = slice(row, row + 8)
                for q in range(groups):
                    extra = summed(maps[0][z], lambda c: s1[c, q, rows, :])
                    if z % 2 == 0:
                        inner = summed(maps[1][z // 2], lambda c: s2[c, q, rows, :])
                        if z % 4 == 0:
                            third = summed(maps[2][z // 4], lambda c: s3[c, q, rows, :])
                            if third is not None:
                                inner = jnp.where(third_cell, third, 0.0 if inner is None else inner)
                        if extra is None:
                            extra = inner
                        else:
                            extra = jnp.where(second_cell, 0.0 if inner is None else inner, extra)
                    buf[slot, rows, 128 * q : 128 * q + 128] = add(in_ref[q, z, rows, :], extra)
            copy = pltpu.make_async_copy(buf.at[slot], out_hbm.at[z], sem.at[slot])
            copy.start()
            copies.append(copy)
        for copy in copies:
            copy.wait()

    return pl.pallas_call(
        kernel,
        in_specs=[VM, HB] + [VM] * 7,
        out_specs=HB,
        out_shape=jax.ShapeDtypeStruct((nz, nx, ny), F32),
        input_output_aliases={1: 0},
        scratch_shapes=[
            pltpu.VMEM((4, groups, nx, 128), F32),
            pltpu.VMEM((maps[1].shape[1], groups, nx, 128), F32),
            pltpu.VMEM((maps[2].shape[1], groups, nx, 128), F32),
            pltpu.VMEM((len(touched), nx, ny), F32),
            pltpu.SemaphoreType.DMA((len(touched),)),
        ],
        compiler_params=params(24),
        name="z_apply",
    )(
        inner,
        partial,
        early,
        from_right,
        from_left,
        *[jnp.asarray(t) for t in tables],
        jnp.asarray(stack_lhs(frame)),
        jnp.asarray(side_rows),
    )


def swap(to_right, to_left, axis):
    count = lax.axis_size(axis)
    right = [(i, (i + 1) % count) for i in range(count)]
    left = [(j, i) for i, j in right]
    return lax.ppermute(to_right, axis, right), lax.ppermute(to_left, axis, left)


def local(field):
    nz, nx, ny = field.shape
    counts = [nx, nx // 2, nx // 4]
    bands = [[jnp.asarray(t) for t in band_tables(level, nz, counts, ny)] for level in range(3)]
    field, message, up, down = x_send(field)
    halo = x_exchange(message)
    below, above = swap(up, down, "gz")
    x1, x2, x3, to_right, to_left = x_apply(field, halo)
    from_left, from_right = swap(to_right, to_left, "gy")
    *combined, own2, own3 = z_first(x2, x3, halo)
    down, up = y_messages(combined, from_left, from_right, nz, bands[0])
    late_below, late_above = swap(up, down, "gz")
    inner, done, partial = main_part((x1, own2, own3), from_left, from_right, bands)
    early = early_part(below, above, bands[0], done)
    return z_apply(inner, partial, early, late_below, late_above)


def solution(mesh):
    placed = (P("gz", "gx", "gy"),)
    return jax.shard_map(
        local, mesh=mesh, in_specs=placed, out_specs=P("gz", "gx", "gy"), check_vma=False
    )
```

```python
import functools

import jax
import jax.numpy as jnp
import ml_dtypes
import numpy as np
from jax import lax
from jax.experimental import pallas as pl
from jax.experimental.pallas import tpu as pltpu
from jax.sharding import PartitionSpec as P

lift_alpha = -1.586134342
lift_beta = -0.05298011854
lift_gamma = 0.8829110762
lift_delta = 0.4435068522
lift_zeta = 1.149604398

BF = jnp.bfloat16
F32 = jnp.float32
MIB = 1024 * 1024


def periodic_lift(u):
    s, d = u[0::2].copy(), u[1::2].copy()
    d = d + lift_alpha * (s + np.roll(s, -1, 0))
    s = s + lift_beta * (np.roll(d, 1, 0) + d)
    d = d + lift_gamma * (s + np.roll(s, -1, 0))
    s = s + lift_delta * (np.roll(d, 1, 0) + d)
    out = np.empty_like(u)
    out[0::2] = s * lift_zeta
    out[1::2] = d / lift_zeta
    return out


@functools.lru_cache(None)
def blocks(n):
    current = np.eye(4 * n)
    found = []
    for level in range(3):
        full = periodic_lift(current)
        m = n >> level
        rows = full[m : 2 * m]
        found.append((rows[:, n : 2 * n], rows[:, :n], rows[:, 2 * n : 3 * n]))
        current = full[0::2]
    return found


def row_space(outer, rank):
    _, sizes, basis = np.linalg.svd(outer, full_matrices=False)
    assert sizes[rank:].max() < 1e-10
    basis = basis[:rank].copy()
    basis[np.abs(basis) < 1e-12] = 0.0
    return basis


LEFT_RANKS = (2, 3, 4)
RIGHT_RANKS = (2, 3, 3)


@functools.lru_cache(None)
def sides(n):
    out = []
    for level, (main, left, right) in enumerate(blocks(n)):
        cl = row_space(left, LEFT_RANKS[level])
        cr = row_space(right, RIGHT_RANKS[level])
        out.append((main, cl, left @ cl.T, cr, right @ cr.T))
    return out


def nested_space(outer):
    first = row_space(outer[0], 2)
    every = np.concatenate(outer)
    rest = every - every @ first.T @ first
    return np.concatenate([first, row_space(rest, 4)])


@functools.lru_cache(None)
def joint_sides(n):
    found = blocks(n)
    cl = nested_space([b[1] for b in found])
    cr = nested_space([b[2] for b in found])
    maps = [(b[0], b[1] @ cl.T, b[2] @ cr.T) for b in found]
    return cl, cr, maps


def hi_lo(table):
    table = np.asarray(table, np.float32)
    hi = table.astype(ml_dtypes.bfloat16)
    lo = (table - hi.astype(np.float32)).astype(ml_dtypes.bfloat16)
    return hi, lo


def stack_lhs(table):
    hi, lo = hi_lo(table)
    return np.concatenate([hi, lo, hi], axis=1)


def stack_rhs(table):
    hi, lo = hi_lo(table)
    return np.concatenate([hi, hi, lo], axis=0)


def split(values):
    hi = values.astype(BF)
    return hi, (values - hi.astype(F32)).astype(BF)


def dot(a, b):
    return lax.dot_general(a, b, (((1,), (0,)), ((), ())), preferred_element_type=F32)


def dot_t(a, b):
    return lax.dot_general(a, b, (((1,), (1,)), ((), ())), preferred_element_type=F32)


def spread_columns(table, step, width):
    out = np.zeros((table.shape[0], width))
    out[:, ::step] = table
    return out


VM = pl.BlockSpec(memory_space=pltpu.VMEM)
HB = pl.BlockSpec(memory_space=pltpu.HBM)
SHORT = pl.CostEstimate(flops=1000, bytes_accessed=1000, transcendentals=0)


def in_hbm(array):
    return pltpu.with_memory_space_constraint(array, pltpu.HBM)


def vmem(shape, dtype=F32):
    return pltpu.VMEM(shape, dtype)


def params(mib):
    return pltpu.CompilerParams(vmem_limit_bytes=mib * MIB)


def x_send(field):
    nz, nx, ny = field.shape
    cl, cr, _ = joint_sides(nx)
    one = np.concatenate([cl, cr])
    group = 4
    wide = np.kron(np.eye(group), one)
    hi_rows, lo_rows = hi_lo(wide)
    pair = np.concatenate([hi_rows, lo_rows])
    height = 12 * group
    step = 8
    steps = nz // step
    order = [0, steps - 1] + list(range(1, steps - 1))
    _, low, _, high, _ = sides(nz)[0]
    assert np.abs(low[:, :-step]).max() == 0 and np.abs(high[:, step:]).max() == 0

    def kernel(u_hbm, c_hbm, u_ref, out_ref, up_ref, down_ref, c_ref, u_sem, c_sem):
        table_copy = pltpu.make_async_copy(c_hbm, c_ref, c_sem)
        copies = [
            pltpu.make_async_copy(
                u_hbm.at[i * step : i * step + step], u_ref.at[i * step : i * step + step], u_sem.at[i]
            )
            for i in range(steps)
        ]
        table_copy.start()
        for i in order:
            copies[i].start()
        table_copy.wait()
        table = c_ref[...]
        for i in order:
            copies[i].wait()
            for g in range(i * step // group, (i + 1) * step // group):
                hi, lo = split(u_ref[group * g : group * g + group].reshape(group * nx, ny))
                both = dot(table, hi)
                out_ref[height * g : height * g + height, :] = (
                    both[:height] + both[height:] + dot(table[:height], lo)
                )
            if i in order[:2]:
                combos, ref = (high, down_ref) if i == 0 else (low, up_ref)
                for c in range(2):
                    ref[c * nx : c * nx + nx, :] = weighted(
                        [(combos[c, z], lambda z=z: u_ref[z]) for z in range(i * step, (i + 1) * step)]
                    )

    return pl.pallas_call(
        kernel,
        in_specs=[HB, HB],
        out_specs=[VM] * 4,
        out_shape=[vmem((nz, nx, ny)), vmem((nz * 12, ny)), vmem((2 * nx, ny)), vmem((2 * nx, ny))],
        scratch_shapes=[
            pltpu.VMEM(pair.shape, BF),
            pltpu.SemaphoreType.DMA((steps,)),
            pltpu.SemaphoreType.DMA,
        ],
        compiler_params=params(16),
        cost_estimate=SHORT,
        name="x_send",
    )(in_hbm(field), in_hbm(jnp.asarray(pair)))


def x_exchange(message):
    count = lax.axis_size("gx")
    right = [(i, (i + 1) % count) for i in range(count)]
    if count == 2:
        return lax.ppermute(message, "gx", right)
    left = [(j, i) for i, j in right]
    rows, ny = message.shape
    grid = message.reshape(rows // 12, 12, ny)
    from_left = lax.ppermute(grid[:, :6], "gx", right)
    from_right = lax.ppermute(grid[:, 6:], "gx", left)
    return jnp.concatenate([from_left, from_right], axis=1).reshape(rows, ny)


def x_apply(field, halo):
    nz, nx, ny = field.shape
    _, _, maps = joint_sides(nx)
    main = np.concatenate([m for m, _, _ in maps])
    outer = np.concatenate([np.concatenate([l, r], axis=1) for _, l, r in maps])
    pad = np.zeros((main.shape[0], 4))
    tables = np.stack(
        [
            stack_lhs(np.concatenate([main, outer, pad], axis=1)),
            stack_lhs(np.concatenate([main, pad, outer], axis=1)),
        ]
    )
    rows = main.shape[0]
    counts = [nx, nx // 2, nx // 4]
    step = 8
    steps = nz // step

    combos = []
    for level, (_, cl, _, cr, _) in enumerate(sides(ny)):
        both = np.zeros((8, 128))
        assert np.abs(cl[:, : ny - 64]).max() == 0 and np.abs(cr[:, 64:]).max() == 0
        both[: cl.shape[0], 64:] = cl[:, ny - 64 :]
        both[4 : 4 + cr.shape[0], :64] = cr[:, :64]
        combos.append(stack_lhs(both))
    combos = np.stack(combos)

    def kernel(u_ref, r_ref, t_ref, c_ref, x1, x2, x3, right_ref, left_ref, e1, e2, e3):
        i = pl.program_id(0)
        lanes = lax.broadcasted_iota(jnp.int32, (rows, 128), 1)
        for z in range(step):
            start = pl.multiple_of(i * (12 * step) + 24 * (z // 2) + 8 * (z % 2), 8)
            hi, lo = split(u_ref[i * step + z])
            rhi, rlo = split(r_ref[pl.ds(start, 16), :])
            stacked = jnp.concatenate([hi, rhi, hi, rhi, lo, rlo], axis=0)
            got = dot(t_ref[z % 2], stacked)
            edge = jnp.where(lanes < 64, got[:, :128], got[:, ny - 128 :])
            ehi, elo = split(edge)
            estack = jnp.concatenate([ehi, ehi, elo], axis=1)
            at = 0
            for ref, eref, n in zip((x1, x2, x3), (e1, e2, e3), counts):
                where = pl.ds(pl.multiple_of((i * step + z) * n, 16), n)
                ref[i * step + z] = got[at : at + n]
                eref[where, :] = estack[at : at + n]
                at += n

        @pl.when(i == steps - 1)
        def _():
            row = 0
            for level, (eref, n) in enumerate(zip((e1, e2, e3), counts)):
                got = dot_t(c_ref[level], eref[...])
                for j in range(nz * n // 512):
                    for c in range(LEFT_RANKS[level]):
                        right_ref[row : row + 1, :] = got[c : c + 1, 512 * j : 512 * j + 512]
                        if c < RIGHT_RANKS[level]:
                            left_ref[row : row + 1, :] = got[4 + c : 5 + c, 512 * j : 512 * j + 512]
                        else:
                            left_ref[row : row + 1, :] = jnp.zeros((1, 512), F32)
                        row += 1
            right_ref[row:, :] = jnp.zeros((24 - row, 512), F32)
            left_ref[row:, :] = jnp.zeros((24 - row, 512), F32)

    return pl.pallas_call(
        kernel,
        grid=(steps,),
        in_specs=[VM] * 4,
        out_specs=[VM] * 5,
        out_shape=[vmem((nz, n, ny)) for n in counts] + [jax.ShapeDtypeStruct((24, 512), F32)] * 2,
        scratch_shapes=[pltpu.VMEM((nz * n, 384), BF) for n in counts],
        compiler_params=params(24),
        cost_estimate=SHORT,
        name="x_apply",
    )(field, halo, jnp.asarray(tables), jnp.asarray(combos))


def add(a, b):
    if a is None:
        return b
    return a if b is None else a + b


def scale(a, c):
    return None if a is None else a * np.float32(c)


def open_lift(values, first, last):
    get = values.get
    low, high = first // 2 - 3, last // 2 + 4
    s = {i: get(2 * i) for i in range(low, high + 1)}
    d = {i: get(2 * i + 1) for i in range(low, high + 1)}
    pick = lambda t, i: t.get(i)
    d1 = {i: add(d[i], scale(add(s[i], pick(s, i + 1)), lift_alpha)) for i in range(low, high + 1)}
    s1 = {i: add(s[i], scale(add(pick(d1, i - 1), d1[i]), lift_beta)) for i in range(low, high + 1)}
    d2 = {i: add(d1[i], scale(add(s1[i], pick(s1, i + 1)), lift_gamma)) for i in range(low, high + 1)}
    s2 = {i: add(s1[i], scale(add(pick(d2, i - 1), d2[i]), lift_delta)) for i in range(low, high + 1)}
    out = {}
    for z in range(first, last + 1):
        if z % 2:
            out[z] = scale(d2[z // 2], 1.0 / lift_zeta)
        else:
            out[z] = scale(s2[z // 2], lift_zeta)
    return out


def lows(values, first, last):
    got = open_lift(values, 2 * first, 2 * last)
    return {i: got[2 * i] for i in range(first, last + 1) if got[2 * i] is not None}


def own_levels(values, nz, level):
    if level >= 1:
        values = lows(values, -2, nz // 2 + 1)
    if level >= 2:
        values = lows(values, -3, nz // 4 + 2)
    return open_lift(values, 0, (nz >> level) - 1)


def z_tables(nz):
    out = []
    for _, cl, pl_, cr, pr in sides(nz):
        out.append((np.concatenate([cl, cr]), np.concatenate([pl_, pr], axis=1)))
    return out


def weighted(parts):
    total = None
    for scalar, get in parts:
        if abs(scalar) < 1e-12:
            continue
        term = get() * np.float32(scalar)
        total = term if total is None else total + term
    return total


def z_first(x2, x3, halo):
    nz, _, ny = x2.shape
    tables = [t for t, _ in z_tables(nz)]
    counts = [x2.shape[1], x3.shape[1]]
    groups = ny // 128

    def kernel(x2, x3, r_ref, o2, o3, of, y2, y3):
        for level, ref, out, own, table, n in zip((1, 2), (x2, x3), (o2, o3), (y2, y3), tables[1:], counts):

            def body(k, _, level=level, ref=ref, out=out, own=own, table=table, n=n):
                row = pl.multiple_of((k // groups) * 8, 8)
                lane = pl.multiple_of((k % groups) * 128, 128)
                get = {}
                for z in range(nz):
                    get[z] = ref[z, pl.ds(row, 8), pl.ds(lane, 128)]
                for z, value in own_levels(get, nz, level).items():
                    own[z, pl.ds(row, 8), pl.ds(lane, 128)] = value
                for c in range(table.shape[0]):
                    out[pl.ds(pl.multiple_of(c * n + row, 8), 8), pl.ds(lane, 128)] = weighted(
                        [(table[c, z], lambda z=z: get[z]) for z in range(nz)]
                    )
                return 0

            lax.fori_loop(0, (n // 8) * groups, body, 0)
        for c in range(4):
            got = weighted(
                [(tables[0][c, z], lambda z=z: r_ref[12 * z : 12 * z + 12, :]) for z in range(nz)]
            )
            of[4 * c : 4 * c + 2, :] = got[0:2]
            of[4 * c + 2 : 4 * c + 4, :] = got[6:8]

    return pl.pallas_call(
        kernel,
        in_specs=[VM] * 3,
        out_specs=[VM] * 5,
        out_shape=[vmem((t.shape[0] * n, ny)) for t, n in zip(tables[1:], counts)]
        + [vmem((16, ny)), vmem((nz // 2, counts[0], ny)), vmem((nz // 4, counts[1], ny))],
        compiler_params=params(16),
        cost_estimate=SHORT,
        name="z_first",
    )(x2, x3, halo)


def y_tables(ny, spread):
    out = []
    for level, (main, _, left, _, right) in enumerate(sides(ny)):
        step = (1 << level) if spread else 1
        width = ny if spread else ny >> level
        fit = lambda t: spread_columns(t.T, step, width)
        out.append((fit(main), fit(left), fit(right)))
    return out


def halo_rows(level, chunk, nz, counts):
    start = 0
    for below in range(level):
        start += (nz * counts[below] // 512) * LEFT_RANKS[below]
    return start + chunk * LEFT_RANKS[level]


LEFT_AT, RIGHT_AT = 32, 56


def halo_base(left, right, level, nz, counts):
    base = np.zeros((128, left.shape[1]))
    for chunk in range(nz * counts[level] // 512):
        row = halo_rows(level, chunk, nz, counts)
        base[LEFT_AT + row : LEFT_AT + row + left.shape[0]] = left
        base[RIGHT_AT + row : RIGHT_AT + row + right.shape[0]] = right
    return base


def turned(left_ref, right_ref):
    wide = jnp.concatenate(
        [jnp.zeros((LEFT_AT, 512), F32), left_ref[...], right_ref[...], jnp.zeros((48, 512), F32)], axis=0
    )
    return wide.T


def band_tables(level, nz, counts, ny):
    assert ny == 512
    main, left, right = y_tables(ny, True)[level]
    base = halo_base(left, right, level, nz, counts)
    own, edge = [], []
    for j in range(2):
        cols = slice(256 * j, 256 * j + 256)
        own.append(stack_rhs(main[cols, cols]))
        tile = base[:, cols].copy()
        if j == 0:
            tile[:32] = main[256:288, cols]
            assert np.abs(main[288:, cols]).max() == 0
        else:
            tile[96:] = main[224:256, cols]
            assert np.abs(main[:224, cols]).max() == 0
        edge.append(stack_rhs(tile))
    return np.stack(own), np.stack(edge)


def three(values):
    hi, lo = split(values)
    return jnp.concatenate([hi, lo, hi], axis=1)


def banded(rows, edge, own_ref, edge_ref):
    edges = three(edge)
    out = []
    for j in range(2):
        own = three(rows[:, 256 * j : 256 * j + 256])
        out.append(dot(own, own_ref[j]) + dot(edges, edge_ref[j]))
    return jnp.concatenate(out, axis=1)


def plain_edge(rows):
    lanes = lax.broadcasted_iota(jnp.int32, (rows.shape[0], 128), 1)
    before = jnp.where(lanes >= 96, rows[:, 128:256], 0.0)
    return jnp.where(lanes < 32, rows[:, 256:384], before)


def late_rows(side, counts, ny):
    ranks = LEFT_RANKS if side == 0 else RIGHT_RANKS
    parts = [ranks[1] * counts[1] * ny // 256, ranks[2] * counts[2] * ny // 512, ny // 16, 8]
    return [0] + [int(n) for n in np.cumsum(parts)]


def late_heights(counts, ny):
    return (max(late_rows(side, counts, ny)[-1] for side in (0, 1)),) * 2


def y_messages(combined, from_left, from_right, nz, band_one):
    c2, c3, cf = combined
    ny = c2.shape[1]
    tables = z_tables(nz)
    nums = [t.shape[0] for t, _ in tables]
    counts = [2 * c2.shape[0] // nums[1], c2.shape[0] // nums[1], c3.shape[0] // nums[2]]
    mains, halos, coefs = [], [], []
    for level, (main, left, right) in enumerate(y_tables(ny, False)):
        mains.append(stack_rhs(main))
        halos.append(stack_rhs(halo_base(left, right, level, nz, counts)))
        chunks = nz * counts[level] // 512
        per = 512 // counts[level]
        table = tables[level][0]
        coef = np.zeros((nums[level], per, 128), np.float32)
        for c in range(nums[level]):
            for zz in range(per):
                for chunk in range(chunks):
                    row = halo_rows(level, chunk, nz, counts)
                    for lane in range(LEFT_RANKS[level]):
                        for base in (LEFT_AT, RIGHT_AT):
                            coef[c, zz, base + row + lane] = table[c, chunk * per + zz]
        coefs.append(coef.reshape(nums[level] * per, 128))
    places = [late_rows(side, counts, ny) for side in (0, 1)]
    heights = late_heights(counts, ny)

    def kernel(c2, c3, cf, fl, fr, own1, edge1, m2, m3, h2, h3, k1, k2, k3, down_ref, up_ref):
        halo = turned(fl, fr)

        def reduced(k, n, num):
            per = 512 // n
            extra = []
            for c in range(num):
                total = None
                for zz in range(per):
                    if np.abs(coefs_of[n][c * per + zz]).max() > 1e-12:
                        term = halo[zz * n : zz * n + n] * k[c * per + zz : c * per + zz + 1, :]
                        total = term if total is None else total + term
                extra.append(total)
            return extra

        coefs_of = dict(zip(counts, coefs))
        got = []
        for c_ref, m, h, k, n, num in zip((c2, c3), (m2, m3), (h2, h3), (k2, k3), counts[1:], nums[1:]):
            extra = jnp.concatenate(reduced(k, n, num), axis=0)
            got.append(dot(three(c_ref[...]), m[...]) + dot(three(extra), h[...]))
        frame = cf[...]
        frame = banded(frame, plain_edge(frame), own1, edge1)
        ones = reduced(k1, counts[0], 4)
        rows8 = lax.broadcasted_iota(jnp.int32, (8, 128), 0)
        for side, ref in enumerate((up_ref, down_ref)):
            at = places[side]
            for level in (1, 2):
                n, lane_groups = counts[level], (ny >> level) // 128
                ranks = LEFT_RANKS if side == 0 else RIGHT_RANKS
                first = 0 if side == 0 else LEFT_RANKS[level] * n
                row = at[level - 1]
                for c in range(ranks[level]):
                    for p in range(lane_groups):
                        ref[row : row + n, :] = got[level - 1][
                            first + c * n : first + c * n + n, 128 * p : 128 * p + 128
                        ]
                        row += n
            for p in range(ny // 128):
                ref[at[2] + 8 * p : at[2] + 8 * p + 8, :] = frame[
                    8 * side : 8 * side + 8, 128 * p : 128 * p + 128
                ]
            turn = jnp.concatenate(ones[2 * side : 2 * side + 2], axis=0).T
            both = []
            for start in (LEFT_AT, RIGHT_AT):
                v = turn[start : start + 8]
                v = v + pltpu.roll(v, 4, 0)
                both.append(v + pltpu.roll(v, 2, 0))
            ref[at[3] : at[4], :] = jnp.where(rows8 < 2, both[0], both[1])
            if heights[side] > at[4]:
                ref[at[4] :, :] = jnp.zeros((heights[side] - at[4], 128), F32)

    return pl.pallas_call(
        kernel,
        in_specs=[VM] * 14,
        out_specs=[VM] * 2,
        out_shape=[vmem((height, 128)) for height in reversed(heights)],
        compiler_params=params(24),
        cost_estimate=SHORT,
        name="y_messages",
    )(
        c2,
        c3,
        cf,
        from_left,
        from_right,
        *band_one,
        *[jnp.asarray(t) for t in mains[1:]],
        *[jnp.asarray(t) for t in halos[1:]],
        *[jnp.asarray(t) for t in coefs],
    )


def touched_layers(nz):
    one, two, three = [np.abs(p).max(axis=1) > 1e-12 for _, p in z_tables(nz)]
    hit = lambda z: one[z] or (z % 2 == 0 and two[z // 2]) or (z % 4 == 0 and three[z // 4])
    return [z for z in range(nz) if hit(z)]


def main_part(xs, from_left, from_right, bands):
    nz, nx, ny = xs[0].shape
    counts = [nx, nx // 2, nx // 4]
    changed = touched_layers(nz)
    untouched = [z for z in range(nz) if z not in changed]
    groups = ny // 128
    masks = []
    for level in range(3):
        chunks = nz * counts[level] // 512
        per = 512 // counts[level]
        lanes_of = np.zeros((chunks, 128))
        for chunk in range(chunks):
            row = halo_rows(level, chunk, nz, counts)
            for base in (LEFT_AT, RIGHT_AT):
                lanes_of[chunk, base + row : base + row + LEFT_RANKS[level]] = 1.0
        if level == 0:
            masks.append(lanes_of)
        else:
            own = sides(nz)[level][0]
            lanes = np.einsum("ocz,cl->ozl", own.reshape(own.shape[0], chunks, per), lanes_of)
            masks.append(lanes.reshape(-1, 128))
    masks = [np.concatenate([m, np.zeros((-m.shape[0] % 8, 128))]).astype(np.float32) for m in masks]

    def kernel(x1, x2, x3, fl, fr, o1, e1, o2, e2, o3, e3, k1, k2, k3, out_ref, done_ref, hbm, w2, halo_ref, sem):
        halo_ref[...] = turned(fl, fr)
        lanes = lax.broadcasted_iota(jnp.int32, (8, 128), 1)
        wide = lax.broadcasted_iota(jnp.int32, (32, 128), 1)
        after, before = wide < 32, wide >= 96

        def in_y(x, level, row, tall, own, edge, mk):
            n = counts[level]
            per = 512 // n
            layers = nz >> level
            values = x[:, row : row + tall, :]
            turns = [halo_ref[zz * n + row : zz * n + row + tall, :] for zz in range(per)]
            edges = []
            for z in range(layers):
                if level == 0:
                    turn = turns[z % per] * mk[z // per : z // per + 1, :]
                else:
                    turn = None
                    for zz in range(per):
                        if np.abs(masks[level][z * per + zz]).max() > 1e-12:
                            turn = add(turn, turns[zz] * mk[z * per + zz : z * per + zz + 1, :])
                edges.append(
                    jnp.where(
                        after[:tall],
                        values[z, :, 256:384],
                        jnp.where(before[:tall], values[z, :, 128:256], turn),
                    )
                )
            got = banded(
                values.reshape(layers * tall, ny), jnp.concatenate(edges, axis=0), own, edge
            )
            return {z: got[tall * z : tall * z + tall] for z in range(layers)}

        def store(to, values, row, indices, height=None):
            for z in indices:
                for q in range(groups):
                    piece = values[z][:, 128 * q : 128 * q + 128]
                    tall = piece.shape[0]
                    if height is None:
                        to[q, z, row : row + tall, :] = piece
                    else:
                        to[q, z * height + row : z * height + row + tall, :] = piece

        for row in range(0, counts[0], 16):
            got = own_levels(in_y(x1, 0, row, 16, o1, e1, k1), nz, 0)
            store(out_ref, got, row, range(nz))

        def leaving(layers):
            return [
                pltpu.make_async_copy(
                    out_ref.at[q, z], hbm.at[z, :, 128 * q : 128 * q + 128], sem.at[z]
                )
                for z in layers
                for q in range(groups)
            ]

        copies = leaving([z for z in untouched if z % 2])
        for copy in copies:
            copy.start()

        store(w2, in_y(x2, 1, 0, counts[1], o2, e2, k2), 0, range(nz // 2), counts[1])
        got = in_y(x3, 2, 0, counts[2], o3, e3, k3)
        for z in range(nz // 4):
            for row in range(0, counts[2], 8):
                where = pl.ds(2 * z * counts[1] + 2 * row, 8, stride=2)
                for q in range(groups):
                    piece = got[z][row : row + 8, 128 * q : 128 * q + 128]
                    w2[q, where, :] = jnp.where(lanes % 4 == 0, piece, w2[q, where, :])

        def merge(k, _):
            row = pl.multiple_of((k // groups) * 8, 8)
            q = k % groups
            where = pl.ds(2 * row, 8, stride=2)
            for z in range(nz // 2):
                inner = w2[q, pl.ds(pl.multiple_of(z * counts[1] + row, 8), 8), :]
                out_ref[q, 2 * z, where, :] = jnp.where(lanes % 2 == 0, inner, out_ref[q, 2 * z, where, :])
            return 0

        lax.fori_loop(0, (counts[1] // 8) * groups, merge, 0)
        more = leaving([z for z in untouched if z % 2 == 0])
        for copy in more:
            copy.start()

        done_ref[...] = jnp.zeros((8, 128), F32)
        for copy in copies + more:
            copy.wait()

    flat = [t for band in bands for t in band]
    return pl.pallas_call(
        kernel,
        in_specs=[VM] * 14,
        out_specs=[VM, VM, HB],
        out_shape=[
            vmem((groups, nz, nx, 128)),
            vmem((8, 128)),
            pltpu.HBM((nz, nx, ny), F32),
        ],
        scratch_shapes=[
            pltpu.VMEM((groups, nz // 2 * counts[1], 128), F32),
            pltpu.VMEM((512, 128), F32),
            pltpu.SemaphoreType.DMA((nz,)),
        ],
        compiler_params=params(32),
        cost_estimate=SHORT,
        name="main_part",
    )(*xs, from_left, from_right, *flat, *[jnp.asarray(m) for m in masks])


def early_part(below, above, band, after):
    nx, ny = below.shape[0] // 2, below.shape[1]
    _, _, maps = joint_sides(nx)

    def kernel(b1, a1, o1, e1, xt, after_ref, w_ref):
        del after_ref
        early = []
        for ref in (b1, a1):
            for c in range(2):
                hi, lo = split(ref[c * nx : c * nx + nx, :])
                early.append(dot(xt[...], jnp.concatenate([hi, hi, lo], axis=0)))
        early = jnp.concatenate(early, axis=0)
        w_ref[...] = banded(early, plain_edge(early), o1, e1)

    return pl.pallas_call(
        kernel,
        in_specs=[VM] * 6,
        out_specs=VM,
        out_shape=vmem((4 * nx, ny)),
        compiler_params=params(16),
        cost_estimate=SHORT,
        name="early_part",
    )(below, above, *band, jnp.asarray(stack_lhs(maps[0][0])), after)


def z_apply(inner, partial, early, from_left, from_right):
    groups, nz, nx, _ = inner.shape
    ny = groups * 128
    maps = [p for _, p in z_tables(nz)]
    counts = [nx, nx // 2, nx // 4]
    tables = []
    for level in (1, 2):
        width = ny >> level
        hi = spread_columns(np.eye(width), 1 << level, ny).astype(ml_dtypes.bfloat16)
        tables.append(np.concatenate([hi, hi]))
    places = [late_rows(side, counts, ny) for side in (0, 1)]
    _, _, x_maps = joint_sides(nx)
    frame = np.zeros((4 * nx, 16))
    for c in range(4):
        frame[c * nx : c * nx + nx, 4 * c : 4 * c + 2] = x_maps[0][1][:, :2]
        frame[c * nx : c * nx + nx, 4 * c + 2 : 4 * c + 4] = x_maps[0][2][:, :2]
        assert np.abs(x_maps[0][1][:, 2:]).max() < 1e-12 and np.abs(x_maps[0][2][:, 2:]).max() < 1e-12
    _, left, right = y_tables(ny, True)[0]
    side_hi, side_lo = hi_lo(np.concatenate([left, right, np.zeros((4, ny))]))
    side_rows = np.concatenate([side_hi, side_hi, side_lo, np.zeros((104, ny), side_hi.dtype)])
    touched = sorted(touched_layers(nz), key=lambda z: np.abs(maps[0][z]).max() > 1e-12)

    def kernel(in_ref, base_hbm, w_ref, fr, fl, t2, t3, xf, yf, io_ref, out_hbm, s1, s2, s3, sem):
        del base_hbm
        s3[...] = jnp.zeros(s3.shape, F32)
        halos = [
            jnp.concatenate([ref[at[2] + 8 * p : at[2] + 8 * p + 8, :] for p in range(groups)], axis=1)
            for ref, at in zip((fl, fr), places)
        ]
        hi, lo = split(jnp.concatenate(halos, axis=0))
        none = jnp.zeros((104, 128), F32)
        turn = []
        for ref, at in zip((fl, fr), places):
            values = ref[at[3] : at[4], :]
            high = values.astype(BF).astype(F32)
            turn.append(jnp.concatenate([high, values - high, high, none], axis=0).T.astype(BF))
        left_hand = jnp.concatenate([jnp.concatenate(turn, axis=0), xf[...]], axis=1)
        first = w_ref[...] + dot(left_hand, jnp.concatenate([yf[...], hi, hi, lo], axis=0))
        for c in range(4):
            for q in range(groups):
                s1[c, q] = first[c * nx : c * nx + nx, 128 * q : 128 * q + 128]
        for level, table, to in ((1, t2, s2), (2, t3, s3)):
            n, lane_groups = counts[level], (ny >> level) // 128
            pieces = []
            for side, ref in enumerate((fl, fr)):
                row = places[side][level - 1]
                for c in range((LEFT_RANKS, RIGHT_RANKS)[side][level]):
                    pieces.append(
                        jnp.concatenate(
                            [ref[row + p * n : row + p * n + n, :] for p in range(lane_groups)], axis=1
                        )
                    )
                    row += lane_groups * n
            flat = jnp.concatenate(pieces, axis=0)
            hi, lo = split(flat)
            got = dot(jnp.concatenate([hi, lo], axis=1), table[...])
            for c in range(LEFT_RANKS[level] + RIGHT_RANKS[level]):
                start = c * n
                for q in range(groups):
                    piece = got[start : start + n, 128 * q : 128 * q + 128]
                    if level == 1:
                        to[c, q] = piece
                    else:
                        to[c, q, pl.ds(0, n, stride=2), :] = piece

        lanes = lax.broadcasted_iota(jnp.int32, (8, 128), 1)
        even_lane = lanes % 2 == 0
        third_cell = (lax.broadcasted_iota(jnp.int32, (8, 128), 0) % 2 + lanes % 4) == 0

        def summed(table_row, get):
            total = None
            for c, scalar in enumerate(table_row):
                if abs(scalar) > 1e-12:
                    total = add(total, get(c) * np.float32(scalar))
            return total

        copies = []
        for slot, z in enumerate(touched):

            for t in range(nx // 16):
                full, half = 16 * t, 8 * t
                for q in range(groups):
                    if z % 2:
                        for more in (0, 8):
                            rows = pl.ds(full + more, 8)
                            extra = summed(maps[0][z], lambda c: s1[c, q, rows, :])
                            io_ref[q, z, rows, :] = add(in_ref[q, z, rows, :], extra)
                        continue
                    evens = pl.ds(16 * t, 8, stride=2)
                    odds = pl.ds(16 * t + 1, 8, stride=2)
                    extra = summed(maps[0][z], lambda c: s1[c, q, odds, :])
                    if extra is not None:
                        io_ref[q, z, odds, :] = add(in_ref[q, z, odds, :], extra)
                    rows = pl.ds(half, 8)
                    extra = summed(maps[1][z // 2], lambda c: s2[c, q, rows, :])
                    if z % 4 == 0:
                        third = summed(maps[2][z // 4], lambda c: s3[c, q, rows, :])
                        third = 0.0 if third is None else third
                        extra = jnp.where(third_cell, third, 0.0 if extra is None else extra)
                    one = summed(maps[0][z], lambda c: s1[c, q, evens, :])
                    if one is not None:
                        extra = jnp.where(even_lane, 0.0 if extra is None else extra, one)
                    io_ref[q, z, evens, :] = add(in_ref[q, z, evens, :], extra)
            for q in range(groups):
                copy = pltpu.make_async_copy(
                    io_ref.at[q, z], out_hbm.at[z, :, 128 * q : 128 * q + 128], sem.at[slot]
                )
                copy.start()
                copies.append(copy)
        for copy in copies:
            copy.wait()

    return pl.pallas_call(
        kernel,
        in_specs=[VM, HB] + [VM] * 7,
        out_specs=[VM, HB],
        out_shape=[vmem(inner.shape), jax.ShapeDtypeStruct((nz, nx, ny), F32)],
        input_output_aliases={0: 0, 1: 1},
        scratch_shapes=[
            pltpu.VMEM((4, groups, nx, 128), F32),
            pltpu.VMEM((maps[1].shape[1], groups, nx // 2, 128), F32),
            pltpu.VMEM((maps[2].shape[1], groups, nx // 2, 128), F32),
            pltpu.SemaphoreType.DMA((len(touched),)),
        ],
        compiler_params=params(24),
        name="z_apply",
    )(
        inner,
        partial,
        early,
        from_right,
        from_left,
        *[jnp.asarray(t) for t in tables],
        jnp.asarray(stack_lhs(frame)),
        jnp.asarray(side_rows),
    )


def swap(to_right, to_left, axis):
    count = lax.axis_size(axis)
    right = [(i, (i + 1) % count) for i in range(count)]
    left = [(j, i) for i, j in right]
    return lax.ppermute(to_right, axis, right), lax.ppermute(to_left, axis, left)


def local(field):
    nz, nx, ny = field.shape
    counts = [nx, nx // 2, nx // 4]
    bands = [[jnp.asarray(t) for t in band_tables(level, nz, counts, ny)] for level in range(3)]
    field, message, up, down = x_send(field)
    halo = x_exchange(message)
    below, above = swap(up, down, "gz")
    x1, x2, x3, to_right, to_left = x_apply(field, halo)
    from_left, from_right = swap(to_right, to_left, "gy")
    *combined, own2, own3 = z_first(x2, x3, halo)
    down, up = y_messages(combined, from_left, from_right, nz, bands[0])
    late_below, late_above = swap(up, down, "gz")
    inner, done, partial = main_part((x1, own2, own3), from_left, from_right, bands)
    early = early_part(below, above, bands[0], done)
    return z_apply(inner, partial, early, late_below, late_above)[1]


def solution(mesh):
    placed = (P("gz", "gx", "gy"),)
    return jax.shard_map(
        local, mesh=mesh, in_specs=placed, out_specs=P("gz", "gx", "gy"), check_vma=False
    )
```

```python
import functools

import jax
import jax.numpy as jnp
import ml_dtypes
import numpy as np
from jax import lax
from jax.experimental import pallas as pl
from jax.experimental.pallas import tpu as pltpu
from jax.sharding import PartitionSpec as P

lift_alpha = -1.586134342
lift_beta = -0.05298011854
lift_gamma = 0.8829110762
lift_delta = 0.4435068522
lift_zeta = 1.149604398

BF = jnp.bfloat16
F32 = jnp.float32
MIB = 1024 * 1024


def periodic_lift(u):
    s, d = u[0::2].copy(), u[1::2].copy()
    d = d + lift_alpha * (s + np.roll(s, -1, 0))
    s = s + lift_beta * (np.roll(d, 1, 0) + d)
    d = d + lift_gamma * (s + np.roll(s, -1, 0))
    s = s + lift_delta * (np.roll(d, 1, 0) + d)
    out = np.empty_like(u)
    out[0::2] = s * lift_zeta
    out[1::2] = d / lift_zeta
    return out


@functools.lru_cache(None)
def blocks(n):
    current = np.eye(4 * n)
    found = []
    for level in range(3):
        full = periodic_lift(current)
        m = n >> level
        rows = full[m : 2 * m]
        found.append((rows[:, n : 2 * n], rows[:, :n], rows[:, 2 * n : 3 * n]))
        current = full[0::2]
    return found


def row_space(outer, rank):
    _, sizes, basis = np.linalg.svd(outer, full_matrices=False)
    assert sizes[rank:].max() < 1e-10
    basis = basis[:rank].copy()
    basis[np.abs(basis) < 1e-12] = 0.0
    return basis


LEFT_RANKS = (2, 3, 4)
RIGHT_RANKS = (2, 3, 3)


@functools.lru_cache(None)
def sides(n):
    out = []
    for level, (main, left, right) in enumerate(blocks(n)):
        cl = row_space(left, LEFT_RANKS[level])
        cr = row_space(right, RIGHT_RANKS[level])
        out.append((main, cl, left @ cl.T, cr, right @ cr.T))
    return out


def nested_space(outer):
    first = row_space(outer[0], 2)
    every = np.concatenate(outer)
    rest = every - every @ first.T @ first
    return np.concatenate([first, row_space(rest, 4)])


@functools.lru_cache(None)
def joint_sides(n):
    found = blocks(n)
    cl = nested_space([b[1] for b in found])
    cr = nested_space([b[2] for b in found])
    maps = [(b[0], b[1] @ cl.T, b[2] @ cr.T) for b in found]
    return cl, cr, maps


def hi_lo(table):
    table = np.asarray(table, np.float32)
    hi = table.astype(ml_dtypes.bfloat16)
    lo = (table - hi.astype(np.float32)).astype(ml_dtypes.bfloat16)
    return hi, lo


def stack_lhs(table):
    hi, lo = hi_lo(table)
    return np.concatenate([hi, lo, hi], axis=1)


def stack_rhs(table):
    hi, lo = hi_lo(table)
    return np.concatenate([hi, hi, lo], axis=0)


def split(values):
    hi = values.astype(BF)
    return hi, (values - hi.astype(F32)).astype(BF)


def dot(a, b):
    return lax.dot_general(a, b, (((1,), (0,)), ((), ())), preferred_element_type=F32)


def dot_t(a, b):
    return lax.dot_general(a, b, (((1,), (1,)), ((), ())), preferred_element_type=F32)


def spread_columns(table, step, width):
    out = np.zeros((table.shape[0], width))
    out[:, ::step] = table
    return out


VM = pl.BlockSpec(memory_space=pltpu.VMEM)
HB = pl.BlockSpec(memory_space=pltpu.HBM)
SHORT = pl.CostEstimate(flops=1000, bytes_accessed=1000, transcendentals=0)


def in_hbm(array):
    return pltpu.with_memory_space_constraint(array, pltpu.HBM)


def vmem(shape, dtype=F32):
    return pltpu.VMEM(shape, dtype)


def params(mib):
    return pltpu.CompilerParams(vmem_limit_bytes=mib * MIB)


def x_send(field):
    nz, nx, ny = field.shape
    cl, cr, _ = joint_sides(nx)
    one = np.concatenate([cl, cr])
    group = 4
    wide = np.kron(np.eye(group), one)
    hi_rows, lo_rows = hi_lo(wide)
    pair = np.concatenate([hi_rows, lo_rows])
    height = 12 * group
    step = 8
    steps = nz // step
    order = [0, steps - 1] + list(range(1, steps - 1))
    _, low, _, high, _ = sides(nz)[0]
    assert np.abs(low[:, :-step]).max() == 0 and np.abs(high[:, step:]).max() == 0

    def kernel(u_hbm, c_hbm, u_ref, out_ref, up_ref, down_ref, c_ref, u_sem, c_sem):
        table_copy = pltpu.make_async_copy(c_hbm, c_ref, c_sem)
        copies = [
            pltpu.make_async_copy(
                u_hbm.at[i * step : i * step + step], u_ref.at[i * step : i * step + step], u_sem.at[i]
            )
            for i in range(steps)
        ]
        table_copy.start()
        for i in order:
            copies[i].start()
        table_copy.wait()
        table = c_ref[...]
        for i in order:
            copies[i].wait()
            for g in range(i * step // group, (i + 1) * step // group):
                hi, lo = split(u_ref[group * g : group * g + group].reshape(group * nx, ny))
                both = dot(table, hi)
                out_ref[height * g : height * g + height, :] = (
                    both[:height] + both[height:] + dot(table[:height], lo)
                )
            if i in order[:2]:
                combos, ref = (high, down_ref) if i == 0 else (low, up_ref)
                for c in range(2):
                    ref[c * nx : c * nx + nx, :] = weighted(
                        [(combos[c, z], lambda z=z: u_ref[z]) for z in range(i * step, (i + 1) * step)]
                    )

    return pl.pallas_call(
        kernel,
        in_specs=[HB, HB],
        out_specs=[VM] * 4,
        out_shape=[vmem((nz, nx, ny)), vmem((nz * 12, ny)), vmem((2 * nx, ny)), vmem((2 * nx, ny))],
        scratch_shapes=[
            pltpu.VMEM(pair.shape, BF),
            pltpu.SemaphoreType.DMA((steps,)),
            pltpu.SemaphoreType.DMA,
        ],
        compiler_params=params(16),
        cost_estimate=SHORT,
        name="x_send",
    )(in_hbm(field), in_hbm(jnp.asarray(pair)))


def x_exchange(message):
    count = lax.axis_size("gx")
    right = [(i, (i + 1) % count) for i in range(count)]
    if count == 2:
        return lax.ppermute(message, "gx", right)
    left = [(j, i) for i, j in right]
    rows, ny = message.shape
    grid = message.reshape(rows // 12, 12, ny)
    from_left = lax.ppermute(grid[:, :6], "gx", right)
    from_right = lax.ppermute(grid[:, 6:], "gx", left)
    return jnp.concatenate([from_left, from_right], axis=1).reshape(rows, ny)


def x_apply(field, halo):
    nz, nx, ny = field.shape
    _, _, maps = joint_sides(nx)
    main = np.concatenate([m for m, _, _ in maps])
    outer = np.concatenate([np.concatenate([l, r], axis=1) for _, l, r in maps])
    pad = np.zeros((main.shape[0], 4))
    tables = np.stack(
        [
            stack_lhs(np.concatenate([main, outer, pad], axis=1)),
            stack_lhs(np.concatenate([main, pad, outer], axis=1)),
        ]
    )
    rows = main.shape[0]
    counts = [nx, nx // 2, nx // 4]
    step = 8
    steps = nz // step

    combos = []
    for level, (_, cl, _, cr, _) in enumerate(sides(ny)):
        both = np.zeros((8, 128))
        assert np.abs(cl[:, : ny - 64]).max() == 0 and np.abs(cr[:, 64:]).max() == 0
        both[: cl.shape[0], 64:] = cl[:, ny - 64 :]
        both[4 : 4 + cr.shape[0], :64] = cr[:, :64]
        combos.append(stack_lhs(both))
    combos = np.stack(combos)

    def kernel(u_ref, r_ref, t_ref, c_ref, x1, x2, x3, right_ref, left_ref, e1, e2, e3):
        i = pl.program_id(0)
        lanes = lax.broadcasted_iota(jnp.int32, (rows, 128), 1)
        for z in range(step):
            start = pl.multiple_of(i * (12 * step) + 24 * (z // 2) + 8 * (z % 2), 8)
            hi, lo = split(u_ref[i * step + z])
            rhi, rlo = split(r_ref[pl.ds(start, 16), :])
            stacked = jnp.concatenate([hi, rhi, hi, rhi, lo, rlo], axis=0)
            got = dot(t_ref[z % 2], stacked)
            edge = jnp.where(lanes < 64, got[:, :128], got[:, ny - 128 :])
            ehi, elo = split(edge)
            estack = jnp.concatenate([ehi, ehi, elo], axis=1)
            at = 0
            for ref, eref, n in zip((x1, x2, x3), (e1, e2, e3), counts):
                where = pl.ds(pl.multiple_of((i * step + z) * n, 16), n)
                ref[i * step + z] = got[at : at + n]
                eref[where, :] = estack[at : at + n]
                at += n

        @pl.when(i == steps - 1)
        def _():
            row = 0
            for level, (eref, n) in enumerate(zip((e1, e2, e3), counts)):
                got = dot_t(c_ref[level], eref[...])
                for j in range(nz * n // 512):
                    for c in range(LEFT_RANKS[level]):
                        right_ref[row : row + 1, :] = got[c : c + 1, 512 * j : 512 * j + 512]
                        if c < RIGHT_RANKS[level]:
                            left_ref[row : row + 1, :] = got[4 + c : 5 + c, 512 * j : 512 * j + 512]
                        else:
                            left_ref[row : row + 1, :] = jnp.zeros((1, 512), F32)
                        row += 1
            right_ref[row:, :] = jnp.zeros((24 - row, 512), F32)
            left_ref[row:, :] = jnp.zeros((24 - row, 512), F32)

    return pl.pallas_call(
        kernel,
        grid=(steps,),
        in_specs=[VM] * 4,
        out_specs=[VM] * 5,
        out_shape=[vmem((nz, n, ny)) for n in counts] + [jax.ShapeDtypeStruct((24, 512), F32)] * 2,
        scratch_shapes=[pltpu.VMEM((nz * n, 384), BF) for n in counts],
        compiler_params=params(24),
        cost_estimate=SHORT,
        name="x_apply",
    )(field, halo, jnp.asarray(tables), jnp.asarray(combos))


def add(a, b):
    if a is None:
        return b
    return a if b is None else a + b


def scale(a, c):
    return None if a is None else a * np.float32(c)


def open_lift(values, first, last):
    get = values.get
    low, high = first // 2 - 3, last // 2 + 4
    s = {i: get(2 * i) for i in range(low, high + 1)}
    d = {i: get(2 * i + 1) for i in range(low, high + 1)}
    pick = lambda t, i: t.get(i)
    d1 = {i: add(d[i], scale(add(s[i], pick(s, i + 1)), lift_alpha)) for i in range(low, high + 1)}
    s1 = {i: add(s[i], scale(add(pick(d1, i - 1), d1[i]), lift_beta)) for i in range(low, high + 1)}
    d2 = {i: add(d1[i], scale(add(s1[i], pick(s1, i + 1)), lift_gamma)) for i in range(low, high + 1)}
    s2 = {i: add(s1[i], scale(add(pick(d2, i - 1), d2[i]), lift_delta)) for i in range(low, high + 1)}
    out = {}
    for z in range(first, last + 1):
        if z % 2:
            out[z] = scale(d2[z // 2], 1.0 / lift_zeta)
        else:
            out[z] = scale(s2[z // 2], lift_zeta)
    return out


def lows(values, first, last):
    got = open_lift(values, 2 * first, 2 * last)
    return {i: got[2 * i] for i in range(first, last + 1) if got[2 * i] is not None}


def own_levels(values, nz, level):
    if level >= 1:
        values = lows(values, -2, nz // 2 + 1)
    if level >= 2:
        values = lows(values, -3, nz // 4 + 2)
    return open_lift(values, 0, (nz >> level) - 1)


def z_tables(nz):
    out = []
    for _, cl, pl_, cr, pr in sides(nz):
        out.append((np.concatenate([cl, cr]), np.concatenate([pl_, pr], axis=1)))
    return out


def weighted(parts):
    total = None
    for scalar, get in parts:
        if abs(scalar) < 1e-12:
            continue
        term = get() * np.float32(scalar)
        total = term if total is None else total + term
    return total


def z_first(x2, x3, halo):
    nz, _, ny = x2.shape
    tables = [t for t, _ in z_tables(nz)]
    counts = [x2.shape[1], x3.shape[1]]
    groups = ny // 128

    def kernel(x2, x3, r_ref, o2, o3, of, y2, y3):
        for level, ref, out, own, table, n in zip((1, 2), (x2, x3), (o2, o3), (y2, y3), tables[1:], counts):

            def body(k, _, level=level, ref=ref, out=out, own=own, table=table, n=n):
                row = pl.multiple_of((k // groups) * 8, 8)
                lane = pl.multiple_of((k % groups) * 128, 128)
                get = {}
                for z in range(nz):
                    get[z] = ref[z, pl.ds(row, 8), pl.ds(lane, 128)]
                for z, value in own_levels(get, nz, level).items():
                    own[z, pl.ds(row, 8), pl.ds(lane, 128)] = value
                for c in range(table.shape[0]):
                    out[pl.ds(pl.multiple_of(c * n + row, 8), 8), pl.ds(lane, 128)] = weighted(
                        [(table[c, z], lambda z=z: get[z]) for z in range(nz)]
                    )
                return 0

            lax.fori_loop(0, (n // 8) * groups, body, 0)
        for c in range(4):
            got = weighted(
                [(tables[0][c, z], lambda z=z: r_ref[12 * z : 12 * z + 12, :]) for z in range(nz)]
            )
            of[4 * c : 4 * c + 2, :] = got[0:2]
            of[4 * c + 2 : 4 * c + 4, :] = got[6:8]

    return pl.pallas_call(
        kernel,
        in_specs=[VM] * 3,
        out_specs=[VM] * 5,
        out_shape=[vmem((t.shape[0] * n, ny)) for t, n in zip(tables[1:], counts)]
        + [vmem((16, ny)), vmem((nz // 2, counts[0], ny)), vmem((nz // 4, counts[1], ny))],
        compiler_params=params(16),
        cost_estimate=SHORT,
        name="z_first",
    )(x2, x3, halo)


def y_tables(ny, spread):
    out = []
    for level, (main, _, left, _, right) in enumerate(sides(ny)):
        step = (1 << level) if spread else 1
        width = ny if spread else ny >> level
        fit = lambda t: spread_columns(t.T, step, width)
        out.append((fit(main), fit(left), fit(right)))
    return out


def halo_rows(level, chunk, nz, counts):
    start = 0
    for below in range(level):
        start += (nz * counts[below] // 512) * LEFT_RANKS[below]
    return start + chunk * LEFT_RANKS[level]


LEFT_AT, RIGHT_AT = 32, 56


def halo_base(left, right, level, nz, counts):
    base = np.zeros((128, left.shape[1]))
    for chunk in range(nz * counts[level] // 512):
        row = halo_rows(level, chunk, nz, counts)
        base[LEFT_AT + row : LEFT_AT + row + left.shape[0]] = left
        base[RIGHT_AT + row : RIGHT_AT + row + right.shape[0]] = right
    return base


def turned(left_ref, right_ref):
    wide = jnp.concatenate(
        [jnp.zeros((LEFT_AT, 512), F32), left_ref[...], right_ref[...], jnp.zeros((48, 512), F32)], axis=0
    )
    return wide.T


def band_tables(level, nz, counts, ny):
    assert ny == 512
    main, left, right = y_tables(ny, True)[level]
    base = halo_base(left, right, level, nz, counts)
    own, edge = [], []
    for j in range(2):
        cols = slice(256 * j, 256 * j + 256)
        own.append(stack_rhs(main[cols, cols]))
        tile = base[:, cols].copy()
        if j == 0:
            tile[:32] = main[256:288, cols]
            assert np.abs(main[288:, cols]).max() == 0
        else:
            tile[96:] = main[224:256, cols]
            assert np.abs(main[:224, cols]).max() == 0
        edge.append(stack_rhs(tile))
    return np.stack(own), np.stack(edge)


def three(values):
    hi, lo = split(values)
    return jnp.concatenate([hi, lo, hi], axis=1)


def banded(rows, edge, own_ref, edge_ref):
    edges = three(edge)
    out = []
    for j in range(2):
        own = three(rows[:, 256 * j : 256 * j + 256])
        out.append(dot(own, own_ref[j]) + dot(edges, edge_ref[j]))
    return jnp.concatenate(out, axis=1)


def plain_edge(rows):
    lanes = lax.broadcasted_iota(jnp.int32, (rows.shape[0], 128), 1)
    before = jnp.where(lanes >= 96, rows[:, 128:256], 0.0)
    return jnp.where(lanes < 32, rows[:, 256:384], before)


def late_rows(side, counts, ny):
    ranks = LEFT_RANKS if side == 0 else RIGHT_RANKS
    parts = [ranks[1] * counts[1] * ny // 256, ranks[2] * counts[2] * ny // 512, ny // 16, 8]
    return [0] + [int(n) for n in np.cumsum(parts)]


def late_heights(counts, ny):
    return (max(late_rows(side, counts, ny)[-1] for side in (0, 1)),) * 2


def y_messages(combined, from_left, from_right, nz, band_one):
    c2, c3, cf = combined
    ny = c2.shape[1]
    tables = z_tables(nz)
    nums = [t.shape[0] for t, _ in tables]
    counts = [2 * c2.shape[0] // nums[1], c2.shape[0] // nums[1], c3.shape[0] // nums[2]]
    mains, halos, coefs = [], [], []
    for level, (main, left, right) in enumerate(y_tables(ny, False)):
        mains.append(stack_rhs(main))
        halos.append(stack_rhs(halo_base(left, right, level, nz, counts)))
        chunks = nz * counts[level] // 512
        per = 512 // counts[level]
        table = tables[level][0]
        coef = np.zeros((nums[level], per, 128), np.float32)
        for c in range(nums[level]):
            for zz in range(per):
                for chunk in range(chunks):
                    row = halo_rows(level, chunk, nz, counts)
                    for lane in range(LEFT_RANKS[level]):
                        for base in (LEFT_AT, RIGHT_AT):
                            coef[c, zz, base + row + lane] = table[c, chunk * per + zz]
        coefs.append(coef.reshape(nums[level] * per, 128))
    places = [late_rows(side, counts, ny) for side in (0, 1)]
    heights = late_heights(counts, ny)

    def kernel(c2, c3, cf, fl, fr, own1, edge1, m2, m3, h2, h3, k1, k2, k3, down_ref, up_ref):
        halo = turned(fl, fr)

        def reduced(k, n, num):
            per = 512 // n
            extra = []
            for c in range(num):
                total = None
                for zz in range(per):
                    if np.abs(coefs_of[n][c * per + zz]).max() > 1e-12:
                        term = halo[zz * n : zz * n + n] * k[c * per + zz : c * per + zz + 1, :]
                        total = term if total is None else total + term
                extra.append(total)
            return extra

        coefs_of = dict(zip(counts, coefs))
        got = []
        for c_ref, m, h, k, n, num in zip((c2, c3), (m2, m3), (h2, h3), (k2, k3), counts[1:], nums[1:]):
            extra = jnp.concatenate(reduced(k, n, num), axis=0)
            got.append(dot(three(c_ref[...]), m[...]) + dot(three(extra), h[...]))
        frame = cf[...]
        frame = banded(frame, plain_edge(frame), own1, edge1)
        ones = reduced(k1, counts[0], 4)
        rows8 = lax.broadcasted_iota(jnp.int32, (8, 128), 0)
        for side, ref in enumerate((up_ref, down_ref)):
            at = places[side]
            for level in (1, 2):
                n, lane_groups = counts[level], (ny >> level) // 128
                ranks = LEFT_RANKS if side == 0 else RIGHT_RANKS
                first = 0 if side == 0 else LEFT_RANKS[level] * n
                row = at[level - 1]
                for c in range(ranks[level]):
                    for p in range(lane_groups):
                        ref[row : row + n, :] = got[level - 1][
                            first + c * n : first + c * n + n, 128 * p : 128 * p + 128
                        ]
                        row += n
            for p in range(ny // 128):
                ref[at[2] + 8 * p : at[2] + 8 * p + 8, :] = frame[
                    8 * side : 8 * side + 8, 128 * p : 128 * p + 128
                ]
            turn = jnp.concatenate(ones[2 * side : 2 * side + 2], axis=0).T
            both = []
            for start in (LEFT_AT, RIGHT_AT):
                v = turn[start : start + 8]
                v = v + pltpu.roll(v, 4, 0)
                both.append(v + pltpu.roll(v, 2, 0))
            ref[at[3] : at[4], :] = jnp.where(rows8 < 2, both[0], both[1])
            if heights[side] > at[4]:
                ref[at[4] :, :] = jnp.zeros((heights[side] - at[4], 128), F32)

    return pl.pallas_call(
        kernel,
        in_specs=[VM] * 14,
        out_specs=[VM] * 2,
        out_shape=[vmem((height, 128)) for height in reversed(heights)],
        compiler_params=params(24),
        cost_estimate=SHORT,
        name="y_messages",
    )(
        c2,
        c3,
        cf,
        from_left,
        from_right,
        *band_one,
        *[jnp.asarray(t) for t in mains[1:]],
        *[jnp.asarray(t) for t in halos[1:]],
        *[jnp.asarray(t) for t in coefs],
    )


def touched_layers(nz):
    one, two, three = [np.abs(p).max(axis=1) > 1e-12 for _, p in z_tables(nz)]
    hit = lambda z: one[z] or (z % 2 == 0 and two[z // 2]) or (z % 4 == 0 and three[z // 4])
    return [z for z in range(nz) if hit(z)]


def main_part(xs, from_left, from_right, bands):
    nz, nx, ny = xs[0].shape
    counts = [nx, nx // 2, nx // 4]
    changed = touched_layers(nz)
    untouched = [z for z in range(nz) if z not in changed]
    groups = ny // 128
    masks = []
    for level in range(3):
        chunks = nz * counts[level] // 512
        per = 512 // counts[level]
        lanes_of = np.zeros((chunks, 128))
        for chunk in range(chunks):
            row = halo_rows(level, chunk, nz, counts)
            for base in (LEFT_AT, RIGHT_AT):
                lanes_of[chunk, base + row : base + row + LEFT_RANKS[level]] = 1.0
        if level == 0:
            masks.append(lanes_of)
        else:
            own = sides(nz)[level][0]
            lanes = np.einsum("ocz,cl->ozl", own.reshape(own.shape[0], chunks, per), lanes_of)
            masks.append(lanes.reshape(-1, 128))
    masks = [np.concatenate([m, np.zeros((-m.shape[0] % 8, 128))]).astype(np.float32) for m in masks]

    def kernel(x1, x2, x3, fl, fr, o1, e1, o2, e2, o3, e3, k1, k2, k3, out_ref, done_ref, hbm, w2, halo_ref, sem):
        halo_ref[...] = turned(fl, fr)
        lanes = lax.broadcasted_iota(jnp.int32, (8, 128), 1)
        wide = lax.broadcasted_iota(jnp.int32, (32, 128), 1)
        after, before = wide < 32, wide >= 96

        def in_y(x, level, row, tall, own, edge, mk):
            n = counts[level]
            per = 512 // n
            layers = nz >> level
            values = x[:, row : row + tall, :]
            turns = [halo_ref[zz * n + row : zz * n + row + tall, :] for zz in range(per)]
            edges = []
            for z in range(layers):
                if level == 0:
                    turn = turns[z % per] * mk[z // per : z // per + 1, :]
                else:
                    turn = None
                    for zz in range(per):
                        if np.abs(masks[level][z * per + zz]).max() > 1e-12:
                            turn = add(turn, turns[zz] * mk[z * per + zz : z * per + zz + 1, :])
                edges.append(
                    jnp.where(
                        after[:tall],
                        values[z, :, 256:384],
                        jnp.where(before[:tall], values[z, :, 128:256], turn),
                    )
                )
            got = banded(
                values.reshape(layers * tall, ny), jnp.concatenate(edges, axis=0), own, edge
            )
            return {z: got[tall * z : tall * z + tall] for z in range(layers)}

        def store(to, values, row, indices, height=None):
            for z in indices:
                for q in range(groups):
                    piece = values[z][:, 128 * q : 128 * q + 128]
                    tall = piece.shape[0]
                    if height is None:
                        to[q, z, row : row + tall, :] = piece
                    else:
                        to[q, z * height + row : z * height + row + tall, :] = piece

        for row in range(0, counts[0], 16):
            got = own_levels(in_y(x1, 0, row, 16, o1, e1, k1), nz, 0)
            store(out_ref, got, row, range(nz))

        def leaving(layers):
            return [
                pltpu.make_async_copy(
                    out_ref.at[q, z], hbm.at[z, :, 128 * q : 128 * q + 128], sem.at[z]
                )
                for z in layers
                for q in range(groups)
            ]

        copies = leaving([z for z in untouched if z % 2])
        for copy in copies:
            copy.start()

        store(w2, in_y(x2, 1, 0, counts[1], o2, e2, k2), 0, range(nz // 2), counts[1])
        got = in_y(x3, 2, 0, counts[2], o3, e3, k3)
        for z in range(nz // 4):
            for row in range(0, counts[2], 8):
                where = pl.ds(2 * z * counts[1] + 2 * row, 8, stride=2)
                for q in range(groups):
                    piece = got[z][row : row + 8, 128 * q : 128 * q + 128]
                    w2[q, where, :] = jnp.where(lanes % 4 == 0, piece, w2[q, where, :])

        def merge(k, _):
            row = pl.multiple_of((k // groups) * 8, 8)
            q = k % groups
            where = pl.ds(2 * row, 8, stride=2)
            for z in range(nz // 2):
                inner = w2[q, pl.ds(pl.multiple_of(z * counts[1] + row, 8), 8), :]
                out_ref[q, 2 * z, where, :] = jnp.where(lanes % 2 == 0, inner, out_ref[q, 2 * z, where, :])
            return 0

        lax.fori_loop(0, (counts[1] // 8) * groups, merge, 0)
        done_ref[...] = jnp.zeros((8, 128), F32)
        for copy in copies:
            copy.wait()

    flat = [t for band in bands for t in band]
    return pl.pallas_call(
        kernel,
        in_specs=[VM] * 14,
        out_specs=[VM, VM, HB],
        out_shape=[
            vmem((groups, nz, nx, 128)),
            vmem((8, 128)),
            pltpu.HBM((nz, nx, ny), F32),
        ],
        scratch_shapes=[
            pltpu.VMEM((groups, nz // 2 * counts[1], 128), F32),
            pltpu.VMEM((512, 128), F32),
            pltpu.SemaphoreType.DMA((nz,)),
        ],
        compiler_params=params(32),
        cost_estimate=SHORT,
        name="main_part",
    )(*xs, from_left, from_right, *flat, *[jnp.asarray(m) for m in masks])


def early_part(below, above, band, after):
    nx, ny = below.shape[0] // 2, below.shape[1]
    _, _, maps = joint_sides(nx)

    def kernel(b1, a1, o1, e1, xt, after_ref, w_ref):
        del after_ref
        early = []
        for ref in (b1, a1):
            for c in range(2):
                hi, lo = split(ref[c * nx : c * nx + nx, :])
                early.append(dot(xt[...], jnp.concatenate([hi, hi, lo], axis=0)))
        early = jnp.concatenate(early, axis=0)
        w_ref[...] = banded(early, plain_edge(early), o1, e1)

    return pl.pallas_call(
        kernel,
        in_specs=[VM] * 6,
        out_specs=VM,
        out_shape=vmem((4 * nx, ny)),
        compiler_params=params(16),
        cost_estimate=SHORT,
        name="early_part",
    )(below, above, *band, jnp.asarray(stack_lhs(maps[0][0])), after)


def z_apply(inner, partial, early, from_left, from_right):
    groups, nz, nx, _ = inner.shape
    ny = groups * 128
    maps = [p for _, p in z_tables(nz)]
    counts = [nx, nx // 2, nx // 4]
    tables = []
    for level in (1, 2):
        width = ny >> level
        hi = spread_columns(np.eye(width), 1 << level, ny).astype(ml_dtypes.bfloat16)
        tables.append(np.concatenate([hi, hi]))
    places = [late_rows(side, counts, ny) for side in (0, 1)]
    _, _, x_maps = joint_sides(nx)
    frame = np.zeros((4 * nx, 16))
    for c in range(4):
        frame[c * nx : c * nx + nx, 4 * c : 4 * c + 2] = x_maps[0][1][:, :2]
        frame[c * nx : c * nx + nx, 4 * c + 2 : 4 * c + 4] = x_maps[0][2][:, :2]
        assert np.abs(x_maps[0][1][:, 2:]).max() < 1e-12 and np.abs(x_maps[0][2][:, 2:]).max() < 1e-12
    _, left, right = y_tables(ny, True)[0]
    side_hi, side_lo = hi_lo(np.concatenate([left, right, np.zeros((4, ny))]))
    side_rows = np.concatenate([side_hi, side_hi, side_lo, np.zeros((104, ny), side_hi.dtype)])
    touched = sorted(touched_layers(nz), key=lambda z: np.abs(maps[0][z]).max() > 1e-12)
    left_over = [z for z in range(0, nz, 2) if z not in touched]

    def kernel(in_ref, base_hbm, w_ref, fr, fl, t2, t3, xf, yf, io_ref, out_hbm, s1, s2, s3, sem):
        del base_hbm
        copies = []
        for slot, z in enumerate(left_over):
            for q in range(groups):
                copy = pltpu.make_async_copy(
                    io_ref.at[q, z], out_hbm.at[z, :, 128 * q : 128 * q + 128], sem.at[len(touched) + slot]
                )
                copy.start()
                copies.append(copy)
        s3[...] = jnp.zeros(s3.shape, F32)
        halos = [
            jnp.concatenate([ref[at[2] + 8 * p : at[2] + 8 * p + 8, :] for p in range(groups)], axis=1)
            for ref, at in zip((fl, fr), places)
        ]
        hi, lo = split(jnp.concatenate(halos, axis=0))
        none = jnp.zeros((104, 128), F32)
        turn = []
        for ref, at in zip((fl, fr), places):
            values = ref[at[3] : at[4], :]
            high = values.astype(BF).astype(F32)
            turn.append(jnp.concatenate([high, values - high, high, none], axis=0).T.astype(BF))
        left_hand = jnp.concatenate([jnp.concatenate(turn, axis=0), xf[...]], axis=1)
        first = w_ref[...] + dot(left_hand, jnp.concatenate([yf[...], hi, hi, lo], axis=0))
        for c in range(4):
            for q in range(groups):
                s1[c, q] = first[c * nx : c * nx + nx, 128 * q : 128 * q + 128]
        for level, table, to in ((1, t2, s2), (2, t3, s3)):
            n, lane_groups = counts[level], (ny >> level) // 128
            pieces = []
            for side, ref in enumerate((fl, fr)):
                row = places[side][level - 1]
                for c in range((LEFT_RANKS, RIGHT_RANKS)[side][level]):
                    pieces.append(
                        jnp.concatenate(
                            [ref[row + p * n : row + p * n + n, :] for p in range(lane_groups)], axis=1
                        )
                    )
                    row += lane_groups * n
            flat = jnp.concatenate(pieces, axis=0)
            hi, lo = split(flat)
            got = dot(jnp.concatenate([hi, lo], axis=1), table[...])
            for c in range(LEFT_RANKS[level] + RIGHT_RANKS[level]):
                start = c * n
                for q in range(groups):
                    piece = got[start : start + n, 128 * q : 128 * q + 128]
                    if level == 1:
                        to[c, q] = piece
                    else:
                        to[c, q, pl.ds(0, n, stride=2), :] = piece

        lanes = lax.broadcasted_iota(jnp.int32, (8, 128), 1)
        even_lane = lanes % 2 == 0
        third_cell = (lax.broadcasted_iota(jnp.int32, (8, 128), 0) % 2 + lanes % 4) == 0

        def summed(table_row, get):
            total = None
            for c, scalar in enumerate(table_row):
                if abs(scalar) > 1e-12:
                    total = add(total, get(c) * np.float32(scalar))
            return total

        for slot, z in enumerate(touched):

            for t in range(nx // 16):
                full, half = 16 * t, 8 * t
                for q in range(groups):
                    if z % 2:
                        for more in (0, 8):
                            rows = pl.ds(full + more, 8)
                            extra = summed(maps[0][z], lambda c: s1[c, q, rows, :])
                            io_ref[q, z, rows, :] = add(in_ref[q, z, rows, :], extra)
                        continue
                    evens = pl.ds(16 * t, 8, stride=2)
                    odds = pl.ds(16 * t + 1, 8, stride=2)
                    extra = summed(maps[0][z], lambda c: s1[c, q, odds, :])
                    if extra is not None:
                        io_ref[q, z, odds, :] = add(in_ref[q, z, odds, :], extra)
                    rows = pl.ds(half, 8)
                    extra = summed(maps[1][z // 2], lambda c: s2[c, q, rows, :])
                    if z % 4 == 0:
                        third = summed(maps[2][z // 4], lambda c: s3[c, q, rows, :])
                        third = 0.0 if third is None else third
                        extra = jnp.where(third_cell, third, 0.0 if extra is None else extra)
                    one = summed(maps[0][z], lambda c: s1[c, q, evens, :])
                    if one is not None:
                        extra = jnp.where(even_lane, 0.0 if extra is None else extra, one)
                    io_ref[q, z, evens, :] = add(in_ref[q, z, evens, :], extra)
            for q in range(groups):
                copy = pltpu.make_async_copy(
                    io_ref.at[q, z], out_hbm.at[z, :, 128 * q : 128 * q + 128], sem.at[slot]
                )
                copy.start()
                copies.append(copy)
        for copy in copies:
            copy.wait()

    return pl.pallas_call(
        kernel,
        in_specs=[VM, HB] + [VM] * 7,
        out_specs=[VM, HB],
        out_shape=[vmem(inner.shape), jax.ShapeDtypeStruct((nz, nx, ny), F32)],
        input_output_aliases={0: 0, 1: 1},
        scratch_shapes=[
            pltpu.VMEM((4, groups, nx, 128), F32),
            pltpu.VMEM((maps[1].shape[1], groups, nx // 2, 128), F32),
            pltpu.VMEM((maps[2].shape[1], groups, nx // 2, 128), F32),
            pltpu.SemaphoreType.DMA((len(touched) + len(left_over),)),
        ],
        compiler_params=params(24),
        name="z_apply",
    )(
        inner,
        partial,
        early,
        from_right,
        from_left,
        *[jnp.asarray(t) for t in tables],
        jnp.asarray(stack_lhs(frame)),
        jnp.asarray(side_rows),
    )


def swap(to_right, to_left, axis):
    count = lax.axis_size(axis)
    right = [(i, (i + 1) % count) for i in range(count)]
    left = [(j, i) for i, j in right]
    return lax.ppermute(to_right, axis, right), lax.ppermute(to_left, axis, left)


def local(field):
    nz, nx, ny = field.shape
    counts = [nx, nx // 2, nx // 4]
    bands = [[jnp.asarray(t) for t in band_tables(level, nz, counts, ny)] for level in range(3)]
    field, message, up, down = x_send(field)
    halo = x_exchange(message)
    below, above = swap(up, down, "gz")
    x1, x2, x3, to_right, to_left = x_apply(field, halo)
    from_left, from_right = swap(to_right, to_left, "gy")
    *combined, own2, own3 = z_first(x2, x3, halo)
    down, up = y_messages(combined, from_left, from_right, nz, bands[0])
    late_below, late_above = swap(up, down, "gz")
    inner, done, partial = main_part((x1, own2, own3), from_left, from_right, bands)
    early = early_part(below, above, bands[0], done)
    return z_apply(inner, partial, early, late_below, late_above)[1]


def solution(mesh):
    placed = (P("gz", "gx", "gy"),)
    return jax.shard_map(
        local, mesh=mesh, in_specs=placed, out_specs=P("gz", "gx", "gy"), check_vma=False
    )
```
